128 devices in a mesh: seq: 8 (over z, y_hi), fsdp: 16 (over y_lo, x, core).
Axes of the slice: x: 4, y: 4 (y_hi: 2, y_lo: 2; y = y_hi * 2 + y_lo), z: 4, core: 2. Of those that a mesh axis runs over, the one named last changes fastest.
Arguments:
- inputs: bfloat16 [16, 1024, 1024], P('fsdp', 'seq'), may hold values from -6 to 6
- doc_starts: int32 [16, 2], P('fsdp'), may hold values from 1 to 1023, as said below
- route: int32 [16, 8, 128], P('fsdp', 'seq'), may hold values from 0 to 127, each once within a row
- norm_gain: bfloat16 [2, 1024], P(None, 'fsdp'), may hold values from 0.5 to 1.5
- norm_bias: bfloat16 [2, 1024], P(None, 'fsdp'), may hold values from -1 to 1
- w_qkv: bfloat16 [1024, 3072], P('fsdp'), may hold values from -0.1875 to 0.1875
- w_out: bfloat16 [1024, 1024], P('fsdp'), may hold values from -0.75 to 0.75
- w_up: bfloat16 [1024, 4096], P('fsdp'), may hold values from -0.1875 to 0.1875
- w_down: bfloat16 [4096, 1024], P('fsdp'), may hold values from -0.09375 to 0.09375
- exp_gain: bfloat16 [16, 2, 1024], P('fsdp'), may hold values from 0.5 to 1.5
- exp_bias: bfloat16 [16, 2, 1024], P('fsdp'), may hold values from -1 to 1
- exp_in: bfloat16 [16, 2, 1024, 4096], P('fsdp', None, None, 'seq'), may hold values from -0.1875 to 0.1875
- exp_out: bfloat16 [16, 2, 4096, 1024], P('fsdp', None, 'seq'), may hold values from -0.09375 to 0.09375
- centroid: bfloat16 [16, 1024], P('fsdp'), may hold values from -0.1875 to 0.1875
- cotangent: bfloat16 [16, 1024, 1024], P('fsdp', 'seq'), may hold values from -6 to 6
Outputs:
- result: bfloat16 [16, 1024, 1024], P('fsdp', 'seq')
- grad_input: float32 [16, 1024, 1024], P('fsdp', 'seq')
- grad_norm_gain: float32 [2, 1024], P(None, 'fsdp')
- grad_norm_bias: float32 [2, 1024], P(None, 'fsdp')
- grad_qkv: float32 [1024, 3072], P('fsdp')
- grad_out: float32 [1024, 1024], P('fsdp')
- grad_up: float32 [1024, 4096], P('fsdp')
- grad_down: float32 [4096, 1024], P('fsdp')
- grad_exp_gain: float32 [16, 2, 1024], P('fsdp')
- grad_exp_bias: float32 [16, 2, 1024], P('fsdp')
- grad_exp_in: float32 [16, 2, 1024, 4096], P('fsdp', None, None, 'seq')
- grad_exp_out: float32 [16, 2, 4096, 1024], P('fsdp', None, 'seq')
- grad_centroid: float32 [16, 1024], P('fsdp')
The draws below stay inside these ranges and needn't reach their ends.
Inputs may be any that keep to these rules, and one draw needn't show every extreme that they name: `doc_starts`: in each sequence column 0 lies within the first 128 positions and column 1 within the last 128 positions, so the second document runs from the first device of seq to the last. `route`: each device's row is a permutation of its 128 tokens' slots; slot p belongs to expert p // 8, so every device sends each expert exactly 8 tokens.
All inputs are finite; a program needn't handle non-finite values.
Results may differ from the reference program's by a relative error of at most 0.024.
Values may be sent and summed in bfloat16 or wider, within the bound.
A program may use at most 192 MiB of HBM per device.

```python
from functools import partial
import jax
import jax.numpy as jnp
from jax import lax

D = 1024
HEADS = 16
HEAD = 64
FF = 4096
EFF = 4096
LEN = 1024
SEQS = 1
TOK_DEV = 128
BATCH = 16
EXPERTS = 16
SLOT = 8
N_SEQ = 8


def draw_doc_starts(key, part):
    key = jax.random.fold_in(key, 7)
    first_key, last_key = jax.random.split(key)
    local_len = TOK_DEV // SEQS
    first = jax.random.randint(first_key, (BATCH, 1), 1, local_len)
    last = jax.random.randint(last_key, (BATCH, 1), LEN - local_len + 1, LEN)
    return jnp.concatenate([first, last], axis=1).astype(jnp.int32)


def raised(values, key, source, target, parts, factor):
    owner, partner = [(jnp.arange(values.shape[axis_at]) // (values.shape[axis_at] // parts)).reshape([-1 if axis == axis_at else 1 for axis in range(values.ndim)]) for axis_at in (source, target)]
    chosen = jax.random.permutation(key, parts)[partner]
    strong = (owner == chosen) | (owner == (partner + parts // 2) % parts)
    return jnp.where(strong, factor * values, values)


def steps_of(stream_key, shape, cuts, low, largest):
    level, own = 1.0, jax.random.fold_in(stream_key, 6)
    for axis_at, parts in cuts:
        steps = jnp.exp(jax.random.uniform(jax.random.fold_in(own, axis_at), (parts,), jnp.float32, low / len(cuts), largest / len(cuts)))
        level = level * jnp.repeat(steps, shape[axis_at] // parts).reshape([-1 if axis == axis_at else 1 for axis in range(len(shape))])
    return level


def bell_draw(key, shape, scale, most, pieces=(), kind=jnp.bfloat16):
    drawn = jax.random.normal(key, shape, jnp.float32) * scale
    if len(pieces) > 0:
        drawn = steps_of(key, shape, pieces, -0.22, 0.18) * drawn
    return jnp.clip(drawn, min=-most, max=most).astype(kind)


def noise_with(rng, extent, scale, reach, cuts, heavy, held_as=jnp.bfloat16):
    values = scale * jax.random.normal(rng, extent, jnp.float32)
    if cuts:
        values = values * steps_of(rng, extent, cuts, -0.22, 0.18)
    return jnp.clip(raised(values, jax.random.fold_in(rng, 3), *heavy), -reach, reach).astype(held_as)


def setup_inputs(seed: int = 0) -> dict:
    seeds = jax.random.split(jax.random.key(seed), 16)
    inputs = noise_with(seeds[0], (BATCH, LEN, D), 1.0, 6.0, ((0, 16), (1, 8)), (0, 2, 16, 2.0))
    doc_starts = draw_doc_starts(jax.random.fold_in(seeds[15], 71), 0)
    route = jax.vmap(lambda own: jax.random.permutation(own, TOK_DEV))(jax.random.split(seeds[2], EXPERTS * N_SEQ)).reshape((EXPERTS, N_SEQ, TOK_DEV)).astype(jnp.int32)
    norm_gain = jnp.clip(1.0 + 0.1 * jax.random.normal(seeds[3], (2, D), jnp.float32), 0.5, 1.5).astype(jnp.bfloat16)
    norm_bias = bell_draw(seeds[4], (2, D), 0.2, 1.0, ((1, 16),))
    w_qkv = bell_draw(seeds[5], (D, 3 * D), D ** -0.5, 0.1875, ((0, 16),))
    w_out = bell_draw(seeds[6], (D, D), (D // 16) ** -0.5, 0.75, ((0, 16),))
    w_up = bell_draw(seeds[7], (D, FF), D ** -0.5, 0.1875, ((0, 16),))
    w_down = bell_draw(seeds[8], (FF, D), FF ** -0.5, 0.09375, ((0, 16),))
    exp_gain = jnp.clip(1.0 + 0.1 * jax.random.normal(seeds[9], (EXPERTS, 2, D), jnp.float32), 0.5, 1.5).astype(jnp.bfloat16)
    exp_bias = bell_draw(seeds[10], (EXPERTS, 2, D), 0.2, 1.0, ((0, 16),))
    exp_in = bell_draw(seeds[11], (EXPERTS, 2, D, EFF), D ** -0.5, 0.1875, ((0, 16), (3, 8)))
    exp_out = bell_draw(seeds[12], (EXPERTS, 2, EFF, D), EFF ** -0.5, 0.09375, ((0, 16), (2, 8)))
    centroid = bell_draw(seeds[13], (EXPERTS, D), D ** -0.5, 0.1875, ((0, 16),))
    cotangent = bell_draw(seeds[14], (BATCH, LEN, D), 1.0, 6.0, ((0, 16), (1, 8)))
    return {"inputs": inputs, "doc_starts": doc_starts, "route": route, "norm_gain": norm_gain, "norm_bias": norm_bias, "w_qkv": w_qkv, "w_out": w_out, "w_up": w_up, "w_down": w_down, "exp_gain": exp_gain, "exp_bias": exp_bias, "exp_in": exp_in, "exp_out": exp_out, "centroid": centroid, "cotangent": cotangent}


@jax.custom_vjp
def low(v):
    return lax.optimization_barrier(v.astype(jnp.bfloat16)).astype(jnp.float32)

@jax.custom_vjp
def low_back(v):
    return v

def low_keep(v):
    return (low(v), None)

def low_pass(kept, grad):
    return (grad,)

def back_keep(v):
    return (v, None)

def back_low(kept, grad):
    return (low(grad),)
low.defvjp(low_keep, low_pass)
low_back.defvjp(back_keep, back_low)
epsilon = 1e-05
highest = lax.Precision.HIGHEST
masked_score = -1e+30

def norm_rows(values, gain, offset):
    average = lax.optimization_barrier(jnp.mean(values, axis=-1, keepdims=True))
    centered = values - average
    spread = lax.optimization_barrier(jnp.mean(centered * centered, axis=-1, keepdims=True))
    return centered * lax.rsqrt(spread + epsilon) * gain + offset

def documents(position, starts):
    return (position >= starts[0]).astype(jnp.int32) + (position >= starts[1]).astype(jnp.int32)

def attend_one(packed_item):
    queries, keys, values, starts = packed_item
    position = jnp.arange(LEN, dtype=jnp.int32)
    labels = documents(position, starts)
    allowed = (position[None, :] <= position[:, None]) & (labels[None, :] == labels[:, None])
    scores = jnp.einsum('qhd,khd->hqk', queries, keys, precision=highest) * HEAD ** (-0.5)
    scores = low_back(scores)
    scores = jnp.where(allowed[None], scores, masked_score)
    row_max = lax.optimization_barrier(jnp.max(scores, axis=-1, keepdims=True))
    weights = jnp.exp(scores - row_max)
    probs = weights / lax.optimization_barrier(jnp.sum(weights, axis=-1, keepdims=True))
    return jnp.einsum('hqk,khd->qhd', low(probs), values, precision=highest)

def expert_one(packed_item):
    rows, gain, offset, weight_in, weight_out, centre = packed_item
    stream = rows
    for sublayer in range(2):
        normed = low(norm_rows(stream, gain[sublayer], offset[sublayer]))
        pre_act = low_back(jnp.dot(normed, weight_in[sublayer], precision=highest))
        acted = low(jax.nn.gelu(pre_act))
        stream = stream + low_back(jnp.dot(acted, weight_out[sublayer], precision=highest))
    gating = jax.nn.sigmoid(jnp.dot(rows, centre, precision=highest))[:, None]
    return low(rows + gating * (stream - rows))

def layer_forward(doc_starts, route, inputs, norm_gain, norm_bias, w_qkv, w_out, w_up, w_down, exp_gain, exp_bias, exp_in, exp_out, centroid):
    rows_in = inputs.reshape(BATCH * LEN, D)
    normed_one = low(norm_rows(rows_in, norm_gain[0], norm_bias[0]))
    packed = low_back(low(jnp.dot(normed_one, w_qkv, precision=highest)))
    packed = packed.reshape(BATCH, LEN, 3, HEADS, HEAD)
    mixed = lax.map(jax.checkpoint(attend_one), (packed[:, :, 0], packed[:, :, 1], packed[:, :, 2], doc_starts))
    mixed = low_back(low(mixed.reshape(BATCH * LEN, D)))
    after = rows_in + low_back(jnp.dot(mixed, w_out, precision=highest))
    normed_two = low(norm_rows(after, norm_gain[1], norm_bias[1]))
    pre_dense = low_back(jnp.dot(normed_two, w_up, precision=highest))
    acted = low(jax.nn.gelu(pre_dense))
    hidden = low_back(low(after + low_back(jnp.dot(acted, w_down, precision=highest))))
    local_len = LEN // N_SEQ
    blocks = hidden.reshape(EXPERTS, SEQS, N_SEQ, local_len, D).transpose(0, 2, 1, 3, 4).reshape(EXPERTS, N_SEQ, TOK_DEV, D)
    inverse = jnp.argsort(route, axis=-1).astype(jnp.int32)
    slots = jnp.take_along_axis(blocks, inverse[..., None], axis=2)
    grouped = slots.reshape(EXPERTS, N_SEQ, EXPERTS, SLOT, D).transpose(2, 1, 0, 3, 4).reshape(EXPERTS, N_SEQ * EXPERTS * SLOT, D)
    outputs = lax.map(jax.checkpoint(expert_one), (grouped, exp_gain, exp_bias, exp_in, exp_out, centroid))
    returned = outputs.reshape(EXPERTS, N_SEQ, EXPERTS, SLOT, D).transpose(2, 1, 0, 3, 4).reshape(EXPERTS, N_SEQ, TOK_DEV, D)
    tokens_out = jnp.take_along_axis(returned, route[..., None], axis=2)
    return tokens_out.reshape(EXPERTS, N_SEQ, SEQS, local_len, D).transpose(0, 2, 1, 3, 4).reshape(BATCH, LEN, D)

def reference(inputs, doc_starts, route, norm_gain, norm_bias, w_qkv, w_out, w_up, w_down, exp_gain, exp_bias, exp_in, exp_out, centroid, cotangent):
    floats = tuple((array.astype(jnp.float32) for array in (inputs, norm_gain, norm_bias, w_qkv, w_out, w_up, w_down, exp_gain, exp_bias, exp_in, exp_out, centroid)))
    result, pull = jax.vjp(partial(layer_forward, doc_starts, route), *floats)
    grads = pull(cotangent.astype(jnp.float32))
    return (result.astype(jnp.bfloat16), grads[0], grads[1], grads[2], grads[3], grads[4], grads[5], grads[6], grads[7], grads[8], grads[9], grads[10], grads[11])
```

```python
import jax
import jax.numpy as jnp
from jax import lax
from jax.experimental import pallas as pl
from jax.experimental.pallas import tpu as pltpu
from jax.sharding import PartitionSpec as P

HEADS = 16


MESH = pl.DeviceIdType.MESH
epsilon = 1e-05
masked_score = -1e30


def norm_rows(values, gain, offset):
    average = jnp.mean(values, axis=-1, keepdims=True)
    centered = values - average
    spread = jnp.mean(centered * centered, axis=-1, keepdims=True)
    return centered * lax.rsqrt(spread + epsilon) * gain + offset


def labels_of(position, starts):
    return (position[None, :] >= starts[:, 0:1]).astype(jnp.int32) + (
        position[None, :] >= starts[:, 1:2]
    ).astype(jnp.int32)


def row_product(left, right, pattern):
    return jnp.einsum(pattern, left, right, preferred_element_type=jnp.float32)


def gelu_back(pre_act, grad_acted):
    unused, slope_pull = jax.vjp(jax.nn.gelu, pre_act)
    return slope_pull(grad_acted)[0]


def split_sum(values):
    return jnp.sum(values, axis=-1, keepdims=True)


def norm_parts(values):
    average = split_sum(values) * (1.0 / values.shape[-1])
    centered = values - average
    spread = split_sum(centered * centered) * (1.0 / values.shape[-1])
    scale = lax.rsqrt(spread + epsilon)
    return centered * scale, scale


def norm_back(grad_normed, gain, xhat, scale):
    width = 1.0 / xhat.shape[-1]
    u = grad_normed * gain
    return scale * (u - split_sum(u) * width - xhat * (split_sum(u * xhat) * width))


def gelu_parts(pre):
    inner = 0.7978845608028654
    cubic = 0.044715
    square = pre * pre
    t = jnp.tanh(inner * pre * (1.0 + cubic * square))
    half = 0.5 * (1.0 + t)
    slope = half + 0.5 * pre * (1.0 - t * t) * (inner * (1.0 + 3.0 * cubic * square))
    return pre * half, slope


def nn(a, b):
    return lax.dot_general(a, b, (((1,), (0,)), ((), ())), preferred_element_type=jnp.float32)


def nt(a, b):
    return lax.dot_general(a, b, (((1,), (1,)), ((), ())), preferred_element_type=jnp.float32)


def tn(a, b):
    return lax.dot_general(a, b, (((0,), (0,)), ((), ())), preferred_element_type=jnp.float32)


def place():
    s, f = lax.axis_index("seq"), lax.axis_index("fsdp")
    return lax.div(s, 2), lax.rem(s, 2), f, lax.rem(f, 2)


def block(index):
    return pl.ds(pl.multiple_of(index * 128, 128), 128)


def order(i):
    return i + lax.div(i, 2) - 2 * lax.div(i, 3)


class Line:
    def __init__(self, send, recv):
        self.z, self.yh, self.f, self.c = place()
        self.send, self.recv = send, recv

    def index(self, d):
        return lax.rem(self.z + d, 4)

    def copy(self, phase, d, src, dst):
        return pltpu.make_async_remote_copy(
            src_ref=src,
            dst_ref=dst,
            send_sem=self.send.at[phase, d - 1],
            recv_sem=self.recv.at[phase, d - 1],
            device_id=(2 * self.index(d) + self.yh, self.f),
            device_id_type=MESH,
        )

    def spread(self, phase, buf):
        for d in (1, 3, 2):
            self.copy(phase, d, buf.at[block(self.z)], buf.at[block(self.z)]).start()

    def arrived(self, phase, d, buf):
        dst = buf.at[block(self.index(d))]
        pltpu.make_async_remote_copy(
            src_ref=dst,
            dst_ref=dst,
            send_sem=self.send.at[phase, 3 - d],
            recv_sem=self.recv.at[phase, 3 - d],
            device_id=(2 * self.index(d) + self.yh, self.f),
            device_id_type=MESH,
        ).wait_recv()

    def give(self, phase, d, src, dst):
        self.copy(phase, d, src.at[block(self.index(d))], dst.at[block(self.z)]).start()

    def sent(self, phase, buf):
        for d in (1, 3, 2):
            self.copy(phase, d, buf.at[block(self.z)], buf.at[block(self.z)]).wait_send()

    def total(self, phase, own, parts):
        acc = own[block(self.z), :].astype(jnp.float32)
        for d in (1, 3, 2):
            self.arrived(phase, d, parts)
            acc += parts[block(self.index(d)), :].astype(jnp.float32)
        return acc


class Columns:
    def __init__(self, send, recv):
        self.z, self.yh, self.f, self.c = place()
        self.m = self.f - self.c + self.yh
        self.send, self.recv = send, recv

    def device(self, q):
        return (2 * self.z + lax.rem(q, 2), q - lax.rem(q, 2) + self.c)

    def piece(self, q):
        return pl.ds(pl.multiple_of(q * 16, 16), 16)

    def copy(self, phase, d, src, dst):
        q = lax.rem(self.m + d, 16)
        return pltpu.make_async_remote_copy(
            src_ref=src.at[self.piece(q)],
            dst_ref=dst.at[self.piece(self.m)],
            send_sem=self.send.at[phase, d - 1],
            recv_sem=self.recv.at[phase, d - 1],
            device_id=self.device(q),
            device_id_type=MESH,
        )

    def start(self, phase, src, dst):
        def one(i, carry):
            self.copy(phase, i + 1, src, dst).start()
            return carry

        lax.fori_loop(0, 15, one, 0)
        dst[self.piece(self.m), :] = src[self.piece(self.m), :]

    def wait(self, phase, src, dst):
        def one(i, carry):
            q = lax.rem(self.m + 15 - i, 16)
            pltpu.make_async_remote_copy(
                src_ref=dst.at[self.piece(q)],
                dst_ref=dst.at[self.piece(q)],
                send_sem=self.send.at[phase, i],
                recv_sem=self.recv.at[phase, i],
                device_id=self.device(q),
                device_id_type=MESH,
            ).wait_recv()
            return carry

        lax.fori_loop(0, 15, one, 0)

    def sent(self, phase, src, dst):
        def one(i, carry):
            self.copy(phase, i + 1, src, dst).wait_send()
            return carry

        lax.fori_loop(0, 15, one, 0)


def placings(route):
    row = lax.broadcasted_iota(jnp.int32, (256, 128), 0)
    inner = row & 15
    slot = (row >> 4) * 8 + (inner & 7)
    hit = slot == route
    left = jnp.where(hit & (inner < 8), 1.0, 0.0).astype(jnp.bfloat16)
    right = jnp.where(hit & (inner >= 8), 1.0, 0.0).astype(jnp.bfloat16)
    return left, right


def to_pieces(left, right, rows):
    half = rows.shape[1] // 2
    return (nn(left, rows[:, :half]) + nn(right, rows[:, half:])).astype(jnp.bfloat16)


def from_pieces(left, right, pieces):
    return jnp.concatenate([tn(left, pieces), tn(right, pieces)], axis=1).astype(jnp.bfloat16)


def rows_of(pieces):
    wide = pieces.astype(jnp.float32).reshape(16, 2, 8, 512)
    return jnp.concatenate([wide[:, 0].reshape(128, 512), wide[:, 1].reshape(128, 512)], axis=1)


def pieces_of(rows):
    left = rows[:, :512].reshape(16, 1, 8, 512)
    right = rows[:, 512:].reshape(16, 1, 8, 512)
    return jnp.concatenate([left, right], axis=1).reshape(256, 512).astype(jnp.bfloat16)


def expert_kernel(
    hid, cot, route, vec, in_a, in_b, out_a, out_b,
    res, gh, vecg, gin, gout,
    w_in, w_out, sendh, sendc, sendr, sendg, arrh, arrc, arrr, arrg,
    e0, e1, g0, g1, ps0, ps1, pr0, pr1, pb0, pb1,
    act0, act1, dg0, dg1, gp0, gp1,
    arrived, cota, base, xh0, xh1, sc,
    ga_in, ga_out, sb_in, sb_out, rb_in, rb_out,
    wsem, zs, zr, cs, cr, ks, kr, osem,
):
    line, cols = Line(zs, zr), Columns(cs, cr)
    z, yh, f, c = place()
    other = (lax.axis_index("seq"), f + 1 - 2 * c)
    bar = pltpu.get_barrier_semaphore()

    def greet(i, carry):
        pl.semaphore_signal(bar, inc=1, device_id=cols.device(lax.rem(cols.m + i + 1, 16)), device_id_type=MESH)
        return carry

    lax.fori_loop(0, 15, greet, 0)
    for d in (1, 2, 3):
        pl.semaphore_signal(bar, inc=1, device_id=(2 * line.index(d) + yh, f), device_id_type=MESH)
    pl.semaphore_signal(bar, inc=1, device_id=other, device_id_type=MESH)
    loads = []
    for k in range(2):
        loads += [
            pltpu.make_async_copy(in_a.at[k], w_in.at[k, :, 0:512], wsem.at[k, 0]),
            pltpu.make_async_copy(in_b.at[k], w_in.at[k, :, 512:1024], wsem.at[k, 1]),
            pltpu.make_async_copy(out_a.at[k], w_out.at[k, 0:512, :], wsem.at[k, 2]),
            pltpu.make_async_copy(out_b.at[k], w_out.at[k, 512:1024, :], wsem.at[k, 3]),
        ]
    for load in loads:
        load.start()
    left, right = placings(route[0:1, :])
    sendh[...] = to_pieces(left, right, hid[...])
    sendc[...] = to_pieces(left, right, cot[...])
    pl.semaphore_wait(bar, 19)
    cols.start(0, sendh, arrh)
    cols.start(1, sendc, arrc)
    cols.wait(0, sendh, arrh)
    gain = [vec[0:1, :], vec[1:2, :]]
    bias = [vec[2:3, :], vec[3:4, :]]
    rows = rows_of(arrh[...])
    arrived[...] = rows
    xhat, scale = norm_parts(rows)
    xh0[...] = xhat
    sc[0] = jnp.broadcast_to(scale, (128, 128))
    e0[block(z), :] = (xhat * gain[0] + bias[0]).astype(jnp.bfloat16)
    line.spread(0, e0)
    cols.wait(1, sendc, arrc)
    coti = rows_of(arrc[...])
    cota[...] = coti
    gating = jax.nn.sigmoid(split_sum(arrived[...] * vec[4:5, :]))
    sc[2] = jnp.broadcast_to(gating, (128, 128))
    g1[block(z), :] = (gating * coti).astype(jnp.bfloat16)
    line.spread(3, g1)
    for load in loads:
        load.wait()

    def forward(k, j, rows_in, act, dg):
        values = rows_in[block(j), :]
        for n in range(4):
            tile = slice(n * 256, (n + 1) * 256)
            pre = nn(values, w_in[k, :, tile])
            acted, slope = gelu_parts(pre)
            act[block(j), tile] = acted.astype(jnp.bfloat16)
            dg[block(j), tile] = slope

    def project(k, j, act, part):
        values = act[block(j), :]
        for n in range(4):
            tile = slice(n * 256, (n + 1) * 256)
            part[block(j), tile] = nn(values, w_out[k, :, tile]).astype(jnp.bfloat16)

    def backward(k, j, grad, dg, gp, part):
        values = grad[block(j), :]
        for n in range(4):
            tile = slice(n * 256, (n + 1) * 256)
            slope = dg[block(j), tile] * nt(values, w_out[k, tile, :])
            gp[block(j), tile] = slope.astype(jnp.bfloat16)
        pres = gp[block(j), :]
        for n in range(4):
            tile = slice(n * 256, (n + 1) * 256)
            part[block(j), tile] = nt(pres, w_in[k, tile, :]).astype(jnp.bfloat16)

    def sub0(i, carry):
        d = order(i)
        j = line.index(d)

        @pl.when(i > 0)
        def _():
            line.arrived(0, d, e0)

        forward(0, j, e0, act0, dg0)
        project(0, j, act0, ps0)

        @pl.when(i > 0)
        def _():
            line.give(1, d, ps0, pr0)

        return carry

    lax.fori_loop(0, 4, sub0, 0)
    stream = arrived[...] + line.total(1, ps0, pr0)
    base[...] = stream
    xhat, scale = norm_parts(stream)
    xh1[...] = xhat
    sc[1] = jnp.broadcast_to(scale, (128, 128))
    e1[block(z), :] = (xhat * gain[1] + bias[1]).astype(jnp.bfloat16)
    line.spread(2, e1)
    line.sent(1, ps0)

    def sub1(i, carry):
        d = order(i)
        j = line.index(d)

        @pl.when(i > 0)
        def _():
            line.arrived(2, d, e1)
            line.arrived(3, d, g1)

        forward(1, j, e1, act1, dg1)
        backward(1, j, g1, dg1, gp1, ps0)

        @pl.when(i > 0)
        def _():
            line.give(4, d, ps0, pb1)

        project(1, j, act1, ps1)

        @pl.when(i > 0)
        def _():
            line.give(5, d, ps1, pr1)

        return carry

    lax.fori_loop(0, 4, sub1, 0)

    def weight_grads(k, rows_in, gp, act, grad):
        def one(n, carry):
            tile = pl.ds(pl.multiple_of(n * 256, 256), 256)
            tile_b = pl.ds(pl.multiple_of(n * 256 + 512, 256), 256)
            ga_out[k, tile, :] = tn(act[:, tile], grad[...])
            sb_out[k, tile, :] = tn(act[:, tile_b], grad[...]).astype(jnp.bfloat16)
            return carry

        lax.fori_loop(0, 2, one, 0)

        def two(n, carry):
            tile = pl.ds(pl.multiple_of(n * 256, 256), 256)
            ga_in[k, tile, :] = tn(rows_in[:, tile], gp[:, 0:512])
            sb_in[k, tile, :] = tn(rows_in[:, tile], gp[:, 512:1024]).astype(jnp.bfloat16)
            return carry

        lax.fori_loop(0, 4, two, 0)

    def swap(k, i, src, dst):
        return pltpu.make_async_remote_copy(
            src_ref=src.at[k],
            dst_ref=dst.at[k],
            send_sem=ks.at[k, i],
            recv_sem=kr.at[k, i],
            device_id=other,
            device_id_type=MESH,
        )

    weight_grads(1, e1, gp1, act1, g1)
    swap(1, 0, sb_in, rb_in).start()
    swap(1, 1, sb_out, rb_out).start()
    grad_normed = line.total(4, ps0, pb1)
    grad_stream = sc[2][:, 0:1] * cota[...]
    grad_stream += norm_back(grad_normed, gain[1], xh1[...], sc[1][:, 0:1])
    g0[block(z), :] = grad_stream.astype(jnp.bfloat16)
    line.spread(6, g0)
    vecg[1:2, :] = jnp.sum(grad_normed * xh1[...], axis=0, keepdims=True)
    vecg[3:4, :] = jnp.sum(grad_normed, axis=0, keepdims=True)
    line.sent(4, ps0)
    stream = base[...] + line.total(5, ps1, pr1)
    base[...] = grad_stream
    gate = sc[2][:, 0:1]
    diff = stream - arrived[...]
    sendr[...] = pieces_of(arrived[...] + gate * diff)
    grad_gating = split_sum(cota[...] * diff)
    grad_logit = gate * (1.0 - gate) * grad_gating
    vecg[4:5, :] = jnp.sum(grad_logit * arrived[...], axis=0, keepdims=True)
    sc[3] = jnp.broadcast_to(grad_logit, (128, 128))

    def sub0_back(i, carry):
        d = order(i)
        j = line.index(d)

        @pl.when(i > 0)
        def _():
            line.arrived(6, d, g0)

        backward(0, j, g0, dg0, gp0, ps0)

        @pl.when(i > 0)
        def _():
            line.give(7, d, ps0, pb0)

        return carry

    lax.fori_loop(0, 4, sub0_back, 0)
    cols.start(2, sendr, arrr)
    weight_grads(0, e0, gp0, act0, g0)
    swap(0, 0, sb_in, rb_in).start()
    swap(0, 1, sb_out, rb_out).start()
    grad_normed = line.total(7, ps0, pb0)
    vecg[0:1, :] = jnp.sum(grad_normed * xh0[...], axis=0, keepdims=True)
    vecg[2:3, :] = jnp.sum(grad_normed, axis=0, keepdims=True)
    grad_stream = base[...] + norm_back(grad_normed, gain[0], xh0[...], sc[0][:, 0:1])
    grad_stream += (1.0 - sc[2][:, 0:1]) * cota[...] + sc[3][:, 0:1] * vec[4:5, :]
    sendg[...] = pieces_of(grad_stream)
    cols.start(3, sendg, arrg)
    cols.wait(3, sendg, arrg)
    left, right = placings(route[0:1, :])
    gh[...] = from_pieces(left, right, arrg[...])
    cols.wait(2, sendr, arrr)
    res[...] = from_pieces(left, right, arrr[...])
    stores = []
    for k in (1, 0):
        swap(k, 0, sb_in, rb_in).wait_recv()
        swap(k, 1, sb_out, rb_out).wait_recv()
        ga_in[k] += rb_in[k].astype(jnp.float32)
        ga_out[k] += rb_out[k].astype(jnp.float32)
        stores += [
            pltpu.make_async_copy(ga_in.at[k], gin.at[k], osem.at[k, 0]),
            pltpu.make_async_copy(ga_out.at[k], gout.at[k], osem.at[k, 1]),
        ]
        stores[-1].start()
        stores[-2].start()
    vecg[5:8, :] = jnp.zeros((3, 1024), jnp.float32)
    for k in (0, 1):
        swap(k, 0, sb_in, rb_in).wait_send()
        swap(k, 1, sb_out, rb_out).wait_send()
    line.sent(0, e0)
    line.sent(2, e1)
    line.sent(3, g1)
    line.sent(5, ps1)
    line.sent(6, g0)
    line.sent(7, ps0)
    cols.sent(0, sendh, arrh)
    cols.sent(1, sendc, arrc)
    cols.sent(2, sendr, arrr)
    cols.sent(3, sendg, arrg)
    for store in stores:
        store.wait()


def expert_call(hid, cot, route, vec, in_a, in_b, out_a, out_b):
    bf, f32 = jnp.bfloat16, jnp.float32
    vmem, anywhere = pl.BlockSpec(memory_space=pltpu.VMEM), pl.BlockSpec(memory_space=pl.ANY)
    line = [pltpu.VMEM((512, 1024), bf)]
    rows = [pltpu.VMEM((128, 1024), f32)]
    piece = [pltpu.VMEM((256, 512), bf)]
    wide = [pltpu.VMEM((512, 1024), f32)]
    return pl.pallas_call(
        expert_kernel,
        out_shape=(
            jax.ShapeDtypeStruct((128, 1024), bf),
            jax.ShapeDtypeStruct((128, 1024), bf),
            jax.ShapeDtypeStruct((8, 1024), f32),
            jax.ShapeDtypeStruct((2, 1024, 512), f32),
            jax.ShapeDtypeStruct((2, 512, 1024), f32),
        ),
        in_specs=[vmem] * 4 + [anywhere] * 4,
        out_specs=(vmem, vmem, vmem, anywhere, anywhere),
        scratch_shapes=[
            pltpu.VMEM((2, 1024, 1024), bf),
            pltpu.VMEM((2, 1024, 1024), bf),
            *(piece * 8),
            *(line * 10),
            *(line * 2),
            *(wide * 2),
            *(line * 2),
            *(rows * 5),
            pltpu.VMEM((4, 128, 128), f32),
            pltpu.VMEM((2, 1024, 512), f32),
            pltpu.VMEM((2, 512, 1024), f32),
            pltpu.VMEM((2, 1024, 512), bf),
            pltpu.VMEM((2, 512, 1024), bf),
            pltpu.VMEM((2, 1024, 512), bf),
            pltpu.VMEM((2, 512, 1024), bf),
            pltpu.SemaphoreType.DMA((2, 4)),
            pltpu.SemaphoreType.DMA((8, 3)),
            pltpu.SemaphoreType.DMA((8, 3)),
            pltpu.SemaphoreType.DMA((4, 15)),
            pltpu.SemaphoreType.DMA((4, 15)),
            pltpu.SemaphoreType.DMA((2, 2)),
            pltpu.SemaphoreType.DMA((2, 2)),
            pltpu.SemaphoreType.DMA((2, 2)),
        ],
        compiler_params=pltpu.CompilerParams(
            collective_id=1, has_side_effects=True, vmem_limit_bytes=60 << 20
        ),
        name="experts",
    )(hid, cot, route, vec, in_a, in_b, out_a, out_b)


def on_device(
    inputs,
    doc_starts,
    route,
    norm_gain,
    norm_bias,
    w_qkv,
    w_out,
    w_up,
    w_down,
    exp_gain,
    exp_bias,
    exp_in,
    exp_out,
    centroid,
    cotangent,
):
    seq_count, local_len, model_width = inputs.shape
    tok_rows = seq_count * local_len
    head_count = HEADS
    head_width = model_width // head_count
    score_scale = head_width ** (-0.5)
    gains, offsets, qkv_weight, out_weight, up_weight, down_weight = (
        lax.all_gather(norm_gain, "fsdp", axis=1, tiled=True),
        lax.all_gather(norm_bias, "fsdp", axis=1, tiled=True),
        lax.all_gather(w_qkv, "fsdp", axis=0, tiled=True),
        lax.all_gather(w_out, "fsdp", axis=0, tiled=True),
        lax.all_gather(w_up, "fsdp", axis=0, tiled=True),
        lax.all_gather(w_down, "fsdp", axis=0, tiled=True),
    )
    rows_in = inputs.reshape(tok_rows, model_width).astype(jnp.float32)
    normed_one = norm_rows(
        rows_in, gains[0].astype(jnp.float32), offsets[0].astype(jnp.float32)
    ).astype(jnp.bfloat16)
    packed = jnp.dot(normed_one, qkv_weight, preferred_element_type=jnp.float32).astype(
        jnp.bfloat16
    )
    packed = packed.reshape(seq_count, local_len, 3, model_width)
    queries = packed[:, :, 0]
    keys_all, values_all = (
        lax.all_gather(packed[:, :, 1], "seq", axis=1, tiled=True),
        lax.all_gather(packed[:, :, 2], "seq", axis=1, tiled=True),
    )
    key_len = keys_all.shape[1]
    query_pos = lax.axis_index("seq") * local_len + jnp.arange(local_len, dtype=jnp.int32)
    key_pos = jnp.arange(key_len, dtype=jnp.int32)
    allowed = (key_pos[None, None, :] <= query_pos[None, :, None]) & (
        labels_of(key_pos, doc_starts)[:, None, :] == labels_of(query_pos, doc_starts)[:, :, None]
    )
    allowed = allowed[:, None]
    query_heads = queries.reshape(seq_count, local_len, head_count, head_width)
    key_heads = keys_all.reshape(seq_count, key_len, head_count, head_width)
    value_heads = values_all.reshape(seq_count, key_len, head_count, head_width)
    scores = (
        jnp.einsum("sqhd,skhd->shqk", query_heads, key_heads, preferred_element_type=jnp.float32)
        * score_scale
    )
    scores = jnp.where(allowed, scores, masked_score)
    row_max = jnp.max(scores, axis=-1, keepdims=True)
    weights = jnp.exp(scores - row_max)
    row_sum = jnp.sum(weights, axis=-1, keepdims=True)
    log_total = row_max + jnp.log(row_sum)
    probs_low = (weights / row_sum).astype(jnp.bfloat16)
    mixed = jnp.einsum(
        "shqk,skhd->sqhd", probs_low, value_heads, preferred_element_type=jnp.float32
    )
    mixed = mixed.reshape(tok_rows, model_width).astype(jnp.bfloat16)
    after = rows_in + jnp.dot(mixed, out_weight, preferred_element_type=jnp.float32)
    normed_two = norm_rows(
        after, gains[1].astype(jnp.float32), offsets[1].astype(jnp.float32)
    ).astype(jnp.bfloat16)
    pre_dense = jnp.dot(normed_two, up_weight, preferred_element_type=jnp.float32)
    acted = jax.nn.gelu(pre_dense).astype(jnp.bfloat16)
    hidden = (after + jnp.dot(acted, down_weight, preferred_element_type=jnp.float32)).astype(
        jnp.bfloat16
    )
    swap_pairs = []
    core_pairs = []
    for s in range(8):
        for f in range(16):
            same = s % 2 == f % 2
            partner = s * 16 + f if same else (s + 1 - 2 * (s % 2)) * 16 + f + 1 - 2 * (f % 2)
            swap_pairs.append((s * 16 + f, partner))
            core_pairs.append((s * 16 + f, s * 16 + f + 1 - 2 * (f % 2)))
    both = ("seq", "fsdp")
    in_a = lax.ppermute(exp_in[0], both, swap_pairs)
    out_a = lax.ppermute(exp_out[0], both, swap_pairs)
    in_b = lax.ppermute(in_a, both, core_pairs)
    out_b = lax.ppermute(out_a, both, core_pairs)
    mine = lax.rem(lax.axis_index("seq"), 2) == lax.rem(lax.axis_index("fsdp"), 2)
    vec = jnp.concatenate([exp_gain[0], exp_bias[0], centroid], axis=0)
    vec = jnp.where(mine, vec, lax.ppermute(vec, both, core_pairs)).astype(jnp.float32)
    vec = jnp.pad(vec, ((0, 3), (0, 0)))
    result, grad_hidden, vec_grads, grad_in, grad_out_e = expert_call(
        hidden, cotangent.reshape(tok_rows, model_width), route.reshape(1, tok_rows), vec, in_a, in_b, out_a, out_b
    )
    result = result.reshape(seq_count, local_len, model_width)
    grad_exp_in = jnp.where(
        mine, grad_in, lax.ppermute(grad_in.astype(jnp.bfloat16), both, swap_pairs).astype(jnp.float32)
    )[None]
    grad_exp_out = jnp.where(
        mine, grad_out_e, lax.ppermute(grad_out_e.astype(jnp.bfloat16), both, swap_pairs).astype(jnp.float32)
    )[None]
    vec_grads = vec_grads[:5].astype(jnp.bfloat16)
    vec_grads = vec_grads.astype(jnp.float32) + lax.ppermute(vec_grads, both, core_pairs).astype(jnp.float32)
    upper = lax.rem(lax.axis_index("seq"), 2) == 1
    vec_grads = jnp.stack([jnp.where(upper, 0.0, vec_grads), jnp.where(upper, vec_grads, 0.0)])
    gains, offsets, qkv_weight, out_weight, up_weight, down_weight = (
        lax.all_gather(norm_gain, "fsdp", axis=1, tiled=True),
        lax.all_gather(norm_bias, "fsdp", axis=1, tiled=True),
        lax.all_gather(w_qkv, "fsdp", axis=0, tiled=True),
        lax.all_gather(w_out, "fsdp", axis=0, tiled=True),
        lax.all_gather(w_up, "fsdp", axis=0, tiled=True),
        lax.all_gather(w_down, "fsdp", axis=0, tiled=True),
    )
    grad_down = jnp.einsum("rf,rd->fd", acted, grad_hidden, preferred_element_type=jnp.float32)
    grad_acted = jnp.einsum(
        "rd,fd->rf", grad_hidden, down_weight, preferred_element_type=jnp.float32
    )
    grad_pre_dense = gelu_back(pre_dense, grad_acted).astype(jnp.bfloat16)
    grad_up = jnp.einsum(
        "rd,rf->df", normed_two, grad_pre_dense, preferred_element_type=jnp.float32
    )
    grad_normed_two = jnp.einsum(
        "rf,df->rd", grad_pre_dense, up_weight, preferred_element_type=jnp.float32
    )
    unused, norm_pull = jax.vjp(
        norm_rows, after, gains[1].astype(jnp.float32), offsets[1].astype(jnp.float32)
    )
    grad_after_norm, gain_two_grad, bias_two_grad = norm_pull(grad_normed_two)
    grad_after = grad_hidden.astype(jnp.float32) + grad_after_norm
    grad_attn = grad_after.astype(jnp.bfloat16)
    grad_out = jnp.einsum("rd,re->de", mixed, grad_attn, preferred_element_type=jnp.float32)
    grad_mixed = jnp.einsum(
        "re,de->rd", grad_attn, out_weight, preferred_element_type=jnp.float32
    ).astype(jnp.bfloat16)
    grad_mixed = grad_mixed.reshape(seq_count, local_len, head_count, head_width)
    scores = (
        jnp.einsum("sqhd,skhd->shqk", query_heads, key_heads, preferred_element_type=jnp.float32)
        * score_scale
    )
    scores = jnp.where(allowed, scores, masked_score)
    probs = jnp.exp(scores - log_total)
    grad_probs = jnp.einsum(
        "sqhd,skhd->shqk", grad_mixed, value_heads, preferred_element_type=jnp.float32
    )
    grad_values = jnp.einsum(
        "shqk,sqhd->skhd",
        probs.astype(jnp.bfloat16),
        grad_mixed,
        preferred_element_type=jnp.float32,
    )
    row_dot = jnp.sum(grad_probs * probs, axis=-1, keepdims=True)
    grad_scores = (probs * (grad_probs - row_dot)).astype(jnp.bfloat16)
    grad_queries = (
        jnp.einsum("shqk,skhd->sqhd", grad_scores, key_heads, preferred_element_type=jnp.float32)
        * score_scale
    )
    grad_keys = (
        jnp.einsum("shqk,sqhd->skhd", grad_scores, query_heads, preferred_element_type=jnp.float32)
        * score_scale
    )
    grad_keys, grad_values = (
        lax.psum_scatter(
            grad_keys.reshape(seq_count, key_len, model_width).astype(jnp.bfloat16),
            "seq",
            scatter_dimension=1,
            tiled=True,
        ).astype(jnp.float32),
        lax.psum_scatter(
            grad_values.reshape(seq_count, key_len, model_width).astype(jnp.bfloat16),
            "seq",
            scatter_dimension=1,
            tiled=True,
        ).astype(jnp.float32),
    )
    grad_queries = grad_queries.reshape(seq_count, local_len, model_width).astype(jnp.bfloat16)
    grad_packed = jnp.stack(
        [grad_queries, grad_keys.astype(jnp.bfloat16), grad_values.astype(jnp.bfloat16)], axis=2
    )
    grad_packed = grad_packed.reshape(tok_rows, 3 * model_width)
    grad_qkv = jnp.einsum("rd,re->de", normed_one, grad_packed, preferred_element_type=jnp.float32)
    grad_normed_one = jnp.einsum(
        "re,de->rd", grad_packed, qkv_weight, preferred_element_type=jnp.float32
    )
    unused, norm_pull = jax.vjp(
        norm_rows, rows_in, gains[0].astype(jnp.float32), offsets[0].astype(jnp.float32)
    )
    grad_rows_in, gain_one_grad, bias_one_grad = norm_pull(grad_normed_one)
    grad_input = (grad_after + grad_rows_in).reshape(seq_count, local_len, model_width)
    dense_terms = (
        jnp.stack([gain_one_grad, gain_two_grad]),
        jnp.stack([bias_one_grad, bias_two_grad]),
        grad_qkv,
        grad_out,
        grad_up,
        grad_down,
    )
    shard_gain, shard_bias, shard_qkv, shard_out, shard_up, shard_down = (
        lax.psum_scatter(
            dense_terms[0].astype(jnp.bfloat16), "fsdp", scatter_dimension=1, tiled=True
        ).astype(jnp.float32),
        lax.psum_scatter(
            dense_terms[1].astype(jnp.bfloat16), "fsdp", scatter_dimension=1, tiled=True
        ).astype(jnp.float32),
        lax.psum_scatter(
            dense_terms[2].astype(jnp.bfloat16), "fsdp", scatter_dimension=0, tiled=True
        ).astype(jnp.float32),
        lax.psum_scatter(
            dense_terms[3].astype(jnp.bfloat16), "fsdp", scatter_dimension=0, tiled=True
        ).astype(jnp.float32),
        lax.psum_scatter(
            dense_terms[4].astype(jnp.bfloat16), "fsdp", scatter_dimension=0, tiled=True
        ).astype(jnp.float32),
        lax.psum_scatter(
            dense_terms[5].astype(jnp.bfloat16), "fsdp", scatter_dimension=0, tiled=True
        ).astype(jnp.float32),
    )
    summed = (
        lax.psum(shard_gain.astype(jnp.bfloat16), "seq").astype(jnp.float32),
        lax.psum(shard_bias.astype(jnp.bfloat16), "seq").astype(jnp.float32),
        lax.psum(shard_qkv.astype(jnp.bfloat16), "seq").astype(jnp.float32),
        lax.psum(shard_out.astype(jnp.bfloat16), "seq").astype(jnp.float32),
        lax.psum(shard_up.astype(jnp.bfloat16), "seq").astype(jnp.float32),
        lax.psum(shard_down.astype(jnp.bfloat16), "seq").astype(jnp.float32),
        lax.psum(vec_grads.astype(jnp.bfloat16), "seq").astype(jnp.float32),
    )
    own = jnp.where(lax.rem(lax.axis_index("fsdp"), 2) == 1, summed[6][1], summed[6][0])
    return (
        result,
        grad_input,
        summed[0],
        summed[1],
        summed[2],
        summed[3],
        summed[4],
        summed[5],
        own[None, 0:2],
        own[None, 2:4],
        grad_exp_in,
        grad_exp_out,
        own[4:5],
    )


def solution(mesh):
    in_specs = (
        P("fsdp", "seq", None),
        P("fsdp", None),
        P("fsdp", "seq", None),
        P(None, "fsdp"),
        P(None, "fsdp"),
        P("fsdp", None),
        P("fsdp", None),
        P("fsdp", None),
        P("fsdp", None),
        P("fsdp", None, None),
        P("fsdp", None, None),
        P("fsdp", None, None, "seq"),
        P("fsdp", None, "seq", None),
        P("fsdp", None),
        P("fsdp", "seq", None),
    )
    out_specs = (
        P("fsdp", "seq", None),
        P("fsdp", "seq", None),
        P(None, "fsdp"),
        P(None, "fsdp"),
        P("fsdp", None),
        P("fsdp", None),
        P("fsdp", None),
        P("fsdp", None),
        P("fsdp", None, None),
        P("fsdp", None, None),
        P("fsdp", None, None, "seq"),
        P("fsdp", None, "seq", None),
        P("fsdp", None),
    )
    return jax.shard_map(
        on_device, mesh=mesh, in_specs=in_specs, out_specs=out_specs, check_vma=False
    )
```

```python
import jax
import jax.numpy as jnp
from jax import lax
from jax.experimental import pallas as pl
from jax.experimental.pallas import tpu as pltpu
from jax.sharding import PartitionSpec as P

MESH = pl.DeviceIdType.MESH
epsilon = 1e-05
masked_score = -1e30


def split_sum(values):
    return jnp.sum(values, axis=-1, keepdims=True)


def norm_parts(values):
    average = split_sum(values) * (1.0 / values.shape[-1])
    centered = values - average
    spread = split_sum(centered * centered) * (1.0 / values.shape[-1])
    scale = lax.rsqrt(spread + epsilon)
    return centered * scale, scale


def norm_back(grad_normed, gain, xhat, scale):
    width = 1.0 / xhat.shape[-1]
    u = grad_normed * gain
    return scale * (u - split_sum(u) * width - xhat * (split_sum(u * xhat) * width))


def gelu_parts(pre):
    inner = 0.7978845608028654
    cubic = 0.044715
    square = pre * pre
    t = jnp.tanh(inner * pre * (1.0 + cubic * square))
    half = 0.5 * (1.0 + t)
    slope = half + 0.5 * pre * (1.0 - t * t) * (inner * (1.0 + 3.0 * cubic * square))
    return pre * half, slope


def nn(a, b):
    return lax.dot_general(a, b, (((1,), (0,)), ((), ())), preferred_element_type=jnp.float32)


def nt(a, b):
    return lax.dot_general(a, b, (((1,), (1,)), ((), ())), preferred_element_type=jnp.float32)


def tn(a, b):
    return lax.dot_general(a, b, (((0,), (0,)), ((), ())), preferred_element_type=jnp.float32)


def place():
    s, f = lax.axis_index("seq"), lax.axis_index("fsdp")
    return lax.div(s, 2), lax.rem(s, 2), f, lax.rem(f, 2)


def block(index):
    return pl.ds(pl.multiple_of(index * 128, 128), 128)


def order(i):
    return i + lax.div(i, 2) - 2 * lax.div(i, 3)


class Line:
    def __init__(self, send, recv):
        self.z, self.yh, self.f, self.c = place()
        self.send, self.recv = send, recv

    def index(self, d):
        return lax.rem(self.z + d, 4)

    def copy(self, phase, d, src, dst):
        return pltpu.make_async_remote_copy(
            src_ref=src,
            dst_ref=dst,
            send_sem=self.send.at[phase, d - 1],
            recv_sem=self.recv.at[phase, d - 1],
            device_id=(2 * self.index(d) + self.yh, self.f),
            device_id_type=MESH,
        )

    def spread(self, phase, buf):
        for d in (1, 3, 2):
            self.copy(phase, d, buf.at[block(self.z)], buf.at[block(self.z)]).start()

    def arrived(self, phase, d, buf):
        dst = buf.at[block(self.index(d))]
        pltpu.make_async_remote_copy(
            src_ref=dst,
            dst_ref=dst,
            send_sem=self.send.at[phase, 3 - d],
            recv_sem=self.recv.at[phase, 3 - d],
            device_id=(2 * self.index(d) + self.yh, self.f),
            device_id_type=MESH,
        ).wait_recv()

    def give(self, phase, d, src, dst):
        self.copy(phase, d, src.at[block(self.index(d))], dst.at[block(self.z)]).start()

    def sent(self, phase, buf):
        for d in (1, 3, 2):
            self.copy(phase, d, buf.at[block(self.z)], buf.at[block(self.z)]).wait_send()

    def total(self, phase, own, parts):
        acc = own[block(self.z), :].astype(jnp.float32)
        for d in (1, 3, 2):
            self.arrived(phase, d, parts)
            acc += parts[block(self.index(d)), :].astype(jnp.float32)
        return acc


class Columns:
    def __init__(self, send, recv):
        self.z, self.yh, self.f, self.c = place()
        self.m = self.f - self.c + self.yh
        self.send, self.recv = send, recv

    def device(self, q):
        return (2 * self.z + lax.rem(q, 2), q - lax.rem(q, 2) + self.c)

    def piece(self, q):
        return pl.ds(pl.multiple_of(q * 16, 16), 16)

    def copy(self, phase, d, src, dst):
        q = lax.rem(self.m + d, 16)
        return pltpu.make_async_remote_copy(
            src_ref=src.at[self.piece(q)],
            dst_ref=dst.at[self.piece(self.m)],
            send_sem=self.send.at[phase, d - 1],
            recv_sem=self.recv.at[phase, d - 1],
            device_id=self.device(q),
            device_id_type=MESH,
        )

    def start(self, phase, src, dst):
        def one(i, carry):
            self.copy(phase, i + 1, src, dst).start()
            return carry

        lax.fori_loop(0, 15, one, 0)
        dst[self.piece(self.m), :] = src[self.piece(self.m), :]

    def wait(self, phase, src, dst):
        def one(i, carry):
            q = lax.rem(self.m + 15 - i, 16)
            pltpu.make_async_remote_copy(
                src_ref=dst.at[self.piece(q)],
                dst_ref=dst.at[self.piece(q)],
                send_sem=self.send.at[phase, i],
                recv_sem=self.recv.at[phase, i],
                device_id=self.device(q),
                device_id_type=MESH,
            ).wait_recv()
            return carry

        lax.fori_loop(0, 15, one, 0)

    def sent(self, phase, src, dst):
        def one(i, carry):
            self.copy(phase, i + 1, src, dst).wait_send()
            return carry

        lax.fori_loop(0, 15, one, 0)


def placings(route):
    row = lax.broadcasted_iota(jnp.int32, (256, 128), 0)
    inner = row & 15
    slot = (row >> 4) * 8 + (inner & 7)
    hit = slot == route
    left = jnp.where(hit & (inner < 8), 1.0, 0.0).astype(jnp.bfloat16)
    right = jnp.where(hit & (inner >= 8), 1.0, 0.0).astype(jnp.bfloat16)
    return left, right


def to_pieces(left, right, rows):
    half = rows.shape[1] // 2
    return (nn(left, rows[:, :half]) + nn(right, rows[:, half:])).astype(jnp.bfloat16)


def from_pieces(left, right, pieces):
    return jnp.concatenate([tn(left, pieces), tn(right, pieces)], axis=1).astype(jnp.bfloat16)


def rows_of(pieces):
    wide = pieces.astype(jnp.float32).reshape(16, 2, 8, 512)
    return jnp.concatenate([wide[:, 0].reshape(128, 512), wide[:, 1].reshape(128, 512)], axis=1)


def pieces_of(rows):
    left = rows[:, :512].reshape(16, 1, 8, 512)
    right = rows[:, 512:].reshape(16, 1, 8, 512)
    return jnp.concatenate([left, right], axis=1).reshape(256, 512).astype(jnp.bfloat16)


def expert_kernel(
    hid, cot, route, vec, exp_in, exp_out, in_a, out_a,
    res, gh, vecg, gin, gout,
    w_in, w_out, sendh, sendc, sendr, sendg, arrh, arrc, arrr, arrg,
    e0, e1, g0, g1, ps0, ps1, pr0, pr1, pb0, pb1,
    act0, act1, dg0, dg1, gp0, gp1,
    arrived, cota, base, xh0, xh1, sc,
    ga_in, ga_out, sb_in, sb_out, rb_in, rb_out, vmine, vcore, vline, vsum, vswap,
    wsem, zs, zr, cs, cr, ks, kr, osem, bs, br, ss, sr, vs, vr,
):
    line, cols = Line(zs, zr), Columns(cs, cr)
    z, yh, f, c = place()
    other = (lax.axis_index("seq"), f + 1 - 2 * c)
    swap_mate = (2 * z + 1 - yh, f + 1 - 2 * c)
    bar = pltpu.get_barrier_semaphore()

    def meet(i, carry):
        greet(bar, cols.device(lax.rem(cols.m + i + 1, 16)))
        return carry

    lax.fori_loop(0, 15, meet, 0)
    for d in (1, 2, 3):
        greet(bar, (2 * line.index(d) + yh, f))
    greet(bar, other)
    greet(bar, swap_mate)
    same = c == yh

    def slot(k, i, half):
        return w_in.at[k, :, half] if i == 0 else w_out.at[k, half, :]

    low, high = slice(0, 512), slice(512, 1024)

    def load(k, i):
        src = (exp_in, exp_out)[i].at[k]
        return pltpu.make_async_copy(src, slot(k, i, low), wsem.at[k, i])

    def swapped(i):
        return pltpu.make_async_copy((in_a, out_a)[i], slot(0, i, low), wsem.at[0, i])

    def swap_in(i):
        return remote((exp_in, exp_out)[i].at[1], slot(1, i, low), ss.at[i], sr.at[i], swap_mate)

    def share(k, i):
        return remote(slot(k, i, low), slot(k, i, high), bs.at[k, i], br.at[k, i], other)

    @pl.when(same)
    def _():
        for i in range(2):
            load(0, i).start()
            load(1, i).start()

    @pl.when(jnp.logical_not(same))
    def _():
        for i in range(2):
            swapped(i).start()

    left, right = placings(route[0:1, :])
    sendh[...] = to_pieces(left, right, hid[...])
    sendc[...] = to_pieces(left, right, cot[...])
    pl.semaphore_wait(bar, 20)
    cols.start(0, sendh, arrh)

    @pl.when(same)
    def _():
        for i in range(2):
            load(0, i).wait()

    @pl.when(jnp.logical_not(same))
    def _():
        for i in range(2):
            swapped(i).wait()

    for i in range(2):
        share(0, i).start()
    cols.start(1, sendc, arrc)

    @pl.when(jnp.logical_not(same))
    def _():
        for i in range(2):
            swap_in(i).start()

    cols.wait(0, sendh, arrh)
    gain = [vec[0:1, :], vec[1:2, :]]
    bias = [vec[2:3, :], vec[3:4, :]]
    rows = rows_of(arrh[...])
    arrived[...] = rows
    xhat, scale = norm_parts(rows)
    xh0[...] = xhat
    sc[0] = jnp.broadcast_to(scale, (128, 128))
    e0[block(z), :] = (xhat * gain[0] + bias[0]).astype(jnp.bfloat16)
    line.spread(0, e0)
    cols.wait(1, sendc, arrc)
    coti = rows_of(arrc[...])
    cota[...] = coti
    gating = jax.nn.sigmoid(split_sum(arrived[...] * vec[4:5, :]))
    sc[2] = jnp.broadcast_to(gating, (128, 128))
    g1[block(z), :] = (gating * coti).astype(jnp.bfloat16)
    line.spread(3, g1)
    for i in range(2):
        share(0, i).wait_recv()

    def forward(k, j, rows_in, act, dg):
        values = rows_in[block(j), :]
        for n in range(4):
            tile = slice(n * 256, (n + 1) * 256)
            pre = nn(values, w_in[k, :, tile])
            acted, slope = gelu_parts(pre)
            act[block(j), tile] = acted.astype(jnp.bfloat16)
            dg[block(j), tile] = slope

    def project(k, j, act, part):
        values = act[block(j), :]
        for n in range(4):
            tile = slice(n * 256, (n + 1) * 256)
            part[block(j), tile] = nn(values, w_out[k, :, tile]).astype(jnp.bfloat16)

    def backward(k, j, grad, dg, gp, part):
        values = grad[block(j), :]
        for n in range(4):
            tile = slice(n * 256, (n + 1) * 256)
            slope = dg[block(j), tile] * nt(values, w_out[k, tile, :])
            gp[block(j), tile] = slope.astype(jnp.bfloat16)
        pres = gp[block(j), :]
        for n in range(4):
            tile = slice(n * 256, (n + 1) * 256)
            part[block(j), tile] = nt(pres, w_in[k, tile, :]).astype(jnp.bfloat16)

    def sub0(i, carry):
        d = order(i)
        j = line.index(d)

        @pl.when(i > 0)
        def _():
            line.arrived(0, d, e0)

        forward(0, j, e0, act0, dg0)
        project(0, j, act0, ps0)

        @pl.when(i > 0)
        def _():
            line.give(1, d, ps0, pr0)

        return carry

    lax.fori_loop(0, 4, sub0, 0)

    @pl.when(same)
    def _():
        for i in range(2):
            load(1, i).wait()

    @pl.when(jnp.logical_not(same))
    def _():
        for i in range(2):
            swap_in(i).wait()

    for i in range(2):
        share(1, i).start()
    stream = arrived[...] + line.total(1, ps0, pr0)
    base[...] = stream
    xhat, scale = norm_parts(stream)
    xh1[...] = xhat
    sc[1] = jnp.broadcast_to(scale, (128, 128))
    e1[block(z), :] = (xhat * gain[1] + bias[1]).astype(jnp.bfloat16)
    line.spread(2, e1)
    line.sent(1, ps0)
    for i in range(2):
        share(1, i).wait_recv()

    def sub1(i, carry):
        d = order(i)
        j = line.index(d)

        @pl.when(i > 0)
        def _():
            line.arrived(2, d, e1)
            line.arrived(3, d, g1)

        forward(1, j, e1, act1, dg1)
        backward(1, j, g1, dg1, gp1, ps0)

        @pl.when(i > 0)
        def _():
            line.give(4, d, ps0, pb1)

        project(1, j, act1, ps1)

        @pl.when(i > 0)
        def _():
            line.give(5, d, ps1, pr1)

        return carry

    lax.fori_loop(0, 4, sub1, 0)

    def weight_grads(k, rows_in, gp, act, grad):
        def one(n, carry):
            tile = pl.ds(pl.multiple_of(n * 256, 256), 256)
            tile_b = pl.ds(pl.multiple_of(n * 256 + 512, 256), 256)
            ga_out[k, tile, :] = tn(act[:, tile], grad[...])
            sb_out[k, tile, :] = tn(act[:, tile_b], grad[...]).astype(jnp.bfloat16)
            return carry

        lax.fori_loop(0, 2, one, 0)

        def two(n, carry):
            tile = pl.ds(pl.multiple_of(n * 256, 256), 256)
            ga_in[k, tile, :] = tn(rows_in[:, tile], gp[:, 0:512])
            sb_in[k, tile, :] = tn(rows_in[:, tile], gp[:, 512:1024]).astype(jnp.bfloat16)
            return carry

        lax.fori_loop(0, 4, two, 0)

    def swap(k, i, src, dst):
        return pltpu.make_async_remote_copy(
            src_ref=src.at[k],
            dst_ref=dst.at[k],
            send_sem=ks.at[k, i],
            recv_sem=kr.at[k, i],
            device_id=other,
            device_id_type=MESH,
        )

    weight_grads(1, e1, gp1, act1, g1)
    swap(1, 0, sb_in, rb_in).start()
    swap(1, 1, sb_out, rb_out).start()
    grad_normed = line.total(4, ps0, pb1)
    grad_stream = sc[2][:, 0:1] * cota[...]
    grad_stream += norm_back(grad_normed, gain[1], xh1[...], sc[1][:, 0:1])
    g0[block(z), :] = grad_stream.astype(jnp.bfloat16)
    line.spread(6, g0)
    vmine[1:2, :] = jnp.sum(grad_normed * xh1[...], axis=0, keepdims=True)
    vmine[3:4, :] = jnp.sum(grad_normed, axis=0, keepdims=True)
    line.sent(4, ps0)
    stream = base[...] + line.total(5, ps1, pr1)
    base[...] = grad_stream
    gate = sc[2][:, 0:1]
    diff = stream - arrived[...]
    sendr[...] = pieces_of(arrived[...] + gate * diff)
    grad_gating = split_sum(cota[...] * diff)
    grad_logit = gate * (1.0 - gate) * grad_gating
    vmine[4:5, :] = jnp.sum(grad_logit * arrived[...], axis=0, keepdims=True)
    sc[3] = jnp.broadcast_to(grad_logit, (128, 128))

    def sub0_back(i, carry):
        d = order(i)
        j = line.index(d)

        @pl.when(i > 0)
        def _():
            line.arrived(6, d, g0)

        backward(0, j, g0, dg0, gp0, ps0)

        @pl.when(i > 0)
        def _():
            line.give(7, d, ps0, pb0)

        return carry

    lax.fori_loop(0, 4, sub0_back, 0)
    cols.start(2, sendr, arrr)
    weight_grads(0, e0, gp0, act0, g0)
    swap(0, 0, sb_in, rb_in).start()
    swap(0, 1, sb_out, rb_out).start()
    grad_normed = line.total(7, ps0, pb0)
    vmine[0:1, :] = jnp.sum(grad_normed * xh0[...], axis=0, keepdims=True)
    vmine[2:3, :] = jnp.sum(grad_normed, axis=0, keepdims=True)
    grad_stream = base[...] + norm_back(grad_normed, gain[0], xh0[...], sc[0][:, 0:1])
    grad_stream += (1.0 - sc[2][:, 0:1]) * cota[...] + sc[3][:, 0:1] * vec[4:5, :]
    sendg[...] = pieces_of(grad_stream)
    cols.start(3, sendg, arrg)
    vmine[5:8, :] = jnp.zeros((3, 1024), jnp.float32)
    give_core = remote(vmine, vcore, vs.at[0], vr.at[0], other)
    give_core.start()
    give_core.wait_recv()
    vline[z] = vmine[...] + vcore[...]

    def give_line(d, at):
        return remote(vline.at[at], vline.at[at], vs.at[4 - d], vr.at[4 - d], (2 * line.index(4 - d) + yh, f))

    for d in (1, 2, 3):
        give_line(d, z).start()
    cols.wait(3, sendg, arrg)
    left, right = placings(route[0:1, :])
    gh[...] = from_pieces(left, right, arrg[...])
    for d in (1, 2, 3):
        give_line(d, line.index(d)).wait_recv()
    vsum[...] = vline[0] + vline[1] + vline[2] + vline[3]
    give_mate = remote(vsum, vswap, vs.at[4], vr.at[4], swap_mate)

    @pl.when(jnp.logical_not(same))
    def _():
        give_mate.start()

    cols.wait(2, sendr, arrr)
    res[...] = from_pieces(left, right, arrr[...])
    for k in (0, 1):
        swap(k, 0, sb_in, rb_in).wait()
        swap(k, 1, sb_out, rb_out).wait()
    stores = []
    for k in (1, 0):
        sb_in[k] = (ga_in[k] + rb_in[k].astype(jnp.float32)).astype(jnp.bfloat16)
        sb_out[k] = (ga_out[k] + rb_out[k].astype(jnp.float32)).astype(jnp.bfloat16)
        stores += [
            pltpu.make_async_copy(sb_in.at[k], gin.at[k], osem.at[k, 0]),
            pltpu.make_async_copy(sb_out.at[k], gout.at[k], osem.at[k, 1]),
        ]
        stores[-1].start()
        stores[-2].start()

    @pl.when(same)
    def _():
        vecg[...] = vsum[...]

    @pl.when(jnp.logical_not(same))
    def _():
        give_mate.wait()
        vecg[...] = vswap[...]

    give_core.wait_send()
    for d in (1, 2, 3):
        give_line(d, z).wait_send()
    for k in (0, 1):
        for i in range(2):
            share(k, i).wait_send()
    line.sent(0, e0)
    line.sent(2, e1)
    line.sent(3, g1)
    line.sent(5, ps1)
    line.sent(6, g0)
    line.sent(7, ps0)
    cols.sent(0, sendh, arrh)
    cols.sent(1, sendc, arrc)
    cols.sent(2, sendr, arrr)
    cols.sent(3, sendg, arrg)
    for store in stores:
        store.wait()


def expert_call(hid, cot, route, vec, exp_in, exp_out, in_a, out_a):
    bf, f32 = jnp.bfloat16, jnp.float32
    vmem, anywhere = pl.BlockSpec(memory_space=pltpu.VMEM), pl.BlockSpec(memory_space=pl.ANY)
    line = [pltpu.VMEM((512, 1024), bf)]
    rows = [pltpu.VMEM((128, 1024), f32)]
    piece = [pltpu.VMEM((256, 512), bf)]
    wide = [pltpu.VMEM((512, 1024), f32)]
    return pl.pallas_call(
        expert_kernel,
        out_shape=(
            jax.ShapeDtypeStruct((128, 1024), bf),
            jax.ShapeDtypeStruct((128, 1024), bf),
            jax.ShapeDtypeStruct((8, 1024), f32),
            jax.ShapeDtypeStruct((2, 1024, 512), bf),
            jax.ShapeDtypeStruct((2, 512, 1024), bf),
        ),
        in_specs=[vmem] * 4 + [anywhere] * 4,
        out_specs=(vmem, vmem, vmem, anywhere, anywhere),
        scratch_shapes=[
            pltpu.VMEM((2, 1024, 1024), bf),
            pltpu.VMEM((2, 1024, 1024), bf),
            *(piece * 8),
            *(line * 10),
            *(line * 2),
            *(wide * 2),
            *(line * 2),
            *(rows * 5),
            pltpu.VMEM((4, 128, 128), f32),
            pltpu.VMEM((2, 1024, 512), f32),
            pltpu.VMEM((2, 512, 1024), f32),
            pltpu.VMEM((2, 1024, 512), bf),
            pltpu.VMEM((2, 512, 1024), bf),
            pltpu.VMEM((2, 1024, 512), bf),
            pltpu.VMEM((2, 512, 1024), bf),
            pltpu.VMEM((8, 1024), f32),
            pltpu.VMEM((8, 1024), f32),
            pltpu.VMEM((4, 8, 1024), f32),
            pltpu.VMEM((8, 1024), f32),
            pltpu.VMEM((8, 1024), f32),
            pltpu.SemaphoreType.DMA((2, 2)),
            pltpu.SemaphoreType.DMA((8, 3)),
            pltpu.SemaphoreType.DMA((8, 3)),
            pltpu.SemaphoreType.DMA((4, 15)),
            pltpu.SemaphoreType.DMA((4, 15)),
            pltpu.SemaphoreType.DMA((2, 2)),
            pltpu.SemaphoreType.DMA((2, 2)),
            pltpu.SemaphoreType.DMA((2, 2)),
            pltpu.SemaphoreType.DMA((2, 2)),
            pltpu.SemaphoreType.DMA((2, 2)),
            pltpu.SemaphoreType.DMA((2,)),
            pltpu.SemaphoreType.DMA((2,)),
            pltpu.SemaphoreType.DMA((5,)),
            pltpu.SemaphoreType.DMA((5,)),
        ],
        compiler_params=pltpu.CompilerParams(
            collective_id=1, has_side_effects=True, vmem_limit_bytes=60 << 20
        ),
        name="experts",
    )(hid, cot, route, vec, exp_in, exp_out, in_a, out_a)


def remote(src, dst, send, recv, device):
    return pltpu.make_async_remote_copy(
        src_ref=src, dst_ref=dst, send_sem=send, recv_sem=recv, device_id=device, device_id_type=MESH
    )


def greet(bar, device):
    pl.semaphore_signal(bar, inc=1, device_id=device, device_id_type=MESH)


class Owners:
    def __init__(self, send, recv, core_send, core_recv):
        self.s, self.f = lax.axis_index("seq"), lax.axis_index("fsdp")
        self.c, self.col = lax.rem(self.f, 2), lax.div(self.f, 2)
        self.send, self.recv = send, recv
        self.core_send, self.core_recv = core_send, core_recv

    def device(self, col):
        return (self.s, 2 * col + self.c)

    def copy(self, phase, i, src, dst):
        return remote(
            src, dst, self.send.at[phase, i], self.recv.at[phase, i], self.device(lax.rem(self.col + i + 1, 8))
        )

    def start(self, phase, src, full):
        def one(i, carry):
            self.copy(phase, i, src, full.at[self.col, self.c]).start()
            return carry

        lax.fori_loop(0, 7, one, 0)

    def wait(self, phase, full):
        def one(i, carry):
            q = lax.rem(self.col + 7 - i, 8)
            dst = full.at[q, self.c]
            remote(dst, dst, self.send.at[phase, i], self.recv.at[phase, i], self.device(q)).wait_recv()
            return carry

        lax.fori_loop(0, 7, one, 0)

    def sent(self, phase, src, full):
        def one(i, carry):
            self.copy(phase, i, src, full.at[self.col, self.c]).wait_send()
            return carry

        lax.fori_loop(0, 7, one, 0)

    def core(self, phase, full):
        own = full.at[:, self.c]
        return remote(
            own, own, self.core_send.at[phase], self.core_recv.at[phase], (self.s, self.f + 1 - 2 * self.c)
        )

    def core_wait(self, phase, full):
        dst = full.at[:, 1 - self.c]
        remote(
            dst, dst, self.core_send.at[phase], self.core_recv.at[phase], (self.s, self.f + 1 - 2 * self.c)
        ).wait_recv()


def labels(position, first, second):
    return jnp.where(position >= first, 1, 0) + jnp.where(position >= second, 1, 0)


def masks(j, yh, docs):
    first, second = docs[0, 0], docs[0, 1]
    wide = 128 * (j + 1)
    row = lax.broadcasted_iota(jnp.int32, (128, wide), 0) + 128 * (2 * j + yh)
    lane = lax.broadcasted_iota(jnp.int32, (128, wide), 1)
    start = (lane >> 7) * 256 + (lane & 127)
    row_label = labels(row, first, second)
    found = []
    for parity in (yh, 1 - yh):
        key = start + 128 * parity
        found.append((key <= row) & (labels(key, first, second) == row_label))
    return found


def probabilities(q, keys, seen):
    scores = [jnp.where(ok, nt(q, k) * 0.125, masked_score) for k, ok in zip(keys, seen)]
    top = jnp.maximum(
        jnp.max(scores[0], axis=-1, keepdims=True), jnp.max(scores[1], axis=-1, keepdims=True)
    )
    weights = [jnp.exp(s - top) for s in scores]
    inverse = 1.0 / (split_sum(weights[0]) + split_sum(weights[1]))
    return [w * inverse for w in weights]


def head_lanes(h):
    lane = lax.broadcasted_iota(jnp.int32, (128, 128), 1)
    return lane < 64 if h == 0 else lane >= 64


def only(keep, values):
    return jnp.where(keep, values.astype(jnp.float32), 0.0).astype(jnp.bfloat16)


def wide_tile(full, tile):
    part = full[:, :, :, tile]
    return part.reshape(1024, part.shape[-1])


def dense_forward_kernel(
    x, gain_tile, docs, w_qkv, w_out, w_up, w_down, exp_in, exp_out,
    hid, mixed, after, gains, o_n1, o_n2, o_act, o_dg, o_q, o_kv, o_kvo, o_wq, o_wo, o_wu, o_wd, o_ain, o_aout,
    sq, su, wq, wo, wu, wd, gmine, gother,
    n1, n2, qb, kvb, kvo, mixs, act, dg, ps, pr,
    zs, zr, ys, yr, fs, fr, ks, kr, gs, gr, ss, sr, osem,
):
    line, own = Line(zs, zr), Owners(fs, fr, ks, kr)
    z, yh, f, c = place()
    s = lax.axis_index("seq")
    col = lax.div(f, 2)
    bar = pltpu.get_barrier_semaphore()
    other = (s, f + 1 - 2 * c)
    mate = (2 * z + 1 - yh, f)
    swap_mate = (2 * z + 1 - yh, f + 1 - 2 * c)
    for d in (1, 2, 3):
        greet(bar, (2 * line.index(d) + yh, f))
    for device in (other, mate, swap_mate):
        greet(bar, device)

    def meet(i, carry):
        greet(bar, own.device(lax.rem(col + i + 1, 8)))
        return carry

    lax.fori_loop(0, 7, meet, 0)
    for part in range(3):
        sq[:, 256 * part : 256 * part + 256] = w_qkv[:, pl.ds(pl.multiple_of(1024 * part + 256 * z, 256), 256)]
    low = lax.broadcasted_iota(jnp.int32, (64, 128), 1) < 64
    odd = lax.rem(z, 2) == 1
    for n in range(8):
        at = 512 * n + 128 * lax.div(z, 2)
        a = w_up[:, pl.ds(pl.multiple_of(at, 128), 128)].astype(jnp.float32)
        b = w_up[:, pl.ds(pl.multiple_of(at + 256, 128), 128)].astype(jnp.float32)
        kept = jnp.where(low, a, pltpu.roll(b, 64, 1))
        moved = jnp.where(low, pltpu.roll(a, 64, 1), b)
        su[:, 128 * n : 128 * n + 128] = jnp.where(odd, moved, kept).astype(jnp.bfloat16)
    xhat = norm_parts(x[...].astype(jnp.float32))[0]
    pl.semaphore_wait(bar, 13)
    tile_at = pl.ds(pl.multiple_of(128 * col, 128), 128)

    def gain_copy(i):
        return remote(
            gain_tile, gmine.at[:, tile_at], gs.at[i], gr.at[i], own.device(lax.rem(col + i + 1, 8))
        )

    def push_gain(i, carry):
        gain_copy(i).start()
        return carry

    lax.fori_loop(0, 7, push_gain, 0)
    gmine[:, tile_at] = gain_tile[...]
    own.start(0, sq, wq)
    wq[col, c] = sq[...]

    def wait_gain(i, carry):
        q = lax.rem(col + 7 - i, 8)
        dst = gmine.at[:, pl.ds(pl.multiple_of(128 * q, 128), 128)]
        remote(dst, dst, gs.at[i], gr.at[i], own.device(q)).wait_recv()
        return carry

    lax.fori_loop(0, 7, wait_gain, 0)
    gain_core = remote(gmine, gother, gs.at[7], gr.at[7], other)
    gain_core.start()
    gain_core.wait_recv()
    vectors = gmine[...].astype(jnp.float32) + gother[...].astype(jnp.float32)
    gains[...] = vectors[0:8]
    n1[block(z), :] = (xhat * gains[0:1, :] + gains[2:3, :]).astype(jnp.bfloat16)
    line.spread(0, n1)
    own.start(1, w_out, wo)
    wo[col, c] = w_out[...]
    own.start(2, su, wu)
    wu[col, c] = su[...]
    down_rows = w_down.at[pl.ds(pl.multiple_of(64 * z, 64), 64)]
    own.start(3, down_rows, wd)
    wd[col, c] = down_rows[...]
    own.wait(0, wq)
    own.core(0, wq).start()
    own.core_wait(0, wq)

    def kv_copy(i, j):
        return remote(kvb.at[block(j)], kvo.at[block(j)], ys.at[i], yr.at[i], mate)

    def project_qkv(i, carry):
        d = order(i)
        j = line.index(d)

        @pl.when(i > 0)
        def _():
            line.arrived(0, d, n1)

        values = n1[block(j), :]
        qb[block(j), :] = nn(values, wide_tile(wq, slice(0, 256))).astype(jnp.bfloat16)
        kvb[block(j), 0:256] = nn(values, wide_tile(wq, slice(256, 512))).astype(jnp.bfloat16)
        kvb[block(j), 256:512] = nn(values, wide_tile(wq, slice(512, 768))).astype(jnp.bfloat16)
        kv_copy(i, j).start()
        return carry

    lax.fori_loop(0, 4, project_qkv, 0)
    own.wait(1, wo)
    own.core(1, wo).start()
    for i in range(4):
        kv_copy(i, line.index(order(i))).wait_recv()
    swaps = [
        remote(exp_in.at[0], o_ain, ss.at[0], sr.at[0], swap_mate),
        remote(exp_out.at[0], o_aout, ss.at[1], sr.at[1], swap_mate),
    ]

    @pl.when(c != yh)
    def _():
        for swap in swaps:
            swap.start()

    for j in range(4):
        seen = masks(j, yh, docs)
        wide = slice(0, 128 * (j + 1))
        for p in range(2):
            lanes = slice(128 * p, 128 * p + 128)
            value_lanes = slice(256 + 128 * p, 384 + 128 * p)
            q = qb[128 * j : 128 * j + 128, lanes]
            keys = [kvb[wide, lanes], kvo[wide, lanes]]
            values = [kvb[wide, value_lanes], kvo[wide, value_lanes]]
            outs = []
            for h in range(2):
                probs = probabilities(only(head_lanes(h), q), keys, seen)
                outs.append(
                    nn(probs[0].astype(jnp.bfloat16), values[0]) + nn(probs[1].astype(jnp.bfloat16), values[1])
                )
            mixs[128 * j : 128 * j + 128, lanes] = jnp.where(head_lanes(0), outs[0], outs[1]).astype(jnp.bfloat16)
    my_lanes = pl.ds(pl.multiple_of(256 * z, 256), 256)
    for d in (1, 3, 2):
        line.copy(1, d, mixs.at[block(line.index(d))], mixed.at[:, my_lanes]).start()
    mixed[:, my_lanes] = mixs[block(z), :]
    own.wait(2, wu)
    own.core(2, wu).start()
    own.wait(3, wd)
    own.core(3, wd).start()
    own.core_wait(1, wo)
    for d in (1, 3, 2):
        j = line.index(d)
        dst = mixed.at[:, pl.ds(pl.multiple_of(256 * j, 256), 256)]
        remote(dst, dst, zs.at[1, 3 - d], zr.at[1, 3 - d], (2 * j + yh, f)).wait_recv()
    for n in range(4):
        tile = slice(256 * n, 256 * n + 256)
        after[:, tile] = x[:, tile].astype(jnp.float32) + nn(mixed[...], wide_tile(wo, tile))
    xhat = norm_parts(after[...])[0]
    n2[block(z), :] = (xhat * gains[1:2, :] + gains[3:4, :]).astype(jnp.bfloat16)
    line.spread(2, n2)
    own.core_wait(2, wu)
    own.core_wait(3, wd)
    stores = [
        pltpu.make_async_copy(src, dst, osem.at[k])
        for k, (src, dst) in enumerate(
            [(n1, o_n1), (qb, o_q), (kvb, o_kv), (kvo, o_kvo), (wq, o_wq), (wo, o_wo), (wu, o_wu), (wd, o_wd)]
        )
    ]
    for store in stores:
        store.start()

    def feed(i, carry):
        d = order(i)
        j = line.index(d)

        @pl.when(i > 0)
        def _():
            line.arrived(2, d, n2)

        values = n2[block(j), :]
        for n in range(4):
            tile = slice(n * 256, (n + 1) * 256)
            acted, slope = gelu_parts(nn(values, wide_tile(wu, tile)))
            act[block(j), tile] = acted.astype(jnp.bfloat16)
            dg[block(j), tile] = slope
        values = act[block(j), :]
        for n in range(4):
            tile = slice(n * 256, (n + 1) * 256)
            ps[block(j), tile] = nn(values, wide_tile(wd, tile)).astype(jnp.bfloat16)

        @pl.when(i > 0)
        def _():
            line.give(3, d, ps, pr)

        return carry

    lax.fori_loop(0, 4, feed, 0)
    late = [
        pltpu.make_async_copy(src, dst, osem.at[8 + k])
        for k, (src, dst) in enumerate([(n2, o_n2), (act, o_act), (dg, o_dg)])
    ]
    for store in late:
        store.start()
    hid[...] = (after[...] + line.total(3, ps, pr)).astype(jnp.bfloat16)
    gain_core.wait_send()

    def sent_gain(i, carry):
        gain_copy(i).wait_send()
        return carry

    lax.fori_loop(0, 7, sent_gain, 0)
    own.sent(0, sq, wq)
    own.sent(1, w_out, wo)
    own.sent(2, su, wu)
    own.sent(3, down_rows, wd)
    for phase, full in enumerate((wq, wo, wu, wd)):
        own.core(phase, full).wait_send()
    for i in range(4):
        kv_copy(i, line.index(order(i))).wait_send()
    line.sent(0, n1)
    for d in (1, 3, 2):
        line.copy(1, d, mixs.at[block(line.index(d))], mixed.at[:, my_lanes]).wait_send()
    line.sent(2, n2)
    line.sent(3, ps)

    @pl.when(c != yh)
    def _():
        for swap in swaps:
            swap.wait()

    for store in stores + late:
        store.wait()


def dense_forward_call(x, gain_tile, docs, w_qkv, w_out, w_up, w_down, exp_in, exp_out):
    bf, f32 = jnp.bfloat16, jnp.float32
    vmem, anywhere = pl.BlockSpec(memory_space=pltpu.VMEM), pl.BlockSpec(memory_space=pl.ANY)
    smem = pl.BlockSpec(memory_space=pltpu.SMEM)
    shape = jax.ShapeDtypeStruct
    line = [pltpu.VMEM((512, 1024), bf)]
    weight = [(8, 2, 64, 768), (8, 2, 64, 1024), (8, 2, 64, 1024), (8, 2, 64, 1024)]
    saved = [
        shape((512, 1024), bf), shape((512, 1024), bf), shape((512, 1024), bf), shape((512, 1024), f32),
        shape((512, 256), bf), shape((512, 512), bf), shape((512, 512), bf),
    ] + [shape(w, bf) for w in weight] + [shape((1024, 512), bf), shape((512, 1024), bf)]
    dma = pltpu.SemaphoreType.DMA
    return pl.pallas_call(
        dense_forward_kernel,
        out_shape=[shape((128, 1024), bf), shape((128, 1024), bf), shape((128, 1024), f32), shape((8, 1024), f32)]
        + saved,
        in_specs=[vmem, vmem, smem, vmem, vmem, vmem, vmem, anywhere, anywhere],
        out_specs=[vmem] * 4 + [anywhere] * len(saved),
        scratch_shapes=[
            pltpu.VMEM((64, 768), bf),
            pltpu.VMEM((64, 1024), bf),
            *[pltpu.VMEM(w, bf) for w in weight],
            pltpu.VMEM((16, 1024), bf),
            pltpu.VMEM((16, 1024), bf),
            *(line * 2),
            pltpu.VMEM((512, 256), bf),
            pltpu.VMEM((512, 512), bf),
            pltpu.VMEM((512, 512), bf),
            pltpu.VMEM((512, 256), bf),
            *line,
            pltpu.VMEM((512, 1024), f32),
            *(line * 2),
            dma((4, 3)), dma((4, 3)), dma((4,)), dma((4,)), dma((4, 7)), dma((4, 7)),
            dma((4,)), dma((4,)), dma((8,)), dma((8,)), dma((2,)), dma((2,)), dma((11,)),
        ],
        compiler_params=pltpu.CompilerParams(collective_id=2, has_side_effects=True, vmem_limit_bytes=60 << 20),
        name="dense_forward",
    )(x, gain_tile, docs, w_qkv, w_out, w_up, w_down, exp_in, exp_out)


class Plane:
    def __init__(self, cols, send, recv):
        self.cols, self.send, self.recv = cols, send, recv

    def copy(self, phase, i, src_of, dst):
        q = lax.rem(self.cols.m + i + 1, 16)
        return remote(
            src_of(q), dst.at[self.cols.m], self.send.at[phase, i], self.recv.at[phase, i], self.cols.device(q)
        )

    def start(self, phase, src_of, dst):
        def one(i, carry):
            self.copy(phase, i, src_of, dst).start()
            return carry

        lax.fori_loop(0, 15, one, 0)

    def wait(self, phase, dst):
        def one(i, carry):
            q = lax.rem(self.cols.m + 15 - i, 16)
            piece = dst.at[q]
            remote(piece, piece, self.send.at[phase, i], self.recv.at[phase, i], self.cols.device(q)).wait_recv()
            return carry

        lax.fori_loop(0, 15, one, 0)

    def sent(self, phase, src_of, dst):
        def one(i, carry):
            self.copy(phase, i, src_of, dst).wait_send()
            return carry

        lax.fori_loop(0, 15, one, 0)


class Everyone:
    def __init__(self, send, recv):
        self.s, self.f = lax.axis_index("seq"), lax.axis_index("fsdp")
        self.send, self.recv = send, recv

    def copy(self, phase, i, buf):
        own = buf.at[self.s]
        return remote(
            own, own, self.send.at[phase, i], self.recv.at[phase, i], (lax.rem(self.s + i + 1, 8), self.f)
        )

    def start(self, phase, buf):
        for i in range(7):
            self.copy(phase, i, buf).start()

    def wait(self, phase, buf):
        for i in range(7):
            q = lax.rem(self.s + 7 - i, 8)
            dst = buf.at[q]
            remote(dst, dst, self.send.at[phase, i], self.recv.at[phase, i], (q, self.f)).wait_recv()

    def sent(self, phase, buf):
        for i in range(7):
            self.copy(phase, i, buf).wait_send()


def dense_backward_kernel(
    gh, x, after, docs, gains, mixed, n1_h, n2_h, act_h, dg_h, q_h, kv_h, kvo_h, wq_h, wo_h, wu_h, wd_h, gin, gout,
    gx, gq, go, gu, gd, gvec, rin, rout,
    ghs, n1, n2, act, dg, gp, qb, kvb, kvo, wq, wo, wu, wd,
    ps, pr, ps2, pr2, gms, gm, dp, dkv, dkvo, kvs, kvr,
    md, mu, mo, mq, td, tu, to, tq, rd, ru, ro, rq,
    gad, gaf, vmine, vcore, vplane, vline, outz, bd, bu, bo, bq,
    lsem, zs, zr, ys, yr, ks, kr, cs, cr, qs, qr, ss, sr, vs, vr,
):
    line = Line(zs, zr)
    cols = Columns(cs, cr)
    plane, everyone = Plane(cols, cs, cr), Everyone(qs, qr)
    z, yh, f, c = place()
    s = lax.axis_index("seq")
    col, m = lax.div(f, 2), cols.m
    bar = pltpu.get_barrier_semaphore()
    other = (s, f + 1 - 2 * c)
    mate = (2 * z + 1 - yh, f)
    swap_mate = (2 * z + 1 - yh, f + 1 - 2 * c)

    def meet(i, carry):
        greet(bar, cols.device(lax.rem(m + i + 1, 16)))
        return carry

    lax.fori_loop(0, 15, meet, 0)
    for i in range(7):
        greet(bar, (lax.rem(s + i + 1, 8), f))
    greet(bar, other)
    greet(bar, swap_mate)
    loads = [
        pltpu.make_async_copy(src, dst, lsem.at[k])
        for k, (src, dst) in enumerate(
            [
                (wd_h, wd), (dg_h, dg), (wu_h, wu), (act_h, act), (n2_h, n2), (wo_h, wo), (q_h, qb), (kv_h, kvb),
                (kvo_h, kvo), (wq_h, wq), (n1_h, n1),
            ]
        )
    ]
    for load in loads:
        load.start()
    ghs[block(z), :] = gh[...]
    pl.semaphore_wait(bar, 24)
    line.spread(0, ghs)
    swaps = [
        remote(gin, rin, ss.at[0], sr.at[0], swap_mate),
        remote(gout, rout, ss.at[1], sr.at[1], swap_mate),
    ]

    @pl.when(c != yh)
    def _():
        for swap in swaps:
            swap.start()

    for load in loads[:3]:
        load.wait()

    def feed(i, carry):
        d = order(i)
        j = line.index(d)

        @pl.when(i > 0)
        def _():
            line.arrived(0, d, ghs)

        values = ghs[block(j), :]
        for n in range(4):
            tile = slice(n * 256, (n + 1) * 256)
            rows = wd[2 * n : 2 * n + 2].reshape(256, 1024)
            gp[block(j), tile] = (dg[block(j), tile] * nt(values, rows)).astype(jnp.bfloat16)
        pres = gp[block(j), :]
        for n in range(4):
            tile = slice(n * 256, (n + 1) * 256)
            rows = wu[2 * n : 2 * n + 2].reshape(256, 1024)
            ps[block(j), tile] = nt(pres, rows).astype(jnp.bfloat16)

        @pl.when(i > 0)
        def _():
            line.give(1, d, ps, pr)

        return carry

    lax.fori_loop(0, 4, feed, 0)
    for load in loads[3:6]:
        load.wait()

    def weight_grad(lhs, rhs, mine, theirs):
        def one(n, carry):
            rows = lhs[:, pl.ds(pl.multiple_of(n * 256, 256), 256)]
            grad = tn(rows, rhs[...])
            for half in range(2):
                first = grad[128 * half : 128 * half + 64].astype(jnp.bfloat16)
                second = grad[128 * half + 64 : 128 * half + 128].astype(jnp.bfloat16)
                low = c == 0
                mine[2 * n + half] = jnp.where(low, first, second)
                theirs[2 * n + half] = jnp.where(low, second, first)
            return carry

        lax.fori_loop(0, 4, one, 0)

    def core_copy(phase, src, dst):
        return remote(src, dst, ks.at[phase], kr.at[phase], other)

    def piece_of(mine):
        return lambda q: mine.at[lax.div(q, 2), pl.ds(pl.multiple_of(32 * lax.rem(q, 2), 32), 32)]

    def reduce_core(phase, mine, theirs, got, dst):
        core_copy(phase, theirs, got).wait()

        def one(n, carry):
            mine[n] = (mine[n].astype(jnp.float32) + got[n].astype(jnp.float32)).astype(jnp.bfloat16)
            return carry

        lax.fori_loop(0, 8, one, 0)
        plane.start(phase, piece_of(mine), dst)
        dst[m] = mine[col, pl.ds(pl.multiple_of(32 * yh, 32), 32), :]

    def plane_total(phase, dst):
        plane.wait(phase, dst)
        acc = dst[0].astype(jnp.float32)
        for q in range(1, 16):
            acc += dst[q].astype(jnp.float32)
        return acc

    weight_grad(act, ghs, md, td)
    core_copy(0, td, rd).start()
    weight_grad(n2, gp, mu, tu)
    core_copy(1, tu, ru).start()
    reduce_core(0, md, td, rd, gad.at[0])
    grad_normed = line.total(1, ps, pr)
    xhat, scale = norm_parts(after[...])
    vmine[1:2, :] = jnp.sum(grad_normed * xhat, axis=0, keepdims=True)
    vmine[3:4, :] = jnp.sum(grad_normed, axis=0, keepdims=True)
    grad_after = gh[...].astype(jnp.float32) + norm_back(grad_normed, gains[1:2, :], xhat, scale)
    gx[...] = grad_after
    grad_attn = grad_after.astype(jnp.bfloat16)
    for n in range(4):
        gms[:, 256 * n : 256 * n + 256] = nt(grad_attn, wo[2 * n : 2 * n + 2].reshape(256, 1024)).astype(
            jnp.bfloat16
        )

    def gm_copy(d):
        lanes = pl.ds(pl.multiple_of(256 * line.index(d), 256), 256)
        return line.copy(2, d, gms.at[:, lanes], gm.at[block(z)])

    for d in (1, 3, 2):
        gm_copy(d).start()
    gm[block(z), :] = gms[:, pl.ds(pl.multiple_of(256 * z, 256), 256)]
    reduce_core(1, mu, tu, ru, gad.at[1])
    gp[block(0), :] = grad_attn
    weight_grad(mixed, gp.at[block(0)], mo, to)
    core_copy(2, to, ro).start()
    for load in loads[6:]:
        load.wait()
    for d in (1, 3, 2):
        line.arrived(2, d, gm)
    dkv[...] = jnp.zeros_like(dkv)
    dkvo[...] = jnp.zeros_like(dkvo)

    def kv_copy(j):
        return remote(kvs.at[block(j)], kvr.at[block(j)], ys.at[j], yr.at[j], mate)

    for j in (3, 2, 1, 0):
        seen = masks(j, yh, docs)
        wide = slice(0, 128 * (j + 1))
        rows = slice(128 * j, 128 * j + 128)
        for p in range(2):
            lanes = slice(128 * p, 128 * p + 128)
            value_lanes = slice(256 + 128 * p, 384 + 128 * p)
            q, grad = qb[rows, lanes], gm[rows, lanes]
            keys = [kvb[wide, lanes], kvo[wide, lanes]]
            values = [kvb[wide, value_lanes], kvo[wide, value_lanes]]
            outs = []
            for h in range(2):
                q_h, grad_h = only(head_lanes(h), q), only(head_lanes(h), grad)
                probs = probabilities(q_h, keys, seen)
                back = [nt(grad_h, v) for v in values]
                dot = split_sum(probs[0] * back[0]) + split_sum(probs[1] * back[1])
                slopes = [(pr_ * (b - dot)).astype(jnp.bfloat16) for pr_, b in zip(probs, back)]
                outs.append(nn(slopes[0], keys[0]) + nn(slopes[1], keys[1]))
                for k, acc in enumerate((dkv, dkvo)):
                    acc[wide, lanes] += tn(slopes[k], q_h) * 0.125
                    acc[wide, value_lanes] += tn(probs[k].astype(jnp.bfloat16), grad_h)
            dp[rows, lanes] = (jnp.where(head_lanes(0), outs[0], outs[1]) * 0.125).astype(jnp.bfloat16)
        kvs[rows, :] = dkvo[rows, :].astype(jnp.bfloat16)
        kv_copy(j).start()
    reduce_core(2, mo, to, ro, gad.at[2])
    for j in (3, 2, 1, 0):
        rows = slice(128 * j, 128 * j + 128)
        kv_copy(j).wait_recv()
        dp[rows, 256:768] = (dkv[rows, :] + kvr[rows, :].astype(jnp.float32)).astype(jnp.bfloat16)

    def last(i, carry):
        d = order(3 - i)
        j = line.index(d)
        values = dp[block(j), :]
        for n in range(4):
            tile = slice(n * 256, (n + 1) * 256)
            rows = wq[2 * n : 2 * n + 2].reshape(256, 768)
            ps2[block(j), tile] = nt(values, rows).astype(jnp.bfloat16)

        @pl.when(i < 3)
        def _():
            line.give(3, d, ps2, pr2)

        return carry

    lax.fori_loop(0, 4, last, 0)
    weight_grad(n1, dp, mq, tq)
    core_copy(3, tq, rq).start()
    bd[s] = plane_total(0, gad.at[0]).astype(jnp.bfloat16)
    everyone.start(0, bd)
    bu[s] = plane_total(1, gad.at[1]).astype(jnp.bfloat16)
    everyone.start(1, bu)
    reduce_core(3, mq, tq, rq, gaf)
    grad_normed = line.total(3, ps2, pr2)
    xhat, scale = norm_parts(x[...].astype(jnp.float32))
    vmine[0:1, :] = jnp.sum(grad_normed * xhat, axis=0, keepdims=True)
    vmine[2:3, :] = jnp.sum(grad_normed, axis=0, keepdims=True)
    vmine[4:8, :] = jnp.zeros((4, 1024), jnp.float32)
    give_core = remote(vmine, vcore, vs.at[0], vr.at[0], other)
    give_core.start()
    gx[...] += norm_back(grad_normed, gains[0:1, :], xhat, scale)
    total_out = plane_total(2, gad.at[2])
    for n in range(4):
        outz[4 + n] = total_out[:, 256 * n : 256 * n + 256].astype(jnp.bfloat16)

    def out_copy(d):
        return line.copy(4, d, outz.at[4 + line.index(d)], outz.at[z])

    for d in (1, 3, 2):
        out_copy(d).start()
    give_core.wait()
    vmine[...] += vcore[...]

    def tile_of(q):
        return vmine.at[:, pl.ds(pl.multiple_of(128 * lax.div(q, 2), 128), 128)]

    plane.start(4, tile_of, vplane)
    vplane[m] = vmine[:, pl.ds(pl.multiple_of(128 * col, 128), 128)]
    acc = outz[4 + z].astype(jnp.float32)
    for d in (1, 3, 2):
        dst = outz.at[line.index(d)]
        remote(dst, dst, zs.at[4, 3 - d], zr.at[4, 3 - d], (2 * line.index(d) + yh, f)).wait_recv()
        acc += outz[line.index(d)].astype(jnp.float32)
    bo[s] = acc.astype(jnp.bfloat16)
    everyone.start(2, bo)
    bq[s] = plane_total(3, gaf).astype(jnp.bfloat16)
    everyone.start(3, bq)
    plane.wait(4, vplane)
    vline[z] = jnp.sum(vplane[...], axis=0)

    def vec_copy(d):
        return line.copy(5, d, vline.at[z], vline.at[z])

    for d in (1, 3, 2):
        vec_copy(d).start()
    everyone.wait(0, bd)
    everyone.wait(1, bu)
    for zz in range(4):
        for half in range(2):
            gd[64 * zz + 32 * half : 64 * zz + 32 * half + 32, :] = bd[2 * zz + half].astype(jnp.float32)
    for half in range(2):
        rows = slice(32 * half, 32 * half + 32)
        lane = lax.broadcasted_iota(jnp.int32, (32, 128), 1) < 64
        for n in range(8):
            tile = slice(128 * n, 128 * n + 128)
            quarter = [bu[2 * zz + half, :, tile].astype(jnp.float32) for zz in range(4)]
            turned = [pltpu.roll(v, 64, 1) for v in quarter]
            at = 512 * n
            gu[rows, at : at + 128] = jnp.where(lane, quarter[0], turned[1])
            gu[rows, at + 128 : at + 256] = jnp.where(lane, quarter[2], turned[3])
            gu[rows, at + 256 : at + 384] = jnp.where(lane, turned[0], quarter[1])
            gu[rows, at + 384 : at + 512] = jnp.where(lane, turned[2], quarter[3])
    everyone.wait(2, bo)
    for zz in range(4):
        for half in range(2):
            go[32 * half : 32 * half + 32, 256 * zz : 256 * zz + 256] = bo[2 * zz + half].astype(jnp.float32)
    everyone.wait(3, bq)
    for zz in range(4):
        for half in range(2):
            for part in range(3):
                gq[32 * half : 32 * half + 32, 1024 * part + 256 * zz : 1024 * part + 256 * zz + 256] = bq[
                    2 * zz + half, :, 256 * part : 256 * part + 256
                ].astype(jnp.float32)
    for d in (1, 3, 2):
        dst = vline.at[line.index(d)]
        remote(dst, dst, zs.at[5, 3 - d], zr.at[5, 3 - d], (2 * line.index(d) + yh, f)).wait_recv()
    gvec[...] = jnp.sum(vline[...], axis=0)
    line.sent(0, ghs)
    line.sent(1, ps)
    for d in (1, 3, 2):
        gm_copy(d).wait_send()
        out_copy(d).wait_send()
        vec_copy(d).wait_send()
    line.sent(3, ps2)
    for j in range(4):
        kv_copy(j).wait_send()
    for phase, (mine, dst) in enumerate(((md, gad.at[0]), (mu, gad.at[1]), (mo, gad.at[2]), (mq, gaf))):
        plane.sent(phase, piece_of(mine), dst)
    plane.sent(4, tile_of, vplane)
    for phase, buf in enumerate((bd, bu, bo, bq)):
        everyone.sent(phase, buf)

    @pl.when(c != yh)
    def _():
        for swap in swaps:
            swap.wait()


def dense_backward_call(gh, x, after, docs, gains, mixed, saved, gin, gout):
    bf, f32 = jnp.bfloat16, jnp.float32
    vmem, anywhere = pl.BlockSpec(memory_space=pltpu.VMEM), pl.BlockSpec(memory_space=pl.ANY)
    smem = pl.BlockSpec(memory_space=pltpu.SMEM)
    shape, V = jax.ShapeDtypeStruct, pltpu.VMEM
    line = [V((512, 1024), bf)]
    dma = pltpu.SemaphoreType.DMA
    wide, narrow = [V((8, 64, 1024), bf)], [V((8, 64, 768), bf)]
    return pl.pallas_call(
        dense_backward_kernel,
        out_shape=[
            shape((128, 1024), f32), shape((64, 3072), f32), shape((64, 1024), f32), shape((64, 4096), f32),
            shape((256, 1024), f32), shape((8, 128), f32), shape((2, 1024, 512), bf), shape((2, 512, 1024), bf),
        ],
        in_specs=[vmem, vmem, vmem, smem, vmem, vmem] + [anywhere] * 13,
        out_specs=[vmem] * 6 + [anywhere] * 2,
        scratch_shapes=[
            *(line * 4), V((512, 1024), f32), *line,
            V((512, 256), bf), V((512, 512), bf), V((512, 512), bf),
            V((8, 2, 64, 768), bf), V((8, 2, 64, 1024), bf), V((8, 2, 64, 1024), bf), V((8, 2, 64, 1024), bf),
            *(line * 4),
            V((128, 1024), bf), V((512, 256), bf), V((512, 768), bf), V((512, 512), f32), V((512, 512), f32),
            V((512, 512), bf), V((512, 512), bf),
            *(wide * 3), *narrow, *(wide * 3), *narrow, *(wide * 3), *narrow,
            V((3, 16, 32, 1024), bf), V((16, 32, 768), bf),
            V((8, 1024), f32), V((8, 1024), f32), V((16, 8, 128), f32), V((4, 8, 128), f32),
            V((8, 32, 256), bf),
            V((8, 32, 1024), bf), V((8, 32, 1024), bf), V((8, 32, 256), bf), V((8, 32, 768), bf),
            dma((11,)), dma((6, 3)), dma((6, 3)), dma((4,)), dma((4,)), dma((4,)), dma((4,)),
            dma((5, 15)), dma((5, 15)), dma((4, 7)), dma((4, 7)), dma((2,)), dma((2,)), dma((1,)), dma((1,)),
        ],
        compiler_params=pltpu.CompilerParams(collective_id=3, has_side_effects=True, vmem_limit_bytes=62 << 20),
        name="dense_backward",
    )(gh, x, after, docs, gains, mixed, *saved, gin, gout)


def on_device(
    inputs,
    doc_starts,
    route,
    norm_gain,
    norm_bias,
    w_qkv,
    w_out,
    w_up,
    w_down,
    exp_gain,
    exp_bias,
    exp_in,
    exp_out,
    centroid,
    cotangent,
):
    tok_rows, width = 128, 1024
    x = inputs.reshape(tok_rows, width)
    core = lax.rem(lax.axis_index("fsdp"), 2)
    mine = lax.rem(lax.axis_index("seq"), 2) == core
    share = jnp.pad(jnp.concatenate([norm_gain, norm_bias]), ((0, 12), (0, 0)))
    none = jnp.zeros_like(share)
    gain_tile = jnp.where(core == 0, jnp.concatenate([share, none], 1), jnp.concatenate([none, share], 1))
    core_pairs = [(i, i + 1 - 2 * (i % 2)) for i in range(128)]
    vec = jnp.concatenate([exp_gain[0], exp_bias[0], centroid], axis=0)
    vec = jnp.where(mine, vec, lax.ppermute(vec, ("seq", "fsdp"), core_pairs)).astype(jnp.float32)
    vec = jnp.pad(vec, ((0, 3), (0, 0)))
    hidden, mixed, after, gains, *saved, in_a, out_a = dense_forward_call(
        x, gain_tile, doc_starts, w_qkv, w_out, w_up, w_down, exp_in[0], exp_out[0]
    )
    result, grad_hidden, vec_grads, grad_in, grad_out = expert_call(
        hidden,
        cotangent.reshape(tok_rows, width),
        route.reshape(1, tok_rows),
        vec,
        exp_in[0],
        exp_out[0],
        in_a,
        out_a,
    )
    grad_x, grad_qkv, grad_wo, grad_up, grad_down, norm_grads, swapped_in, swapped_out = dense_backward_call(
        grad_hidden, x, after, doc_starts, gains, mixed, saved, grad_in, grad_out
    )
    norm_grads = jnp.where(core == 0, norm_grads[:4, :64], norm_grads[:4, 64:])
    return (
        result[None],
        grad_x[None],
        norm_grads[0:2],
        norm_grads[2:4],
        grad_qkv,
        grad_wo,
        grad_up,
        grad_down,
        vec_grads[None, 0:2],
        vec_grads[None, 2:4],
        jnp.where(mine, grad_in, swapped_in).astype(jnp.float32)[None],
        jnp.where(mine, grad_out, swapped_out).astype(jnp.float32)[None],
        vec_grads[4:5],
    )


def solution(mesh):
    in_specs = (
        P("fsdp", "seq", None),
        P("fsdp", None),
        P("fsdp", "seq", None),
        P(None, "fsdp"),
        P(None, "fsdp"),
        P("fsdp", None),
        P("fsdp", None),
        P("fsdp", None),
        P("fsdp", None),
        P("fsdp", None, None),
        P("fsdp", None, None),
        P("fsdp", None, None, "seq"),
        P("fsdp", None, "seq", None),
        P("fsdp", None),
        P("fsdp", "seq", None),
    )
    out_specs = (
        P("fsdp", "seq", None),
        P("fsdp", "seq", None),
        P(None, "fsdp"),
        P(None, "fsdp"),
        P("fsdp", None),
        P("fsdp", None),
        P("fsdp", None),
        P("fsdp", None),
        P("fsdp", None, None),
        P("fsdp", None, None),
        P("fsdp", None, None, "seq"),
        P("fsdp", None, "seq", None),
        P("fsdp", None),
    )
    return jax.shard_map(
        on_device, mesh=mesh, in_specs=in_specs, out_specs=out_specs, check_vma=False
    )
```

```python
import jax
import jax.numpy as jnp
from jax import lax
from jax.experimental import pallas as pl
from jax.experimental.pallas import tpu as pltpu
from jax.sharding import PartitionSpec as P

MESH = pl.DeviceIdType.MESH
epsilon = 1e-05
masked_score = -1e30


def split_sum(values):
    return jnp.sum(values, axis=-1, keepdims=True)


def norm_parts(values):
    average = split_sum(values) * (1.0 / values.shape[-1])
    centered = values - average
    spread = split_sum(centered * centered) * (1.0 / values.shape[-1])
    scale = lax.rsqrt(spread + epsilon)
    return centered * scale, scale


def norm_back(grad_normed, gain, xhat, scale):
    width = 1.0 / xhat.shape[-1]
    u = grad_normed * gain
    return scale * (u - split_sum(u) * width - xhat * (split_sum(u * xhat) * width))


def gelu_parts(pre):
    inner = 0.7978845608028654
    cubic = 0.044715
    square = pre * pre
    t = jnp.tanh(inner * pre * (1.0 + cubic * square))
    half = 0.5 * (1.0 + t)
    slope = half + 0.5 * pre * (1.0 - t * t) * (inner * (1.0 + 3.0 * cubic * square))
    return pre * half, slope


def nn(a, b):
    return lax.dot_general(a, b, (((1,), (0,)), ((), ())), preferred_element_type=jnp.float32)


def nt(a, b):
    return lax.dot_general(a, b, (((1,), (1,)), ((), ())), preferred_element_type=jnp.float32)


def tn(a, b):
    return lax.dot_general(a, b, (((0,), (0,)), ((), ())), preferred_element_type=jnp.float32)


def remote(src, dst, send, recv, device):
    return pltpu.make_async_remote_copy(
        src_ref=src, dst_ref=dst, send_sem=send, recv_sem=recv, device_id=device, device_id_type=MESH
    )


def greet(bar, device):
    pl.semaphore_signal(bar, inc=1, device_id=device, device_id_type=MESH)


def block(index):
    return pl.ds(pl.multiple_of(index * 128, 128), 128)


def order(i):
    return i + lax.div(i, 2) - 2 * lax.div(i, 3)


class Place:
    def __init__(self):
        self.s, self.f = lax.axis_index("seq"), lax.axis_index("fsdp")
        self.z, self.yh = lax.div(self.s, 2), lax.rem(self.s, 2)
        self.yl, self.col, self.c = lax.div(self.f, 8), lax.div(self.f, 2), lax.rem(self.f, 2)
        self.x = lax.rem(self.col, 4)
        self.m = self.f - self.c + self.yh
        self.other = (self.s, self.f + 1 - 2 * self.c)
        self.mate = (2 * self.z + 1 - self.yh, self.f)
        self.swap_mate = (2 * self.z + 1 - self.yh, self.f + 1 - 2 * self.c)
        self.same = self.c == self.yh


class Ring:
    def __init__(self, at, axis, send, recv):
        self.at, self.axis, self.send, self.recv = at, axis, send, recv
        self.pos = {"z": at.z, "x": at.x, "y": 2 * at.yh + at.yl}[axis]

    def index(self, d):
        return lax.rem(self.pos + d, 4)

    def device(self, j):
        at = self.at
        if self.axis == "z":
            return (2 * j + at.yh, at.f)
        if self.axis == "x":
            return (at.s, at.f - 2 * at.x + 2 * j)
        return (2 * at.z + lax.div(j, 2), 8 * lax.rem(j, 2) + at.f - 8 * at.yl)

    def copy(self, phase, d, src, dst):
        sems = self.send.at[phase, d - 1], self.recv.at[phase, d - 1]
        return remote(src, dst, *sems, self.device(self.index(d)))

    def got(self, phase, d, dst):
        sems = self.send.at[phase, 3 - d], self.recv.at[phase, 3 - d]
        remote(dst, dst, *sems, self.device(self.index(d))).wait_recv()

    def spread(self, phase, buf):
        own = buf.at[block(self.pos)]
        for d in (1, 3, 2):
            self.copy(phase, d, own, own).start()

    def arrived(self, phase, d, buf):
        self.got(phase, d, buf.at[block(self.index(d))])

    def give(self, phase, d, src, dst):
        self.copy(phase, d, src.at[block(self.index(d))], dst.at[block(self.pos)]).start()

    def sent(self, phase, buf):
        own = buf.at[block(self.pos)]
        for d in (1, 3, 2):
            self.copy(phase, d, own, own).wait_send()

    def total(self, phase, own, parts):
        acc = own[block(self.pos), :].astype(jnp.float32)
        for d in (1, 3, 2):
            self.arrived(phase, d, parts)
            acc += parts[block(self.index(d)), :].astype(jnp.float32)
        return acc


class Plane:
    def __init__(self, at, send, recv):
        self.at, self.m = at, at.m
        self.send, self.recv = send, recv

    def device(self, q):
        return (2 * self.at.z + lax.rem(q, 2), q - lax.rem(q, 2) + self.at.c)

    def greet(self, bar):
        def one(i, carry):
            greet(bar, self.device(lax.rem(self.m + i + 1, 16)))
            return carry

        lax.fori_loop(0, 15, one, 0)

    def copy(self, phase, i, src_of, dst_of):
        q = lax.rem(self.m + i + 1, 16)
        return remote(src_of(q), dst_of(self.m), self.send.at[phase, i], self.recv.at[phase, i], self.device(q))

    def start(self, phase, src_of, dst_of):
        def one(i, carry):
            self.copy(phase, i, src_of, dst_of).start()
            return carry

        lax.fori_loop(0, 15, one, 0)

    def wait(self, phase, dst_of):
        def one(i, carry):
            q = lax.rem(self.m + 15 - i, 16)
            dst = dst_of(q)
            remote(dst, dst, self.send.at[phase, i], self.recv.at[phase, i], self.device(q)).wait_recv()
            return carry

        lax.fori_loop(0, 15, one, 0)

    def sent(self, phase, src_of, dst_of):
        def one(i, carry):
            self.copy(phase, i, src_of, dst_of).wait_send()
            return carry

        lax.fori_loop(0, 15, one, 0)


def piece(buf):
    return lambda q: buf.at[pl.ds(pl.multiple_of(q * 16, 16), 16)]


def keep_piece(at, src, dst):
    own = pl.ds(pl.multiple_of(at.m * 16, 16), 16)
    dst[own, :] = src[own, :]


def placings(route):
    row = lax.broadcasted_iota(jnp.int32, (256, 128), 0)
    inner = row & 15
    slot = (row >> 4) * 8 + (inner & 7)
    hit = slot == route
    left = jnp.where(hit & (inner < 8), 1.0, 0.0).astype(jnp.bfloat16)
    right = jnp.where(hit & (inner >= 8), 1.0, 0.0).astype(jnp.bfloat16)
    return left, right


def to_pieces(left, right, rows):
    half = rows.shape[1] // 2
    return (nn(left, rows[:, :half]) + nn(right, rows[:, half:])).astype(jnp.bfloat16)


def from_pieces(left, right, pieces):
    return jnp.concatenate([tn(left, pieces), tn(right, pieces)], axis=1).astype(jnp.bfloat16)


def rows_of(pieces):
    wide = pieces.astype(jnp.float32).reshape(16, 2, 8, 512)
    return jnp.concatenate([wide[:, 0].reshape(128, 512), wide[:, 1].reshape(128, 512)], axis=1)


def pieces_of(rows):
    left = rows[:, :512].reshape(16, 1, 8, 512)
    right = rows[:, 512:].reshape(16, 1, 8, 512)
    return jnp.concatenate([left, right], axis=1).reshape(256, 512).astype(jnp.bfloat16)


class Owners:
    def __init__(self, at, xs, xr, ys, yr, ks, kr):
        self.at = at
        self.ring_x, self.ring_y = Ring(at, "x", xs, xr), Ring(at, "y", ys, yr)
        self.ks, self.kr = ks, kr

    def along_y(self, phase, d, src, full):
        at = self.at
        return self.ring_y.copy(phase, d, src, full.at[at.yl, at.x, at.c, at.yh])

    def along_x(self, phase, d, full):
        own = full.at[:, self.at.x, self.at.c]
        return self.ring_x.copy(phase, d, own, own)

    def core(self, phase, full, c):
        half = full.at[:, :, c]
        return remote(half, half, self.ks.at[phase], self.kr.at[phase], self.at.other)

    def start(self, phase, src, full):
        at = self.at
        for d in (1, 3, 2):
            self.along_y(phase, d, src, full).start()
        full[at.yl, at.x, at.c, at.yh] = src[...]

    def step_x(self, phase, full):
        at = self.at
        for d in (1, 3, 2):
            j = self.ring_y.index(d)
            self.ring_y.got(phase, d, full.at[lax.rem(j, 2), at.x, at.c, lax.div(j, 2)])
        for d in (1, 3, 2):
            self.along_x(phase, d, full).start()

    def step_core(self, phase, full):
        for d in (1, 3, 2):
            self.ring_x.got(phase, d, full.at[:, self.ring_x.index(d), self.at.c])
        self.core(phase, full, self.at.c).start()

    def wait(self, phase, full):
        self.core(phase, full, 1 - self.at.c).wait_recv()

    def sent(self, phase, src, full):
        for d in (1, 3, 2):
            self.along_y(phase, d, src, full).wait_send()
            self.along_x(phase, d, full).wait_send()
        self.core(phase, full, self.at.c).wait_send()


def labels(position, first, second):
    return jnp.where(position >= first, 1, 0) + jnp.where(position >= second, 1, 0)


def masks(j, yh, docs):
    first, second = docs[0, 0], docs[0, 1]
    wide = 128 * (j + 1)
    row = lax.broadcasted_iota(jnp.int32, (128, wide), 0) + 128 * (2 * j + yh)
    lane = lax.broadcasted_iota(jnp.int32, (128, wide), 1)
    start = (lane >> 7) * 256 + (lane & 127)
    row_label = labels(row, first, second)
    found = []
    for parity in (yh, 1 - yh):
        key = start + 128 * parity
        found.append((key <= row) & (labels(key, first, second) == row_label))
    return found


def probabilities(q, keys, seen):
    scores = [jnp.where(ok, nt(q, k) * 0.125, masked_score) for k, ok in zip(keys, seen)]
    top = jnp.maximum(
        jnp.max(scores[0], axis=-1, keepdims=True), jnp.max(scores[1], axis=-1, keepdims=True)
    )
    weights = [jnp.exp(s - top) for s in scores]
    inverse = 1.0 / (split_sum(weights[0]) + split_sum(weights[1]))
    return [w * inverse for w in weights]


def head_lanes(h):
    lane = lax.broadcasted_iota(jnp.int32, (128, 128), 1)
    return lane < 64 if h == 0 else lane >= 64


def only(keep, values):
    return jnp.where(keep, values.astype(jnp.float32), 0.0).astype(jnp.bfloat16)


def wide_tile(full, tile):
    part = full[:, :, :, :, :, tile]
    return part.reshape(1024, part.shape[-1])


def tall_tile(full, n):
    part = full[n // 2, 2 * (n % 2) : 2 * (n % 2) + 2]
    return part.reshape(256, part.shape[-1])


def dense_forward_kernel(
    x, gain_tile, docs, route, cot, w_qkv, w_out, w_up, w_down, exp_in, exp_out,
    hid, mixed, after, gains,
    o_n1, o_n2, o_act, o_dg, o_q, o_kv, o_kvo, o_wq, o_wo, o_wu, o_wd, o_cz, o_in0, o_out0, o_in1,
    sq, su, wq, wo, wu, wd, gmine, gother,
    n1, n2, cz, qb, kvb, kvo, mixs, act, dg, ps, pr, sendc, arrc,
    zs, zr, xs, xr, ys, yr, kvs, kvr, ks, kr, gs, gr, cs, cr, ss, sr, osem,
):
    at = Place()
    z, yh, c, col = at.z, at.yh, at.c, at.col
    line, plane = Ring(at, "z", zs, zr), Plane(at, cs, cr)
    own = Owners(at, xs, xr, ys, yr, ks, kr)
    bar = pltpu.get_barrier_semaphore()
    for d in (1, 2, 3):
        greet(bar, line.device(line.index(d)))
    greet(bar, at.other)
    greet(bar, at.swap_mate)
    plane.greet(bar)
    for part in range(3):
        sq[:, 256 * part : 256 * part + 256] = w_qkv[:, pl.ds(pl.multiple_of(1024 * part + 256 * z, 256), 256)]
    xhat = norm_parts(x[...].astype(jnp.float32))[0]
    pl.semaphore_wait(bar, 20)
    tile_at = pl.ds(pl.multiple_of(128 * col, 128), 128)

    def group(i):
        return lax.rem(col + i + 1, 8)

    def gain_copy(i):
        return remote(gain_tile, gmine.at[:, tile_at], gs.at[i], gr.at[i], (at.s, 2 * group(i) + c))

    def push_gain(i, carry):
        gain_copy(i).start()
        return carry

    lax.fori_loop(0, 7, push_gain, 0)
    gmine[:, tile_at] = gain_tile[...]
    half = pl.ds(pl.multiple_of(32 * yh, 32), 32)
    down_rows = w_down.at[pl.ds(pl.multiple_of(64 * z + 32 * yh, 32), 32)]
    sources = (sq.at[half], w_out.at[half], su.at[half], down_rows)
    fulls = (wq, wo, wu, wd)
    own.start(0, sources[0], wq)

    def wait_gain(i, carry):
        q = lax.rem(col + 7 - i, 8)
        dst = gmine.at[:, pl.ds(pl.multiple_of(128 * q, 128), 128)]
        remote(dst, dst, gs.at[i], gr.at[i], (at.s, 2 * q + c)).wait_recv()
        return carry

    lax.fori_loop(0, 7, wait_gain, 0)
    gain_core = remote(gmine, gother, gs.at[7], gr.at[7], at.other)
    gain_core.start()
    gain_core.wait_recv()
    vectors = gmine[...].astype(jnp.float32) + gother[...].astype(jnp.float32)
    gains[...] = vectors[0:8]
    n1[block(z), :] = (xhat * gains[0:1, :] + gains[2:3, :]).astype(jnp.bfloat16)
    line.spread(0, n1)
    own.step_x(0, wq)
    low = lax.broadcasted_iota(jnp.int32, (64, 128), 1) < 64
    odd = lax.rem(z, 2) == 1
    for n in range(8):
        first = 512 * n + 128 * lax.div(z, 2)
        a = w_up[:, pl.ds(pl.multiple_of(first, 128), 128)].astype(jnp.float32)
        b = w_up[:, pl.ds(pl.multiple_of(first + 256, 128), 128)].astype(jnp.float32)
        kept = jnp.where(low, a, pltpu.roll(b, 64, 1))
        moved = jnp.where(low, pltpu.roll(a, 64, 1), b)
        su[:, 128 * n : 128 * n + 128] = jnp.where(odd, moved, kept).astype(jnp.bfloat16)
    for phase in (1, 2, 3):
        own.start(phase, sources[phase], fulls[phase])
    left, right = placings(route[0:1, :])
    sendc[...] = to_pieces(left, right, cot[...])
    own.step_core(0, wq)
    plane.start(0, piece(sendc), piece(arrc))
    keep_piece(at, sendc, arrc)
    for phase in (1, 2, 3):
        own.step_x(phase, fulls[phase])
    own.wait(0, wq)

    def kv_copy(i, j):
        return remote(kvb.at[block(j)], kvo.at[block(j)], kvs.at[i], kvr.at[i], at.mate)

    def project_qkv(i, carry):
        d = order(i)
        j = line.index(d)

        @pl.when(i > 0)
        def _():
            line.arrived(0, d, n1)

        values = n1[block(j), :]
        kvb[block(j), 0:256] = nn(values, wide_tile(wq, slice(256, 512))).astype(jnp.bfloat16)
        kvb[block(j), 256:512] = nn(values, wide_tile(wq, slice(512, 768))).astype(jnp.bfloat16)
        kv_copy(i, j).start()
        qb[block(j), :] = nn(values, wide_tile(wq, slice(0, 256))).astype(jnp.bfloat16)
        return carry

    lax.fori_loop(0, 4, project_qkv, 0)
    plane.wait(0, piece(arrc))
    cz[block(z), :] = rows_of(arrc[...]).astype(jnp.bfloat16)
    line.spread(4, cz)
    own.step_core(1, wo)
    for i in range(4):
        kv_copy(i, line.index(order(i))).wait_recv()
    swaps = [
        remote(exp_in.at[0], o_in0, ss.at[0], sr.at[0], at.swap_mate),
        remote(exp_out.at[0], o_out0, ss.at[1], sr.at[1], at.swap_mate),
        remote(exp_in.at[1], o_in1, ss.at[2], sr.at[2], at.swap_mate),
    ]

    @pl.when(c != yh)
    def _():
        for swap in swaps:
            swap.start()

    for j in range(4):
        seen = masks(j, yh, docs)
        wide = slice(0, 128 * (j + 1))
        for p in range(2):
            lanes = slice(128 * p, 128 * p + 128)
            value_lanes = slice(256 + 128 * p, 384 + 128 * p)
            q = qb[128 * j : 128 * j + 128, lanes]
            keys = [kvb[wide, lanes], kvo[wide, lanes]]
            values = [kvb[wide, value_lanes], kvo[wide, value_lanes]]
            outs = []
            for h in range(2):
                probs = probabilities(only(head_lanes(h), q), keys, seen)
                outs.append(
                    nn(probs[0].astype(jnp.bfloat16), values[0]) + nn(probs[1].astype(jnp.bfloat16), values[1])
                )
            mixs[128 * j : 128 * j + 128, lanes] = jnp.where(head_lanes(0), outs[0], outs[1]).astype(jnp.bfloat16)
    my_lanes = pl.ds(pl.multiple_of(256 * z, 256), 256)

    def mix_copy(d):
        return line.copy(1, d, mixs.at[block(line.index(d))], mixed.at[:, my_lanes])

    for d in (1, 3, 2):
        mix_copy(d).start()
    mixed[:, my_lanes] = mixs[block(z), :]
    own.step_core(2, wu)
    own.step_core(3, wd)
    own.wait(1, wo)
    for d in (1, 3, 2):
        line.got(1, d, mixed.at[:, pl.ds(pl.multiple_of(256 * line.index(d), 256), 256)])
    for n in range(4):
        tile = slice(256 * n, 256 * n + 256)
        after[:, tile] = x[:, tile].astype(jnp.float32) + nn(mixed[...], wide_tile(wo, tile))
    xhat = norm_parts(after[...])[0]
    n2[block(z), :] = (xhat * gains[1:2, :] + gains[3:4, :]).astype(jnp.bfloat16)
    line.spread(2, n2)
    own.wait(2, wu)
    own.wait(3, wd)
    stores = [
        pltpu.make_async_copy(src, dst, osem.at[k])
        for k, (src, dst) in enumerate(
            [(n1, o_n1), (qb, o_q), (kvb, o_kv), (kvo, o_kvo), (wq, o_wq), (wo, o_wo), (wu, o_wu), (wd, o_wd)]
        )
    ]
    for store in stores:
        store.start()

    def feed(i, carry):
        d = order(i)
        j = line.index(d)

        @pl.when(i > 0)
        def _():
            line.arrived(2, d, n2)

        values = n2[block(j), :]
        for n in range(4):
            tile = slice(n * 256, (n + 1) * 256)
            acted, slope = gelu_parts(nn(values, wide_tile(wu, tile)))
            act[block(j), tile] = acted.astype(jnp.bfloat16)
            dg[block(j), tile] = slope
        values = act[block(j), :]
        for n in range(4):
            tile = slice(n * 256, (n + 1) * 256)
            ps[block(j), tile] = nn(values, wide_tile(wd, tile)).astype(jnp.bfloat16)

        @pl.when(i > 0)
        def _():
            line.give(3, d, ps, pr)

        return carry

    lax.fori_loop(0, 4, feed, 0)
    for d in (1, 3, 2):
        line.arrived(4, d, cz)
    late = [
        pltpu.make_async_copy(src, dst, osem.at[8 + k])
        for k, (src, dst) in enumerate([(n2, o_n2), (act, o_act), (dg, o_dg), (cz, o_cz)])
    ]
    for store in late:
        store.start()
    gain_core.wait_send()

    def sent_gain(i, carry):
        gain_copy(i).wait_send()
        return carry

    lax.fori_loop(0, 7, sent_gain, 0)
    for phase in range(4):
        own.sent(phase, sources[phase], fulls[phase])
    for i in range(4):
        kv_copy(i, line.index(order(i))).wait_send()
    line.sent(0, n1)
    for d in (1, 3, 2):
        mix_copy(d).wait_send()
    line.sent(2, n2)
    line.sent(4, cz)
    plane.sent(0, piece(sendc), piece(arrc))
    hid[...] = (after[...] + line.total(3, ps, pr)).astype(jnp.bfloat16)
    line.sent(3, ps)

    @pl.when(c != yh)
    def _():
        for swap in swaps:
            swap.wait()

    for store in stores + late:
        store.wait()


def dense_forward_call(x, gain_tile, docs, route, cot, w_qkv, w_out, w_up, w_down, exp_in, exp_out):
    bf, f32 = jnp.bfloat16, jnp.float32
    vmem, anywhere = pl.BlockSpec(memory_space=pltpu.VMEM), pl.BlockSpec(memory_space=pl.ANY)
    smem = pl.BlockSpec(memory_space=pltpu.SMEM)
    shape, V, dma = jax.ShapeDtypeStruct, pltpu.VMEM, pltpu.SemaphoreType.DMA
    line = [V((512, 1024), bf)]
    weight = [(2, 4, 2, 2, 32, 768)] + [(2, 4, 2, 2, 32, 1024)] * 3
    saved = [
        shape((512, 1024), bf), shape((512, 1024), bf), shape((512, 1024), bf), shape((512, 1024), f32),
        shape((512, 256), bf), shape((512, 512), bf), shape((512, 512), bf),
    ] + [shape(w, bf) for w in weight] + [
        shape((512, 1024), bf), shape((1024, 512), bf), shape((512, 1024), bf), shape((1024, 512), bf),
    ]
    return pl.pallas_call(
        dense_forward_kernel,
        out_shape=[shape((128, 1024), bf), shape((128, 1024), bf), shape((128, 1024), f32), shape((8, 1024), f32)]
        + saved,
        in_specs=[vmem, vmem, smem] + [vmem] * 6 + [anywhere, anywhere],
        out_specs=[vmem] * 4 + [anywhere] * len(saved),
        scratch_shapes=[
            V((64, 768), bf), V((64, 1024), bf), *[V(w, bf) for w in weight], V((16, 1024), bf), V((16, 1024), bf),
            *(line * 3), V((512, 256), bf), V((512, 512), bf), V((512, 512), bf), V((512, 256), bf),
            *line, V((512, 1024), f32), *(line * 2), V((256, 512), bf), V((256, 512), bf),
            dma((5, 3)), dma((5, 3)), dma((4, 3)), dma((4, 3)), dma((4, 3)), dma((4, 3)), dma((4,)), dma((4,)),
            dma((4,)), dma((4,)), dma((8,)), dma((8,)), dma((1, 15)), dma((1, 15)), dma((3,)), dma((3,)), dma((12,)),
        ],
        compiler_params=pltpu.CompilerParams(collective_id=2, has_side_effects=True, vmem_limit_bytes=60 << 20),
        name="dense_forward",
    )(x, gain_tile, docs, route, cot, w_qkv, w_out, w_up, w_down, exp_in, exp_out)


def expert_kernel(
    hid, route, vec, cz_h, exp_in, exp_out, in0, out0, in1,
    gh, vecg, mid, gate_out, o_ps, gin1, gout1, gin0, gout0,
    w_in, w_out, sendh, sendg, arrh, arrg, cz,
    e0, e1, g0, g1, ps0, ps1, pr0, pb0, pb1,
    act0, act1, dg0, dg1, gp0, gp1,
    arrived, base, xh0, xh1, sc, gates, dots, dots_in,
    ga_in, ga_out, sb_in, sb_out, rb_in, rb_out, vmine, vcore, vline, vsum, vswap,
    wsem, zs, zr, cs, cr, ks, kr, osem, bs, br, ss, sr, vs, vr,
):
    at = Place()
    z, yh, c, same = at.z, at.yh, at.c, at.same
    line, plane = Ring(at, "z", zs, zr), Plane(at, cs, cr)
    bar = pltpu.get_barrier_semaphore()
    plane.greet(bar)
    for d in (1, 2, 3):
        greet(bar, line.device(line.index(d)))
    greet(bar, at.other)
    greet(bar, at.swap_mate)
    low, high = slice(0, 512), slice(512, 1024)

    def slot(k, i, half):
        return w_in.at[k, :, half] if i == 0 else w_out.at[k, half, :]

    def load(k, i):
        return pltpu.make_async_copy((exp_in, exp_out)[i].at[k], slot(k, i, low), wsem.at[k, i])

    def swapped(k, i):
        return pltpu.make_async_copy((in0, out0)[i] if k == 0 else in1, slot(k, i, low), wsem.at[k, i])

    swap_out = remote(exp_out.at[1], slot(1, 1, low), ss.at[0], sr.at[0], at.swap_mate)

    def share(k, i):
        return remote(slot(k, i, low), slot(k, i, high), bs.at[k, i], br.at[k, i], at.other)

    def on_either(when_same, when_swapped):
        pl.when(same)(when_same)
        pl.when(jnp.logical_not(same))(when_swapped)

    load_c = pltpu.make_async_copy(cz_h, cz, wsem.at[2, 0])

    def begin_same():
        for k, i in ((0, 0), (0, 1), (1, 0), (1, 1)):
            load(k, i).start()

    def begin_swapped():
        for k, i in ((0, 0), (0, 1), (1, 0)):
            swapped(k, i).start()

    on_either(begin_same, begin_swapped)
    load_c.start()
    left, right = placings(route[0:1, :])
    sendh[...] = to_pieces(left, right, hid[...])
    pl.semaphore_wait(bar, 20)
    plane.start(0, piece(sendh), piece(arrh))
    keep_piece(at, sendh, arrh)

    def wait_loads(k, i):
        on_either(lambda: load(k, i).wait(), lambda: swapped(k, i).wait())
        share(k, i).start()

    pl.when(jnp.logical_not(same))(lambda: swap_out.start())
    wait_loads(0, 0)
    wait_loads(0, 1)
    wait_loads(1, 0)
    plane.wait(0, piece(arrh))
    gain = [vec[0:1, :], vec[1:2, :]]
    bias = [vec[2:3, :], vec[3:4, :]]
    rows = rows_of(arrh[...])
    arrived[...] = rows
    xhat, scale = norm_parts(rows)
    xh0[...] = xhat
    sc[0] = jnp.broadcast_to(scale, (128, 128))
    e0[block(z), :] = (xhat * gain[0] + bias[0]).astype(jnp.bfloat16)
    line.spread(0, e0)
    gating = jax.nn.sigmoid(split_sum(rows * vec[4:5, :]))
    gates[z] = jnp.broadcast_to(gating, (128, 128))

    def gate_copy(d):
        return line.copy(3, d, gates.at[z], gates.at[z])

    for d in (1, 3, 2):
        gate_copy(d).start()
    share(0, 0).wait_recv()
    share(0, 1).wait_recv()
    load_c.wait()

    def forward(k, j, rows_in, act, dg):
        values = rows_in[block(j), :]
        for n in range(4):
            tile = slice(n * 256, (n + 1) * 256)
            pre = nn(values, w_in[k, :, tile])
            acted, slope = gelu_parts(pre)
            act[block(j), tile] = acted.astype(jnp.bfloat16)
            dg[block(j), tile] = slope

    def project(k, j, act, part):
        values = act[block(j), :]
        for n in range(4):
            tile = slice(n * 256, (n + 1) * 256)
            part[block(j), tile] = nn(values, w_out[k, :, tile]).astype(jnp.bfloat16)

    def backward(k, j, grad, dg, gp, part):
        values = grad[block(j), :]
        for n in range(4):
            tile = slice(n * 256, (n + 1) * 256)
            slope = dg[block(j), tile] * nt(values, w_out[k, tile, :])
            gp[block(j), tile] = slope.astype(jnp.bfloat16)
        pres = gp[block(j), :]
        for n in range(4):
            tile = slice(n * 256, (n + 1) * 256)
            part[block(j), tile] = nt(pres, w_in[k, tile, :]).astype(jnp.bfloat16)

    def sub0(i, carry):
        d = order(i)
        j = line.index(d)

        @pl.when(i > 0)
        def _():
            line.arrived(0, d, e0)

        forward(0, j, e0, act0, dg0)
        project(0, j, act0, ps0)

        @pl.when(i > 0)
        def _():
            line.give(1, d, ps0, pr0)

        return carry

    lax.fori_loop(0, 4, sub0, 0)
    on_either(lambda: load(1, 1).wait(), lambda: swap_out.wait())
    share(1, 1).start()
    stream = arrived[...] + line.total(1, ps0, pr0)
    base[...] = stream
    xhat, scale = norm_parts(stream)
    xh1[...] = xhat
    sc[1] = jnp.broadcast_to(scale, (128, 128))
    e1[block(z), :] = (xhat * gain[1] + bias[1]).astype(jnp.bfloat16)
    line.spread(2, e1)
    gate = gates[z][:, 0:1]
    mid[...] = arrived[...] + gate * (base[...] - arrived[...])
    gate_out[...] = gates[z]
    line.sent(1, ps0)
    share(1, 0).wait_recv()
    share(1, 1).wait_recv()

    def sub1(i, carry):
        d = order(i)
        j = line.index(d)

        @pl.when(i > 0)
        def _():
            line.got(3, d, gates.at[j])

        g1[block(j), :] = (gates[j][:, 0:1] * cz[block(j), :].astype(jnp.float32)).astype(jnp.bfloat16)

        @pl.when(i > 0)
        def _():
            line.arrived(2, d, e1)

        forward(1, j, e1, act1, dg1)
        backward(1, j, g1, dg1, gp1, ps0)

        @pl.when(i > 0)
        def _():
            line.give(4, d, ps0, pb1)

        return carry

    lax.fori_loop(0, 4, sub1, 0)

    def second_part(i, carry):
        d = order(3 - i)
        j = line.index(d)
        project(1, j, act1, ps1)
        products = cz[block(j), :].astype(jnp.float32) * ps1[block(j), :].astype(jnp.float32)
        dots[j] = jnp.broadcast_to(split_sum(products), (128, 128))

        @pl.when(i < 3)
        def _():
            line.copy(5, d, dots.at[j], dots_in.at[z]).start()

        return carry

    lax.fori_loop(0, 4, second_part, 0)
    keep_ps = pltpu.make_async_copy(ps1, o_ps, wsem.at[2, 1])
    keep_ps.start()

    def weight_grads(k, rows_in, gp, act, grad):
        def one(n, carry):
            tile = pl.ds(pl.multiple_of(n * 256, 256), 256)
            tile_b = pl.ds(pl.multiple_of(n * 256 + 512, 256), 256)
            ga_out[k, tile, :] = tn(act[:, tile], grad[...])
            sb_out[k, tile, :] = tn(act[:, tile_b], grad[...]).astype(jnp.bfloat16)
            return carry

        lax.fori_loop(0, 2, one, 0)

        def two(n, carry):
            tile = pl.ds(pl.multiple_of(n * 256, 256), 256)
            ga_in[k, tile, :] = tn(rows_in[:, tile], gp[:, 0:512])
            sb_in[k, tile, :] = tn(rows_in[:, tile], gp[:, 512:1024]).astype(jnp.bfloat16)
            return carry

        lax.fori_loop(0, 4, two, 0)

    def swap(k, i):
        src, dst = ((sb_in, rb_in), (sb_out, rb_out))[i]
        return remote(src.at[k], dst.at[k], ks.at[k, i], kr.at[k, i], at.other)

    def join_cores(k):
        for i in range(2):
            swap(k, i).wait()
        sb_in[k] = (ga_in[k] + rb_in[k].astype(jnp.float32)).astype(jnp.bfloat16)
        sb_out[k] = (ga_out[k] + rb_out[k].astype(jnp.float32)).astype(jnp.bfloat16)

    weight_grads(1, e1, gp1, act1, g1)
    swap(1, 0).start()
    swap(1, 1).start()
    grad_normed = line.total(4, ps0, pb1)
    cot = cz[block(z), :].astype(jnp.float32)
    grad_stream = gates[z][:, 0:1] * cot
    grad_stream += norm_back(grad_normed, gain[1], xh1[...], sc[1][:, 0:1])
    g0[block(z), :] = grad_stream.astype(jnp.bfloat16)
    line.spread(6, g0)
    vmine[1:2, :] = jnp.sum(grad_normed * xh1[...], axis=0, keepdims=True)
    vmine[3:4, :] = jnp.sum(grad_normed, axis=0, keepdims=True)
    line.sent(4, ps0)
    grad_gating = split_sum(cot * (base[...] - arrived[...])) + dots[z][:, 0:1]
    for d in (1, 3, 2):
        line.got(5, d, dots_in.at[line.index(d)])
        grad_gating += dots_in[line.index(d)][:, 0:1]
    gate = gates[z][:, 0:1]
    grad_logit = gate * (1.0 - gate) * grad_gating
    vmine[4:5, :] = jnp.sum(grad_logit * arrived[...], axis=0, keepdims=True)
    base[...] = grad_stream + (1.0 - gate) * cot + grad_logit * vec[4:5, :]
    join_cores(1)
    kept = [
        pltpu.make_async_copy(sb_in.at[1], gin1, osem.at[1, 0]),
        pltpu.make_async_copy(sb_out.at[1], gout1, osem.at[1, 1]),
    ]
    given = [
        remote(sb_in.at[1], gin1, ss.at[1], sr.at[1], at.swap_mate),
        remote(sb_out.at[1], gout1, ss.at[2], sr.at[2], at.swap_mate),
    ]

    def begin(copies):
        for copy in copies:
            copy.start()

    def finish(copies):
        for copy in copies:
            copy.wait()

    on_either(lambda: begin(kept), lambda: begin(given))

    def sub0_back(i, carry):
        d = order(i)
        j = line.index(d)

        @pl.when(i > 0)
        def _():
            line.arrived(6, d, g0)

        backward(0, j, g0, dg0, gp0, ps0)

        @pl.when(i > 0)
        def _():
            line.give(7, d, ps0, pb0)

        return carry

    lax.fori_loop(0, 4, sub0_back, 0)
    weight_grads(0, e0, gp0, act0, g0)
    swap(0, 0).start()
    swap(0, 1).start()
    grad_normed = line.total(7, ps0, pb0)
    grad_stream = base[...] + norm_back(grad_normed, gain[0], xh0[...], sc[0][:, 0:1])
    sendg[...] = pieces_of(grad_stream)
    plane.start(1, piece(sendg), piece(arrg))
    keep_piece(at, sendg, arrg)
    vmine[0:1, :] = jnp.sum(grad_normed * xh0[...], axis=0, keepdims=True)
    vmine[2:3, :] = jnp.sum(grad_normed, axis=0, keepdims=True)
    vmine[5:8, :] = jnp.zeros((3, 1024), jnp.float32)
    give_core = remote(vmine, vcore, vs.at[0], vr.at[0], at.other)
    give_core.start()
    give_core.wait_recv()
    vline[z] = vmine[...] + vcore[...]

    def give_line(d):
        return line.copy(8, d, vline.at[z], vline.at[z])

    for d in (1, 3, 2):
        give_line(d).start()
    join_cores(0)
    stores = [
        pltpu.make_async_copy(sb_in.at[0], gin0, osem.at[0, 0]),
        pltpu.make_async_copy(sb_out.at[0], gout0, osem.at[0, 1]),
    ]
    begin(stores)
    plane.wait(1, piece(arrg))
    left, right = placings(route[0:1, :])
    gh[...] = from_pieces(left, right, arrg[...])
    for d in (1, 3, 2):
        line.got(8, d, vline.at[line.index(d)])
    vsum[...] = vline[0] + vline[1] + vline[2] + vline[3]
    give_mate = remote(vsum, vswap, vs.at[1], vr.at[1], at.swap_mate)
    pl.when(jnp.logical_not(same))(lambda: give_mate.start())
    give_core.wait_send()
    for d in (1, 3, 2):
        give_line(d).wait_send()
        gate_copy(d).wait_send()
        line.copy(5, d, dots.at[line.index(d)], dots_in.at[z]).wait_send()
    for k in (0, 1):
        for i in range(2):
            share(k, i).wait_send()
    line.sent(0, e0)
    line.sent(2, e1)
    line.sent(6, g0)
    line.sent(7, ps0)
    plane.sent(0, piece(sendh), piece(arrh))
    plane.sent(1, piece(sendg), piece(arrg))
    keep_ps.wait()
    finish(stores)
    on_either(lambda: finish(kept), lambda: finish(given))

    @pl.when(same)
    def _():
        vecg[...] = vsum[...]

    @pl.when(jnp.logical_not(same))
    def _():
        give_mate.wait()
        vecg[...] = vswap[...]


def expert_call(hid, route, vec, cz, exp_in, exp_out, in0, out0, in1):
    bf, f32 = jnp.bfloat16, jnp.float32
    vmem, anywhere = pl.BlockSpec(memory_space=pltpu.VMEM), pl.BlockSpec(memory_space=pl.ANY)
    shape, V, dma = jax.ShapeDtypeStruct, pltpu.VMEM, pltpu.SemaphoreType.DMA
    line, rows, pieces = [V((512, 1024), bf)], [V((128, 1024), f32)], [V((256, 512), bf)]
    wide, small = [V((512, 1024), f32)], [V((4, 128, 128), f32)]
    vectors = [V((8, 1024), f32)]
    return pl.pallas_call(
        expert_kernel,
        out_shape=(
            shape((128, 1024), bf), shape((8, 1024), f32), shape((128, 1024), f32), shape((128, 128), f32),
            shape((512, 1024), bf), shape((1024, 512), bf), shape((512, 1024), bf), shape((1024, 512), bf),
            shape((512, 1024), bf),
        ),
        in_specs=[vmem] * 3 + [anywhere] * 6,
        out_specs=tuple([vmem] * 4 + [anywhere] * 5),
        scratch_shapes=[
            V((2, 1024, 1024), bf), V((2, 1024, 1024), bf), *(pieces * 4), *line,
            *(line * 9), *(line * 2), *(wide * 2), *(line * 2),
            *(rows * 4), *(small * 4),
            V((2, 1024, 512), f32), V((2, 512, 1024), f32),
            V((2, 1024, 512), bf), V((2, 512, 1024), bf), V((2, 1024, 512), bf), V((2, 512, 1024), bf),
            *(vectors * 2), V((4, 8, 1024), f32), *(vectors * 2),
            dma((3, 2)), dma((9, 3)), dma((9, 3)), dma((2, 15)), dma((2, 15)), dma((2, 2)), dma((2, 2)), dma((2, 2)),
            dma((2, 2)), dma((2, 2)), dma((3,)), dma((3,)), dma((2,)), dma((2,)),
        ],
        compiler_params=pltpu.CompilerParams(collective_id=1, has_side_effects=True, vmem_limit_bytes=60 << 20),
        name="experts",
    )(hid, route, vec, cz, exp_in, exp_out, in0, out0, in1)


class Everyone:
    def __init__(self, at, send, recv):
        self.at, self.send, self.recv = at, send, recv

    def copy(self, phase, i, buf):
        own = buf.at[self.at.s]
        to = (lax.rem(self.at.s + i + 1, 8), self.at.f)
        return remote(own, own, self.send.at[phase, i], self.recv.at[phase, i], to)

    def start(self, phase, buf):
        for i in range(7):
            self.copy(phase, i, buf).start()

    def wait(self, phase, buf):
        for i in range(7):
            q = lax.rem(self.at.s + 7 - i, 8)
            dst = buf.at[q]
            remote(dst, dst, self.send.at[phase, i], self.recv.at[phase, i], (q, self.at.f)).wait_recv()

    def sent(self, phase, buf):
        for i in range(7):
            self.copy(phase, i, buf).wait_send()


def dense_backward_kernel(
    gh, x, after, docs, gains, mixed, route, mid, gate, n1_h, n2_h, act_h, dg_h, q_h, kv_h, kvo_h, wq_h, wo_h, wu_h,
    wd_h, ps_h, gin0, gout0,
    gx, gq, go, gu, gd, gvec, res, fin0, fout0,
    ghs, n1, n2, act, dg, gp, qb, kvb, kvo, wq, wo, wu, wd,
    ps, pr, ps2, pr2, ps3, pr3, gms, gm, dp, dkv, dkvo, kvs, kvr,
    md, mu, mo, mq, td, tu, to, tq, rd, ru, ro, rq, xd, xu, xo, sd, su, so, yd, yu, yo, rp, sendr, arrr,
    vmine, vcore, vplane, vline, outz, bd, bu, bo, bq,
    lsem, zs, zr, xs, xr, ys, yr, kvss, kvsr, ks, kr, cs, cr, qs, qr, ss, sr, vs, vr,
):
    at = Place()
    z, yh, c, col = at.z, at.yh, at.c, at.col
    line, ring_x, ring_y = Ring(at, "z", zs, zr), Ring(at, "x", xs, xr), Ring(at, "y", ys, yr)
    plane, everyone = Plane(at, cs, cr), Everyone(at, qs, qr)
    bar = pltpu.get_barrier_semaphore()
    plane.greet(bar)
    for d in (1, 2, 3):
        greet(bar, line.device(line.index(d)))
        greet(bar, (2 * line.index(d) + 1 - yh, at.f))
    greet(bar, at.other)
    greet(bar, at.swap_mate)
    loads = [
        pltpu.make_async_copy(src, dst, lsem.at[k])
        for k, (src, dst) in enumerate(
            [
                (wd_h, wd), (dg_h, dg), (wu_h, wu), (act_h, act), (n2_h, n2), (wo_h, wo), (ps_h, ps3), (q_h, qb),
                (kv_h, kvb), (kvo_h, kvo), (wq_h, wq), (n1_h, n1),
            ]
        )
    ]
    for load in loads:
        load.start()
    ghs[block(z), :] = gh[...]
    pl.semaphore_wait(bar, 23)
    line.spread(0, ghs)
    swaps = [
        remote(gin0, fin0, ss.at[0], sr.at[0], at.swap_mate),
        remote(gout0, fout0, ss.at[1], sr.at[1], at.swap_mate),
    ]
    keeps = [
        pltpu.make_async_copy(gin0, fin0, lsem.at[12]),
        pltpu.make_async_copy(gout0, fout0, lsem.at[13]),
    ]

    @pl.when(at.same)
    def _():
        for keep in keeps:
            keep.start()

    @pl.when(jnp.logical_not(at.same))
    def _():
        for swap in swaps:
            swap.start()

    for load in loads[:3]:
        load.wait()

    def feed(i, carry):
        d = order(i)
        j = line.index(d)

        @pl.when(i > 0)
        def _():
            line.arrived(0, d, ghs)

        values = ghs[block(j), :]
        for n in range(4):
            tile = slice(n * 256, (n + 1) * 256)
            gp[block(j), tile] = (dg[block(j), tile] * nt(values, tall_tile(wd, n))).astype(jnp.bfloat16)
        pres = gp[block(j), :]
        for n in range(4):
            tile = slice(n * 256, (n + 1) * 256)
            ps[block(j), tile] = nt(pres, tall_tile(wu, n)).astype(jnp.bfloat16)

        @pl.when(i > 0)
        def _():
            line.give(1, d, ps, pr)

        return carry

    lax.fori_loop(0, 4, feed, 0)
    for load in loads[3:7]:
        load.wait()

    def weight_grad(lhs, rhs, mine, theirs):
        def one(n, carry):
            rows = lhs[:, pl.ds(pl.multiple_of(n * 256, 256), 256)]
            grad = tn(rows, rhs[...])
            for half in range(2):
                first = grad[128 * half : 128 * half + 64].astype(jnp.bfloat16)
                second = grad[128 * half + 64 : 128 * half + 128].astype(jnp.bfloat16)
                here = lax.div(n, 2), 2 * lax.rem(n, 2) + half
                mine[here] = jnp.where(c == 0, first, second)
                theirs[here] = jnp.where(c == 0, second, first)
            return carry

        lax.fori_loop(0, 4, one, 0)

    def core_copy(phase, src, dst):
        return remote(src, dst, ks.at[phase], kr.at[phase], at.other)

    def join_cores(phase, mine, theirs, got):
        core_copy(phase, theirs, got).wait()

        def one(n, carry):
            here = lax.div(n, 4), lax.rem(n, 4)
            mine[here] = (mine[here].astype(jnp.float32) + got[here].astype(jnp.float32)).astype(jnp.bfloat16)
            return carry

        lax.fori_loop(0, 8, one, 0)

    def x_copy(phase, d, mine, dst):
        return ring_x.copy(phase, d, mine.at[:, ring_x.index(d)], dst.at[at.x])

    def y_copy(phase, d, part, dst):
        j = ring_y.index(d)
        src = part.at[lax.rem(j, 2), pl.ds(pl.multiple_of(32 * lax.div(j, 2), 32), 32)]
        return ring_y.copy(phase, d, src, dst.at[ring_y.pos])

    def to_x(phase, mine, dst):
        for d in (1, 3, 2):
            x_copy(phase, d, mine, dst).start()

    def to_y(phase, mine, got, part, dst):
        acc = mine[:, at.x].astype(jnp.float32)
        for d in (1, 3, 2):
            j = ring_x.index(d)
            ring_x.got(phase, d, got.at[j])
            acc += got[j].astype(jnp.float32)
        part[...] = acc.astype(jnp.bfloat16)
        for d in (1, 3, 2):
            y_copy(phase, d, part, dst).start()

    def y_total(phase, part, got):
        acc = part[at.yl, pl.ds(pl.multiple_of(32 * yh, 32), 32), :].astype(jnp.float32)
        for d in (1, 3, 2):
            j = ring_y.index(d)
            ring_y.got(phase, d, got.at[j])
            acc += got[j].astype(jnp.float32)
        return acc

    weight_grad(act, ghs, md, td)
    core_copy(0, td, rd).start()
    weight_grad(n2, gp, mu, tu)
    core_copy(1, tu, ru).start()
    join_cores(0, md, td, rd)
    to_x(0, md, xd)
    join_cores(1, mu, tu, ru)
    to_x(1, mu, xu)
    grad_normed = line.total(1, ps, pr)
    xhat, scale = norm_parts(after[...])
    vmine[1:2, :] = jnp.sum(grad_normed * xhat, axis=0, keepdims=True)
    vmine[3:4, :] = jnp.sum(grad_normed, axis=0, keepdims=True)
    grad_after = gh[...].astype(jnp.float32) + norm_back(grad_normed, gains[1:2, :], xhat, scale)
    gx[...] = grad_after
    grad_attn = grad_after.astype(jnp.bfloat16)
    for n in range(4):
        gms[:, 256 * n : 256 * n + 256] = nt(grad_attn, tall_tile(wo, n)).astype(jnp.bfloat16)

    def gm_copy(d):
        lanes = pl.ds(pl.multiple_of(256 * line.index(d), 256), 256)
        return line.copy(2, d, gms.at[:, lanes], gm.at[block(z)])

    for d in (1, 3, 2):
        gm_copy(d).start()
    gm[block(z), :] = gms[:, pl.ds(pl.multiple_of(256 * z, 256), 256)]
    for d in (1, 3, 2):
        line.give(6, d, ps3, pr3)
    gp[block(0), :] = grad_attn
    weight_grad(mixed, gp.at[block(0)], mo, to)
    core_copy(2, to, ro).start()
    to_y(0, md, xd, sd, yd)
    join_cores(2, mo, to, ro)
    to_x(2, mo, xo)
    for load in loads[7:]:
        load.wait()
    for d in (1, 3, 2):
        line.arrived(2, d, gm)
    dkv[...] = jnp.zeros_like(dkv)
    dkvo[...] = jnp.zeros_like(dkvo)

    def kv_copy(j):
        return remote(kvs.at[block(j)], kvr.at[block(j)], kvss.at[j], kvsr.at[j], at.mate)

    def attend_back(j):
        seen = masks(j, yh, docs)
        wide = slice(0, 128 * (j + 1))
        rows = slice(128 * j, 128 * j + 128)
        for p in range(2):
            lanes = slice(128 * p, 128 * p + 128)
            value_lanes = slice(256 + 128 * p, 384 + 128 * p)
            q, grad = qb[rows, lanes], gm[rows, lanes]
            keys = [kvb[wide, lanes], kvo[wide, lanes]]
            values = [kvb[wide, value_lanes], kvo[wide, value_lanes]]
            outs = []
            for h in range(2):
                q_h, grad_h = only(head_lanes(h), q), only(head_lanes(h), grad)
                probs = probabilities(q_h, keys, seen)
                back = [nt(grad_h, v) for v in values]
                dot = split_sum(probs[0] * back[0]) + split_sum(probs[1] * back[1])
                slopes = [(prob * (b - dot)).astype(jnp.bfloat16) for prob, b in zip(probs, back)]
                outs.append(nn(slopes[0], keys[0]) + nn(slopes[1], keys[1]))
                for k, acc in enumerate((dkv, dkvo)):
                    acc[wide, lanes] += tn(slopes[k], q_h) * 0.125
                    acc[wide, value_lanes] += tn(probs[k].astype(jnp.bfloat16), grad_h)
            dp[rows, lanes] = (jnp.where(head_lanes(0), outs[0], outs[1]) * 0.125).astype(jnp.bfloat16)
        kvs[rows, :] = dkvo[rows, :].astype(jnp.bfloat16)
        kv_copy(j).start()

    attend_back(3)
    attend_back(2)
    to_y(1, mu, xu, su, yu)
    attend_back(1)
    attend_back(0)
    sendr[...] = pieces_of(mid[...] + gate[:, 0:1] * line.total(6, ps3, pr3))
    plane.start(2, piece(sendr), piece(arrr))
    keep_piece(at, sendr, arrr)
    to_y(2, mo, xo, so, yo)
    for j in (3, 2, 1, 0):
        rows = slice(128 * j, 128 * j + 128)
        kv_copy(j).wait_recv()
        dp[rows, 256:768] = (dkv[rows, :] + kvr[rows, :].astype(jnp.float32)).astype(jnp.bfloat16)

    def last(i, carry):
        d = order(3 - i)
        j = line.index(d)
        values = dp[block(j), :]
        for n in range(4):
            tile = slice(n * 256, (n + 1) * 256)
            ps2[block(j), tile] = nt(values, tall_tile(wq, n)).astype(jnp.bfloat16)

        @pl.when(i < 3)
        def _():
            line.give(3, d, ps2, pr2)

        return carry

    lax.fori_loop(0, 4, last, 0)
    weight_grad(n1, dp, mq, tq)
    core_copy(3, tq, rq).start()
    bd[at.s] = y_total(0, sd, yd).astype(jnp.bfloat16)
    everyone.start(0, bd)
    join_cores(3, mq, tq, rq)

    def piece_q(q):
        return mq.at[lax.div(q, 8), lax.rem(lax.div(q, 2), 4), pl.ds(pl.multiple_of(32 * lax.rem(q, 2), 32), 32)]

    def slot_q(q):
        return rp.at[q]

    plane.start(0, piece_q, slot_q)
    rp[at.m] = mq[at.yl, at.x, pl.ds(pl.multiple_of(32 * yh, 32), 32), :]
    bu[at.s] = y_total(1, su, yu).astype(jnp.bfloat16)
    everyone.start(1, bu)
    total_out = y_total(2, so, yo)
    for n in range(4):
        outz[4 + n] = total_out[:, 256 * n : 256 * n + 256].astype(jnp.bfloat16)

    def out_copy(d):
        return line.copy(4, d, outz.at[4 + line.index(d)], outz.at[z])

    for d in (1, 3, 2):
        out_copy(d).start()
    grad_normed = line.total(3, ps2, pr2)
    xhat, scale = norm_parts(x[...].astype(jnp.float32))
    vmine[0:1, :] = jnp.sum(grad_normed * xhat, axis=0, keepdims=True)
    vmine[2:3, :] = jnp.sum(grad_normed, axis=0, keepdims=True)
    vmine[4:8, :] = jnp.zeros((4, 1024), jnp.float32)
    give_core = remote(vmine, vcore, vs.at[0], vr.at[0], at.other)
    give_core.start()
    gx[...] += norm_back(grad_normed, gains[0:1, :], xhat, scale)
    give_core.wait()
    vmine[...] += vcore[...]

    def tile_of(q):
        return vmine.at[:, pl.ds(pl.multiple_of(128 * lax.div(q, 2), 128), 128)]

    def slot_v(q):
        return vplane.at[q]

    plane.start(1, tile_of, slot_v)
    vplane[at.m] = vmine[:, pl.ds(pl.multiple_of(128 * col, 128), 128)]
    acc = outz[4 + z].astype(jnp.float32)
    for d in (1, 3, 2):
        line.got(4, d, outz.at[line.index(d)])
        acc += outz[line.index(d)].astype(jnp.float32)
    bo[at.s] = acc.astype(jnp.bfloat16)
    everyone.start(2, bo)
    plane.wait(0, slot_q)
    acc = rp[0].astype(jnp.float32)
    for q in range(1, 16):
        acc += rp[q].astype(jnp.float32)
    bq[at.s] = acc.astype(jnp.bfloat16)
    everyone.start(3, bq)
    plane.wait(1, slot_v)
    vline[z] = jnp.sum(vplane[...], axis=0)

    def vec_copy(d):
        return line.copy(5, d, vline.at[z], vline.at[z])

    for d in (1, 3, 2):
        vec_copy(d).start()
    plane.wait(2, piece(arrr))
    left, right = placings(route[0:1, :])
    res[...] = from_pieces(left, right, arrr[...])
    everyone.wait(0, bd)
    everyone.wait(1, bu)
    for zz in range(4):
        for half in range(2):
            gd[64 * zz + 32 * half : 64 * zz + 32 * half + 32, :] = bd[2 * zz + half].astype(jnp.float32)
    for half in range(2):
        rows = slice(32 * half, 32 * half + 32)
        lane = lax.broadcasted_iota(jnp.int32, (32, 128), 1) < 64
        for n in range(8):
            tile = slice(128 * n, 128 * n + 128)
            quarter = [bu[2 * zz + half, :, tile].astype(jnp.float32) for zz in range(4)]
            turned = [pltpu.roll(v, 64, 1) for v in quarter]
            first = 512 * n
            gu[rows, first : first + 128] = jnp.where(lane, quarter[0], turned[1])
            gu[rows, first + 128 : first + 256] = jnp.where(lane, quarter[2], turned[3])
            gu[rows, first + 256 : first + 384] = jnp.where(lane, turned[0], quarter[1])
            gu[rows, first + 384 : first + 512] = jnp.where(lane, turned[2], quarter[3])
    everyone.wait(2, bo)
    for zz in range(4):
        for half in range(2):
            go[32 * half : 32 * half + 32, 256 * zz : 256 * zz + 256] = bo[2 * zz + half].astype(jnp.float32)
    everyone.wait(3, bq)
    for zz in range(4):
        for half in range(2):
            for part in range(3):
                gq[32 * half : 32 * half + 32, 1024 * part + 256 * zz : 1024 * part + 256 * zz + 256] = bq[
                    2 * zz + half, :, 256 * part : 256 * part + 256
                ].astype(jnp.float32)
    for d in (1, 3, 2):
        line.got(5, d, vline.at[line.index(d)])
    gvec[...] = jnp.sum(vline[...], axis=0)
    line.sent(0, ghs)
    line.sent(1, ps)
    line.sent(3, ps2)
    line.sent(6, ps3)
    for d in (1, 3, 2):
        gm_copy(d).wait_send()
        out_copy(d).wait_send()
        vec_copy(d).wait_send()
        for phase, (mine, x_got, part, y_got) in enumerate(((md, xd, sd, yd), (mu, xu, su, yu), (mo, xo, so, yo))):
            x_copy(phase, d, mine, x_got).wait_send()
            y_copy(phase, d, part, y_got).wait_send()
    for j in range(4):
        kv_copy(j).wait_send()
    plane.sent(0, piece_q, slot_q)
    plane.sent(1, tile_of, slot_v)
    plane.sent(2, piece(sendr), piece(arrr))
    for phase, buf in enumerate((bd, bu, bo, bq)):
        everyone.sent(phase, buf)

    @pl.when(at.same)
    def _():
        for keep in keeps:
            keep.wait()

    @pl.when(jnp.logical_not(at.same))
    def _():
        for swap in swaps:
            swap.wait()


def dense_backward_call(gh, x, after, docs, gains, mixed, route, mid, gate, saved, ps, gin0, gout0):
    bf, f32 = jnp.bfloat16, jnp.float32
    vmem, anywhere = pl.BlockSpec(memory_space=pltpu.VMEM), pl.BlockSpec(memory_space=pl.ANY)
    smem = pl.BlockSpec(memory_space=pltpu.SMEM)
    shape, V, dma = jax.ShapeDtypeStruct, pltpu.VMEM, pltpu.SemaphoreType.DMA
    line, pieces = [V((512, 1024), bf)], [V((256, 512), bf)]
    wide, narrow = [V((2, 4, 64, 1024), bf)], [V((2, 4, 64, 768), bf)]
    return pl.pallas_call(
        dense_backward_kernel,
        out_shape=[
            shape((128, 1024), f32), shape((64, 3072), f32), shape((64, 1024), f32), shape((64, 4096), f32),
            shape((256, 1024), f32), shape((8, 128), f32), shape((128, 1024), bf), shape((1024, 512), bf),
            shape((512, 1024), bf),
        ],
        in_specs=[vmem, vmem, vmem, smem] + [vmem] * 5 + [anywhere] * 14,
        out_specs=[vmem] * 7 + [anywhere] * 2,
        scratch_shapes=[
            *(line * 4), V((512, 1024), f32), *line,
            V((512, 256), bf), V((512, 512), bf), V((512, 512), bf),
            V((2, 4, 2, 2, 32, 768), bf), *([V((2, 4, 2, 2, 32, 1024), bf)] * 3),
            *(line * 6),
            V((128, 1024), bf), V((512, 256), bf), V((512, 768), bf), V((512, 512), f32), V((512, 512), f32),
            V((512, 512), bf), V((512, 512), bf),
            *(wide * 3), *narrow, *(wide * 3), *narrow, *(wide * 3), *narrow,
            *([V((4, 2, 64, 1024), bf)] * 3), *([V((2, 64, 1024), bf)] * 3), *([V((4, 32, 1024), bf)] * 3),
            V((16, 32, 768), bf), *(pieces * 2),
            V((8, 1024), f32), V((8, 1024), f32), V((16, 8, 128), f32), V((4, 8, 128), f32),
            V((8, 32, 256), bf),
            V((8, 32, 1024), bf), V((8, 32, 1024), bf), V((8, 32, 256), bf), V((8, 32, 768), bf),
            dma((14,)), dma((7, 3)), dma((7, 3)), dma((3, 3)), dma((3, 3)), dma((3, 3)), dma((3, 3)), dma((4,)),
            dma((4,)), dma((4,)), dma((4,)), dma((3, 15)), dma((3, 15)), dma((4, 7)), dma((4, 7)), dma((2,)),
            dma((2,)), dma((1,)), dma((1,)),
        ],
        compiler_params=pltpu.CompilerParams(collective_id=3, has_side_effects=True, vmem_limit_bytes=62 << 20),
        name="dense_backward",
    )(gh, x, after, docs, gains, mixed, route, mid, gate, *saved, ps, gin0, gout0)


def on_device(
    inputs,
    doc_starts,
    route,
    norm_gain,
    norm_bias,
    w_qkv,
    w_out,
    w_up,
    w_down,
    exp_gain,
    exp_bias,
    exp_in,
    exp_out,
    centroid,
    cotangent,
):
    tok_rows, width = 128, 1024
    x = inputs.reshape(tok_rows, width)
    cot = cotangent.reshape(tok_rows, width)
    slots = route.reshape(1, tok_rows)
    core = lax.rem(lax.axis_index("fsdp"), 2)
    mine = lax.rem(lax.axis_index("seq"), 2) == core
    share = jnp.pad(jnp.concatenate([norm_gain, norm_bias]), ((0, 12), (0, 0)))
    none = jnp.zeros_like(share)
    gain_tile = jnp.where(core == 0, jnp.concatenate([share, none], 1), jnp.concatenate([none, share], 1))
    core_pairs = [(i, i + 1 - 2 * (i % 2)) for i in range(128)]
    vec = jnp.concatenate([exp_gain[0], exp_bias[0], centroid], axis=0)
    vec = jnp.where(mine, vec, lax.ppermute(vec, ("seq", "fsdp"), core_pairs)).astype(jnp.float32)
    vec = jnp.pad(vec, ((0, 3), (0, 0)))
    hidden, mixed, after, gains, *saved, cz, in0, out0, in1 = dense_forward_call(
        x, gain_tile, doc_starts, slots, cot, w_qkv, w_out, w_up, w_down, exp_in[0], exp_out[0]
    )
    grad_hidden, vec_grads, mid, gate, part, grad_in1, grad_out1, grad_in0, grad_out0 = expert_call(
        hidden, slots, vec, cz, exp_in[0], exp_out[0], in0, out0, in1
    )
    grad_x, grad_qkv, grad_wo, grad_up, grad_down, norm_grads, result, grad_in0, grad_out0 = dense_backward_call(
        grad_hidden, x, after, doc_starts, gains, mixed, slots, mid, gate, saved, part, grad_in0, grad_out0
    )
    norm_grads = jnp.where(core == 0, norm_grads[:4, :64], norm_grads[:4, 64:])
    return (
        result[None],
        grad_x[None],
        norm_grads[0:2],
        norm_grads[2:4],
        grad_qkv,
        grad_wo,
        grad_up,
        grad_down,
        vec_grads[None, 0:2],
        vec_grads[None, 2:4],
        jnp.stack([grad_in0, grad_in1]).astype(jnp.float32)[None],
        jnp.stack([grad_out0, grad_out1]).astype(jnp.float32)[None],
        vec_grads[4:5],
    )


def solution(mesh):
    in_specs = (
        P("fsdp", "seq", None),
        P("fsdp", None),
        P("fsdp", "seq", None),
        P(None, "fsdp"),
        P(None, "fsdp"),
        P("fsdp", None),
        P("fsdp", None),
        P("fsdp", None),
        P("fsdp", None),
        P("fsdp", None, None),
        P("fsdp", None, None),
        P("fsdp", None, None, "seq"),
        P("fsdp", None, "seq", None),
        P("fsdp", None),
        P("fsdp", "seq", None),
    )
    out_specs = (
        P("fsdp", "seq", None),
        P("fsdp", "seq", None),
        P(None, "fsdp"),
        P(None, "fsdp"),
        P("fsdp", None),
        P("fsdp", None),
        P("fsdp", None),
        P("fsdp", None),
        P("fsdp", None, None),
        P("fsdp", None, None),
        P("fsdp", None, None, "seq"),
        P("fsdp", None, "seq", None),
        P("fsdp", None),
    )
    return jax.shard_map(
        on_device, mesh=mesh, in_specs=in_specs, out_specs=out_specs, check_vma=False
    )
```

```python
import jax
import jax.numpy as jnp
from jax import lax
from jax.experimental import pallas as pl
from jax.experimental.pallas import tpu as pltpu
from jax.sharding import PartitionSpec as P

MESH = pl.DeviceIdType.MESH
epsilon = 1e-05
masked_score = -1e30


def split_sum(values):
    return jnp.sum(values, axis=-1, keepdims=True)


def norm_parts(values):
    average = split_sum(values) * (1.0 / values.shape[-1])
    centered = values - average
    spread = split_sum(centered * centered) * (1.0 / values.shape[-1])
    scale = lax.rsqrt(spread + epsilon)
    return centered * scale, scale


def norm_back(grad_normed, gain, xhat, scale):
    width = 1.0 / xhat.shape[-1]
    u = grad_normed * gain
    return scale * (u - split_sum(u) * width - xhat * (split_sum(u * xhat) * width))


def gelu_parts(pre):
    inner = 0.7978845608028654
    cubic = 0.044715
    square = pre * pre
    t = jnp.tanh(inner * pre * (1.0 + cubic * square))
    half = 0.5 * (1.0 + t)
    slope = half + 0.5 * pre * (1.0 - t * t) * (inner * (1.0 + 3.0 * cubic * square))
    return pre * half, slope


def nn(a, b):
    return lax.dot_general(a, b, (((1,), (0,)), ((), ())), preferred_element_type=jnp.float32)


def nt(a, b):
    return lax.dot_general(a, b, (((1,), (1,)), ((), ())), preferred_element_type=jnp.float32)


def tn(a, b):
    return lax.dot_general(a, b, (((0,), (0,)), ((), ())), preferred_element_type=jnp.float32)


def remote(src, dst, send, recv, device):
    return pltpu.make_async_remote_copy(
        src_ref=src, dst_ref=dst, send_sem=send, recv_sem=recv, device_id=device, device_id_type=MESH
    )


def greet(bar, device):
    pl.semaphore_signal(bar, inc=1, device_id=device, device_id_type=MESH)


def block(index):
    return pl.ds(pl.multiple_of(index * 128, 128), 128)


def order(i):
    return i + lax.div(i, 2) - 2 * lax.div(i, 3)


class Place:
    def __init__(self):
        self.s, self.f = lax.axis_index("seq"), lax.axis_index("fsdp")
        self.z, self.yh = lax.div(self.s, 2), lax.rem(self.s, 2)
        self.yl, self.col, self.c = lax.div(self.f, 8), lax.div(self.f, 2), lax.rem(self.f, 2)
        self.x = lax.rem(self.col, 4)
        self.m = self.f - self.c + self.yh
        self.other = (self.s, self.f + 1 - 2 * self.c)
        self.mate = (2 * self.z + 1 - self.yh, self.f)
        self.swap_mate = (2 * self.z + 1 - self.yh, self.f + 1 - 2 * self.c)
        self.same = self.c == self.yh


class Ring:
    def __init__(self, at, axis, send, recv):
        self.at, self.axis, self.send, self.recv = at, axis, send, recv
        self.pos = {"z": at.z, "x": at.x, "y": 2 * at.yh + at.yl}[axis]

    def index(self, d):
        return lax.rem(self.pos + d, 4)

    def device(self, j):
        at = self.at
        if self.axis == "z":
            return (2 * j + at.yh, at.f)
        if self.axis == "x":
            return (at.s, at.f - 2 * at.x + 2 * j)
        return (2 * at.z + lax.div(j, 2), 8 * lax.rem(j, 2) + at.f - 8 * at.yl)

    def copy(self, phase, d, src, dst):
        sems = self.send.at[phase, d - 1], self.recv.at[phase, d - 1]
        return remote(src, dst, *sems, self.device(self.index(d)))

    def got(self, phase, d, dst):
        sems = self.send.at[phase, 3 - d], self.recv.at[phase, 3 - d]
        remote(dst, dst, *sems, self.device(self.index(d))).wait_recv()

    def spread(self, phase, buf):
        own = buf.at[block(self.pos)]
        for d in (1, 3, 2):
            self.copy(phase, d, own, own).start()

    def near(self, phase, d, buf):
        own = buf.at[block(self.pos)]
        return self.copy(phase, d, own, own)

    def half(self, buf, d, upper):
        return buf.at[pl.ds(pl.multiple_of(128 * self.index(d) + 64 * upper, 64), 64)]

    def onward(self, phase, buf, upper):
        rows = self.half(buf, 3 if upper else 1, upper)
        slot = 3 if upper else 1
        to = self.device(self.index(1 if upper else 3))
        return remote(rows, rows, self.send.at[phase, slot], self.recv.at[phase, slot], to)

    def begin(self, phase, buf):
        for d in (1, 3):
            self.near(phase, d, buf).start()

    def relay(self, phase, buf):
        for d in (1, 3):
            self.arrived(phase, d, buf)
        for upper in (0, 1):
            self.onward(phase, buf, upper).start()

    def far(self, phase, buf):
        for upper in (0, 1):
            slot = 3 if upper else 1
            rows = self.half(buf, 2, upper)
            to = self.device(self.index(1 if upper else 3))
            remote(rows, rows, self.send.at[phase, slot], self.recv.at[phase, slot], to).wait_recv()

    def ready(self, phase, i, buf):
        pl.when(i == 1)(lambda: self.relay(phase, buf))
        pl.when(i == 3)(lambda: self.far(phase, buf))

    def sent_all(self, phase, buf):
        for d in (1, 3):
            self.near(phase, d, buf).wait_send()
        for upper in (0, 1):
            self.onward(phase, buf, upper).wait_send()

    def arrived(self, phase, d, buf):
        self.got(phase, d, buf.at[block(self.index(d))])

    def give(self, phase, d, src, dst):
        self.copy(phase, d, src.at[block(self.index(d))], dst.at[block(self.pos)]).start()

    def sent(self, phase, buf):
        own = buf.at[block(self.pos)]
        for d in (1, 3, 2):
            self.copy(phase, d, own, own).wait_send()

    def total(self, phase, own, parts):
        acc = own[block(self.pos), :].astype(jnp.float32)
        for d in (1, 3, 2):
            self.arrived(phase, d, parts)
            acc += parts[block(self.index(d)), :].astype(jnp.float32)
        return acc


class Plane:
    def __init__(self, at, send, recv):
        self.at, self.m = at, at.m
        self.send, self.recv = send, recv

    def device(self, q):
        return (2 * self.at.z + lax.rem(q, 2), q - lax.rem(q, 2) + self.at.c)

    def greet(self, bar):
        def one(i, carry):
            greet(bar, self.device(lax.rem(self.m + i + 1, 16)))
            return carry

        lax.fori_loop(0, 15, one, 0)

    def copy(self, phase, i, src_of, dst_of):
        q = lax.rem(self.m + i + 1, 16)
        return remote(src_of(q), dst_of(self.m), self.send.at[phase, i], self.recv.at[phase, i], self.device(q))

    def start(self, phase, src_of, dst_of):
        def one(i, carry):
            self.copy(phase, i, src_of, dst_of).start()
            return carry

        lax.fori_loop(0, 15, one, 0)

    def wait(self, phase, dst_of):
        def one(i, carry):
            q = lax.rem(self.m + 15 - i, 16)
            dst = dst_of(q)
            remote(dst, dst, self.send.at[phase, i], self.recv.at[phase, i], self.device(q)).wait_recv()
            return carry

        lax.fori_loop(0, 15, one, 0)

    def sent(self, phase, src_of, dst_of):
        def one(i, carry):
            self.copy(phase, i, src_of, dst_of).wait_send()
            return carry

        lax.fori_loop(0, 15, one, 0)


def piece(buf):
    return lambda q: buf.at[pl.ds(pl.multiple_of(q * 16, 16), 16)]


def keep_piece(at, src, dst):
    own = pl.ds(pl.multiple_of(at.m * 16, 16), 16)
    dst[own, :] = src[own, :]


def placings(route):
    row = lax.broadcasted_iota(jnp.int32, (256, 128), 0)
    inner = row & 15
    slot = (row >> 4) * 8 + (inner & 7)
    hit = slot == route
    left = jnp.where(hit & (inner < 8), 1.0, 0.0).astype(jnp.bfloat16)
    right = jnp.where(hit & (inner >= 8), 1.0, 0.0).astype(jnp.bfloat16)
    return left, right


def to_pieces(left, right, rows):
    half = rows.shape[1] // 2
    return (nn(left, rows[:, :half]) + nn(right, rows[:, half:])).astype(jnp.bfloat16)


def from_pieces(left, right, pieces):
    return jnp.concatenate([tn(left, pieces), tn(right, pieces)], axis=1).astype(jnp.bfloat16)


def rows_of(pieces):
    wide = pieces.astype(jnp.float32).reshape(16, 2, 8, 512)
    return jnp.concatenate([wide[:, 0].reshape(128, 512), wide[:, 1].reshape(128, 512)], axis=1)


def pieces_of(rows):
    left = rows[:, :512].reshape(16, 1, 8, 512)
    right = rows[:, 512:].reshape(16, 1, 8, 512)
    return jnp.concatenate([left, right], axis=1).reshape(256, 512).astype(jnp.bfloat16)


class Gather:
    def __init__(self, at, phase, first, src, full, xs, xr, ys, yr, ks, kr):
        self.at, self.phase, self.src, self.full = at, phase, src, full
        self.x_first = first == "x"
        self.rings = [Ring(at, "y", ys, yr), Ring(at, "x", xs, xr)]
        if self.x_first:
            self.rings.reverse()
        self.ks, self.kr = ks, kr

    def pushed(self, d):
        at = self.at
        return self.rings[0].copy(self.phase, d, self.src, self.full.at[at.yl, at.x, at.c, at.yh])

    def passed(self, d):
        at = self.at
        own = self.full.at[at.yl, :, at.c, at.yh] if self.x_first else self.full.at[:, at.x, at.c]
        return self.rings[1].copy(self.phase, d, own, own)

    def core(self, c):
        half = self.full.at[:, :, c]
        return remote(half, half, self.ks.at[self.phase], self.kr.at[self.phase], self.at.other)

    def start(self):
        at = self.at
        for d in (1, 3, 2):
            self.pushed(d).start()
        self.full[at.yl, at.x, at.c, at.yh] = self.src[...]

    def turn(self):
        at, full = self.at, self.full
        for d in (1, 3, 2):
            j = self.rings[0].index(d)
            dst = full.at[at.yl, j, at.c, at.yh] if self.x_first else full.at[lax.rem(j, 2), at.x, at.c, lax.div(j, 2)]
            self.rings[0].got(self.phase, d, dst)
        for d in (1, 3, 2):
            self.passed(d).start()

    def share(self):
        at, full = self.at, self.full
        for d in (1, 3, 2):
            j = self.rings[1].index(d)
            dst = full.at[lax.rem(j, 2), :, at.c, lax.div(j, 2)] if self.x_first else full.at[:, j, at.c]
            self.rings[1].got(self.phase, d, dst)
        self.core(at.c).start()

    def wait(self):
        self.core(1 - self.at.c).wait_recv()

    def sent(self):
        for d in (1, 3, 2):
            self.pushed(d).wait_send()
            self.passed(d).wait_send()
        self.core(self.at.c).wait_send()


def labels(position, first, second):
    return jnp.where(position >= first, 1, 0) + jnp.where(position >= second, 1, 0)


def masks(j, yh, docs):
    first, second = docs[0, 0], docs[0, 1]
    wide = 128 * (j + 1)
    row = lax.broadcasted_iota(jnp.int32, (128, wide), 0) + 128 * (2 * j + yh)
    lane = lax.broadcasted_iota(jnp.int32, (128, wide), 1)
    start = (lane >> 7) * 256 + (lane & 127)
    row_label = labels(row, first, second)
    found = []
    for parity in (yh, 1 - yh):
        key = start + 128 * parity
        found.append((key <= row) & (labels(key, first, second) == row_label))
    return found


def probabilities(q, keys, seen):
    scores = [jnp.where(ok, nt(q, k) * 0.125, masked_score) for k, ok in zip(keys, seen)]
    top = jnp.maximum(
        jnp.max(scores[0], axis=-1, keepdims=True), jnp.max(scores[1], axis=-1, keepdims=True)
    )
    weights = [jnp.exp(s - top) for s in scores]
    inverse = 1.0 / (split_sum(weights[0]) + split_sum(weights[1]))
    return [w * inverse for w in weights]


def head_lanes(h):
    lane = lax.broadcasted_iota(jnp.int32, (128, 128), 1)
    return lane < 64 if h == 0 else lane >= 64


def only(keep, values):
    return jnp.where(keep, values.astype(jnp.float32), 0.0).astype(jnp.bfloat16)


def wide_tile(full, tile):
    part = full[:, :, :, :, :, tile]
    return part.reshape(1024, part.shape[-1])


def tall_tile(full, n):
    part = full[n // 2, 2 * (n % 2) : 2 * (n % 2) + 2]
    return part.reshape(256, part.shape[-1])


def dense_forward_kernel(
    x, gain, bias, docs, route, cot, w_qkv, w_out, w_up, w_down, exp_in, exp_out,
    hid, mixed, after, gains,
    o_x, o_n1, o_n2, o_act, o_dg, o_q, o_kv, o_kvo, o_wq, o_wo, o_wu, o_wd, o_cz, o_in0, o_out0, o_in1,
    sq, su, wq, wo, wu, wd, gtile, gmine, gother,
    xa, n1, n2, cz, qb, kvb, kvo, mixs, act, dg, ps, pr, sendc, arrc,
    zs, zr, xs, xr, ys, yr, kvs, kvr, ks, kr, gs, gr, cs, cr, ss, sr, osem,
):
    at = Place()
    z, yh, c, col = at.z, at.yh, at.c, at.col
    line, plane = Ring(at, "z", zs, zr), Plane(at, cs, cr)
    bar = pltpu.get_barrier_semaphore()
    for d in (1, 2, 3):
        greet(bar, line.device(line.index(d)))
    greet(bar, at.other)
    greet(bar, at.swap_mate)
    plane.greet(bar)
    xa[block(z), :] = x[...]
    for part in range(3):
        sq[:, 256 * part : 256 * part + 256] = w_qkv[:, pl.ds(pl.multiple_of(1024 * part + 256 * z, 256), 256)]
    gtile[...] = jnp.zeros_like(gtile)
    for k, ref in enumerate((gain, bias)):
        values = ref[...].astype(jnp.float32)
        none = jnp.zeros_like(values)
        here = jnp.where(c == 0, jnp.concatenate([values, none], 1), jnp.concatenate([none, values], 1))
        gtile[2 * k : 2 * k + 2, :] = here
    half = pl.ds(pl.multiple_of(32 * yh, 32), 32)
    down_rows = w_down.at[pl.ds(pl.multiple_of(64 * z + 32 * yh, 32), 32)]
    sems = (xs, xr, ys, yr, ks, kr)
    left_q, right_q = (wq.at[:, :, :, :, :, 0:384], wq.at[:, :, :, :, :, 384:768])
    qkv_a = Gather(at, 0, "y", sq.at[half, 0:384], left_q, *sems)
    qkv_b = Gather(at, 1, "x", sq.at[half, 384:768], right_q, *sems)
    out = Gather(at, 2, "y", w_out.at[half], wo, *sems)
    up = Gather(at, 3, "y", su.at[half], wu, *sems)
    down = Gather(at, 4, "x", down_rows, wd, *sems)
    pl.semaphore_wait(bar, 20)
    line.begin(0, xa)
    tile_at = pl.ds(pl.multiple_of(128 * col, 128), 128)

    def gain_copy(i):
        to = (at.s, 2 * lax.rem(col + i + 1, 8) + c)
        return remote(gtile, gmine.at[:, tile_at], gs.at[i], gr.at[i], to)

    def push_gain(i, carry):
        gain_copy(i).start()
        return carry

    lax.fori_loop(0, 7, push_gain, 0)
    gmine[:, tile_at] = gtile[...]
    qkv_a.start()
    qkv_b.start()
    low = lax.broadcasted_iota(jnp.int32, (64, 128), 1) < 64
    odd = lax.rem(z, 2) == 1
    for n in range(8):
        first = 512 * n + 128 * lax.div(z, 2)
        a = w_up[:, pl.ds(pl.multiple_of(first, 128), 128)].astype(jnp.float32)
        b = w_up[:, pl.ds(pl.multiple_of(first + 256, 128), 128)].astype(jnp.float32)
        kept = jnp.where(low, a, pltpu.roll(b, 64, 1))
        moved = jnp.where(low, pltpu.roll(a, 64, 1), b)
        su[:, 128 * n : 128 * n + 128] = jnp.where(odd, moved, kept).astype(jnp.bfloat16)
    out.start()
    qkv_a.turn()
    qkv_b.turn()
    down.start()
    up.start()

    def wait_gain(i, carry):
        q = lax.rem(col + 7 - i, 8)
        dst = gmine.at[:, pl.ds(pl.multiple_of(128 * q, 128), 128)]
        remote(dst, dst, gs.at[i], gr.at[i], (at.s, 2 * q + c)).wait_recv()
        return carry

    lax.fori_loop(0, 7, wait_gain, 0)
    gain_core = remote(gmine, gother, gs.at[7], gr.at[7], at.other)
    gain_core.start()
    left, right = placings(route[0:1, :])
    sendc[...] = to_pieces(left, right, cot[...])
    line.relay(0, xa)
    out.turn()
    down.turn()
    up.turn()
    plane.start(0, piece(sendc), piece(arrc))
    keep_piece(at, sendc, arrc)
    gain_core.wait_recv()
    gains[...] = gmine[...] + gother[...]
    qkv_a.share()
    qkv_b.share()

    def kv_copy(i, j):
        return remote(kvb.at[block(j)], kvo.at[block(j)], kvs.at[i], kvr.at[i], at.mate)

    def project_qkv(i, carry):
        j = line.index(order(i))
        pl.when(i == 3)(lambda: line.far(0, xa))
        xhat = norm_parts(xa[block(j), :].astype(jnp.float32))[0]
        n1[block(j), :] = (xhat * gains[0:1, :] + gains[2:3, :]).astype(jnp.bfloat16)

        @pl.when(i == 0)
        def _():
            qkv_a.wait()
            qkv_b.wait()

        values = n1[block(j), :]
        kvb[block(j), 0:256] = nn(values, wide_tile(wq, slice(256, 512))).astype(jnp.bfloat16)
        kvb[block(j), 256:512] = nn(values, wide_tile(wq, slice(512, 768))).astype(jnp.bfloat16)
        kv_copy(i, j).start()
        qb[block(j), :] = nn(values, wide_tile(wq, slice(0, 256))).astype(jnp.bfloat16)
        return carry

    lax.fori_loop(0, 4, project_qkv, 0)
    plane.wait(0, piece(arrc))
    cz[block(z), :] = rows_of(arrc[...]).astype(jnp.bfloat16)
    line.spread(4, cz)
    for i in range(4):
        kv_copy(i, line.index(order(i))).wait_recv()
    swaps = [
        remote(exp_in.at[0], o_in0, ss.at[0], sr.at[0], at.swap_mate),
        remote(exp_out.at[0], o_out0, ss.at[1], sr.at[1], at.swap_mate),
        remote(exp_in.at[1], o_in1, ss.at[2], sr.at[2], at.swap_mate),
    ]

    @pl.when(c != yh)
    def _():
        for swap in swaps:
            swap.start()

    my_lanes = pl.ds(pl.multiple_of(256 * z, 256), 256)

    def mix_copy(d):
        return line.copy(1, d, mixs.at[block(line.index(d))], mixed.at[:, my_lanes])

    for j in range(4):
        seen = masks(j, yh, docs)
        wide = slice(0, 128 * (j + 1))
        for p in range(2):
            lanes = slice(128 * p, 128 * p + 128)
            value_lanes = slice(256 + 128 * p, 384 + 128 * p)
            q = qb[128 * j : 128 * j + 128, lanes]
            keys = [kvb[wide, lanes], kvo[wide, lanes]]
            values = [kvb[wide, value_lanes], kvo[wide, value_lanes]]
            outs = []
            for h in range(2):
                probs = probabilities(only(head_lanes(h), q), keys, seen)
                outs.append(
                    nn(probs[0].astype(jnp.bfloat16), values[0]) + nn(probs[1].astype(jnp.bfloat16), values[1])
                )
            mixs[128 * j : 128 * j + 128, lanes] = jnp.where(head_lanes(0), outs[0], outs[1]).astype(jnp.bfloat16)
        pl.when(z != j)(lambda: mix_copy(lax.rem(j + 4 - z, 4)).start())
    mixed[:, my_lanes] = mixs[block(z), :]
    out.share()
    out.wait()
    for d in (1, 3, 2):
        line.got(1, d, mixed.at[:, pl.ds(pl.multiple_of(256 * line.index(d), 256), 256)])
    for n in range(4):
        tile = slice(256 * n, 256 * n + 256)
        after[:, tile] = x[:, tile].astype(jnp.float32) + nn(mixed[...], wide_tile(wo, tile))
    xhat = norm_parts(after[...])[0]
    n2[block(z), :] = (xhat * gains[1:2, :] + gains[3:4, :]).astype(jnp.bfloat16)
    line.begin(2, n2)
    up.share()
    down.share()
    up.wait()
    down.wait()
    stores = [
        pltpu.make_async_copy(src, dst, osem.at[k])
        for k, (src, dst) in enumerate(
            [(xa, o_x), (n1, o_n1), (qb, o_q), (kvb, o_kv), (kvo, o_kvo), (wq, o_wq), (wo, o_wo), (wu, o_wu), (wd, o_wd)]
        )
    ]
    for store in stores:
        store.start()

    def feed(i, carry):
        d = order(i)
        j = line.index(d)
        line.ready(2, i, n2)
        values = n2[block(j), :]
        for n in range(4):
            tile = slice(n * 256, (n + 1) * 256)
            acted, slope = gelu_parts(nn(values, wide_tile(wu, tile)))
            act[block(j), tile] = acted.astype(jnp.bfloat16)
            dg[block(j), tile] = slope
        values = act[block(j), :]
        for n in range(4):
            tile = slice(n * 256, (n + 1) * 256)
            ps[block(j), tile] = nn(values, wide_tile(wd, tile)).astype(jnp.bfloat16)

        @pl.when(i > 0)
        def _():
            line.give(3, d, ps, pr)

        return carry

    lax.fori_loop(0, 4, feed, 0)
    for d in (1, 3, 2):
        line.arrived(4, d, cz)
    late = [
        pltpu.make_async_copy(src, dst, osem.at[9 + k])
        for k, (src, dst) in enumerate([(n2, o_n2), (act, o_act), (dg, o_dg), (cz, o_cz)])
    ]
    for store in late:
        store.start()
    gain_core.wait_send()

    def sent_gain(i, carry):
        gain_copy(i).wait_send()
        return carry

    lax.fori_loop(0, 7, sent_gain, 0)
    for weight in (qkv_a, qkv_b, out, up, down):
        weight.sent()
    for i in range(4):
        kv_copy(i, line.index(order(i))).wait_send()
    line.sent_all(0, xa)
    for d in (1, 3, 2):
        mix_copy(d).wait_send()
    line.sent_all(2, n2)
    line.sent(4, cz)
    plane.sent(0, piece(sendc), piece(arrc))
    hid[...] = (after[...] + line.total(3, ps, pr)).astype(jnp.bfloat16)
    line.sent(3, ps)

    @pl.when(c != yh)
    def _():
        for swap in swaps:
            swap.wait()

    for store in stores + late:
        store.wait()


def dense_forward_call(x, gain, bias, docs, route, cot, w_qkv, w_out, w_up, w_down, exp_in, exp_out):
    bf, f32 = jnp.bfloat16, jnp.float32
    vmem, anywhere = pl.BlockSpec(memory_space=pltpu.VMEM), pl.BlockSpec(memory_space=pl.ANY)
    smem = pl.BlockSpec(memory_space=pltpu.SMEM)
    shape, V, dma = jax.ShapeDtypeStruct, pltpu.VMEM, pltpu.SemaphoreType.DMA
    line = [V((512, 1024), bf)]
    weight = [(2, 4, 2, 2, 32, 768)] + [(2, 4, 2, 2, 32, 1024)] * 3
    saved = [
        shape((512, 1024), bf), shape((512, 1024), bf), shape((512, 1024), bf), shape((512, 1024), bf),
        shape((512, 1024), f32), shape((512, 256), bf), shape((512, 512), bf), shape((512, 512), bf),
    ] + [shape(w, bf) for w in weight] + [
        shape((512, 1024), bf), shape((1024, 512), bf), shape((512, 1024), bf), shape((1024, 512), bf),
    ]
    return pl.pallas_call(
        dense_forward_kernel,
        out_shape=[shape((128, 1024), bf), shape((128, 1024), bf), shape((128, 1024), f32), shape((8, 1024), f32)]
        + saved,
        in_specs=[vmem] * 3 + [smem] + [vmem] * 6 + [anywhere, anywhere],
        out_specs=[vmem] * 4 + [anywhere] * len(saved),
        scratch_shapes=[
            V((64, 768), bf), V((64, 1024), bf), *[V(w, bf) for w in weight], V((8, 128), f32), V((8, 1024), f32),
            V((8, 1024), f32),
            *(line * 4), V((512, 256), bf), V((512, 512), bf), V((512, 512), bf), V((512, 256), bf),
            *line, V((512, 1024), f32), *(line * 2), V((256, 512), bf), V((256, 512), bf),
            dma((5, 4)), dma((5, 4)), dma((5, 3)), dma((5, 3)), dma((5, 3)), dma((5, 3)), dma((4,)), dma((4,)),
            dma((5,)), dma((5,)), dma((8,)), dma((8,)), dma((1, 15)), dma((1, 15)), dma((3,)), dma((3,)), dma((13,)),
        ],
        compiler_params=pltpu.CompilerParams(collective_id=2, has_side_effects=True, vmem_limit_bytes=60 << 20),
        name="dense_forward",
    )(x, gain, bias, docs, route, cot, w_qkv, w_out, w_up, w_down, exp_in, exp_out)


def expert_kernel(
    hid, route, exp_gain, exp_bias, centroid, cz_h, exp_in, exp_out, in0, out0, in1,
    gh, vecg, mid, gate_out, o_ps, gin1, gout1, gin0, gout0,
    w_in, w_out, sendh, sendg, arrh, arrg, cz,
    e0, e1, g0, g1, ps0, ps1, pr0, pb0, pb1,
    act0, act1, dg0, dg1, gp0, gp1,
    arrived, base, xh0, xh1, sc, gates, dots, dots_in,
    ga_in, ga_out, sb_in, sb_out, rb_in, rb_out, vec, vec_own, vec_other, vmine, vcore, vline, vsum, vswap,
    wsem, zs, zr, cs, cr, ks, kr, osem, bs, br, ss, sr, vs, vr,
):
    at = Place()
    z, yh, c, same = at.z, at.yh, at.c, at.same
    line, plane = Ring(at, "z", zs, zr), Plane(at, cs, cr)
    bar = pltpu.get_barrier_semaphore()
    plane.greet(bar)
    for d in (1, 2, 3):
        greet(bar, line.device(line.index(d)))
    greet(bar, at.other)
    greet(bar, at.swap_mate)
    low, high = slice(0, 512), slice(512, 1024)

    def slot(k, i, half):
        return w_in.at[k, :, half] if i == 0 else w_out.at[k, half, :]

    def load(k, i):
        return pltpu.make_async_copy((exp_in, exp_out)[i].at[k], slot(k, i, low), wsem.at[k, i])

    def swapped(k, i):
        return pltpu.make_async_copy((in0, out0)[i] if k == 0 else in1, slot(k, i, low), wsem.at[k, i])

    swap_out = remote(exp_out.at[1], slot(1, 1, low), ss.at[0], sr.at[0], at.swap_mate)

    def share(k, i):
        return remote(slot(k, i, low), slot(k, i, high), bs.at[k, i], br.at[k, i], at.other)

    def on_either(when_same, when_swapped):
        pl.when(same)(when_same)
        pl.when(jnp.logical_not(same))(when_swapped)

    load_c = pltpu.make_async_copy(cz_h, cz, wsem.at[2, 0])

    def begin_same():
        for k, i in ((0, 0), (0, 1), (1, 0), (1, 1)):
            load(k, i).start()

    def begin_swapped():
        for k, i in ((0, 0), (0, 1), (1, 0)):
            swapped(k, i).start()

    on_either(begin_same, begin_swapped)
    load_c.start()
    left, right = placings(route[0:1, :])
    sendh[...] = to_pieces(left, right, hid[...])
    vec_own[0:2, :] = exp_gain[...].astype(jnp.float32)
    vec_own[2:4, :] = exp_bias[...].astype(jnp.float32)
    vec_own[4:5, :] = centroid[...].astype(jnp.float32)
    vec_own[5:8, :] = jnp.zeros((3, 1024), jnp.float32)
    pl.semaphore_wait(bar, 20)
    plane.start(0, piece(sendh), piece(arrh))
    keep_piece(at, sendh, arrh)
    trade = remote(vec_own, vec_other, vs.at[2], vr.at[2], at.other)
    trade.start()

    def wait_loads(k, i):
        on_either(lambda: load(k, i).wait(), lambda: swapped(k, i).wait())
        share(k, i).start()

    wait_loads(0, 0)
    wait_loads(0, 1)
    trade.wait()
    vec[...] = jnp.where(same, vec_own[...], vec_other[...])
    plane.wait(0, piece(arrh))
    gain = [vec[0:1, :], vec[1:2, :]]
    bias = [vec[2:3, :], vec[3:4, :]]
    rows = rows_of(arrh[...])
    arrived[...] = rows
    xhat, scale = norm_parts(rows)
    xh0[...] = xhat
    sc[0] = jnp.broadcast_to(scale, (128, 128))
    e0[block(z), :] = (xhat * gain[0] + bias[0]).astype(jnp.bfloat16)
    line.begin(0, e0)
    pl.when(jnp.logical_not(same))(lambda: swap_out.start())
    wait_loads(1, 0)
    gating = jax.nn.sigmoid(split_sum(rows * vec[4:5, :]))
    gates[z] = jnp.broadcast_to(gating, (128, 128))

    def gate_copy(d):
        return line.copy(3, d, gates.at[z], gates.at[z])

    for d in (1, 3, 2):
        gate_copy(d).start()
    share(0, 0).wait_recv()
    share(0, 1).wait_recv()
    load_c.wait()

    def forward(k, j, rows_in, act, dg):
        values = rows_in[block(j), :]
        for n in range(4):
            tile = slice(n * 256, (n + 1) * 256)
            pre = nn(values, w_in[k, :, tile])
            acted, slope = gelu_parts(pre)
            act[block(j), tile] = acted.astype(jnp.bfloat16)
            dg[block(j), tile] = slope

    def project(k, j, act, part):
        values = act[block(j), :]
        for n in range(4):
            tile = slice(n * 256, (n + 1) * 256)
            part[block(j), tile] = nn(values, w_out[k, :, tile]).astype(jnp.bfloat16)

    def backward(k, j, grad, dg, gp, part):
        values = grad[block(j), :]
        for n in range(4):
            tile = slice(n * 256, (n + 1) * 256)
            slope = dg[block(j), tile] * nt(values, w_out[k, tile, :])
            gp[block(j), tile] = slope.astype(jnp.bfloat16)
        pres = gp[block(j), :]
        for n in range(4):
            tile = slice(n * 256, (n + 1) * 256)
            part[block(j), tile] = nt(pres, w_in[k, tile, :]).astype(jnp.bfloat16)

    def sub0(i, carry):
        d = order(i)
        j = line.index(d)

        line.ready(0, i, e0)
        forward(0, j, e0, act0, dg0)
        project(0, j, act0, ps0)

        @pl.when(i > 0)
        def _():
            line.give(1, d, ps0, pr0)

        return carry

    lax.fori_loop(0, 4, sub0, 0)
    on_either(lambda: load(1, 1).wait(), lambda: swap_out.wait())
    share(1, 1).start()
    stream = arrived[...] + line.total(1, ps0, pr0)
    base[...] = stream
    xhat, scale = norm_parts(stream)
    xh1[...] = xhat
    sc[1] = jnp.broadcast_to(scale, (128, 128))
    e1[block(z), :] = (xhat * gain[1] + bias[1]).astype(jnp.bfloat16)
    line.begin(2, e1)
    gate = gates[z][:, 0:1]
    mid[...] = arrived[...] + gate * (base[...] - arrived[...])
    gate_out[...] = gates[z]
    line.sent(1, ps0)
    share(1, 0).wait_recv()
    share(1, 1).wait_recv()

    def sub1(i, carry):
        d = order(i)
        j = line.index(d)

        @pl.when(i > 0)
        def _():
            line.got(3, d, gates.at[j])

        g1[block(j), :] = (gates[j][:, 0:1] * cz[block(j), :].astype(jnp.float32)).astype(jnp.bfloat16)

        line.ready(2, i, e1)
        forward(1, j, e1, act1, dg1)
        backward(1, j, g1, dg1, gp1, ps0)

        @pl.when(i > 0)
        def _():
            line.give(4, d, ps0, pb1)

        return carry

    lax.fori_loop(0, 4, sub1, 0)

    def second_part(i, carry):
        d = order(3 - i)
        j = line.index(d)
        project(1, j, act1, ps1)
        products = cz[block(j), :].astype(jnp.float32) * ps1[block(j), :].astype(jnp.float32)
        dots[j] = jnp.broadcast_to(split_sum(products), (128, 128))

        @pl.when(i < 3)
        def _():
            line.copy(5, d, dots.at[j], dots_in.at[z]).start()

        return carry

    lax.fori_loop(0, 4, second_part, 0)
    keep_ps = pltpu.make_async_copy(ps1, o_ps, wsem.at[2, 1])
    keep_ps.start()

    def weight_grads(k, rows_in, gp, act, grad):
        def one(n, carry):
            tile = pl.ds(pl.multiple_of(n * 256, 256), 256)
            tile_b = pl.ds(pl.multiple_of(n * 256 + 512, 256), 256)
            ga_out[k, tile, :] = tn(act[:, tile], grad[...])
            sb_out[k, tile, :] = tn(act[:, tile_b], grad[...]).astype(jnp.bfloat16)
            return carry

        lax.fori_loop(0, 2, one, 0)

        def two(n, carry):
            tile = pl.ds(pl.multiple_of(n * 256, 256), 256)
            ga_in[k, tile, :] = tn(rows_in[:, tile], gp[:, 0:512])
            sb_in[k, tile, :] = tn(rows_in[:, tile], gp[:, 512:1024]).astype(jnp.bfloat16)
            return carry

        lax.fori_loop(0, 4, two, 0)

    def swap(k, i):
        src, dst = ((sb_in, rb_in), (sb_out, rb_out))[i]
        return remote(src.at[k], dst.at[k], ks.at[k, i], kr.at[k, i], at.other)

    def join_cores(k):
        for i in range(2):
            swap(k, i).wait()
        sb_in[k] = (ga_in[k] + rb_in[k].astype(jnp.float32)).astype(jnp.bfloat16)
        sb_out[k] = (ga_out[k] + rb_out[k].astype(jnp.float32)).astype(jnp.bfloat16)

    weight_grads(1, e1, gp1, act1, g1)
    swap(1, 0).start()
    swap(1, 1).start()
    grad_normed = line.total(4, ps0, pb1)
    cot = cz[block(z), :].astype(jnp.float32)
    grad_stream = gates[z][:, 0:1] * cot
    grad_stream += norm_back(grad_normed, gain[1], xh1[...], sc[1][:, 0:1])
    g0[block(z), :] = grad_stream.astype(jnp.bfloat16)
    line.begin(6, g0)
    vmine[1:2, :] = jnp.sum(grad_normed * xh1[...], axis=0, keepdims=True)
    vmine[3:4, :] = jnp.sum(grad_normed, axis=0, keepdims=True)
    line.sent(4, ps0)
    grad_gating = split_sum(cot * (base[...] - arrived[...])) + dots[z][:, 0:1]
    for d in (1, 3, 2):
        line.got(5, d, dots_in.at[line.index(d)])
        grad_gating += dots_in[line.index(d)][:, 0:1]
    gate = gates[z][:, 0:1]
    grad_logit = gate * (1.0 - gate) * grad_gating
    vmine[4:5, :] = jnp.sum(grad_logit * arrived[...], axis=0, keepdims=True)
    base[...] = grad_stream + (1.0 - gate) * cot + grad_logit * vec[4:5, :]
    join_cores(1)
    kept = [
        pltpu.make_async_copy(sb_in.at[1], gin1, osem.at[1, 0]),
        pltpu.make_async_copy(sb_out.at[1], gout1, osem.at[1, 1]),
    ]
    given = [
        remote(sb_in.at[1], gin1, ss.at[1], sr.at[1], at.swap_mate),
        remote(sb_out.at[1], gout1, ss.at[2], sr.at[2], at.swap_mate),
    ]

    def begin(copies):
        for copy in copies:
            copy.start()

    def finish(copies):
        for copy in copies:
            copy.wait()

    on_either(lambda: begin(kept), lambda: begin(given))

    def sub0_back(i, carry):
        d = order(i)
        j = line.index(d)

        line.ready(6, i, g0)
        backward(0, j, g0, dg0, gp0, ps0)

        @pl.when(i > 0)
        def _():
            line.give(7, d, ps0, pb0)

        return carry

    lax.fori_loop(0, 4, sub0_back, 0)
    weight_grads(0, e0, gp0, act0, g0)
    swap(0, 0).start()
    swap(0, 1).start()
    grad_normed = line.total(7, ps0, pb0)
    grad_stream = base[...] + norm_back(grad_normed, gain[0], xh0[...], sc[0][:, 0:1])
    sendg[...] = pieces_of(grad_stream)
    plane.start(1, piece(sendg), piece(arrg))
    keep_piece(at, sendg, arrg)
    vmine[0:1, :] = jnp.sum(grad_normed * xh0[...], axis=0, keepdims=True)
    vmine[2:3, :] = jnp.sum(grad_normed, axis=0, keepdims=True)
    vmine[5:8, :] = jnp.zeros((3, 1024), jnp.float32)
    give_core = remote(vmine, vcore, vs.at[0], vr.at[0], at.other)
    give_core.start()
    give_core.wait_recv()
    vline[z] = vmine[...] + vcore[...]

    def give_line(d):
        return line.copy(8, d, vline.at[z], vline.at[z])

    for d in (1, 3, 2):
        give_line(d).start()
    join_cores(0)
    stores = [
        pltpu.make_async_copy(sb_in.at[0], gin0, osem.at[0, 0]),
        pltpu.make_async_copy(sb_out.at[0], gout0, osem.at[0, 1]),
    ]
    begin(stores)
    plane.wait(1, piece(arrg))
    left, right = placings(route[0:1, :])
    gh[...] = from_pieces(left, right, arrg[...])
    for d in (1, 3, 2):
        line.got(8, d, vline.at[line.index(d)])
    vsum[...] = vline[0] + vline[1] + vline[2] + vline[3]
    give_mate = remote(vsum, vswap, vs.at[1], vr.at[1], at.swap_mate)
    pl.when(jnp.logical_not(same))(lambda: give_mate.start())
    give_core.wait_send()
    for d in (1, 3, 2):
        give_line(d).wait_send()
        gate_copy(d).wait_send()
        line.copy(5, d, dots.at[line.index(d)], dots_in.at[z]).wait_send()
    for k in (0, 1):
        for i in range(2):
            share(k, i).wait_send()
    line.sent_all(0, e0)
    line.sent_all(2, e1)
    line.sent_all(6, g0)
    line.sent(7, ps0)
    plane.sent(0, piece(sendh), piece(arrh))
    plane.sent(1, piece(sendg), piece(arrg))
    keep_ps.wait()
    finish(stores)
    on_either(lambda: finish(kept), lambda: finish(given))

    @pl.when(same)
    def _():
        vecg[...] = vsum[...]

    @pl.when(jnp.logical_not(same))
    def _():
        give_mate.wait()
        vecg[...] = vswap[...]


def expert_call(hid, route, exp_gain, exp_bias, centroid, cz, exp_in, exp_out, in0, out0, in1):
    bf, f32 = jnp.bfloat16, jnp.float32
    vmem, anywhere = pl.BlockSpec(memory_space=pltpu.VMEM), pl.BlockSpec(memory_space=pl.ANY)
    shape, V, dma = jax.ShapeDtypeStruct, pltpu.VMEM, pltpu.SemaphoreType.DMA
    line, rows, pieces = [V((512, 1024), bf)], [V((128, 1024), f32)], [V((256, 512), bf)]
    wide, small = [V((512, 1024), f32)], [V((4, 128, 128), f32)]
    vectors = [V((8, 1024), f32)]
    return pl.pallas_call(
        expert_kernel,
        out_shape=(
            shape((128, 1024), bf), shape((8, 1024), f32), shape((128, 1024), f32), shape((128, 128), f32),
            shape((512, 1024), bf), shape((1024, 512), bf), shape((512, 1024), bf), shape((1024, 512), bf),
            shape((512, 1024), bf),
        ),
        in_specs=[vmem] * 5 + [anywhere] * 6,
        out_specs=tuple([vmem] * 4 + [anywhere] * 5),
        scratch_shapes=[
            V((2, 1024, 1024), bf), V((2, 1024, 1024), bf), *(pieces * 4), *line,
            *(line * 9), *(line * 2), *(wide * 2), *(line * 2),
            *(rows * 4), *(small * 4),
            V((2, 1024, 512), f32), V((2, 512, 1024), f32),
            V((2, 1024, 512), bf), V((2, 512, 1024), bf), V((2, 1024, 512), bf), V((2, 512, 1024), bf),
            *(vectors * 5), V((4, 8, 1024), f32), *(vectors * 2),
            dma((3, 2)), dma((9, 4)), dma((9, 4)), dma((2, 15)), dma((2, 15)), dma((2, 2)), dma((2, 2)), dma((2, 2)),
            dma((2, 2)), dma((2, 2)), dma((3,)), dma((3,)), dma((3,)), dma((3,)),
        ],
        compiler_params=pltpu.CompilerParams(collective_id=1, has_side_effects=True, vmem_limit_bytes=60 << 20),
        name="experts",
    )(hid, route, exp_gain, exp_bias, centroid, cz, exp_in, exp_out, in0, out0, in1)


class Everyone:
    def __init__(self, at, send, recv):
        self.at, self.send, self.recv = at, send, recv

    def copy(self, phase, i, buf):
        own = buf.at[self.at.s]
        to = (lax.rem(self.at.s + i + 1, 8), self.at.f)
        return remote(own, own, self.send.at[phase, i], self.recv.at[phase, i], to)

    def start(self, phase, buf):
        for i in range(7):
            self.copy(phase, i, buf).start()

    def wait(self, phase, buf):
        for i in range(7):
            q = lax.rem(self.at.s + 7 - i, 8)
            dst = buf.at[q]
            remote(dst, dst, self.send.at[phase, i], self.recv.at[phase, i], (q, self.at.f)).wait_recv()

    def sent(self, phase, buf):
        for i in range(7):
            self.copy(phase, i, buf).wait_send()


def dense_backward_kernel(
    gh, after, docs, gains, mixed, route, mid, gate, x_h, n1_h, n2_h, act_h, dg_h, q_h, kv_h, kvo_h, wq_h, wo_h, wu_h,
    wd_h, ps_h, gin0, gout0,
    gx, bd, bu, bo, bq, gvec, res, fin0, fout0,
    ghs, xa, xh, n1, n2, act, dg, gp, qb, kvb, kvo, wq, wo, wu, wd,
    ps, pr, ps2, pr2, ps3, pr3, gms, gm, dp, dkv, dkvo, kvs, kvr,
    md, mu, mo, mq, td, tu, to, tq, rd, ru, ro, rq, xd, xu, xo, sd, su, so, yd, yu, yo, rp, sendr, arrr,
    vmine, vcore, vplane, vline, outz,
    lsem, zs, zr, xs, xr, ys, yr, kvss, kvsr, ks, kr, cs, cr, qs, qr, ss, sr, vs, vr,
):
    at = Place()
    z, yh, c, col = at.z, at.yh, at.c, at.col
    line, ring_x, ring_y = Ring(at, "z", zs, zr), Ring(at, "x", xs, xr), Ring(at, "y", ys, yr)
    plane, everyone = Plane(at, cs, cr), Everyone(at, qs, qr)
    bar = pltpu.get_barrier_semaphore()
    plane.greet(bar)
    for d in (1, 2, 3):
        greet(bar, line.device(line.index(d)))
        greet(bar, (2 * line.index(d) + 1 - yh, at.f))
    greet(bar, at.other)
    greet(bar, at.swap_mate)
    loads = [
        pltpu.make_async_copy(src, dst, lsem.at[k])
        for k, (src, dst) in enumerate(
            [
                (wd_h, wd), (dg_h, dg), (wu_h, wu), (act_h, act), (n2_h, n2), (wo_h, wo), (ps_h, ps3), (q_h, qb),
                (kv_h, kvb), (kvo_h, kvo), (wq_h, wq), (n1_h, n1), (x_h, xa),
            ]
        )
    ]
    for load in loads:
        load.start()
    ghs[block(z), :] = gh[...]
    pl.semaphore_wait(bar, 23)
    line.begin(0, ghs)
    swaps = [
        remote(gin0, fin0, ss.at[0], sr.at[0], at.swap_mate),
        remote(gout0, fout0, ss.at[1], sr.at[1], at.swap_mate),
    ]
    keeps = [
        pltpu.make_async_copy(gin0, fin0, lsem.at[13]),
        pltpu.make_async_copy(gout0, fout0, lsem.at[14]),
    ]

    @pl.when(at.same)
    def _():
        for keep in keeps:
            keep.start()

    @pl.when(jnp.logical_not(at.same))
    def _():
        for swap in swaps:
            swap.start()

    for load in loads[:3]:
        load.wait()

    def feed(i, carry):
        d = order(i)
        j = line.index(d)

        line.ready(0, i, ghs)
        values = ghs[block(j), :]
        for n in range(4):
            tile = slice(n * 256, (n + 1) * 256)
            gp[block(j), tile] = (dg[block(j), tile] * nt(values, tall_tile(wd, n))).astype(jnp.bfloat16)
        pres = gp[block(j), :]
        for n in range(4):
            tile = slice(n * 256, (n + 1) * 256)
            ps[block(j), tile] = nt(pres, tall_tile(wu, n)).astype(jnp.bfloat16)

        @pl.when(i > 0)
        def _():
            line.give(1, d, ps, pr)

        return carry

    lax.fori_loop(0, 4, feed, 0)
    for load in loads[3:7]:
        load.wait()

    def weight_grad(lhs, rhs, mine, theirs):
        def one(n, carry):
            rows = lhs[:, pl.ds(pl.multiple_of(n * 256, 256), 256)]
            grad = tn(rows, rhs[...])
            for half in range(2):
                first = grad[128 * half : 128 * half + 64].astype(jnp.bfloat16)
                second = grad[128 * half + 64 : 128 * half + 128].astype(jnp.bfloat16)
                here = lax.div(n, 2), 2 * lax.rem(n, 2) + half
                mine[here] = jnp.where(c == 0, first, second)
                theirs[here] = jnp.where(c == 0, second, first)
            return carry

        lax.fori_loop(0, 4, one, 0)

    def core_copy(phase, src, dst):
        return remote(src, dst, ks.at[phase], kr.at[phase], at.other)

    def join_cores(phase, mine, theirs, got):
        core_copy(phase, theirs, got).wait()

        def one(n, carry):
            here = lax.div(n, 4), lax.rem(n, 4)
            mine[here] = (mine[here].astype(jnp.float32) + got[here].astype(jnp.float32)).astype(jnp.bfloat16)
            return carry

        lax.fori_loop(0, 8, one, 0)

    def x_copy(phase, d, mine, dst):
        return ring_x.copy(phase, d, mine.at[:, ring_x.index(d)], dst.at[at.x])

    def y_copy(phase, d, part, dst):
        j = ring_y.index(d)
        src = part.at[lax.rem(j, 2), pl.ds(pl.multiple_of(32 * lax.div(j, 2), 32), 32)]
        return ring_y.copy(phase, d, src, dst.at[ring_y.pos])

    def to_x(phase, mine, dst):
        for d in (1, 3, 2):
            x_copy(phase, d, mine, dst).start()

    def to_y(phase, mine, got, part, dst):
        acc = mine[:, at.x].astype(jnp.float32)
        for d in (1, 3, 2):
            j = ring_x.index(d)
            ring_x.got(phase, d, got.at[j])
            acc += got[j].astype(jnp.float32)
        part[...] = acc.astype(jnp.bfloat16)
        for d in (1, 3, 2):
            y_copy(phase, d, part, dst).start()

    def y_total(phase, part, got):
        acc = part[at.yl, pl.ds(pl.multiple_of(32 * yh, 32), 32), :].astype(jnp.float32)
        for d in (1, 3, 2):
            j = ring_y.index(d)
            ring_y.got(phase, d, got.at[j])
            acc += got[j].astype(jnp.float32)
        return acc

    weight_grad(act, ghs, md, td)
    core_copy(0, td, rd).start()
    weight_grad(n2, gp, mu, tu)
    core_copy(1, tu, ru).start()
    join_cores(0, md, td, rd)
    to_x(0, md, xd)
    join_cores(1, mu, tu, ru)
    to_x(1, mu, xu)
    grad_normed = line.total(1, ps, pr)
    xhat, scale = norm_parts(after[...])
    vmine[1:2, :] = jnp.sum(grad_normed * xhat, axis=0, keepdims=True)
    vmine[3:4, :] = jnp.sum(grad_normed, axis=0, keepdims=True)
    grad_after = gh[...].astype(jnp.float32) + norm_back(grad_normed, gains[1:2, :], xhat, scale)
    gx[...] = grad_after
    grad_attn = grad_after.astype(jnp.bfloat16)
    for n in range(4):
        gms[:, 256 * n : 256 * n + 256] = nt(grad_attn, tall_tile(wo, n)).astype(jnp.bfloat16)

    def gm_copy(d):
        lanes = pl.ds(pl.multiple_of(256 * line.index(d), 256), 256)
        return line.copy(2, d, gms.at[:, lanes], gm.at[block(z)])

    for d in (1, 3, 2):
        gm_copy(d).start()
    gm[block(z), :] = gms[:, pl.ds(pl.multiple_of(256 * z, 256), 256)]
    for d in (1, 3, 2):
        line.give(6, d, ps3, pr3)
    gp[block(0), :] = grad_attn
    weight_grad(mixed, gp.at[block(0)], mo, to)
    core_copy(2, to, ro).start()
    to_y(0, md, xd, sd, yd)
    join_cores(2, mo, to, ro)
    to_x(2, mo, xo)
    for load in loads[7:]:
        load.wait()
    for d in (1, 3, 2):
        line.arrived(2, d, gm)
    dkv[...] = jnp.zeros_like(dkv)
    dkvo[...] = jnp.zeros_like(dkvo)

    def kv_copy(j):
        return remote(kvs.at[block(j)], kvr.at[block(j)], kvss.at[j], kvsr.at[j], at.mate)

    def attend_back(j):
        seen = masks(j, yh, docs)
        wide = slice(0, 128 * (j + 1))
        rows = slice(128 * j, 128 * j + 128)
        for p in range(2):
            lanes = slice(128 * p, 128 * p + 128)
            value_lanes = slice(256 + 128 * p, 384 + 128 * p)
            q, grad = qb[rows, lanes], gm[rows, lanes]
            keys = [kvb[wide, lanes], kvo[wide, lanes]]
            values = [kvb[wide, value_lanes], kvo[wide, value_lanes]]
            outs = []
            for h in range(2):
                q_h, grad_h = only(head_lanes(h), q), only(head_lanes(h), grad)
                probs = probabilities(q_h, keys, seen)
                back = [nt(grad_h, v) for v in values]
                dot = split_sum(probs[0] * back[0]) + split_sum(probs[1] * back[1])
                slopes = [(prob * (b - dot)).astype(jnp.bfloat16) for prob, b in zip(probs, back)]
                outs.append(nn(slopes[0], keys[0]) + nn(slopes[1], keys[1]))
                for k, acc in enumerate((dkv, dkvo)):
                    acc[wide, lanes] += tn(slopes[k], q_h) * 0.125
                    acc[wide, value_lanes] += tn(probs[k].astype(jnp.bfloat16), grad_h)
            dp[rows, lanes] = (jnp.where(head_lanes(0), outs[0], outs[1]) * 0.125).astype(jnp.bfloat16)
        kvs[rows, :] = dkvo[rows, :].astype(jnp.bfloat16)
        kv_copy(j).start()

    for j in (3, 2, 1, 0):
        attend_back(j)
    bd[at.s] = y_total(0, sd, yd).astype(jnp.bfloat16)
    everyone.start(0, bd)
    to_y(1, mu, xu, su, yu)
    vmine[0:1, :] = jnp.zeros((1, 1024), jnp.float32)
    vmine[2:3, :] = jnp.zeros((1, 1024), jnp.float32)
    vmine[4:8, :] = jnp.zeros((4, 1024), jnp.float32)
    for j in (3, 2, 1, 0):
        rows = slice(128 * j, 128 * j + 128)
        kv_copy(j).wait_recv()
        dp[rows, 256:768] = (dkv[rows, :] + kvr[rows, :].astype(jnp.float32)).astype(jnp.bfloat16)

    def last(i, carry):
        d = order(3 - i)
        j = line.index(d)
        values = dp[block(j), :]
        xh[...] = norm_parts(xa[block(j), :].astype(jnp.float32))[0]
        for n in range(4):
            tile = slice(n * 256, (n + 1) * 256)
            part = nt(values, tall_tile(wq, n))
            ps2[block(j), tile] = part.astype(jnp.bfloat16)
            vmine[0:1, tile] += jnp.sum(part * xh[:, tile], axis=0, keepdims=True)
            vmine[2:3, tile] += jnp.sum(part, axis=0, keepdims=True)

        @pl.when(i < 3)
        def _():
            line.give(3, d, ps2, pr2)

        return carry

    lax.fori_loop(0, 4, last, 0)
    give_core = remote(vmine, vcore, vs.at[0], vr.at[0], at.other)
    give_core.start()
    weight_grad(n1, dp, mq, tq)
    core_copy(3, tq, rq).start()

    def tile_of(q):
        return vmine.at[:, pl.ds(pl.multiple_of(128 * lax.div(q, 2), 128), 128)]

    def slot_v(q):
        return vplane.at[q]

    give_core.wait()
    vmine[...] += vcore[...]
    join_cores(3, mq, tq, rq)

    def piece_q(q):
        return mq.at[lax.div(q, 8), lax.rem(lax.div(q, 2), 4), pl.ds(pl.multiple_of(32 * lax.rem(q, 2), 32), 32)]

    def slot_q(q):
        return rp.at[q]

    plane.start(0, piece_q, slot_q)
    rp[at.m] = mq[at.yl, at.x, pl.ds(pl.multiple_of(32 * yh, 32), 32), :]
    plane.start(1, tile_of, slot_v)
    vplane[at.m] = vmine[:, pl.ds(pl.multiple_of(128 * col, 128), 128)]
    to_y(2, mo, xo, so, yo)
    bu[at.s] = y_total(1, su, yu).astype(jnp.bfloat16)
    everyone.start(1, bu)
    sendr[...] = pieces_of(mid[...] + gate[:, 0:1] * line.total(6, ps3, pr3))
    plane.start(2, piece(sendr), piece(arrr))
    keep_piece(at, sendr, arrr)
    total_out = y_total(2, so, yo)
    for n in range(4):
        outz[4 + n] = total_out[:, 256 * n : 256 * n + 256].astype(jnp.bfloat16)

    def out_copy(d):
        return line.copy(4, d, outz.at[4 + line.index(d)], outz.at[z])

    for d in (1, 3, 2):
        out_copy(d).start()
    grad_normed = line.total(3, ps2, pr2)
    xhat, scale = norm_parts(xa[block(z), :].astype(jnp.float32))
    gx[...] += norm_back(grad_normed, gains[0:1, :], xhat, scale)
    plane.wait(0, slot_q)
    acc = rp[0].astype(jnp.float32)
    for q in range(1, 16):
        acc += rp[q].astype(jnp.float32)
    bq[at.s] = acc.astype(jnp.bfloat16)
    everyone.start(3, bq)
    acc = outz[4 + z].astype(jnp.float32)
    for d in (1, 3, 2):
        line.got(4, d, outz.at[line.index(d)])
        acc += outz[line.index(d)].astype(jnp.float32)
    bo[at.s] = acc.astype(jnp.bfloat16)
    everyone.start(2, bo)
    plane.wait(1, slot_v)
    vline[z] = jnp.sum(vplane[...], axis=0)

    def vec_copy(d):
        return line.copy(5, d, vline.at[z], vline.at[z])

    for d in (1, 3, 2):
        vec_copy(d).start()
    plane.wait(2, piece(arrr))
    left, right = placings(route[0:1, :])
    res[...] = from_pieces(left, right, arrr[...])
    everyone.wait(0, bd)
    everyone.wait(1, bu)
    everyone.wait(2, bo)
    for d in (1, 3, 2):
        line.got(5, d, vline.at[line.index(d)])
    gvec[...] = jnp.sum(vline[...], axis=0)
    everyone.wait(3, bq)
    line.sent_all(0, ghs)
    line.sent(1, ps)
    line.sent(3, ps2)
    line.sent(6, ps3)
    for d in (1, 3, 2):
        gm_copy(d).wait_send()
        out_copy(d).wait_send()
        vec_copy(d).wait_send()
        for phase, (mine, x_got, part, y_got) in enumerate(((md, xd, sd, yd), (mu, xu, su, yu), (mo, xo, so, yo))):
            x_copy(phase, d, mine, x_got).wait_send()
            y_copy(phase, d, part, y_got).wait_send()
    for j in range(4):
        kv_copy(j).wait_send()
    plane.sent(0, piece_q, slot_q)
    plane.sent(1, tile_of, slot_v)
    plane.sent(2, piece(sendr), piece(arrr))
    for phase, buf in enumerate((bd, bu, bo, bq)):
        everyone.sent(phase, buf)

    @pl.when(at.same)
    def _():
        for keep in keeps:
            keep.wait()

    @pl.when(jnp.logical_not(at.same))
    def _():
        for swap in swaps:
            swap.wait()


def dense_backward_call(gh, after, docs, gains, mixed, route, mid, gate, saved, ps, gin0, gout0):
    bf, f32 = jnp.bfloat16, jnp.float32
    vmem, anywhere = pl.BlockSpec(memory_space=pltpu.VMEM), pl.BlockSpec(memory_space=pl.ANY)
    smem = pl.BlockSpec(memory_space=pltpu.SMEM)
    shape, V, dma = jax.ShapeDtypeStruct, pltpu.VMEM, pltpu.SemaphoreType.DMA
    line, pieces = [V((512, 1024), bf)], [V((256, 512), bf)]
    wide, narrow = [V((2, 4, 64, 1024), bf)], [V((2, 4, 64, 768), bf)]
    return pl.pallas_call(
        dense_backward_kernel,
        out_shape=[
            shape((128, 1024), f32), shape((8, 32, 1024), bf), shape((8, 32, 1024), bf), shape((8, 32, 256), bf),
            shape((8, 32, 768), bf), shape((8, 128), f32), shape((128, 1024), bf), shape((1024, 512), bf),
            shape((512, 1024), bf),
        ],
        in_specs=[vmem, vmem, smem] + [vmem] * 5 + [anywhere] * 15,
        out_specs=[vmem] * 7 + [anywhere] * 2,
        scratch_shapes=[
            *(line * 2), V((128, 1024), f32), *(line * 3), V((512, 1024), f32), *line,
            V((512, 256), bf), V((512, 512), bf), V((512, 512), bf),
            V((2, 4, 2, 2, 32, 768), bf), *([V((2, 4, 2, 2, 32, 1024), bf)] * 3),
            *(line * 6),
            V((128, 1024), bf), V((512, 256), bf), V((512, 768), bf), V((512, 512), f32), V((512, 512), f32),
            V((512, 512), bf), V((512, 512), bf),
            *(wide * 3), *narrow, *(wide * 3), *narrow, *(wide * 3), *narrow,
            *([V((4, 2, 64, 1024), bf)] * 3), *([V((2, 64, 1024), bf)] * 3), *([V((4, 32, 1024), bf)] * 3),
            V((16, 32, 768), bf), *(pieces * 2),
            V((8, 1024), f32), V((8, 1024), f32), V((16, 8, 128), f32), V((4, 8, 128), f32),
            V((8, 32, 256), bf),
            dma((15,)), dma((7, 4)), dma((7, 4)), dma((3, 3)), dma((3, 3)), dma((3, 3)), dma((3, 3)), dma((4,)),
            dma((4,)), dma((4,)), dma((4,)), dma((3, 15)), dma((3, 15)), dma((4, 7)), dma((4, 7)), dma((2,)),
            dma((2,)), dma((1,)), dma((1,)),
        ],
        compiler_params=pltpu.CompilerParams(collective_id=3, has_side_effects=True, vmem_limit_bytes=62 << 20),
        name="dense_backward",
    )(gh, after, docs, gains, mixed, route, mid, gate, *saved, ps, gin0, gout0)


def finish_kernel(
    gvec, vecg, res, gx, bd, bu, bo, bq, in0, in1, out0, out1,
    ng, nb, eg, eb, cen, o_res, o_gx, o_gq, o_go, o_gu, o_gd, o_in, o_out,
    b_in, b_out, f_in, f_out, vd, vu, vo, vq, gq, go, gu, gd, isem, osem,
):
    whole = [pltpu.make_async_copy(res, o_res, osem.at[0]), pltpu.make_async_copy(gx, o_gx, osem.at[1])]
    pairs = [
        (in0, b_in.at[0]), (in1, b_in.at[1]), (out0, b_out.at[0]), (out1, b_out.at[1]), (bd, vd), (bu, vu), (bo, vo),
        (bq, vq),
    ]
    loads = [pltpu.make_async_copy(src, dst, isem.at[k]) for k, (src, dst) in enumerate(pairs)]
    for copy in loads + whole:
        copy.start()
    c = lax.rem(lax.axis_index("fsdp"), 2)
    mine = jnp.where(c == 0, gvec[0:4, 0:64], gvec[0:4, 64:128])
    ng[...] = mine[0:2]
    nb[...] = mine[2:4]
    eg[...] = vecg[0:2, :]
    eb[...] = vecg[2:4, :]
    cen[...] = vecg[4:5, :]
    stores = []

    def store(src, dst):
        stores.append(pltpu.make_async_copy(src, dst, osem.at[2 + len(stores)]))
        stores[-1].start()

    for k in range(4):
        loads[k].wait()
        low, wide, out = ((b_in, f_in, o_in), (b_out, f_out, o_out))[k // 2]
        wide[k % 2] = low[k % 2].astype(jnp.float32)
        store(wide.at[k % 2], out.at[k % 2])
    for k in range(4, 8):
        loads[k].wait()
    lane = lax.broadcasted_iota(jnp.int32, (32, 128), 1) < 64
    for half in range(2):
        rows = slice(32 * half, 32 * half + 32)
        for z in range(4):
            gd[64 * z + 32 * half : 64 * z + 32 * half + 32, :] = vd[2 * z + half].astype(jnp.float32)
            go[rows, 256 * z : 256 * z + 256] = vo[2 * z + half].astype(jnp.float32)
            for part in range(3):
                gq[rows, 1024 * part + 256 * z : 1024 * part + 256 * z + 256] = vq[
                    2 * z + half, :, 256 * part : 256 * part + 256
                ].astype(jnp.float32)
        for n in range(8):
            tile = slice(128 * n, 128 * n + 128)
            quarter = [vu[2 * z + half, :, tile].astype(jnp.float32) for z in range(4)]
            turned = [pltpu.roll(v, 64, 1) for v in quarter]
            first = 512 * n
            gu[rows, first : first + 128] = jnp.where(lane, quarter[0], turned[1])
            gu[rows, first + 128 : first + 256] = jnp.where(lane, quarter[2], turned[3])
            gu[rows, first + 256 : first + 384] = jnp.where(lane, turned[0], quarter[1])
            gu[rows, first + 384 : first + 512] = jnp.where(lane, turned[2], quarter[3])
    for src, dst in ((gq, o_gq), (go, o_go), (gu, o_gu), (gd, o_gd)):
        store(src, dst)
    for copy in whole + stores:
        copy.wait()


def finish_call(gvec, vecg, res, gx, bd, bu, bo, bq, in0, in1, out0, out1):
    bf, f32 = jnp.bfloat16, jnp.float32
    vmem, anywhere = pl.BlockSpec(memory_space=pltpu.VMEM), pl.BlockSpec(memory_space=pl.ANY)
    shape, V, dma = jax.ShapeDtypeStruct, pltpu.VMEM, pltpu.SemaphoreType.DMA
    return pl.pallas_call(
        finish_kernel,
        out_shape=[
            shape((2, 64), f32), shape((2, 64), f32), shape((2, 1024), f32), shape((2, 1024), f32),
            shape((1, 1024), f32), shape((128, 1024), bf), shape((128, 1024), f32), shape((64, 3072), f32),
            shape((64, 1024), f32), shape((64, 4096), f32), shape((256, 1024), f32), shape((2, 1024, 512), f32),
            shape((2, 512, 1024), f32),
        ],
        in_specs=[vmem] * 2 + [anywhere] * 10,
        out_specs=[vmem] * 5 + [anywhere] * 8,
        scratch_shapes=[
            V((2, 1024, 512), bf), V((2, 512, 1024), bf), V((2, 1024, 512), f32), V((2, 512, 1024), f32),
            V((8, 32, 1024), bf), V((8, 32, 1024), bf), V((8, 32, 256), bf), V((8, 32, 768), bf),
            V((64, 3072), f32), V((64, 1024), f32), V((64, 4096), f32), V((256, 1024), f32),
            dma((8,)), dma((10,)),
        ],
        compiler_params=pltpu.CompilerParams(vmem_limit_bytes=62 << 20),
        name="finish",
    )(gvec, vecg, res, gx, bd, bu, bo, bq, in0, in1, out0, out1)


def on_device(
    inputs,
    doc_starts,
    route,
    norm_gain,
    norm_bias,
    w_qkv,
    w_out,
    w_up,
    w_down,
    exp_gain,
    exp_bias,
    exp_in,
    exp_out,
    centroid,
    cotangent,
):
    tok_rows, width = 128, 1024
    x = inputs.reshape(tok_rows, width)
    cot = cotangent.reshape(tok_rows, width)
    slots = route.reshape(1, tok_rows)
    hidden, mixed, after, gains, *saved, cz, in0, out0, in1 = dense_forward_call(
        x, norm_gain, norm_bias, doc_starts, slots, cot, w_qkv, w_out, w_up, w_down, exp_in[0], exp_out[0]
    )
    grad_hidden, vec_grads, mid, gate, part, grad_in1, grad_out1, grad_in0, grad_out0 = expert_call(
        hidden, slots, exp_gain[0], exp_bias[0], centroid, cz, exp_in[0], exp_out[0], in0, out0, in1
    )
    grad_x, down, up, out, qkv, norm_grads, result, grad_in0, grad_out0 = dense_backward_call(
        grad_hidden, after, doc_starts, gains, mixed, slots, mid, gate, saved, part, grad_in0, grad_out0
    )
    gain, bias, e_gain, e_bias, center, result, grad_x, g_qkv, g_out, g_up, g_down, e_in, e_out = finish_call(
        norm_grads, vec_grads, result, grad_x, down, up, out, qkv, grad_in0, grad_in1, grad_out0, grad_out1
    )
    return (
        result[None],
        grad_x[None],
        gain,
        bias,
        g_qkv,
        g_out,
        g_up,
        g_down,
        e_gain[None],
        e_bias[None],
        e_in[None],
        e_out[None],
        center,
    )


def solution(mesh):
    in_specs = (
        P("fsdp", "seq", None),
        P("fsdp", None),
        P("fsdp", "seq", None),
        P(None, "fsdp"),
        P(None, "fsdp"),
        P("fsdp", None),
        P("fsdp", None),
        P("fsdp", None),
        P("fsdp", None),
        P("fsdp", None, None),
        P("fsdp", None, None),
        P("fsdp", None, None, "seq"),
        P("fsdp", None, "seq", None),
        P("fsdp", None),
        P("fsdp", "seq", None),
    )
    out_specs = (
        P("fsdp", "seq", None),
        P("fsdp", "seq", None),
        P(None, "fsdp"),
        P(None, "fsdp"),
        P("fsdp", None),
        P("fsdp", None),
        P("fsdp", None),
        P("fsdp", None),
        P("fsdp", None, None),
        P("fsdp", None, None),
        P("fsdp", None, None, "seq"),
        P("fsdp", None, "seq", None),
        P("fsdp", None),
    )
    return jax.shard_map(
        on_device, mesh=mesh, in_specs=in_specs, out_specs=out_specs, check_vma=False
    )
```

```python
import jax
import jax.numpy as jnp
from jax import lax
from jax.experimental import pallas as pl
from jax.experimental.pallas import tpu as pltpu
from jax.sharding import PartitionSpec as P

MESH = pl.DeviceIdType.MESH
epsilon = 1e-05
masked_score = -1e30


def split_sum(values):
    return jnp.sum(values, axis=-1, keepdims=True)


def norm_parts(values):
    average = split_sum(values) * (1.0 / values.shape[-1])
    centered = values - average
    spread = split_sum(centered * centered) * (1.0 / values.shape[-1])
    scale = lax.rsqrt(spread + epsilon)
    return centered * scale, scale


def norm_back(grad_normed, gain, xhat, scale):
    width = 1.0 / xhat.shape[-1]
    u = grad_normed * gain
    return scale * (u - split_sum(u) * width - xhat * (split_sum(u * xhat) * width))


def gelu_parts(pre):
    inner = 0.7978845608028654
    cubic = 0.044715
    square = pre * pre
    t = jnp.tanh(inner * pre * (1.0 + cubic * square))
    half = 0.5 * (1.0 + t)
    slope = half + 0.5 * pre * (1.0 - t * t) * (inner * (1.0 + 3.0 * cubic * square))
    return pre * half, slope


def nn(a, b):
    return lax.dot_general(a, b, (((1,), (0,)), ((), ())), preferred_element_type=jnp.float32)


def nt(a, b):
    return lax.dot_general(a, b, (((1,), (1,)), ((), ())), preferred_element_type=jnp.float32)


def tn(a, b):
    return lax.dot_general(a, b, (((0,), (0,)), ((), ())), preferred_element_type=jnp.float32)


def remote(src, dst, send, recv, device):
    return pltpu.make_async_remote_copy(
        src_ref=src, dst_ref=dst, send_sem=send, recv_sem=recv, device_id=device, device_id_type=MESH
    )


def greet(bar, device):
    pl.semaphore_signal(bar, inc=1, device_id=device, device_id_type=MESH)


def block(index):
    return pl.ds(pl.multiple_of(index * 128, 128), 128)


def order(i):
    return i + lax.div(i, 2) - 2 * lax.div(i, 3)


class Place:
    def __init__(self):
        self.s, self.f = lax.axis_index("seq"), lax.axis_index("fsdp")
        self.z, self.yh = lax.div(self.s, 2), lax.rem(self.s, 2)
        self.yl, self.col, self.c = lax.div(self.f, 8), lax.div(self.f, 2), lax.rem(self.f, 2)
        self.x = lax.rem(self.col, 4)
        self.m = self.f - self.c + self.yh
        self.other = (self.s, self.f + 1 - 2 * self.c)
        self.mate = (2 * self.z + 1 - self.yh, self.f)
        self.swap_mate = (2 * self.z + 1 - self.yh, self.f + 1 - 2 * self.c)
        self.same = self.c == self.yh


class Ring:
    def __init__(self, at, axis, send, recv):
        self.at, self.axis, self.send, self.recv = at, axis, send, recv
        self.pos = {"z": at.z, "x": at.x, "y": 2 * at.yh + at.yl}[axis]

    def index(self, d):
        return lax.rem(self.pos + d, 4)

    def device(self, j):
        at = self.at
        if self.axis == "z":
            return (2 * j + at.yh, at.f)
        if self.axis == "x":
            return (at.s, at.f - 2 * at.x + 2 * j)
        return (2 * at.z + lax.div(j, 2), 8 * lax.rem(j, 2) + at.f - 8 * at.yl)

    def copy(self, phase, d, src, dst):
        sems = self.send.at[phase, d - 1], self.recv.at[phase, d - 1]
        return remote(src, dst, *sems, self.device(self.index(d)))

    def got(self, phase, d, dst):
        sems = self.send.at[phase, 3 - d], self.recv.at[phase, 3 - d]
        remote(dst, dst, *sems, self.device(self.index(d))).wait_recv()

    def spread(self, phase, buf):
        own = buf.at[block(self.pos)]
        for d in (1, 3, 2):
            self.copy(phase, d, own, own).start()

    def near(self, phase, d, buf):
        own = buf.at[block(self.pos)]
        return self.copy(phase, d, own, own)

    def half(self, buf, d, upper):
        return buf.at[pl.ds(pl.multiple_of(128 * self.index(d) + 64 * upper, 64), 64)]

    def onward(self, phase, buf, upper):
        rows = self.half(buf, 3 if upper else 1, upper)
        slot = 3 if upper else 1
        to = self.device(self.index(1 if upper else 3))
        return remote(rows, rows, self.send.at[phase, slot], self.recv.at[phase, slot], to)

    def begin(self, phase, buf):
        for d in (1, 3):
            self.near(phase, d, buf).start()

    def relay(self, phase, buf):
        for d in (1, 3):
            self.arrived(phase, d, buf)
        for upper in (0, 1):
            self.onward(phase, buf, upper).start()

    def far(self, phase, buf):
        for upper in (0, 1):
            slot = 3 if upper else 1
            rows = self.half(buf, 2, upper)
            to = self.device(self.index(1 if upper else 3))
            remote(rows, rows, self.send.at[phase, slot], self.recv.at[phase, slot], to).wait_recv()

    def ready(self, phase, i, buf):
        pl.when(i == 1)(lambda: self.relay(phase, buf))
        pl.when(i == 3)(lambda: self.far(phase, buf))

    def sent_all(self, phase, buf):
        for d in (1, 3):
            self.near(phase, d, buf).wait_send()
        for upper in (0, 1):
            self.onward(phase, buf, upper).wait_send()

    def arrived(self, phase, d, buf):
        self.got(phase, d, buf.at[block(self.index(d))])

    def give(self, phase, d, src, dst):
        self.copy(phase, d, src.at[block(self.index(d))], dst.at[block(self.pos)]).start()

    def sent(self, phase, buf):
        own = buf.at[block(self.pos)]
        for d in (1, 3, 2):
            self.copy(phase, d, own, own).wait_send()

    def total(self, phase, own, parts):
        acc = own[block(self.pos), :].astype(jnp.float32)
        for d in (1, 3, 2):
            self.arrived(phase, d, parts)
            acc += parts[block(self.index(d)), :].astype(jnp.float32)
        return acc


class Plane:
    def __init__(self, at, send, recv):
        self.at, self.m = at, at.m
        self.send, self.recv = send, recv

    def device(self, q):
        return (2 * self.at.z + lax.rem(q, 2), q - lax.rem(q, 2) + self.at.c)

    def greet(self, bar):
        def one(i, carry):
            greet(bar, self.device(lax.rem(self.m + i + 1, 16)))
            return carry

        lax.fori_loop(0, 15, one, 0)

    def copy(self, phase, i, src_of, dst_of):
        q = lax.rem(self.m + i + 1, 16)
        return remote(src_of(q), dst_of(self.m), self.send.at[phase, i], self.recv.at[phase, i], self.device(q))

    def start(self, phase, src_of, dst_of):
        def one(i, carry):
            self.copy(phase, i, src_of, dst_of).start()
            return carry

        lax.fori_loop(0, 15, one, 0)

    def wait(self, phase, dst_of):
        def one(i, carry):
            q = lax.rem(self.m + 15 - i, 16)
            dst = dst_of(q)
            remote(dst, dst, self.send.at[phase, i], self.recv.at[phase, i], self.device(q)).wait_recv()
            return carry

        lax.fori_loop(0, 15, one, 0)

    def sent(self, phase, src_of, dst_of):
        def one(i, carry):
            self.copy(phase, i, src_of, dst_of).wait_send()
            return carry

        lax.fori_loop(0, 15, one, 0)


def piece(buf):
    return lambda q: buf.at[pl.ds(pl.multiple_of(q * 16, 16), 16)]


def keep_piece(at, src, dst):
    own = pl.ds(pl.multiple_of(at.m * 16, 16), 16)
    dst[own, :] = src[own, :]


def placings(route):
    row = lax.broadcasted_iota(jnp.int32, (256, 128), 0)
    inner = row & 15
    slot = (row >> 4) * 8 + (inner & 7)
    hit = slot == route
    left = jnp.where(hit & (inner < 8), 1.0, 0.0).astype(jnp.bfloat16)
    right = jnp.where(hit & (inner >= 8), 1.0, 0.0).astype(jnp.bfloat16)
    return left, right


def to_pieces(left, right, rows):
    half = rows.shape[1] // 2
    return (nn(left, rows[:, :half]) + nn(right, rows[:, half:])).astype(jnp.bfloat16)


def from_pieces(left, right, pieces):
    return jnp.concatenate([tn(left, pieces), tn(right, pieces)], axis=1).astype(jnp.bfloat16)


def rows_of(pieces):
    wide = pieces.astype(jnp.float32).reshape(16, 2, 8, 512)
    return jnp.concatenate([wide[:, 0].reshape(128, 512), wide[:, 1].reshape(128, 512)], axis=1)


def pieces_of(rows):
    left = rows[:, :512].reshape(16, 1, 8, 512)
    right = rows[:, 512:].reshape(16, 1, 8, 512)
    return jnp.concatenate([left, right], axis=1).reshape(256, 512).astype(jnp.bfloat16)


class Gather:
    def __init__(self, at, phase, first, src, full, xs, xr, ys, yr, ks, kr):
        self.at, self.phase, self.src, self.full = at, phase, src, full
        self.x_first = first == "x"
        self.rings = [Ring(at, "y", ys, yr), Ring(at, "x", xs, xr)]
        if self.x_first:
            self.rings.reverse()
        self.ks, self.kr = ks, kr

    def pushed(self, d):
        at = self.at
        return self.rings[0].copy(self.phase, d, self.src, self.full.at[at.yl, at.x, at.c, at.yh])

    def passed(self, d):
        at = self.at
        own = self.full.at[at.yl, :, at.c, at.yh] if self.x_first else self.full.at[:, at.x, at.c]
        return self.rings[1].copy(self.phase, d, own, own)

    def core(self, c):
        half = self.full.at[:, :, c]
        return remote(half, half, self.ks.at[self.phase], self.kr.at[self.phase], self.at.other)

    def start(self):
        at = self.at
        for d in (1, 3, 2):
            self.pushed(d).start()
        self.full[at.yl, at.x, at.c, at.yh] = self.src[...]

    def turn(self):
        at, full = self.at, self.full
        for d in (1, 3, 2):
            j = self.rings[0].index(d)
            dst = full.at[at.yl, j, at.c, at.yh] if self.x_first else full.at[lax.rem(j, 2), at.x, at.c, lax.div(j, 2)]
            self.rings[0].got(self.phase, d, dst)
        for d in (1, 3, 2):
            self.passed(d).start()

    def share(self):
        at, full = self.at, self.full
        for d in (1, 3, 2):
            j = self.rings[1].index(d)
            dst = full.at[lax.rem(j, 2), :, at.c, lax.div(j, 2)] if self.x_first else full.at[:, j, at.c]
            self.rings[1].got(self.phase, d, dst)
        self.core(at.c).start()

    def wait(self):
        self.core(1 - self.at.c).wait_recv()

    def sent(self):
        for d in (1, 3, 2):
            self.pushed(d).wait_send()
            self.passed(d).wait_send()
        self.core(self.at.c).wait_send()


def labels(position, first, second):
    return jnp.where(position >= first, 1, 0) + jnp.where(position >= second, 1, 0)


def mask(j, yh, parity, docs):
    first, second = docs[0, 0], docs[0, 1]
    wide = 128 * (j + 1)
    row = lax.broadcasted_iota(jnp.int32, (128, wide), 0) + 128 * (2 * j + yh)
    lane = lax.broadcasted_iota(jnp.int32, (128, wide), 1)
    key = (lane >> 7) * 256 + (lane & 127) + 128 * parity
    return (key <= row) & (labels(key, first, second) == labels(row, first, second))


def masked_scores(q, keys, seen):
    return jnp.where(seen, nt(q, keys) * 0.125, masked_score)


def probabilities(q, keys, seen):
    scores = [masked_scores(q, k, ok) for k, ok in zip(keys, seen)]
    top = jnp.maximum(
        jnp.max(scores[0], axis=-1, keepdims=True), jnp.max(scores[1], axis=-1, keepdims=True)
    )
    weights = [jnp.exp(s - top) for s in scores]
    inverse = 1.0 / (split_sum(weights[0]) + split_sum(weights[1]))
    return [w * inverse for w in weights]


def head_lanes(h):
    lane = lax.broadcasted_iota(jnp.int32, (128, 128), 1)
    return lane < 64 if h == 0 else lane >= 64


def only(keep, values):
    return jnp.where(keep, values.astype(jnp.float32), 0.0).astype(jnp.bfloat16)


def wide_tile(full, tile):
    part = full[:, :, :, :, :, tile]
    return part.reshape(1024, part.shape[-1])


def tall_tile(full, n):
    part = full[n // 2, 2 * (n % 2) : 2 * (n % 2) + 2]
    return part.reshape(256, part.shape[-1])


def dense_forward_kernel(
    x, gain, bias, docs, route, cot, w_qkv, w_out, w_up, w_down, exp_in, exp_out,
    hid, mixed, after, gains,
    o_x, o_n1, o_n2, o_act, o_dg, o_q, o_kv, o_kvo, o_wq, o_wo, o_wu, o_wd, o_cz, o_in0, o_out0,
    sq, su, wq, wo, wu, wd, gtile, gmine, gother,
    xa, n1, n2, cz, qb, kvb, kvo, mixs, act, dg, ps, pr, sendc, arrc, stats, own_sum,
    zs, zr, xs, xr, ys, yr, kvs, kvr, ks, kr, gs, gr, cs, cr, ss, sr, osem,
):
    at = Place()
    z, yh, c, col = at.z, at.yh, at.c, at.col
    line, plane = Ring(at, "z", zs, zr), Plane(at, cs, cr)
    bar = pltpu.get_barrier_semaphore()
    for d in (1, 2, 3):
        greet(bar, line.device(line.index(d)))
    greet(bar, at.other)
    greet(bar, at.swap_mate)
    plane.greet(bar)
    xa[block(z), :] = x[...]
    for part in range(3):
        sq[:, 256 * part : 256 * part + 256] = w_qkv[:, pl.ds(pl.multiple_of(1024 * part + 256 * z, 256), 256)]
    gtile[...] = jnp.zeros_like(gtile)
    for k, ref in enumerate((gain, bias)):
        values = ref[...].astype(jnp.float32)
        none = jnp.zeros_like(values)
        here = jnp.where(c == 0, jnp.concatenate([values, none], 1), jnp.concatenate([none, values], 1))
        gtile[2 * k : 2 * k + 2, :] = here
    half = pl.ds(pl.multiple_of(32 * yh, 32), 32)
    down_rows = w_down.at[pl.ds(pl.multiple_of(64 * z + 32 * yh, 32), 32)]
    sems = (xs, xr, ys, yr, ks, kr)
    left_q, right_q = (wq.at[:, :, :, :, :, 0:384], wq.at[:, :, :, :, :, 384:768])
    qkv_a = Gather(at, 0, "y", sq.at[half, 0:384], left_q, *sems)
    qkv_b = Gather(at, 1, "x", sq.at[half, 384:768], right_q, *sems)
    out = Gather(at, 2, "y", w_out.at[half], wo, *sems)
    up = Gather(at, 3, "y", su.at[half], wu, *sems)
    down = Gather(at, 4, "x", down_rows, wd, *sems)
    low = lax.broadcasted_iota(jnp.int32, (64, 128), 1) < 64
    odd = lax.rem(z, 2) == 1
    for n in range(8):
        first = 512 * n + 128 * lax.div(z, 2)
        a = w_up[:, pl.ds(pl.multiple_of(first, 128), 128)].astype(jnp.float32)
        b = w_up[:, pl.ds(pl.multiple_of(first + 256, 128), 128)].astype(jnp.float32)
        kept = jnp.where(low, a, pltpu.roll(b, 64, 1))
        moved = jnp.where(low, pltpu.roll(a, 64, 1), b)
        su[:, 128 * n : 128 * n + 128] = jnp.where(odd, moved, kept).astype(jnp.bfloat16)
    left, right = placings(route[0:1, :])
    sendc[...] = to_pieces(left, right, cot[...])
    pl.semaphore_wait(bar, 20)
    line.begin(0, xa)
    tile_at = pl.ds(pl.multiple_of(128 * col, 128), 128)

    def gain_copy(i):
        to = (at.s, 2 * lax.rem(col + i + 1, 8) + c)
        return remote(gtile, gmine.at[:, tile_at], gs.at[i], gr.at[i], to)

    def push_gain(i, carry):
        gain_copy(i).start()
        return carry

    lax.fori_loop(0, 7, push_gain, 0)
    gmine[:, tile_at] = gtile[...]
    qkv_a.start()
    qkv_b.start()
    plane.start(0, piece(sendc), piece(arrc))
    keep_piece(at, sendc, arrc)
    for weight in (out, up, down):
        weight.start()
    qkv_a.turn()
    qkv_b.turn()
    line.relay(0, xa)

    def wait_gain(i, carry):
        q = lax.rem(col + 7 - i, 8)
        dst = gmine.at[:, pl.ds(pl.multiple_of(128 * q, 128), 128)]
        remote(dst, dst, gs.at[i], gr.at[i], (at.s, 2 * q + c)).wait_recv()
        return carry

    lax.fori_loop(0, 7, wait_gain, 0)
    gain_core = remote(gmine, gother, gs.at[7], gr.at[7], at.other)
    gain_core.start()
    gain_core.wait_recv()
    gains[...] = gmine[...] + gother[...]
    qkv_a.share()
    qkv_b.share()
    out.turn()
    up.turn()

    def kv_copy(i, j):
        return remote(kvb.at[block(j)], kvo.at[block(j)], kvs.at[i], kvr.at[i], at.mate)

    def project_qkv(i, carry):
        j = line.index(order(i))
        pl.when(i == 3)(lambda: line.far(0, xa))
        xhat = norm_parts(xa[block(j), :].astype(jnp.float32))[0]
        n1[block(j), :] = (xhat * gains[0:1, :] + gains[2:3, :]).astype(jnp.bfloat16)

        @pl.when(i == 0)
        def _():
            qkv_a.wait()
            qkv_b.wait()

        values = n1[block(j), :]
        kvb[block(j), 0:256] = nn(values, wide_tile(wq, slice(256, 512))).astype(jnp.bfloat16)
        kvb[block(j), 256:512] = nn(values, wide_tile(wq, slice(512, 768))).astype(jnp.bfloat16)
        kv_copy(i, j).start()
        qb[block(j), :] = nn(values, wide_tile(wq, slice(0, 256))).astype(jnp.bfloat16)
        return carry

    lax.fori_loop(0, 4, project_qkv, 0)
    down.turn()
    plane.wait(0, piece(arrc))
    cz[block(z), :] = rows_of(arrc[...]).astype(jnp.bfloat16)
    line.spread(4, cz)

    def heads(j, keys, parity):
        seen = mask(j, yh, parity, docs)
        wide = slice(0, 128 * (j + 1))
        for p in range(2):
            lanes = slice(128 * p, 128 * p + 128)
            q = qb[128 * j : 128 * j + 128, lanes]
            for h in range(2):
                scores = masked_scores(only(head_lanes(h), q), keys[wide, lanes], seen)
                yield 4 * j + 2 * p + h, h, lanes, scores, keys[wide, 256 + 128 * p : 384 + 128 * p]

    first = None
    for j in range(4):
        for k, h, lanes, scores, values in heads(j, kvb, yh):
            top = jnp.max(scores, axis=-1, keepdims=True)
            weights = jnp.exp(scores - top)
            stats[k] = jnp.where(head_lanes(0), top, split_sum(weights))
            summed = nn(weights.astype(jnp.bfloat16), values)
            if h == 0:
                first = summed
            else:
                own_sum[128 * j : 128 * j + 128, lanes] = jnp.where(head_lanes(0), first, summed)
    for i in range(4):
        kv_copy(i, line.index(order(i))).wait_recv()
    swaps = [
        remote(exp_in.at[0], o_in0, ss.at[0], sr.at[0], at.swap_mate),
        remote(exp_out.at[0], o_out0, ss.at[1], sr.at[1], at.swap_mate),
    ]

    @pl.when(c != yh)
    def _():
        swaps[0].start()

    my_lanes = pl.ds(pl.multiple_of(256 * z, 256), 256)

    def mix_copy(d):
        return line.copy(1, d, mixs.at[block(line.index(d))], mixed.at[:, my_lanes])

    for j in range(4):
        rows = slice(128 * j, 128 * j + 128)
        for k, h, lanes, scores, values in heads(j, kvo, 1 - yh):
            top, total = stats[k][:, 0:1], stats[k][:, 64:65]
            new_top = jnp.maximum(top, jnp.max(scores, axis=-1, keepdims=True))
            kept = jnp.exp(top - new_top)
            weights = jnp.exp(scores - new_top)
            inverse = 1.0 / (total * kept + split_sum(weights))
            summed = (own_sum[rows, lanes] * kept + nn(weights.astype(jnp.bfloat16), values)) * inverse
            if h == 0:
                first = summed
            else:
                mixs[rows, lanes] = jnp.where(head_lanes(0), first, summed).astype(jnp.bfloat16)
        pl.when(z != j)(lambda: mix_copy(lax.rem(j + 4 - z, 4)).start())
    mixed[:, my_lanes] = mixs[block(z), :]
    out.share()
    out.wait()
    for d in (1, 3, 2):
        line.got(1, d, mixed.at[:, pl.ds(pl.multiple_of(256 * line.index(d), 256), 256)])
    for n in range(4):
        tile = slice(256 * n, 256 * n + 256)
        after[:, tile] = x[:, tile].astype(jnp.float32) + nn(mixed[...], wide_tile(wo, tile))
    xhat = norm_parts(after[...])[0]
    n2[block(z), :] = (xhat * gains[1:2, :] + gains[3:4, :]).astype(jnp.bfloat16)
    line.begin(2, n2)
    up.share()
    down.share()
    @pl.when(c != yh)
    def _():
        swaps[1].start()

    up.wait()
    down.wait()
    stores = [
        pltpu.make_async_copy(src, dst, osem.at[k])
        for k, (src, dst) in enumerate(
            [(xa, o_x), (n1, o_n1), (qb, o_q), (kvb, o_kv), (kvo, o_kvo), (wq, o_wq), (wo, o_wo), (wu, o_wu), (wd, o_wd)]
        )
    ]
    for store in stores:
        store.start()

    def feed(i, carry):
        d = order(i)
        j = line.index(d)
        line.ready(2, i, n2)
        values = n2[block(j), :]
        for n in range(4):
            tile = slice(n * 256, (n + 1) * 256)
            acted, slope = gelu_parts(nn(values, wide_tile(wu, tile)))
            act[block(j), tile] = acted.astype(jnp.bfloat16)
            dg[block(j), tile] = slope
        values = act[block(j), :]
        for n in range(4):
            tile = slice(n * 256, (n + 1) * 256)
            ps[block(j), tile] = nn(values, wide_tile(wd, tile)).astype(jnp.bfloat16)

        @pl.when(i > 0)
        def _():
            line.give(3, d, ps, pr)

        return carry

    lax.fori_loop(0, 4, feed, 0)
    for d in (1, 3, 2):
        line.arrived(4, d, cz)
    late = [
        pltpu.make_async_copy(src, dst, osem.at[9 + k])
        for k, (src, dst) in enumerate([(n2, o_n2), (act, o_act), (dg, o_dg), (cz, o_cz)])
    ]
    for store in late:
        store.start()
    gain_core.wait_send()

    def sent_gain(i, carry):
        gain_copy(i).wait_send()
        return carry

    lax.fori_loop(0, 7, sent_gain, 0)
    for weight in (qkv_a, qkv_b, out, up, down):
        weight.sent()
    for i in range(4):
        kv_copy(i, line.index(order(i))).wait_send()
    line.sent_all(0, xa)
    for d in (1, 3, 2):
        mix_copy(d).wait_send()
    line.sent_all(2, n2)
    line.sent(4, cz)
    plane.sent(0, piece(sendc), piece(arrc))
    hid[...] = (after[...] + line.total(3, ps, pr)).astype(jnp.bfloat16)
    line.sent(3, ps)

    @pl.when(c != yh)
    def _():
        for swap in swaps:
            swap.wait()

    for store in stores + late:
        store.wait()


def dense_forward_call(x, gain, bias, docs, route, cot, w_qkv, w_out, w_up, w_down, exp_in, exp_out):
    bf, f32 = jnp.bfloat16, jnp.float32
    vmem, anywhere = pl.BlockSpec(memory_space=pltpu.VMEM), pl.BlockSpec(memory_space=pl.ANY)
    smem = pl.BlockSpec(memory_space=pltpu.SMEM)
    shape, V, dma = jax.ShapeDtypeStruct, pltpu.VMEM, pltpu.SemaphoreType.DMA
    line = [V((512, 1024), bf)]
    weight = [(2, 4, 2, 2, 32, 768)] + [(2, 4, 2, 2, 32, 1024)] * 3
    saved = [
        shape((512, 1024), bf), shape((512, 1024), bf), shape((512, 1024), bf), shape((512, 1024), bf),
        shape((512, 1024), f32), shape((512, 256), bf), shape((512, 512), bf), shape((512, 512), bf),
    ] + [shape(w, bf) for w in weight] + [
        shape((512, 1024), bf), shape((1024, 512), bf), shape((512, 1024), bf),
    ]
    return pl.pallas_call(
        dense_forward_kernel,
        out_shape=[shape((128, 1024), bf), shape((128, 1024), bf), shape((128, 1024), f32), shape((8, 1024), f32)]
        + saved,
        in_specs=[vmem] * 3 + [smem] + [vmem] * 6 + [anywhere, anywhere],
        out_specs=[vmem] * 4 + [anywhere] * len(saved),
        scratch_shapes=[
            V((64, 768), bf), V((64, 1024), bf), *[V(w, bf) for w in weight], V((8, 128), f32), V((8, 1024), f32),
            V((8, 1024), f32),
            *(line * 4), V((512, 256), bf), V((512, 512), bf), V((512, 512), bf), V((512, 256), bf),
            *line, V((512, 1024), f32), *(line * 2), V((256, 512), bf), V((256, 512), bf),
            V((16, 128, 128), f32), V((512, 256), f32), dma((5, 4)), dma((5, 4)), dma((5, 3)), dma((5, 3)), dma((5, 3)), dma((5, 3)), dma((4,)), dma((4,)),
            dma((5,)), dma((5,)), dma((8,)), dma((8,)), dma((1, 15)), dma((1, 15)), dma((3,)), dma((3,)), dma((13,)),
        ],
        compiler_params=pltpu.CompilerParams(collective_id=2, has_side_effects=True, vmem_limit_bytes=60 << 20),
        name="dense_forward",
    )(x, gain, bias, docs, route, cot, w_qkv, w_out, w_up, w_down, exp_in, exp_out)


def expert_kernel(
    hid, route, exp_gain, exp_bias, centroid, cz_h, exp_in, exp_out, in0, out0,
    gh, vecg, mid, gate_out, o_ps, gin1, gout1, gin0, gout0,
    w_in, w_out, sendh, sendg, arrh, arrg, cz,
    e0, e1, g0, g1, ps0, ps1, pr0, pb0, pb1,
    act0, act1, dg0, dg1, gp0, gp1,
    arrived, base, xh0, xh1, sc, gates, dots, dots_in,
    ga_in, ga_out, sb_in, sb_out, rb_in, rb_out, vec, vec_own, vec_other, vmine, vcore, vline, vsum, vswap,
    wsem, zs, zr, cs, cr, ks, kr, osem, bs, br, ss, sr, vs, vr,
):
    at = Place()
    z, yh, c, same = at.z, at.yh, at.c, at.same
    line, plane = Ring(at, "z", zs, zr), Plane(at, cs, cr)
    bar = pltpu.get_barrier_semaphore()
    plane.greet(bar)
    for d in (1, 2, 3):
        greet(bar, line.device(line.index(d)))
    greet(bar, at.other)
    greet(bar, at.swap_mate)
    low, high = slice(0, 512), slice(512, 1024)

    def slot(k, i, half):
        return w_in.at[k, :, half] if i == 0 else w_out.at[k, half, :]

    def load(k, i):
        return pltpu.make_async_copy((exp_in, exp_out)[i].at[k], slot(k, i, low), wsem.at[k, i])

    def swapped(k, i):
        return pltpu.make_async_copy((in0, out0)[i], slot(k, i, low), wsem.at[k, i])

    swap_out = remote(exp_out.at[1], slot(1, 1, low), ss.at[0], sr.at[0], at.swap_mate)
    swap_in = remote(exp_in.at[1], slot(1, 0, low), ss.at[3], sr.at[3], at.swap_mate)

    def share(k, i):
        return remote(slot(k, i, low), slot(k, i, high), bs.at[k, i], br.at[k, i], at.other)

    def on_either(when_same, when_swapped):
        pl.when(same)(when_same)
        pl.when(jnp.logical_not(same))(when_swapped)

    load_c = pltpu.make_async_copy(cz_h, cz, wsem.at[2, 0])

    def begin_same():
        for k, i in ((0, 0), (0, 1), (1, 0), (1, 1)):
            load(k, i).start()

    def begin_swapped():
        for k, i in ((0, 0), (0, 1)):
            swapped(k, i).start()

    on_either(begin_same, begin_swapped)
    load_c.start()
    left, right = placings(route[0:1, :])
    sendh[...] = to_pieces(left, right, hid[...])
    vec_own[0:2, :] = exp_gain[...].astype(jnp.float32)
    vec_own[2:4, :] = exp_bias[...].astype(jnp.float32)
    vec_own[4:5, :] = centroid[...].astype(jnp.float32)
    vec_own[5:8, :] = jnp.zeros((3, 1024), jnp.float32)
    pl.semaphore_wait(bar, 20)
    plane.start(0, piece(sendh), piece(arrh))
    keep_piece(at, sendh, arrh)
    trade = remote(vec_own, vec_other, vs.at[2], vr.at[2], at.other)
    trade.start()

    def wait_loads(k, i):
        on_either(lambda: load(k, i).wait(), lambda: swapped(k, i).wait())
        share(k, i).start()

    wait_loads(0, 0)
    wait_loads(0, 1)
    trade.wait()
    vec[...] = jnp.where(same, vec_own[...], vec_other[...])
    plane.wait(0, piece(arrh))
    gain = [vec[0:1, :], vec[1:2, :]]
    bias = [vec[2:3, :], vec[3:4, :]]
    rows = rows_of(arrh[...])
    arrived[...] = rows
    xhat, scale = norm_parts(rows)
    xh0[...] = xhat
    sc[0] = jnp.broadcast_to(scale, (128, 128))
    e0[block(z), :] = (xhat * gain[0] + bias[0]).astype(jnp.bfloat16)
    line.begin(0, e0)

    @pl.when(jnp.logical_not(same))
    def _():
        swap_in.start()
        swap_out.start()

    gating = jax.nn.sigmoid(split_sum(rows * vec[4:5, :]))
    gates[z] = jnp.broadcast_to(gating, (128, 128))

    def gate_copy(d):
        return line.copy(3, d, gates.at[z], gates.at[z])

    for d in (1, 3, 2):
        gate_copy(d).start()
    share(0, 0).wait_recv()
    share(0, 1).wait_recv()
    load_c.wait()

    def forward(k, j, rows_in, act, dg):
        values = rows_in[block(j), :]
        for n in range(4):
            tile = slice(n * 256, (n + 1) * 256)
            pre = nn(values, w_in[k, :, tile])
            acted, slope = gelu_parts(pre)
            act[block(j), tile] = acted.astype(jnp.bfloat16)
            dg[block(j), tile] = slope

    def project(k, j, act, part):
        values = act[block(j), :]
        for n in range(4):
            tile = slice(n * 256, (n + 1) * 256)
            part[block(j), tile] = nn(values, w_out[k, :, tile]).astype(jnp.bfloat16)

    def backward(k, j, grad, dg, gp, part):
        values = grad[block(j), :]
        for n in range(4):
            tile = slice(n * 256, (n + 1) * 256)
            slope = dg[block(j), tile] * nt(values, w_out[k, tile, :])
            gp[block(j), tile] = slope.astype(jnp.bfloat16)
        pres = gp[block(j), :]
        for n in range(4):
            tile = slice(n * 256, (n + 1) * 256)
            part[block(j), tile] = nt(pres, w_in[k, tile, :]).astype(jnp.bfloat16)

    def sub0(i, carry):
        d = order(i)
        j = line.index(d)

        line.ready(0, i, e0)
        forward(0, j, e0, act0, dg0)
        project(0, j, act0, ps0)

        @pl.when(i > 0)
        def _():
            line.give(1, d, ps0, pr0)

        return carry

    lax.fori_loop(0, 4, sub0, 0)
    on_either(lambda: load(1, 0).wait(), lambda: swap_in.wait())
    share(1, 0).start()
    on_either(lambda: load(1, 1).wait(), lambda: swap_out.wait())
    share(1, 1).start()
    stream = arrived[...] + line.total(1, ps0, pr0)
    base[...] = stream
    xhat, scale = norm_parts(stream)
    xh1[...] = xhat
    sc[1] = jnp.broadcast_to(scale, (128, 128))
    e1[block(z), :] = (xhat * gain[1] + bias[1]).astype(jnp.bfloat16)
    line.begin(2, e1)
    gate = gates[z][:, 0:1]
    mid[...] = arrived[...] + gate * (base[...] - arrived[...])
    gate_out[...] = gates[z]
    line.sent(1, ps0)
    share(1, 0).wait_recv()
    share(1, 1).wait_recv()

    def sub1(i, carry):
        d = order(i)
        j = line.index(d)

        @pl.when(i > 0)
        def _():
            line.got(3, d, gates.at[j])

        g1[block(j), :] = (gates[j][:, 0:1] * cz[block(j), :].astype(jnp.float32)).astype(jnp.bfloat16)

        line.ready(2, i, e1)
        forward(1, j, e1, act1, dg1)
        backward(1, j, g1, dg1, gp1, ps0)

        @pl.when(i > 0)
        def _():
            line.give(4, d, ps0, pb1)

        return carry

    lax.fori_loop(0, 4, sub1, 0)

    def second_part(i, carry):
        d = order(3 - i)
        j = line.index(d)
        project(1, j, act1, ps1)
        products = cz[block(j), :].astype(jnp.float32) * ps1[block(j), :].astype(jnp.float32)
        dots[j] = jnp.broadcast_to(split_sum(products), (128, 128))

        @pl.when(i < 3)
        def _():
            line.copy(5, d, dots.at[j], dots_in.at[z]).start()

        return carry

    lax.fori_loop(0, 4, second_part, 0)
    keep_ps = pltpu.make_async_copy(ps1, o_ps, wsem.at[2, 1])
    keep_ps.start()

    def weight_grads(k, rows_in, gp, act, grad):
        def one(n, carry):
            tile = pl.ds(pl.multiple_of(n * 256, 256), 256)
            tile_b = pl.ds(pl.multiple_of(n * 256 + 512, 256), 256)
            ga_out[k, tile, :] = tn(act[:, tile], grad[...])
            sb_out[k, tile, :] = tn(act[:, tile_b], grad[...]).astype(jnp.bfloat16)
            return carry

        lax.fori_loop(0, 2, one, 0)

        def two(n, carry):
            tile = pl.ds(pl.multiple_of(n * 256, 256), 256)
            ga_in[k, tile, :] = tn(rows_in[:, tile], gp[:, 0:512])
            sb_in[k, tile, :] = tn(rows_in[:, tile], gp[:, 512:1024]).astype(jnp.bfloat16)
            return carry

        lax.fori_loop(0, 4, two, 0)

    def swap(k, i):
        src, dst = ((sb_in, rb_in), (sb_out, rb_out))[i]
        return remote(src.at[k], dst.at[k], ks.at[k, i], kr.at[k, i], at.other)

    def join_cores(k):
        for i in range(2):
            swap(k, i).wait()
        sb_in[k] = (ga_in[k] + rb_in[k].astype(jnp.float32)).astype(jnp.bfloat16)
        sb_out[k] = (ga_out[k] + rb_out[k].astype(jnp.float32)).astype(jnp.bfloat16)

    weight_grads(1, e1, gp1, act1, g1)
    swap(1, 0).start()
    swap(1, 1).start()
    grad_normed = line.total(4, ps0, pb1)
    cot = cz[block(z), :].astype(jnp.float32)
    grad_stream = gates[z][:, 0:1] * cot
    grad_stream += norm_back(grad_normed, gain[1], xh1[...], sc[1][:, 0:1])
    g0[block(z), :] = grad_stream.astype(jnp.bfloat16)
    line.begin(6, g0)
    vmine[1:2, :] = jnp.sum(grad_normed * xh1[...], axis=0, keepdims=True)
    vmine[3:4, :] = jnp.sum(grad_normed, axis=0, keepdims=True)
    line.sent(4, ps0)
    grad_gating = split_sum(cot * (base[...] - arrived[...])) + dots[z][:, 0:1]
    for d in (1, 3, 2):
        line.got(5, d, dots_in.at[line.index(d)])
        grad_gating += dots_in[line.index(d)][:, 0:1]
    gate = gates[z][:, 0:1]
    grad_logit = gate * (1.0 - gate) * grad_gating
    vmine[4:5, :] = jnp.sum(grad_logit * arrived[...], axis=0, keepdims=True)
    base[...] = grad_stream + (1.0 - gate) * cot + grad_logit * vec[4:5, :]
    join_cores(1)
    kept = [
        pltpu.make_async_copy(sb_in.at[1], gin1, osem.at[1, 0]),
        pltpu.make_async_copy(sb_out.at[1], gout1, osem.at[1, 1]),
    ]
    given = [
        remote(sb_in.at[1], gin1, ss.at[1], sr.at[1], at.swap_mate),
        remote(sb_out.at[1], gout1, ss.at[2], sr.at[2], at.swap_mate),
    ]

    def begin(copies):
        for copy in copies:
            copy.start()

    def finish(copies):
        for copy in copies:
            copy.wait()

    on_either(lambda: begin(kept), lambda: begin(given))

    def sub0_back(i, carry):
        d = order(i)
        j = line.index(d)

        line.ready(6, i, g0)
        backward(0, j, g0, dg0, gp0, ps0)

        @pl.when(i > 0)
        def _():
            line.give(7, d, ps0, pb0)

        return carry

    lax.fori_loop(0, 4, sub0_back, 0)
    weight_grads(0, e0, gp0, act0, g0)
    swap(0, 0).start()
    swap(0, 1).start()
    grad_normed = line.total(7, ps0, pb0)
    grad_stream = base[...] + norm_back(grad_normed, gain[0], xh0[...], sc[0][:, 0:1])
    sendg[...] = pieces_of(grad_stream)
    plane.start(1, piece(sendg), piece(arrg))
    keep_piece(at, sendg, arrg)
    vmine[0:1, :] = jnp.sum(grad_normed * xh0[...], axis=0, keepdims=True)
    vmine[2:3, :] = jnp.sum(grad_normed, axis=0, keepdims=True)
    vmine[5:8, :] = jnp.zeros((3, 1024), jnp.float32)
    give_core = remote(vmine, vcore, vs.at[0], vr.at[0], at.other)
    give_core.start()
    give_core.wait_recv()
    vline[z] = vmine[...] + vcore[...]

    def give_line(d):
        return line.copy(8, d, vline.at[z], vline.at[z])

    for d in (1, 3, 2):
        give_line(d).start()
    join_cores(0)
    stores = [
        pltpu.make_async_copy(sb_in.at[0], gin0, osem.at[0, 0]),
        pltpu.make_async_copy(sb_out.at[0], gout0, osem.at[0, 1]),
    ]
    begin(stores)
    plane.wait(1, piece(arrg))
    left, right = placings(route[0:1, :])
    gh[...] = from_pieces(left, right, arrg[...])
    for d in (1, 3, 2):
        line.got(8, d, vline.at[line.index(d)])
    vsum[...] = vline[0] + vline[1] + vline[2] + vline[3]
    give_mate = remote(vsum, vswap, vs.at[1], vr.at[1], at.swap_mate)
    pl.when(jnp.logical_not(same))(lambda: give_mate.start())
    give_core.wait_send()
    for d in (1, 3, 2):
        give_line(d).wait_send()
        gate_copy(d).wait_send()
        line.copy(5, d, dots.at[line.index(d)], dots_in.at[z]).wait_send()
    for k in (0, 1):
        for i in range(2):
            share(k, i).wait_send()
    line.sent_all(0, e0)
    line.sent_all(2, e1)
    line.sent_all(6, g0)
    line.sent(7, ps0)
    plane.sent(0, piece(sendh), piece(arrh))
    plane.sent(1, piece(sendg), piece(arrg))
    keep_ps.wait()
    finish(stores)
    on_either(lambda: finish(kept), lambda: finish(given))

    @pl.when(same)
    def _():
        vecg[...] = vsum[...]

    @pl.when(jnp.logical_not(same))
    def _():
        give_mate.wait()
        vecg[...] = vswap[...]


def expert_call(hid, route, exp_gain, exp_bias, centroid, cz, exp_in, exp_out, in0, out0):
    bf, f32 = jnp.bfloat16, jnp.float32
    vmem, anywhere = pl.BlockSpec(memory_space=pltpu.VMEM), pl.BlockSpec(memory_space=pl.ANY)
    shape, V, dma = jax.ShapeDtypeStruct, pltpu.VMEM, pltpu.SemaphoreType.DMA
    line, rows, pieces = [V((512, 1024), bf)], [V((128, 1024), f32)], [V((256, 512), bf)]
    wide, small = [V((512, 1024), f32)], [V((4, 128, 128), f32)]
    vectors = [V((8, 1024), f32)]
    return pl.pallas_call(
        expert_kernel,
        out_shape=(
            shape((128, 1024), bf), shape((8, 1024), f32), shape((128, 1024), f32), shape((128, 128), f32),
            shape((512, 1024), bf), shape((1024, 512), bf), shape((512, 1024), bf), shape((1024, 512), bf),
            shape((512, 1024), bf),
        ),
        in_specs=[vmem] * 5 + [anywhere] * 5,
        out_specs=tuple([vmem] * 4 + [anywhere] * 5),
        scratch_shapes=[
            V((2, 1024, 1024), bf), V((2, 1024, 1024), bf), *(pieces * 4), *line,
            *(line * 9), *(line * 2), *(wide * 2), *(line * 2),
            *(rows * 4), *(small * 4),
            V((2, 1024, 512), f32), V((2, 512, 1024), f32),
            V((2, 1024, 512), bf), V((2, 512, 1024), bf), V((2, 1024, 512), bf), V((2, 512, 1024), bf),
            *(vectors * 5), V((4, 8, 1024), f32), *(vectors * 2),
            dma((3, 2)), dma((9, 4)), dma((9, 4)), dma((2, 15)), dma((2, 15)), dma((2, 2)), dma((2, 2)), dma((2, 2)),
            dma((2, 2)), dma((2, 2)), dma((4,)), dma((4,)), dma((3,)), dma((3,)),
        ],
        compiler_params=pltpu.CompilerParams(collective_id=1, has_side_effects=True, vmem_limit_bytes=60 << 20),
        name="experts",
    )(hid, route, exp_gain, exp_bias, centroid, cz, exp_in, exp_out, in0, out0)


class Everyone:
    def __init__(self, at, send, recv):
        self.at, self.send, self.recv = at, send, recv

    def copy(self, phase, i, buf):
        own = buf.at[self.at.s]
        to = (lax.rem(self.at.s + i + 1, 8), self.at.f)
        return remote(own, own, self.send.at[phase, i], self.recv.at[phase, i], to)

    def start(self, phase, buf):
        for i in range(7):
            self.copy(phase, i, buf).start()

    def wait(self, phase, buf):
        for i in range(7):
            q = lax.rem(self.at.s + 7 - i, 8)
            dst = buf.at[q]
            remote(dst, dst, self.send.at[phase, i], self.recv.at[phase, i], (q, self.at.f)).wait_recv()

    def sent(self, phase, buf):
        for i in range(7):
            self.copy(phase, i, buf).wait_send()


def dense_backward_kernel(
    gh, after, docs, gains, mixed, route, mid, gate, x_h, n1_h, n2_h, act_h, dg_h, q_h, kv_h, kvo_h, wq_h, wo_h, wu_h,
    wd_h, ps_h, gin0, gout0,
    gx, bd, bu, bo, bq, gvec, res, fin0, fout0,
    ghs, xa, xh, n1, n2, act, dg, gp, qb, kvb, kvo, wq, wo, wu, wd,
    ps, pr, ps2, pr2, ps3, pr3, prob, gms, gm, dp, dkv, dkvo, kvs, kvr,
    md, mu, mo, mq, mkv, td, tu, to, tq, tkv, rd, ru, ro, rq, rkv, xd, xu, xo, sd, su, so, yd, yu, yo, rp, rpkv, sendr, arrr,
    vmine, vcore, vplane, vline, outz,
    lsem, zs, zr, xs, xr, ys, yr, kvss, kvsr, ks, kr, cs, cr, qs, qr, ss, sr, vs, vr,
):
    at = Place()
    z, yh, c, col = at.z, at.yh, at.c, at.col
    line, ring_x, ring_y = Ring(at, "z", zs, zr), Ring(at, "x", xs, xr), Ring(at, "y", ys, yr)
    plane, everyone = Plane(at, cs, cr), Everyone(at, qs, qr)
    bar = pltpu.get_barrier_semaphore()
    plane.greet(bar)
    for d in (1, 2, 3):
        greet(bar, line.device(line.index(d)))
        greet(bar, (2 * line.index(d) + 1 - yh, at.f))
    greet(bar, at.other)
    greet(bar, at.swap_mate)
    loads = [
        pltpu.make_async_copy(src, dst, lsem.at[k])
        for k, (src, dst) in enumerate(
            [
                (q_h, qb), (kv_h, kvb), (kvo_h, kvo), (wd_h, wd), (dg_h, dg), (wu_h, wu), (act_h, act), (n2_h, n2),
                (wo_h, wo), (ps_h, ps3), (wq_h, wq), (n1_h, n1), (x_h, xa),
            ]
        )
    ]
    for load in loads:
        load.start()
    ghs[block(z), :] = gh[...]
    pl.semaphore_wait(bar, 23)
    line.begin(0, ghs)
    swaps = [
        remote(gin0, fin0, ss.at[0], sr.at[0], at.swap_mate),
        remote(gout0, fout0, ss.at[1], sr.at[1], at.swap_mate),
    ]
    @pl.when(jnp.logical_not(at.same))
    def _():
        for swap in swaps:
            swap.start()

    for load in loads[:3]:
        load.wait()
    for j in range(4):
        seen = [mask(j, yh, parity, docs) for parity in (yh, 1 - yh)]
        wide = slice(0, 128 * (j + 1))
        for p in range(2):
            lanes = slice(128 * p, 128 * p + 128)
            keys = [kvb[wide, lanes], kvo[wide, lanes]]
            q = qb[128 * j : 128 * j + 128, lanes]
            for h in range(2):
                found = probabilities(only(head_lanes(h), q), keys, seen)
                for k in range(2):
                    prob[k, 4 * j + 2 * p + h, :, wide] = found[k].astype(jnp.bfloat16)
    for load in loads[3:6]:
        load.wait()

    def feed(i, carry):
        d = order(i)
        j = line.index(d)

        line.ready(0, i, ghs)
        values = ghs[block(j), :]
        for n in range(4):
            tile = slice(n * 256, (n + 1) * 256)
            gp[block(j), tile] = (dg[block(j), tile] * nt(values, tall_tile(wd, n))).astype(jnp.bfloat16)
        pres = gp[block(j), :]
        for n in range(4):
            tile = slice(n * 256, (n + 1) * 256)
            ps[block(j), tile] = nt(pres, tall_tile(wu, n)).astype(jnp.bfloat16)

        @pl.when(i > 0)
        def _():
            line.give(1, d, ps, pr)

        return carry

    lax.fori_loop(0, 4, feed, 0)
    for load in loads[6:10]:
        load.wait()

    def weight_grad(lhs, rhs, mine, theirs):
        def one(n, carry):
            rows = lhs[:, pl.ds(pl.multiple_of(n * 256, 256), 256)]
            grad = tn(rows, rhs[...])
            for half in range(2):
                first = grad[128 * half : 128 * half + 64].astype(jnp.bfloat16)
                second = grad[128 * half + 64 : 128 * half + 128].astype(jnp.bfloat16)
                here = lax.div(n, 2), 2 * lax.rem(n, 2) + half
                mine[here] = jnp.where(c == 0, first, second)
                theirs[here] = jnp.where(c == 0, second, first)
            return carry

        lax.fori_loop(0, 4, one, 0)

    def core_copy(phase, src, dst):
        return remote(src, dst, ks.at[phase], kr.at[phase], at.other)

    def join_cores(phase, mine, theirs, got):
        core_copy(phase, theirs, got).wait()

        def one(n, carry):
            here = lax.div(n, 4), lax.rem(n, 4)
            mine[here] = (mine[here].astype(jnp.float32) + got[here].astype(jnp.float32)).astype(jnp.bfloat16)
            return carry

        lax.fori_loop(0, 8, one, 0)

    def x_copy(phase, d, mine, dst):
        return ring_x.copy(phase, d, mine.at[:, ring_x.index(d)], dst.at[at.x])

    def y_copy(phase, d, part, dst):
        j = ring_y.index(d)
        src = part.at[lax.rem(j, 2), pl.ds(pl.multiple_of(32 * lax.div(j, 2), 32), 32)]
        return ring_y.copy(phase, d, src, dst.at[ring_y.pos])

    def to_x(phase, mine, dst):
        for d in (1, 3, 2):
            x_copy(phase, d, mine, dst).start()

    def to_y(phase, mine, got, part, dst):
        acc = mine[:, at.x].astype(jnp.float32)
        for d in (1, 3, 2):
            j = ring_x.index(d)
            ring_x.got(phase, d, got.at[j])
            acc += got[j].astype(jnp.float32)
        part[...] = acc.astype(jnp.bfloat16)
        for d in (1, 3, 2):
            y_copy(phase, d, part, dst).start()

    def y_total(phase, part, got):
        acc = part[at.yl, pl.ds(pl.multiple_of(32 * yh, 32), 32), :].astype(jnp.float32)
        for d in (1, 3, 2):
            j = ring_y.index(d)
            ring_y.got(phase, d, got.at[j])
            acc += got[j].astype(jnp.float32)
        return acc

    weight_grad(act, ghs, md, td)
    core_copy(0, td, rd).start()
    weight_grad(n2, gp, mu, tu)
    core_copy(1, tu, ru).start()
    join_cores(0, md, td, rd)
    to_x(0, md, xd)
    join_cores(1, mu, tu, ru)
    to_x(1, mu, xu)
    grad_normed = line.total(1, ps, pr)
    xhat, scale = norm_parts(after[...])
    vmine[1:2, :] = jnp.sum(grad_normed * xhat, axis=0, keepdims=True)
    vmine[3:4, :] = jnp.sum(grad_normed, axis=0, keepdims=True)
    grad_after = gh[...].astype(jnp.float32) + norm_back(grad_normed, gains[1:2, :], xhat, scale)
    gx[...] = grad_after
    grad_attn = grad_after.astype(jnp.bfloat16)
    for n in range(4):
        gms[:, 256 * n : 256 * n + 256] = nt(grad_attn, tall_tile(wo, n)).astype(jnp.bfloat16)

    def gm_copy(d):
        lanes = pl.ds(pl.multiple_of(256 * line.index(d), 256), 256)
        return line.copy(2, d, gms.at[:, lanes], gm.at[block(z)])

    for d in (1, 3, 2):
        gm_copy(d).start()
    gm[block(z), :] = gms[:, pl.ds(pl.multiple_of(256 * z, 256), 256)]
    for d in (1, 3, 2):
        line.give(6, d, ps3, pr3)
    gp[block(0), :] = grad_attn
    weight_grad(mixed, gp.at[block(0)], mo, to)
    core_copy(2, to, ro).start()
    for load in loads[10:]:
        load.wait()
    for j in range(4):
        xh[block(j), :] = norm_parts(xa[block(j), :].astype(jnp.float32))[0]
    join_cores(2, mo, to, ro)
    to_x(2, mo, xo)
    for d in (1, 3, 2):
        line.arrived(2, d, gm)
    dkv[...] = jnp.zeros_like(dkv)
    dkvo[...] = jnp.zeros_like(dkvo)

    def kv_copy(j):
        return remote(kvs.at[block(j)], kvr.at[block(j)], kvss.at[j], kvsr.at[j], at.mate)

    def attend_back(j):
        wide = slice(0, 128 * (j + 1))
        rows = slice(128 * j, 128 * j + 128)
        for p in range(2):
            lanes = slice(128 * p, 128 * p + 128)
            value_lanes = slice(256 + 128 * p, 384 + 128 * p)
            q, grad = qb[rows, lanes], gm[rows, lanes]
            keys = [kvb[wide, lanes], kvo[wide, lanes]]
            values = [kvb[wide, value_lanes], kvo[wide, value_lanes]]
            outs = []
            for h in range(2):
                q_h, grad_h = only(head_lanes(h), q), only(head_lanes(h), grad)
                probs = [prob[k, 4 * j + 2 * p + h, :, wide].astype(jnp.float32) for k in range(2)]
                back = [nt(grad_h, v) for v in values]
                dot = split_sum(probs[0] * back[0]) + split_sum(probs[1] * back[1])
                slopes = [(share * (b - dot)).astype(jnp.bfloat16) for share, b in zip(probs, back)]
                outs.append(nn(slopes[0], keys[0]) + nn(slopes[1], keys[1]))
                for k, acc in enumerate((dkv, dkvo)):
                    acc[wide, lanes] += tn(slopes[k], q_h) * 0.125
                    acc[wide, value_lanes] += tn(prob[k, 4 * j + 2 * p + h, :, wide], grad_h)
            dp[rows, lanes] = (jnp.where(head_lanes(0), outs[0], outs[1]) * 0.125).astype(jnp.bfloat16)
        kvs[rows, :] = dkvo[rows, :].astype(jnp.bfloat16)
        kv_copy(j).start()

    for j in (3, 2, 1, 0):
        attend_back(j)
    to_y(0, md, xd, sd, yd)
    weight_grad(n1, dp.at[:, 0:256], mq, tq)
    core_copy(3, tq, rq).start()
    vmine[0:1, :] = jnp.zeros((1, 1024), jnp.float32)
    vmine[2:3, :] = jnp.zeros((1, 1024), jnp.float32)
    vmine[4:8, :] = jnp.zeros((4, 1024), jnp.float32)
    for j in (3, 2, 1, 0):
        rows = slice(128 * j, 128 * j + 128)
        kv_copy(j).wait_recv()
        dp[rows, 256:768] = (dkv[rows, :] + kvr[rows, :].astype(jnp.float32)).astype(jnp.bfloat16)
    weight_grad(n1, dp.at[:, 256:768], mkv, tkv)
    core_copy(4, tkv, rkv).start()

    def piece_of(mine):
        def at_piece(q):
            return mine.at[lax.div(q, 8), lax.rem(lax.div(q, 2), 4), pl.ds(pl.multiple_of(32 * lax.rem(q, 2), 32), 32)]

        return at_piece

    def slot_of(got):
        return lambda q: got.at[q]

    def to_plane(phase, mine, got):
        plane.start(phase, piece_of(mine), slot_of(got))
        got[at.m] = mine[at.yl, at.x, pl.ds(pl.multiple_of(32 * yh, 32), 32), :]

    def plane_total(phase, got):
        plane.wait(phase, slot_of(got))
        acc = got[0].astype(jnp.float32)
        for q in range(1, 16):
            acc += got[q].astype(jnp.float32)
        return acc.astype(jnp.bfloat16)

    join_cores(3, mq, tq, rq)
    to_plane(0, mq, rp)
    bd[at.s] = y_total(0, sd, yd).astype(jnp.bfloat16)
    everyone.start(0, bd)
    join_cores(4, mkv, tkv, rkv)
    to_plane(3, mkv, rpkv)

    def last(i, carry):
        d = order(3 - i)
        j = line.index(d)
        values = dp[block(j), :]
        for n in range(4):
            tile = slice(n * 256, (n + 1) * 256)
            part = nt(values, tall_tile(wq, n))
            ps2[block(j), tile] = part.astype(jnp.bfloat16)
            vmine[0:1, tile] += jnp.sum(part * xh[block(j), tile], axis=0, keepdims=True)
            vmine[2:3, tile] += jnp.sum(part, axis=0, keepdims=True)

        @pl.when(i < 3)
        def _():
            line.give(3, d, ps2, pr2)

        return carry

    lax.fori_loop(0, 4, last, 0)
    give_core = remote(vmine, vcore, vs.at[0], vr.at[0], at.other)
    give_core.start()
    to_y(1, mu, xu, su, yu)

    def tile_of(q):
        return vmine.at[:, pl.ds(pl.multiple_of(128 * lax.div(q, 2), 128), 128)]

    give_core.wait()
    vmine[...] += vcore[...]
    plane.start(1, tile_of, slot_of(vplane))
    vplane[at.m] = vmine[:, pl.ds(pl.multiple_of(128 * col, 128), 128)]
    to_y(2, mo, xo, so, yo)
    bu[at.s] = y_total(1, su, yu).astype(jnp.bfloat16)
    everyone.start(1, bu)
    sendr[...] = pieces_of(mid[...] + gate[:, 0:1] * line.total(6, ps3, pr3))
    plane.start(2, piece(sendr), piece(arrr))
    keep_piece(at, sendr, arrr)
    total_out = y_total(2, so, yo)
    for n in range(4):
        outz[4 + n] = total_out[:, 256 * n : 256 * n + 256].astype(jnp.bfloat16)

    def out_copy(d):
        return line.copy(4, d, outz.at[4 + line.index(d)], outz.at[z])

    for d in (1, 3, 2):
        out_copy(d).start()
    grad_normed = line.total(3, ps2, pr2)
    scale = norm_parts(xa[block(z), :].astype(jnp.float32))[1]
    gx[...] += norm_back(grad_normed, gains[0:1, :], xh[block(z), :], scale)
    bq[at.s, :, 0:256] = plane_total(0, rp)
    bq[at.s, :, 256:768] = plane_total(3, rpkv)
    everyone.start(3, bq)
    acc = outz[4 + z].astype(jnp.float32)
    for d in (1, 3, 2):
        line.got(4, d, outz.at[line.index(d)])
        acc += outz[line.index(d)].astype(jnp.float32)
    bo[at.s] = acc.astype(jnp.bfloat16)
    everyone.start(2, bo)
    plane.wait(1, slot_of(vplane))
    vline[z] = jnp.sum(vplane[...], axis=0)

    def vec_copy(d):
        return line.copy(5, d, vline.at[z], vline.at[z])

    for d in (1, 3, 2):
        vec_copy(d).start()
    plane.wait(2, piece(arrr))
    left, right = placings(route[0:1, :])
    res[...] = from_pieces(left, right, arrr[...])
    everyone.wait(0, bd)
    everyone.wait(1, bu)
    everyone.wait(2, bo)
    for d in (1, 3, 2):
        line.got(5, d, vline.at[line.index(d)])
    gvec[...] = jnp.sum(vline[...], axis=0)
    everyone.wait(3, bq)
    line.sent_all(0, ghs)
    line.sent(1, ps)
    line.sent(3, ps2)
    line.sent(6, ps3)
    for d in (1, 3, 2):
        gm_copy(d).wait_send()
        out_copy(d).wait_send()
        vec_copy(d).wait_send()
        for phase, (mine, x_got, part, y_got) in enumerate(((md, xd, sd, yd), (mu, xu, su, yu), (mo, xo, so, yo))):
            x_copy(phase, d, mine, x_got).wait_send()
            y_copy(phase, d, part, y_got).wait_send()
    for j in range(4):
        kv_copy(j).wait_send()
    plane.sent(0, piece_of(mq), slot_of(rp))
    plane.sent(3, piece_of(mkv), slot_of(rpkv))
    plane.sent(1, tile_of, slot_of(vplane))
    plane.sent(2, piece(sendr), piece(arrr))
    for phase, buf in enumerate((bd, bu, bo, bq)):
        everyone.sent(phase, buf)

    @pl.when(jnp.logical_not(at.same))
    def _():
        for swap in swaps:
            swap.wait()


def dense_backward_call(gh, after, docs, gains, mixed, route, mid, gate, saved, ps, gin0, gout0):
    bf, f32 = jnp.bfloat16, jnp.float32
    vmem, anywhere = pl.BlockSpec(memory_space=pltpu.VMEM), pl.BlockSpec(memory_space=pl.ANY)
    smem = pl.BlockSpec(memory_space=pltpu.SMEM)
    shape, V, dma = jax.ShapeDtypeStruct, pltpu.VMEM, pltpu.SemaphoreType.DMA
    line, pieces = [V((512, 1024), bf)], [V((256, 512), bf)]
    wide, narrow = [V((2, 4, 64, 1024), bf)], [V((2, 4, 64, 256), bf), V((2, 4, 64, 512), bf)]
    return pl.pallas_call(
        dense_backward_kernel,
        out_shape=[
            shape((128, 1024), f32), shape((8, 32, 1024), bf), shape((8, 32, 1024), bf), shape((8, 32, 256), bf),
            shape((8, 32, 768), bf), shape((8, 128), f32), shape((128, 1024), bf), shape((1024, 512), bf),
            shape((512, 1024), bf),
        ],
        in_specs=[vmem, vmem, smem] + [vmem] * 5 + [anywhere] * 15,
        out_specs=[vmem] * 7 + [anywhere] * 2,
        scratch_shapes=[
            *(line * 2), V((512, 1024), f32), *(line * 3), V((512, 1024), f32), *line,
            V((512, 256), bf), V((512, 512), bf), V((512, 512), bf),
            V((2, 4, 2, 2, 32, 768), bf), *([V((2, 4, 2, 2, 32, 1024), bf)] * 3),
            *(line * 6), V((2, 16, 128, 512), bf),
            V((128, 1024), bf), V((512, 256), bf), V((512, 768), bf), V((512, 512), f32), V((512, 512), f32),
            V((512, 512), bf), V((512, 512), bf),
            *(wide * 3), *narrow, *(wide * 3), *narrow, *(wide * 3), *narrow,
            *([V((4, 2, 64, 1024), bf)] * 3), *([V((2, 64, 1024), bf)] * 3), *([V((4, 32, 1024), bf)] * 3),
            V((16, 32, 256), bf), V((16, 32, 512), bf), *(pieces * 2),
            V((8, 1024), f32), V((8, 1024), f32), V((16, 8, 128), f32), V((4, 8, 128), f32),
            V((8, 32, 256), bf),
            dma((13,)), dma((7, 4)), dma((7, 4)), dma((3, 3)), dma((3, 3)), dma((3, 3)), dma((3, 3)), dma((4,)),
            dma((4,)), dma((5,)), dma((5,)), dma((4, 15)), dma((4, 15)), dma((4, 7)), dma((4, 7)), dma((2,)),
            dma((2,)), dma((1,)), dma((1,)),
        ],
        compiler_params=pltpu.CompilerParams(collective_id=3, has_side_effects=True, vmem_limit_bytes=62 << 20),
        name="dense_backward",
    )(gh, after, docs, gains, mixed, route, mid, gate, *saved, ps, gin0, gout0)


def finish_kernel(
    gvec, vecg, res, gx, bd, bu, bo, bq, in0, in1, out0, out1, swapped_in, swapped_out,
    ng, nb, eg, eb, cen, o_res, o_gx, o_gq, o_go, o_gu, o_gd, o_in, o_out,
    b_in, b_out, f_in, f_out, vd, vu, vo, vq, gq, go, gu, gd, vres, vgx, isem, osem,
):
    at = Place()
    swapped = [
        pltpu.make_async_copy(swapped_in, b_in.at[0], isem.at[0]),
        pltpu.make_async_copy(swapped_out, b_out.at[0], isem.at[2]),
    ]
    pairs = [
        (in0, b_in.at[0]), (in1, b_in.at[1]), (out0, b_out.at[0]), (out1, b_out.at[1]), (bd, vd), (bu, vu), (bo, vo),
        (bq, vq), (res, vres), (gx, vgx),
    ]
    loads = [pltpu.make_async_copy(src, dst, isem.at[k]) for k, (src, dst) in enumerate(pairs)]

    @pl.when(at.same)
    def _():
        loads[0].start()
        loads[2].start()

    @pl.when(jnp.logical_not(at.same))
    def _():
        for copy in swapped:
            copy.start()

    for k in (1, 3, 4, 5, 6, 7, 8, 9):
        loads[k].start()
    c = at.c
    mine = jnp.where(c == 0, gvec[0:4, 0:64], gvec[0:4, 64:128])
    ng[...] = mine[0:2]
    nb[...] = mine[2:4]
    eg[...] = vecg[0:2, :]
    eb[...] = vecg[2:4, :]
    cen[...] = vecg[4:5, :]
    stores = []

    def store(src, dst):
        stores.append(pltpu.make_async_copy(src, dst, osem.at[len(stores)]))
        stores[-1].start()

    for k in range(4):
        loads[k].wait()
        low, wide, out = ((b_in, f_in, o_in), (b_out, f_out, o_out))[k // 2]
        wide[k % 2] = low[k % 2].astype(jnp.float32)
        store(wide.at[k % 2], out.at[k % 2])
    for k in range(4, 10):
        loads[k].wait()
    store(vres, o_res)
    store(vgx, o_gx)
    lane = lax.broadcasted_iota(jnp.int32, (32, 128), 1) < 64
    for half in range(2):
        rows = slice(32 * half, 32 * half + 32)
        for z in range(4):
            gd[64 * z + 32 * half : 64 * z + 32 * half + 32, :] = vd[2 * z + half].astype(jnp.float32)
            go[rows, 256 * z : 256 * z + 256] = vo[2 * z + half].astype(jnp.float32)
            for part in range(3):
                gq[rows, 1024 * part + 256 * z : 1024 * part + 256 * z + 256] = vq[
                    2 * z + half, :, 256 * part : 256 * part + 256
                ].astype(jnp.float32)
        for n in range(8):
            tile = slice(128 * n, 128 * n + 128)
            quarter = [vu[2 * z + half, :, tile].astype(jnp.float32) for z in range(4)]
            turned = [pltpu.roll(v, 64, 1) for v in quarter]
            first = 512 * n
            gu[rows, first : first + 128] = jnp.where(lane, quarter[0], turned[1])
            gu[rows, first + 128 : first + 256] = jnp.where(lane, quarter[2], turned[3])
            gu[rows, first + 256 : first + 384] = jnp.where(lane, turned[0], quarter[1])
            gu[rows, first + 384 : first + 512] = jnp.where(lane, turned[2], quarter[3])
    for src, dst in ((gq, o_gq), (go, o_go), (gu, o_gu), (gd, o_gd)):
        store(src, dst)
    for copy in stores:
        copy.wait()


def finish_call(gvec, vecg, res, gx, bd, bu, bo, bq, in0, in1, out0, out1, swapped_in, swapped_out):
    bf, f32 = jnp.bfloat16, jnp.float32
    vmem, anywhere = pl.BlockSpec(memory_space=pltpu.VMEM), pl.BlockSpec(memory_space=pl.ANY)
    shape, V, dma = jax.ShapeDtypeStruct, pltpu.VMEM, pltpu.SemaphoreType.DMA
    return pl.pallas_call(
        finish_kernel,
        out_shape=[
            shape((2, 64), f32), shape((2, 64), f32), shape((2, 1024), f32), shape((2, 1024), f32),
            shape((1, 1024), f32), shape((128, 1024), bf), shape((128, 1024), f32), shape((64, 3072), f32),
            shape((64, 1024), f32), shape((64, 4096), f32), shape((256, 1024), f32), shape((2, 1024, 512), f32),
            shape((2, 512, 1024), f32),
        ],
        in_specs=[vmem] * 2 + [anywhere] * 12,
        out_specs=[vmem] * 5 + [anywhere] * 8,
        scratch_shapes=[
            V((2, 1024, 512), bf), V((2, 512, 1024), bf), V((2, 1024, 512), f32), V((2, 512, 1024), f32),
            V((8, 32, 1024), bf), V((8, 32, 1024), bf), V((8, 32, 256), bf), V((8, 32, 768), bf),
            V((64, 3072), f32), V((64, 1024), f32), V((64, 4096), f32), V((256, 1024), f32),
            V((128, 1024), bf), V((128, 1024), f32), dma((10,)), dma((10,)),
        ],
        compiler_params=pltpu.CompilerParams(vmem_limit_bytes=62 << 20),
        name="finish",
    )(gvec, vecg, res, gx, bd, bu, bo, bq, in0, in1, out0, out1, swapped_in, swapped_out)


def on_device(
    inputs,
    doc_starts,
    route,
    norm_gain,
    norm_bias,
    w_qkv,
    w_out,
    w_up,
    w_down,
    exp_gain,
    exp_bias,
    exp_in,
    exp_out,
    centroid,
    cotangent,
):
    tok_rows, width = 128, 1024
    x = inputs.reshape(tok_rows, width)
    cot = cotangent.reshape(tok_rows, width)
    slots = route.reshape(1, tok_rows)
    hidden, mixed, after, gains, *saved, cz, in0, out0 = dense_forward_call(
        x, norm_gain, norm_bias, doc_starts, slots, cot, w_qkv, w_out, w_up, w_down, exp_in[0], exp_out[0]
    )
    grad_hidden, vec_grads, mid, gate, part, grad_in1, grad_out1, grad_in0, grad_out0 = expert_call(
        hidden, slots, exp_gain[0], exp_bias[0], centroid, cz, exp_in[0], exp_out[0], in0, out0
    )
    grad_x, down, up, out, qkv, norm_grads, result, swapped_in, swapped_out = dense_backward_call(
        grad_hidden, after, doc_starts, gains, mixed, slots, mid, gate, saved, part, grad_in0, grad_out0
    )
    gain, bias, e_gain, e_bias, center, result, grad_x, g_qkv, g_out, g_up, g_down, e_in, e_out = finish_call(
        norm_grads,
        vec_grads,
        result,
        grad_x,
        down,
        up,
        out,
        qkv,
        grad_in0,
        grad_in1,
        grad_out0,
        grad_out1,
        swapped_in,
        swapped_out,
    )
    return (
        result[None],
        grad_x[None],
        gain,
        bias,
        g_qkv,
        g_out,
        g_up,
        g_down,
        e_gain[None],
        e_bias[None],
        e_in[None],
        e_out[None],
        center,
    )


def solution(mesh):
    in_specs = (
        P("fsdp", "seq", None),
        P("fsdp", None),
        P("fsdp", "seq", None),
        P(None, "fsdp"),
        P(None, "fsdp"),
        P("fsdp", None),
        P("fsdp", None),
        P("fsdp", None),
        P("fsdp", None),
        P("fsdp", None, None),
        P("fsdp", None, None),
        P("fsdp", None, None, "seq"),
        P("fsdp", None, "seq", None),
        P("fsdp", None),
        P("fsdp", "seq", None),
    )
    out_specs = (
        P("fsdp", "seq", None),
        P("fsdp", "seq", None),
        P(None, "fsdp"),
        P(None, "fsdp"),
        P("fsdp", None),
        P("fsdp", None),
        P("fsdp", None),
        P("fsdp", None),
        P("fsdp", None, None),
        P("fsdp", None, None),
        P("fsdp", None, None, "seq"),
        P("fsdp", None, "seq", None),
        P("fsdp", None),
    )
    return jax.shard_map(
        on_device, mesh=mesh, in_specs=in_specs, out_specs=out_specs, check_vma=False
    )
```

```python
import jax
import jax.numpy as jnp
from jax import lax
from jax.experimental import pallas as pl
from jax.experimental.pallas import tpu as pltpu
from jax.sharding import PartitionSpec as P

MESH = pl.DeviceIdType.MESH
epsilon = 1e-05
masked_score = -1e30


def split_sum(values):
    return jnp.sum(values, axis=-1, keepdims=True)


def norm_parts(values):
    average = split_sum(values) * (1.0 / values.shape[-1])
    centered = values - average
    spread = split_sum(centered * centered) * (1.0 / values.shape[-1])
    scale = lax.rsqrt(spread + epsilon)
    return centered * scale, scale


def norm_back(grad_normed, gain, xhat, scale):
    width = 1.0 / xhat.shape[-1]
    u = grad_normed * gain
    return scale * (u - split_sum(u) * width - xhat * (split_sum(u * xhat) * width))


def gelu_parts(pre):
    inner = 0.7978845608028654
    cubic = 0.044715
    square = pre * pre
    t = jnp.tanh(inner * pre * (1.0 + cubic * square))
    half = 0.5 * (1.0 + t)
    slope = half + 0.5 * pre * (1.0 - t * t) * (inner * (1.0 + 3.0 * cubic * square))
    return pre * half, slope


def nn(a, b):
    return lax.dot_general(a, b, (((1,), (0,)), ((), ())), preferred_element_type=jnp.float32)


def nt(a, b):
    return lax.dot_general(a, b, (((1,), (1,)), ((), ())), preferred_element_type=jnp.float32)


def tn(a, b):
    return lax.dot_general(a, b, (((0,), (0,)), ((), ())), preferred_element_type=jnp.float32)


def remote(src, dst, send, recv, device):
    return pltpu.make_async_remote_copy(
        src_ref=src, dst_ref=dst, send_sem=send, recv_sem=recv, device_id=device, device_id_type=MESH
    )


def greet(bar, device):
    pl.semaphore_signal(bar, inc=1, device_id=device, device_id_type=MESH)


def block(index):
    return pl.ds(pl.multiple_of(index * 128, 128), 128)


def order(i):
    return i + lax.div(i, 2) - 2 * lax.div(i, 3)


class Place:
    def __init__(self):
        self.s, self.f = lax.axis_index("seq"), lax.axis_index("fsdp")
        self.z, self.yh = lax.div(self.s, 2), lax.rem(self.s, 2)
        self.yl, self.col, self.c = lax.div(self.f, 8), lax.div(self.f, 2), lax.rem(self.f, 2)
        self.x = lax.rem(self.col, 4)
        self.m = self.f - self.c + self.yh
        self.other = (self.s, self.f + 1 - 2 * self.c)
        self.mate = (2 * self.z + 1 - self.yh, self.f)
        self.swap_mate = (2 * self.z + 1 - self.yh, self.f + 1 - 2 * self.c)
        self.same = self.c == self.yh


class Ring:
    def __init__(self, at, axis, send, recv):
        self.at, self.axis, self.send, self.recv = at, axis, send, recv
        self.pos = {"z": at.z, "x": at.x, "y": 2 * at.yh + at.yl}[axis]

    def index(self, d):
        return lax.rem(self.pos + d, 4)

    def device(self, j):
        at = self.at
        if self.axis == "z":
            return (2 * j + at.yh, at.f)
        if self.axis == "x":
            return (at.s, at.f - 2 * at.x + 2 * j)
        return (2 * at.z + lax.div(j, 2), 8 * lax.rem(j, 2) + at.f - 8 * at.yl)

    def copy(self, phase, d, src, dst):
        sems = self.send.at[phase, d - 1], self.recv.at[phase, d - 1]
        return remote(src, dst, *sems, self.device(self.index(d)))

    def got(self, phase, d, dst):
        sems = self.send.at[phase, 3 - d], self.recv.at[phase, 3 - d]
        remote(dst, dst, *sems, self.device(self.index(d))).wait_recv()

    def spread(self, phase, buf):
        own = buf.at[block(self.pos)]
        for d in (1, 3, 2):
            self.copy(phase, d, own, own).start()

    def half(self, buf, d, upper):
        return buf.at[pl.ds(pl.multiple_of(128 * self.index(d) + 64 * upper, 64), 64)]

    def moving(self, phase, slot, rows, up):
        to = self.device(self.index(1 if up else 3))
        return remote(rows, rows, self.send.at[phase, slot], self.recv.at[phase, slot], to)

    def parts(self, phase, buf):
        for slot, up, upper in ((2, 0, 0), (0, 1, 1), (3, 0, 1), (1, 1, 0)):
            yield self.moving(phase, slot, self.half(buf, 0, upper), up)

    def onward(self, phase, buf, up):
        return self.moving(phase, 4 + up, self.half(buf, 3 if up else 1, up), up)

    def begin(self, phase, buf):
        for part in self.parts(phase, buf):
            part.start()

    def relay(self, phase, buf):
        for up in (0, 1):
            self.moving(phase, 0 if up else 2, self.half(buf, 3 if up else 1, up), up).wait_recv()
            self.onward(phase, buf, up).start()

    def above(self, phase, buf):
        self.moving(phase, 3, self.half(buf, 1, 1), 0).wait_recv()

    def below(self, phase, buf):
        self.moving(phase, 1, self.half(buf, 3, 0), 1).wait_recv()

    def far(self, phase, buf):
        for up in (0, 1):
            self.moving(phase, 4 + up, self.half(buf, 2, up), up).wait_recv()

    def ready(self, phase, i, buf):
        @pl.when(i == 1)
        def _():
            self.relay(phase, buf)
            self.above(phase, buf)

        pl.when(i == 2)(lambda: self.below(phase, buf))
        pl.when(i == 3)(lambda: self.far(phase, buf))

    def sent_all(self, phase, buf):
        for part in self.parts(phase, buf):
            part.wait_send()
        for up in (0, 1):
            self.onward(phase, buf, up).wait_send()

    def arrived(self, phase, d, buf):
        self.got(phase, d, buf.at[block(self.index(d))])

    def give(self, phase, d, src, dst):
        self.copy(phase, d, src.at[block(self.index(d))], dst.at[block(self.pos)]).start()

    def sent(self, phase, buf):
        own = buf.at[block(self.pos)]
        for d in (1, 3, 2):
            self.copy(phase, d, own, own).wait_send()

    def total(self, phase, own, parts):
        acc = own[block(self.pos), :].astype(jnp.float32)
        for d in (1, 3, 2):
            self.arrived(phase, d, parts)
            acc += parts[block(self.index(d)), :].astype(jnp.float32)
        return acc


class Plane:
    def __init__(self, at, send, recv):
        self.at, self.m = at, at.m
        self.send, self.recv = send, recv

    def device(self, q):
        return (2 * self.at.z + lax.rem(q, 2), q - lax.rem(q, 2) + self.at.c)

    def greet(self, bar):
        def one(i, carry):
            greet(bar, self.device(lax.rem(self.m + i + 1, 16)))
            return carry

        lax.fori_loop(0, 15, one, 0)

    def copy(self, phase, i, src_of, dst_of):
        q = lax.rem(self.m + i + 1, 16)
        return remote(src_of(q), dst_of(self.m), self.send.at[phase, i], self.recv.at[phase, i], self.device(q))

    def start(self, phase, src_of, dst_of):
        def one(i, carry):
            self.copy(phase, i, src_of, dst_of).start()
            return carry

        lax.fori_loop(0, 15, one, 0)

    def wait(self, phase, dst_of):
        def one(i, carry):
            q = lax.rem(self.m + 15 - i, 16)
            dst = dst_of(q)
            remote(dst, dst, self.send.at[phase, i], self.recv.at[phase, i], self.device(q)).wait_recv()
            return carry

        lax.fori_loop(0, 15, one, 0)

    def sent(self, phase, src_of, dst_of):
        def one(i, carry):
            self.copy(phase, i, src_of, dst_of).wait_send()
            return carry

        lax.fori_loop(0, 15, one, 0)


def piece(buf):
    return lambda q: buf.at[pl.ds(pl.multiple_of(q * 16, 16), 16)]


def keep_piece(at, src, dst):
    own = pl.ds(pl.multiple_of(at.m * 16, 16), 16)
    dst[own, :] = src[own, :]


def placings(route):
    row = lax.broadcasted_iota(jnp.int32, (256, 128), 0)
    inner = row & 15
    slot = (row >> 4) * 8 + (inner & 7)
    hit = slot == route
    left = jnp.where(hit & (inner < 8), 1.0, 0.0).astype(jnp.bfloat16)
    right = jnp.where(hit & (inner >= 8), 1.0, 0.0).astype(jnp.bfloat16)
    return left, right


def to_pieces(left, right, rows):
    half = rows.shape[1] // 2
    return (nn(left, rows[:, :half]) + nn(right, rows[:, half:])).astype(jnp.bfloat16)


def from_pieces(left, right, pieces):
    return jnp.concatenate([tn(left, pieces), tn(right, pieces)], axis=1).astype(jnp.bfloat16)


def rows_of(pieces):
    wide = pieces.astype(jnp.float32).reshape(16, 2, 8, 512)
    return jnp.concatenate([wide[:, 0].reshape(128, 512), wide[:, 1].reshape(128, 512)], axis=1)


def pieces_of(rows):
    left = rows[:, :512].reshape(16, 1, 8, 512)
    right = rows[:, 512:].reshape(16, 1, 8, 512)
    return jnp.concatenate([left, right], axis=1).reshape(256, 512).astype(jnp.bfloat16)


class Gather:
    def __init__(self, at, phase, first, src, full, xs, xr, ys, yr, ks, kr):
        self.at, self.phase, self.src, self.full = at, phase, src, full
        self.x_first = first == "x"
        self.rings = [Ring(at, "y", ys, yr), Ring(at, "x", xs, xr)]
        if self.x_first:
            self.rings.reverse()
        self.ks, self.kr = ks, kr

    def pushed(self, d):
        at = self.at
        return self.rings[0].copy(self.phase, d, self.src, self.full.at[at.yl, at.x, at.c, at.yh])

    def passed(self, d):
        at = self.at
        own = self.full.at[at.yl, :, at.c, at.yh] if self.x_first else self.full.at[:, at.x, at.c]
        return self.rings[1].copy(self.phase, d, own, own)

    def core(self, c):
        half = self.full.at[:, :, c]
        return remote(half, half, self.ks.at[self.phase], self.kr.at[self.phase], self.at.other)

    def start(self):
        at = self.at
        for d in (1, 3, 2):
            self.pushed(d).start()
        self.full[at.yl, at.x, at.c, at.yh] = self.src[...]

    def turn(self):
        at, full = self.at, self.full
        for d in (1, 3, 2):
            j = self.rings[0].index(d)
            dst = full.at[at.yl, j, at.c, at.yh] if self.x_first else full.at[lax.rem(j, 2), at.x, at.c, lax.div(j, 2)]
            self.rings[0].got(self.phase, d, dst)
        for d in (1, 3, 2):
            self.passed(d).start()

    def share(self):
        at, full = self.at, self.full
        for d in (1, 3, 2):
            j = self.rings[1].index(d)
            dst = full.at[lax.rem(j, 2), :, at.c, lax.div(j, 2)] if self.x_first else full.at[:, j, at.c]
            self.rings[1].got(self.phase, d, dst)
        self.core(at.c).start()

    def wait(self):
        self.core(1 - self.at.c).wait_recv()

    def sent(self):
        for d in (1, 3, 2):
            self.pushed(d).wait_send()
            self.passed(d).wait_send()
        self.core(self.at.c).wait_send()


def labels(position, first, second):
    return jnp.where(position >= first, 1, 0) + jnp.where(position >= second, 1, 0)


def mask(j, yh, parity, docs):
    first, second = docs[0, 0], docs[0, 1]
    wide = 128 * (j + 1)
    row = lax.broadcasted_iota(jnp.int32, (128, wide), 0) + 128 * (2 * j + yh)
    lane = lax.broadcasted_iota(jnp.int32, (128, wide), 1)
    key = (lane >> 7) * 256 + (lane & 127) + 128 * parity
    return (key <= row) & (labels(key, first, second) == labels(row, first, second))


def masked_scores(q, keys, seen):
    return jnp.where(seen, nt(q, keys) * 0.125, masked_score)


def probabilities(q, keys, seen):
    scores = [masked_scores(q, k, ok) for k, ok in zip(keys, seen)]
    top = jnp.maximum(
        jnp.max(scores[0], axis=-1, keepdims=True), jnp.max(scores[1], axis=-1, keepdims=True)
    )
    weights = [jnp.exp(s - top) for s in scores]
    inverse = 1.0 / (split_sum(weights[0]) + split_sum(weights[1]))
    return [w * inverse for w in weights]


def head_lanes(h):
    lane = lax.broadcasted_iota(jnp.int32, (128, 128), 1)
    return lane < 64 if h == 0 else lane >= 64


def only(keep, values):
    return jnp.where(keep, values.astype(jnp.float32), 0.0).astype(jnp.bfloat16)


def wide_tile(full, tile):
    part = full[:, :, :, :, :, tile]
    return part.reshape(1024, part.shape[-1])


def tall_tile(full, n):
    part = full[n // 2, 2 * (n % 2) : 2 * (n % 2) + 2]
    return part.reshape(256, part.shape[-1])


def dense_forward_kernel(
    x, gain, bias, docs, route, cot, w_qkv, w_out, w_up, w_down, exp_in, exp_out,
    hid, mixed, after, gains,
    o_x, o_n1, o_n2, o_act, o_dg, o_q, o_kv, o_kvo, o_wq, o_wo, o_wu, o_wd, o_cz, o_in0, o_out0,
    sq, su, wq, wo, wu, wd, gtile, gmine, gother,
    xa, n1, n2, cz, qb, kvb, kvo, mixs, act, dg, ps, pr, sendc, arrc, stats, own_sum,
    zs, zr, xs, xr, ys, yr, kvs, kvr, ks, kr, gs, gr, cs, cr, ss, sr, osem,
):
    at = Place()
    z, yh, c, col = at.z, at.yh, at.c, at.col
    line, plane = Ring(at, "z", zs, zr), Plane(at, cs, cr)
    bar = pltpu.get_barrier_semaphore()
    for d in (1, 2, 3):
        greet(bar, line.device(line.index(d)))
    greet(bar, at.other)
    greet(bar, at.swap_mate)
    plane.greet(bar)
    xa[block(z), :] = x[...]
    for part in range(3):
        sq[:, 256 * part : 256 * part + 256] = w_qkv[:, pl.ds(pl.multiple_of(1024 * part + 256 * z, 256), 256)]
    gtile[...] = jnp.zeros_like(gtile)
    for k, ref in enumerate((gain, bias)):
        values = ref[...].astype(jnp.float32)
        none = jnp.zeros_like(values)
        here = jnp.where(c == 0, jnp.concatenate([values, none], 1), jnp.concatenate([none, values], 1))
        gtile[2 * k : 2 * k + 2, :] = here
    half = pl.ds(pl.multiple_of(32 * yh, 32), 32)
    down_rows = w_down.at[pl.ds(pl.multiple_of(64 * z + 32 * yh, 32), 32)]
    sems = (xs, xr, ys, yr, ks, kr)
    left_q, right_q = (wq.at[:, :, :, :, :, 0:384], wq.at[:, :, :, :, :, 384:768])
    qkv_a = Gather(at, 0, "y", sq.at[half, 0:384], left_q, *sems)
    qkv_b = Gather(at, 1, "x", sq.at[half, 384:768], right_q, *sems)
    out = Gather(at, 2, "y", w_out.at[half], wo, *sems)
    up = Gather(at, 3, "y", su.at[half], wu, *sems)
    down = Gather(at, 4, "x", down_rows, wd, *sems)
    low = lax.broadcasted_iota(jnp.int32, (64, 128), 1) < 64
    odd = lax.rem(z, 2) == 1
    for n in range(8):
        first = 512 * n + 128 * lax.div(z, 2)
        a = w_up[:, pl.ds(pl.multiple_of(first, 128), 128)].astype(jnp.float32)
        b = w_up[:, pl.ds(pl.multiple_of(first + 256, 128), 128)].astype(jnp.float32)
        kept = jnp.where(low, a, pltpu.roll(b, 64, 1))
        moved = jnp.where(low, pltpu.roll(a, 64, 1), b)
        su[:, 128 * n : 128 * n + 128] = jnp.where(odd, moved, kept).astype(jnp.bfloat16)
    left, right = placings(route[0:1, :])
    sendc[...] = to_pieces(left, right, cot[...])
    pl.semaphore_wait(bar, 20)
    line.begin(0, xa)
    tile_at = pl.ds(pl.multiple_of(128 * col, 128), 128)

    def gain_copy(i):
        to = (at.s, 2 * lax.rem(col + i + 1, 8) + c)
        return remote(gtile, gmine.at[:, tile_at], gs.at[i], gr.at[i], to)

    def push_gain(i, carry):
        gain_copy(i).start()
        return carry

    lax.fori_loop(0, 7, push_gain, 0)
    gmine[:, tile_at] = gtile[...]
    qkv_a.start()
    qkv_b.start()
    plane.start(0, piece(sendc), piece(arrc))
    keep_piece(at, sendc, arrc)
    qkv_a.turn()
    qkv_b.turn()
    for weight in (out, up, down):
        weight.start()
    line.relay(0, xa)

    def wait_gain(i, carry):
        q = lax.rem(col + 7 - i, 8)
        dst = gmine.at[:, pl.ds(pl.multiple_of(128 * q, 128), 128)]
        remote(dst, dst, gs.at[i], gr.at[i], (at.s, 2 * q + c)).wait_recv()
        return carry

    lax.fori_loop(0, 7, wait_gain, 0)
    gain_core = remote(gmine, gother, gs.at[7], gr.at[7], at.other)
    gain_core.start()
    gain_core.wait_recv()
    gains[...] = gmine[...] + gother[...]
    qkv_a.share()
    qkv_b.share()
    out.turn()
    up.turn()

    def kv_copy(i, j):
        return remote(kvb.at[block(j)], kvo.at[block(j)], kvs.at[i], kvr.at[i], at.mate)

    def project_qkv(i, carry):
        j = line.index(order(i))
        pl.when(i == 1)(lambda: line.above(0, xa))
        pl.when(i == 2)(lambda: line.below(0, xa))
        pl.when(i == 3)(lambda: line.far(0, xa))
        xhat = norm_parts(xa[block(j), :].astype(jnp.float32))[0]
        n1[block(j), :] = (xhat * gains[0:1, :] + gains[2:3, :]).astype(jnp.bfloat16)

        @pl.when(i == 0)
        def _():
            qkv_a.wait()
            qkv_b.wait()

        values = n1[block(j), :]
        kvb[block(j), 0:256] = nn(values, wide_tile(wq, slice(256, 512))).astype(jnp.bfloat16)
        kvb[block(j), 256:512] = nn(values, wide_tile(wq, slice(512, 768))).astype(jnp.bfloat16)
        kv_copy(i, j).start()
        qb[block(j), :] = nn(values, wide_tile(wq, slice(0, 256))).astype(jnp.bfloat16)
        return carry

    lax.fori_loop(0, 4, project_qkv, 0)
    down.turn()
    plane.wait(0, piece(arrc))
    cz[block(z), :] = rows_of(arrc[...]).astype(jnp.bfloat16)
    line.spread(4, cz)

    def heads(j, keys, parity):
        seen = mask(j, yh, parity, docs)
        wide = slice(0, 128 * (j + 1))
        for p in range(2):
            lanes = slice(128 * p, 128 * p + 128)
            q = qb[128 * j : 128 * j + 128, lanes]
            for h in range(2):
                scores = masked_scores(only(head_lanes(h), q), keys[wide, lanes], seen)
                yield 4 * j + 2 * p + h, h, lanes, scores, keys[wide, 256 + 128 * p : 384 + 128 * p]

    first = None
    for j in range(4):
        for k, h, lanes, scores, values in heads(j, kvb, yh):
            top = jnp.max(scores, axis=-1, keepdims=True)
            weights = jnp.exp(scores - top)
            stats[k] = jnp.where(head_lanes(0), top, split_sum(weights))
            summed = nn(weights.astype(jnp.bfloat16), values)
            if h == 0:
                first = summed
            else:
                own_sum[128 * j : 128 * j + 128, lanes] = jnp.where(head_lanes(0), first, summed)
    for i in range(4):
        kv_copy(i, line.index(order(i))).wait_recv()
    swaps = [
        remote(exp_in.at[0], o_in0, ss.at[0], sr.at[0], at.swap_mate),
        remote(exp_out.at[0], o_out0, ss.at[1], sr.at[1], at.swap_mate),
    ]

    @pl.when(c != yh)
    def _():
        swaps[0].start()

    my_lanes = pl.ds(pl.multiple_of(256 * z, 256), 256)

    def mix_copy(d):
        return line.copy(1, d, mixs.at[block(line.index(d))], mixed.at[:, my_lanes])

    for j in range(4):
        rows = slice(128 * j, 128 * j + 128)
        for k, h, lanes, scores, values in heads(j, kvo, 1 - yh):
            top, total = stats[k][:, 0:1], stats[k][:, 64:65]
            new_top = jnp.maximum(top, jnp.max(scores, axis=-1, keepdims=True))
            kept = jnp.exp(top - new_top)
            weights = jnp.exp(scores - new_top)
            inverse = 1.0 / (total * kept + split_sum(weights))
            summed = (own_sum[rows, lanes] * kept + nn(weights.astype(jnp.bfloat16), values)) * inverse
            if h == 0:
                first = summed
            else:
                mixs[rows, lanes] = jnp.where(head_lanes(0), first, summed).astype(jnp.bfloat16)
        pl.when(z != j)(lambda: mix_copy(lax.rem(j + 4 - z, 4)).start())
    mixed[:, my_lanes] = mixs[block(z), :]
    out.share()
    out.wait()
    for d in (1, 3, 2):
        line.got(1, d, mixed.at[:, pl.ds(pl.multiple_of(256 * line.index(d), 256), 256)])
    for n in range(4):
        tile = slice(256 * n, 256 * n + 256)
        after[:, tile] = x[:, tile].astype(jnp.float32) + nn(mixed[...], wide_tile(wo, tile))
    xhat = norm_parts(after[...])[0]
    n2[block(z), :] = (xhat * gains[1:2, :] + gains[3:4, :]).astype(jnp.bfloat16)
    line.begin(2, n2)
    up.share()
    down.share()
    @pl.when(c != yh)
    def _():
        swaps[1].start()

    up.wait()
    down.wait()
    stores = [
        pltpu.make_async_copy(src, dst, osem.at[k])
        for k, (src, dst) in enumerate(
            [(xa, o_x), (n1, o_n1), (qb, o_q), (kvb, o_kv), (kvo, o_kvo), (wq, o_wq), (wo, o_wo), (wu, o_wu), (wd, o_wd)]
        )
    ]
    for store in stores:
        store.start()

    def feed(i, carry):
        d = order(i)
        j = line.index(d)
        line.ready(2, i, n2)
        values = n2[block(j), :]
        for n in range(4):
            tile = slice(n * 256, (n + 1) * 256)
            acted, slope = gelu_parts(nn(values, wide_tile(wu, tile)))
            act[block(j), tile] = acted.astype(jnp.bfloat16)
            dg[block(j), tile] = slope
        values = act[block(j), :]
        for n in range(4):
            tile = slice(n * 256, (n + 1) * 256)
            ps[block(j), tile] = nn(values, wide_tile(wd, tile)).astype(jnp.bfloat16)

        @pl.when(i > 0)
        def _():
            line.give(3, d, ps, pr)

        return carry

    lax.fori_loop(0, 4, feed, 0)
    for d in (1, 3, 2):
        line.arrived(4, d, cz)
    late = [
        pltpu.make_async_copy(src, dst, osem.at[9 + k])
        for k, (src, dst) in enumerate([(n2, o_n2), (act, o_act), (dg, o_dg), (cz, o_cz)])
    ]
    for store in late:
        store.start()
    gain_core.wait_send()

    def sent_gain(i, carry):
        gain_copy(i).wait_send()
        return carry

    lax.fori_loop(0, 7, sent_gain, 0)
    for weight in (qkv_a, qkv_b, out, up, down):
        weight.sent()
    for i in range(4):
        kv_copy(i, line.index(order(i))).wait_send()
    line.sent_all(0, xa)
    for d in (1, 3, 2):
        mix_copy(d).wait_send()
    line.sent_all(2, n2)
    line.sent(4, cz)
    plane.sent(0, piece(sendc), piece(arrc))
    hid[...] = (after[...] + line.total(3, ps, pr)).astype(jnp.bfloat16)
    line.sent(3, ps)

    @pl.when(c != yh)
    def _():
        for swap in swaps:
            swap.wait()

    for store in stores + late:
        store.wait()


def dense_forward_call(x, gain, bias, docs, route, cot, w_qkv, w_out, w_up, w_down, exp_in, exp_out):
    bf, f32 = jnp.bfloat16, jnp.float32
    vmem, anywhere = pl.BlockSpec(memory_space=pltpu.VMEM), pl.BlockSpec(memory_space=pl.ANY)
    smem = pl.BlockSpec(memory_space=pltpu.SMEM)
    shape, V, dma = jax.ShapeDtypeStruct, pltpu.VMEM, pltpu.SemaphoreType.DMA
    line = [V((512, 1024), bf)]
    weight = [(2, 4, 2, 2, 32, 768)] + [(2, 4, 2, 2, 32, 1024)] * 3
    saved = [
        shape((512, 1024), bf), shape((512, 1024), bf), shape((512, 1024), bf), shape((512, 1024), bf),
        shape((512, 1024), f32), shape((512, 256), bf), shape((512, 512), bf), shape((512, 512), bf),
    ] + [shape(w, bf) for w in weight] + [
        shape((512, 1024), bf), shape((1024, 512), bf), shape((512, 1024), bf),
    ]
    return pl.pallas_call(
        dense_forward_kernel,
        out_shape=[shape((128, 1024), bf), shape((128, 1024), bf), shape((128, 1024), f32), shape((8, 1024), f32)]
        + saved,
        in_specs=[vmem] * 3 + [smem] + [vmem] * 6 + [anywhere, anywhere],
        out_specs=[vmem] * 4 + [anywhere] * len(saved),
        scratch_shapes=[
            V((64, 768), bf), V((64, 1024), bf), *[V(w, bf) for w in weight], V((8, 128), f32), V((8, 1024), f32),
            V((8, 1024), f32),
            *(line * 4), V((512, 256), bf), V((512, 512), bf), V((512, 512), bf), V((512, 256), bf),
            *line, V((512, 1024), f32), *(line * 2), V((256, 512), bf), V((256, 512), bf),
            V((16, 128, 128), f32), V((512, 256), f32), dma((5, 6)), dma((5, 6)), dma((5, 3)), dma((5, 3)), dma((5, 3)), dma((5, 3)), dma((4,)), dma((4,)),
            dma((5,)), dma((5,)), dma((8,)), dma((8,)), dma((1, 15)), dma((1, 15)), dma((3,)), dma((3,)), dma((13,)),
        ],
        compiler_params=pltpu.CompilerParams(collective_id=2, has_side_effects=True, vmem_limit_bytes=60 << 20),
        name="dense_forward",
    )(x, gain, bias, docs, route, cot, w_qkv, w_out, w_up, w_down, exp_in, exp_out)


def expert_kernel(
    hid, route, exp_gain, exp_bias, centroid, cz_h, exp_in, exp_out, in0, out0,
    gh, vecg, mid, gate_out, o_ps, gin1, gout1, gin0, gout0,
    w_in, w_out, sendh, sendg, arrh, arrg, cz,
    e0, e1, g0, g1, ps0, ps1, pr0, pb0, pb1,
    act0, act1, dg0, dg1, gp0, gp1,
    arrived, base, xh0, xh1, sc, gates, dots, dots_in,
    ga_in, ga_out, sb_in, sb_out, rb_in, rb_out, vec, vec_own, vec_other, vmine, vcore, vline,
    wsem, zs, zr, cs, cr, ks, kr, osem, bs, br, ss, sr, vs, vr,
):
    at = Place()
    z, yh, c, same = at.z, at.yh, at.c, at.same
    line, plane = Ring(at, "z", zs, zr), Plane(at, cs, cr)
    bar = pltpu.get_barrier_semaphore()
    plane.greet(bar)
    for d in (1, 2, 3):
        greet(bar, line.device(line.index(d)))
    greet(bar, at.other)
    greet(bar, at.swap_mate)
    low, high = slice(0, 512), slice(512, 1024)

    def slot(k, i, half):
        return w_in.at[k, :, half] if i == 0 else w_out.at[k, half, :]

    def load(k, i):
        return pltpu.make_async_copy((exp_in, exp_out)[i].at[k], slot(k, i, low), wsem.at[k, i])

    def swapped(k, i):
        return pltpu.make_async_copy((in0, out0)[i], slot(k, i, low), wsem.at[k, i])

    swap_out = remote(exp_out.at[1], slot(1, 1, low), ss.at[0], sr.at[0], at.swap_mate)
    swap_in = remote(exp_in.at[1], slot(1, 0, low), ss.at[3], sr.at[3], at.swap_mate)

    def share(k, i):
        return remote(slot(k, i, low), slot(k, i, high), bs.at[k, i], br.at[k, i], at.other)

    def on_either(when_same, when_swapped):
        pl.when(same)(when_same)
        pl.when(jnp.logical_not(same))(when_swapped)

    load_c = pltpu.make_async_copy(cz_h, cz, wsem.at[2, 0])

    def begin_same():
        for k, i in ((0, 0), (0, 1), (1, 0), (1, 1)):
            load(k, i).start()

    def begin_swapped():
        for k, i in ((0, 0), (0, 1)):
            swapped(k, i).start()

    on_either(begin_same, begin_swapped)
    load_c.start()
    left, right = placings(route[0:1, :])
    sendh[...] = to_pieces(left, right, hid[...])
    vec_own[0:2, :] = exp_gain[...].astype(jnp.float32)
    vec_own[2:4, :] = exp_bias[...].astype(jnp.float32)
    vec_own[4:5, :] = centroid[...].astype(jnp.float32)
    vec_own[5:8, :] = jnp.zeros((3, 1024), jnp.float32)
    pl.semaphore_wait(bar, 20)
    plane.start(0, piece(sendh), piece(arrh))
    keep_piece(at, sendh, arrh)
    trade = remote(vec_own, vec_other, vs.at[2], vr.at[2], at.other)
    trade.start()

    def wait_loads(k, i):
        on_either(lambda: load(k, i).wait(), lambda: swapped(k, i).wait())
        share(k, i).start()

    wait_loads(0, 0)
    wait_loads(0, 1)
    trade.wait()
    vec[...] = jnp.where(same, vec_own[...], vec_other[...])
    plane.wait(0, piece(arrh))
    gain = [vec[0:1, :], vec[1:2, :]]
    bias = [vec[2:3, :], vec[3:4, :]]
    rows = rows_of(arrh[...])
    arrived[...] = rows
    xhat, scale = norm_parts(rows)
    xh0[...] = xhat
    sc[0] = jnp.broadcast_to(scale, (128, 128))
    e0[block(z), :] = (xhat * gain[0] + bias[0]).astype(jnp.bfloat16)
    line.begin(0, e0)

    @pl.when(jnp.logical_not(same))
    def _():
        swap_in.start()
        swap_out.start()

    gating = jax.nn.sigmoid(split_sum(rows * vec[4:5, :]))
    gates[z] = jnp.broadcast_to(gating, (128, 128))

    def gate_copy(d):
        return line.copy(3, d, gates.at[z], gates.at[z])

    for d in (1, 3, 2):
        gate_copy(d).start()
    share(0, 0).wait_recv()
    share(0, 1).wait_recv()
    load_c.wait()

    def forward(k, j, rows_in, act, dg):
        values = rows_in[block(j), :]
        for n in range(4):
            tile = slice(n * 256, (n + 1) * 256)
            pre = nn(values, w_in[k, :, tile])
            acted, slope = gelu_parts(pre)
            act[block(j), tile] = acted.astype(jnp.bfloat16)
            dg[block(j), tile] = slope

    def project(k, j, act, part):
        values = act[block(j), :]
        for n in range(4):
            tile = slice(n * 256, (n + 1) * 256)
            part[block(j), tile] = nn(values, w_out[k, :, tile]).astype(jnp.bfloat16)

    def backward(k, j, grad, dg, gp, part):
        values = grad[block(j), :]
        for n in range(4):
            tile = slice(n * 256, (n + 1) * 256)
            slope = dg[block(j), tile] * nt(values, w_out[k, tile, :])
            gp[block(j), tile] = slope.astype(jnp.bfloat16)
        pres = gp[block(j), :]
        for n in range(4):
            tile = slice(n * 256, (n + 1) * 256)
            part[block(j), tile] = nt(pres, w_in[k, tile, :]).astype(jnp.bfloat16)

    def sub0(i, carry):
        d = order(i)
        j = line.index(d)

        line.ready(0, i, e0)
        forward(0, j, e0, act0, dg0)
        project(0, j, act0, ps0)

        @pl.when(i > 0)
        def _():
            line.give(1, d, ps0, pr0)

        return carry

    lax.fori_loop(0, 4, sub0, 0)
    on_either(lambda: load(1, 0).wait(), lambda: swap_in.wait())
    share(1, 0).start()
    on_either(lambda: load(1, 1).wait(), lambda: swap_out.wait())
    share(1, 1).start()
    stream = arrived[...] + line.total(1, ps0, pr0)
    base[...] = stream
    xhat, scale = norm_parts(stream)
    xh1[...] = xhat
    sc[1] = jnp.broadcast_to(scale, (128, 128))
    e1[block(z), :] = (xhat * gain[1] + bias[1]).astype(jnp.bfloat16)
    line.begin(2, e1)
    gate = gates[z][:, 0:1]
    mid[...] = arrived[...] + gate * (base[...] - arrived[...])
    gate_out[...] = gates[z]
    line.sent(1, ps0)
    share(1, 0).wait_recv()
    share(1, 1).wait_recv()

    def sub1(i, carry):
        d = order(i)
        j = line.index(d)

        @pl.when(i > 0)
        def _():
            line.got(3, d, gates.at[j])

        g1[block(j), :] = (gates[j][:, 0:1] * cz[block(j), :].astype(jnp.float32)).astype(jnp.bfloat16)

        line.ready(2, i, e1)
        forward(1, j, e1, act1, dg1)
        backward(1, j, g1, dg1, gp1, ps0)

        @pl.when(i > 0)
        def _():
            line.give(4, d, ps0, pb1)

        return carry

    lax.fori_loop(0, 4, sub1, 0)

    def second_part(i, carry):
        d = order(3 - i)
        j = line.index(d)
        project(1, j, act1, ps1)
        products = cz[block(j), :].astype(jnp.float32) * ps1[block(j), :].astype(jnp.float32)
        dots[j] = jnp.broadcast_to(split_sum(products), (128, 128))

        @pl.when(i < 3)
        def _():
            line.copy(5, d, dots.at[j], dots_in.at[z]).start()

        return carry

    lax.fori_loop(0, 4, second_part, 0)
    keep_ps = pltpu.make_async_copy(ps1, o_ps, wsem.at[2, 1])
    keep_ps.start()

    def weight_grads(k, rows_in, gp, act, grad):
        def one(n, carry):
            tile = pl.ds(pl.multiple_of(n * 256, 256), 256)
            tile_b = pl.ds(pl.multiple_of(n * 256 + 512, 256), 256)
            ga_out[k, tile, :] = tn(act[:, tile], grad[...])
            sb_out[k, tile, :] = tn(act[:, tile_b], grad[...]).astype(jnp.bfloat16)
            return carry

        lax.fori_loop(0, 2, one, 0)

        def two(n, carry):
            tile = pl.ds(pl.multiple_of(n * 256, 256), 256)
            ga_in[k, tile, :] = tn(rows_in[:, tile], gp[:, 0:512])
            sb_in[k, tile, :] = tn(rows_in[:, tile], gp[:, 512:1024]).astype(jnp.bfloat16)
            return carry

        lax.fori_loop(0, 4, two, 0)

    def swap(k, i):
        src, dst = ((sb_in, rb_in), (sb_out, rb_out))[i]
        return remote(src.at[k], dst.at[k], ks.at[k, i], kr.at[k, i], at.other)

    def join_cores(k):
        for i in range(2):
            swap(k, i).wait()
        sb_in[k] = (ga_in[k] + rb_in[k].astype(jnp.float32)).astype(jnp.bfloat16)
        sb_out[k] = (ga_out[k] + rb_out[k].astype(jnp.float32)).astype(jnp.bfloat16)

    weight_grads(1, e1, gp1, act1, g1)
    swap(1, 0).start()
    swap(1, 1).start()
    grad_normed = line.total(4, ps0, pb1)
    cot = cz[block(z), :].astype(jnp.float32)
    grad_stream = gates[z][:, 0:1] * cot
    grad_stream += norm_back(grad_normed, gain[1], xh1[...], sc[1][:, 0:1])
    g0[block(z), :] = grad_stream.astype(jnp.bfloat16)
    line.begin(6, g0)
    vmine[1:2, :] = jnp.sum(grad_normed * xh1[...], axis=0, keepdims=True)
    vmine[3:4, :] = jnp.sum(grad_normed, axis=0, keepdims=True)
    line.sent(4, ps0)
    grad_gating = split_sum(cot * (base[...] - arrived[...])) + dots[z][:, 0:1]
    for d in (1, 3, 2):
        line.got(5, d, dots_in.at[line.index(d)])
        grad_gating += dots_in[line.index(d)][:, 0:1]
    gate = gates[z][:, 0:1]
    grad_logit = gate * (1.0 - gate) * grad_gating
    vmine[4:5, :] = jnp.sum(grad_logit * arrived[...], axis=0, keepdims=True)
    base[...] = grad_stream + (1.0 - gate) * cot + grad_logit * vec[4:5, :]
    join_cores(1)
    kept = [
        pltpu.make_async_copy(sb_in.at[1], gin1, osem.at[1, 0]),
        pltpu.make_async_copy(sb_out.at[1], gout1, osem.at[1, 1]),
    ]
    given = [
        remote(sb_in.at[1], gin1, ss.at[1], sr.at[1], at.swap_mate),
        remote(sb_out.at[1], gout1, ss.at[2], sr.at[2], at.swap_mate),
    ]

    def begin(copies):
        for copy in copies:
            copy.start()

    def finish(copies):
        for copy in copies:
            copy.wait()

    on_either(lambda: begin(kept), lambda: begin(given))

    def sub0_back(i, carry):
        d = order(i)
        j = line.index(d)

        line.ready(6, i, g0)
        backward(0, j, g0, dg0, gp0, ps0)

        @pl.when(i > 0)
        def _():
            line.give(7, d, ps0, pb0)

        return carry

    lax.fori_loop(0, 4, sub0_back, 0)
    weight_grads(0, e0, gp0, act0, g0)
    swap(0, 0).start()
    swap(0, 1).start()
    grad_normed = line.total(7, ps0, pb0)
    grad_stream = base[...] + norm_back(grad_normed, gain[0], xh0[...], sc[0][:, 0:1])
    sendg[...] = pieces_of(grad_stream)
    plane.start(1, piece(sendg), piece(arrg))
    keep_piece(at, sendg, arrg)
    vmine[0:1, :] = jnp.sum(grad_normed * xh0[...], axis=0, keepdims=True)
    vmine[2:3, :] = jnp.sum(grad_normed, axis=0, keepdims=True)
    vmine[5:8, :] = jnp.zeros((3, 1024), jnp.float32)
    give_core = remote(vmine, vcore, vs.at[0], vr.at[0], at.other)
    give_core.start()
    give_core.wait_recv()
    vline[z] = vmine[...] + vcore[...]

    def give_line(d):
        return line.copy(8, d, vline.at[z], vline.at[z])

    for d in (1, 3, 2):
        give_line(d).start()
    join_cores(0)
    stores = [
        pltpu.make_async_copy(sb_in.at[0], gin0, osem.at[0, 0]),
        pltpu.make_async_copy(sb_out.at[0], gout0, osem.at[0, 1]),
    ]
    begin(stores)
    plane.wait(1, piece(arrg))
    left, right = placings(route[0:1, :])
    gh[...] = from_pieces(left, right, arrg[...])
    for d in (1, 3, 2):
        line.got(8, d, vline.at[line.index(d)])
    vecg[...] = vline[0] + vline[1] + vline[2] + vline[3]
    give_core.wait_send()
    for d in (1, 3, 2):
        give_line(d).wait_send()
        gate_copy(d).wait_send()
        line.copy(5, d, dots.at[line.index(d)], dots_in.at[z]).wait_send()
    for k in (0, 1):
        for i in range(2):
            share(k, i).wait_send()
    line.sent_all(0, e0)
    line.sent_all(2, e1)
    line.sent_all(6, g0)
    line.sent(7, ps0)
    plane.sent(0, piece(sendh), piece(arrh))
    plane.sent(1, piece(sendg), piece(arrg))
    keep_ps.wait()
    finish(stores)
    on_either(lambda: finish(kept), lambda: finish(given))


def expert_call(hid, route, exp_gain, exp_bias, centroid, cz, exp_in, exp_out, in0, out0):
    bf, f32 = jnp.bfloat16, jnp.float32
    vmem, anywhere = pl.BlockSpec(memory_space=pltpu.VMEM), pl.BlockSpec(memory_space=pl.ANY)
    shape, V, dma = jax.ShapeDtypeStruct, pltpu.VMEM, pltpu.SemaphoreType.DMA
    line, rows, pieces = [V((512, 1024), bf)], [V((128, 1024), f32)], [V((256, 512), bf)]
    wide, small = [V((512, 1024), f32)], [V((4, 128, 128), f32)]
    vectors = [V((8, 1024), f32)]
    return pl.pallas_call(
        expert_kernel,
        out_shape=(
            shape((128, 1024), bf), shape((8, 1024), f32), shape((128, 1024), f32), shape((128, 128), f32),
            shape((512, 1024), bf), shape((1024, 512), bf), shape((512, 1024), bf), shape((1024, 512), bf),
            shape((512, 1024), bf),
        ),
        in_specs=[vmem] * 5 + [anywhere] * 5,
        out_specs=tuple([vmem] * 4 + [anywhere] * 5),
        scratch_shapes=[
            V((2, 1024, 1024), bf), V((2, 1024, 1024), bf), *(pieces * 4), *line,
            *(line * 9), *(line * 2), *(wide * 2), *(line * 2),
            *(rows * 4), *(small * 4),
            V((2, 1024, 512), f32), V((2, 512, 1024), f32),
            V((2, 1024, 512), bf), V((2, 512, 1024), bf), V((2, 1024, 512), bf), V((2, 512, 1024), bf),
            *(vectors * 5), V((4, 8, 1024), f32),
            dma((3, 2)), dma((9, 6)), dma((9, 6)), dma((2, 15)), dma((2, 15)), dma((2, 2)), dma((2, 2)), dma((2, 2)),
            dma((2, 2)), dma((2, 2)), dma((4,)), dma((4,)), dma((3,)), dma((3,)),
        ],
        compiler_params=pltpu.CompilerParams(collective_id=1, has_side_effects=True, vmem_limit_bytes=60 << 20),
        name="experts",
    )(hid, route, exp_gain, exp_bias, centroid, cz, exp_in, exp_out, in0, out0)


class Everyone:
    def __init__(self, at, send, recv):
        self.at, self.send, self.recv = at, send, recv

    def copy(self, phase, i, buf):
        own = buf.at[self.at.s]
        to = (lax.rem(self.at.s + i + 1, 8), self.at.f)
        return remote(own, own, self.send.at[phase, i], self.recv.at[phase, i], to)

    def start(self, phase, buf):
        for i in range(7):
            self.copy(phase, i, buf).start()

    def wait(self, phase, buf):
        for i in range(7):
            q = lax.rem(self.at.s + 7 - i, 8)
            dst = buf.at[q]
            remote(dst, dst, self.send.at[phase, i], self.recv.at[phase, i], (q, self.at.f)).wait_recv()

    def sent(self, phase, buf):
        for i in range(7):
            self.copy(phase, i, buf).wait_send()


def dense_backward_kernel(
    gh, after, docs, gains, mixed, route, mid, gate, vec_sum, x_h, n1_h, n2_h, act_h, dg_h, q_h, kv_h, kvo_h, wq_h, wo_h, wu_h,
    wd_h, ps_h, gin0, gout0,
    gx, bd, bu, bo, bq, gvec, res, vec_swap, fin0, fout0,
    ghs, xa, xh, n1, n2, act, dg, gp, qb, kvb, kvo, wq, wo, wu, wd,
    ps, pr, ps2, pr2, ps3, pr3, prob, gms, gm, dp, dkv, dkvo, kvs, kvr,
    md, mu, mo, mq, mkv, td, tu, to, tq, tkv, rd, ru, ro, rq, rkv, xd, xu, xo, sd, su, so, yd, yu, yo, rp, rpkv, sendr, arrr,
    vmine, vcore, vplane, vline, outz,
    lsem, zs, zr, xs, xr, ys, yr, kvss, kvsr, ks, kr, cs, cr, qs, qr, ss, sr, vs, vr, fs, fr,
):
    at = Place()
    z, yh, c, col = at.z, at.yh, at.c, at.col
    line, ring_x, ring_y = Ring(at, "z", zs, zr), Ring(at, "x", xs, xr), Ring(at, "y", ys, yr)
    plane, everyone = Plane(at, cs, cr), Everyone(at, qs, qr)
    bar = pltpu.get_barrier_semaphore()
    plane.greet(bar)
    for d in (1, 2, 3):
        greet(bar, line.device(line.index(d)))
        greet(bar, (2 * line.index(d) + 1 - yh, at.f))
    greet(bar, at.other)
    greet(bar, at.swap_mate)
    loads = [
        pltpu.make_async_copy(src, dst, lsem.at[k])
        for k, (src, dst) in enumerate(
            [
                (q_h, qb), (kv_h, kvb), (kvo_h, kvo), (wd_h, wd), (dg_h, dg), (wu_h, wu), (act_h, act), (n2_h, n2),
                (wo_h, wo), (ps_h, ps3), (wq_h, wq), (n1_h, n1), (x_h, xa),
            ]
        )
    ]
    for load in loads:
        load.start()
    ghs[block(z), :] = gh[...]
    pl.semaphore_wait(bar, 23)
    line.begin(0, ghs)
    swaps = [
        remote(gin0, fin0, ss.at[0], sr.at[0], at.swap_mate),
        remote(gout0, fout0, ss.at[1], sr.at[1], at.swap_mate),
    ]
    give_vec = remote(vec_sum, vec_swap, ss.at[2], sr.at[2], at.swap_mate)

    @pl.when(jnp.logical_not(at.same))
    def _():
        give_vec.start()
        for swap in swaps:
            swap.start()

    for load in loads[:3]:
        load.wait()
    for j in range(4):
        seen = [mask(j, yh, parity, docs) for parity in (yh, 1 - yh)]
        wide = slice(0, 128 * (j + 1))
        for p in range(2):
            lanes = slice(128 * p, 128 * p + 128)
            keys = [kvb[wide, lanes], kvo[wide, lanes]]
            q = qb[128 * j : 128 * j + 128, lanes]
            for h in range(2):
                found = probabilities(only(head_lanes(h), q), keys, seen)
                for k in range(2):
                    prob[k, 4 * j + 2 * p + h, :, wide] = found[k].astype(jnp.bfloat16)
    for load in loads[3:6]:
        load.wait()

    def feed(i, carry):
        d = order(i)
        j = line.index(d)

        line.ready(0, i, ghs)
        values = ghs[block(j), :]
        for n in range(4):
            tile = slice(n * 256, (n + 1) * 256)
            gp[block(j), tile] = (dg[block(j), tile] * nt(values, tall_tile(wd, n))).astype(jnp.bfloat16)
        pres = gp[block(j), :]
        for n in range(4):
            tile = slice(n * 256, (n + 1) * 256)
            ps[block(j), tile] = nt(pres, tall_tile(wu, n)).astype(jnp.bfloat16)

        @pl.when(i > 0)
        def _():
            line.give(1, d, ps, pr)

        return carry

    lax.fori_loop(0, 4, feed, 0)
    for load in loads[6:10]:
        load.wait()

    def weight_grad(lhs, rhs, mine, theirs):
        def one(n, carry):
            rows = lhs[:, pl.ds(pl.multiple_of(n * 256, 256), 256)]
            grad = tn(rows, rhs[...])
            for half in range(2):
                first = grad[128 * half : 128 * half + 64].astype(jnp.bfloat16)
                second = grad[128 * half + 64 : 128 * half + 128].astype(jnp.bfloat16)
                here = lax.div(n, 2), 2 * lax.rem(n, 2) + half
                mine[here] = jnp.where(c == 0, first, second)
                theirs[here] = jnp.where(c == 0, second, first)
            return carry

        lax.fori_loop(0, 4, one, 0)

    def core_copy(phase, src, dst):
        return remote(src, dst, ks.at[phase], kr.at[phase], at.other)

    def join_cores(phase, mine, theirs, got):
        core_copy(phase, theirs, got).wait()

        def one(n, carry):
            here = lax.div(n, 4), lax.rem(n, 4)
            mine[here] = (mine[here].astype(jnp.float32) + got[here].astype(jnp.float32)).astype(jnp.bfloat16)
            return carry

        lax.fori_loop(0, 8, one, 0)

    def x_copy(phase, d, mine, dst):
        return ring_x.copy(phase, d, mine.at[:, ring_x.index(d)], dst.at[at.x])

    def y_copy(phase, d, part, dst):
        j = ring_y.index(d)
        src = part.at[lax.rem(j, 2), pl.ds(pl.multiple_of(32 * lax.div(j, 2), 32), 32)]
        return ring_y.copy(phase, d, src, dst.at[ring_y.pos])

    def to_x(phase, mine, dst):
        for d in (1, 3, 2):
            x_copy(phase, d, mine, dst).start()

    def to_y(phase, mine, got, part, dst):
        acc = mine[:, at.x].astype(jnp.float32)
        for d in (1, 3, 2):
            j = ring_x.index(d)
            ring_x.got(phase, d, got.at[j])
            acc += got[j].astype(jnp.float32)
        part[...] = acc.astype(jnp.bfloat16)
        for d in (1, 3, 2):
            y_copy(phase, d, part, dst).start()

    def fin_copy(phase, d, buf):
        own = buf.at[yh, z]
        return line.copy(phase, d, own, own)

    def fin_mate(phase, buf):
        own = buf.at[yh]
        return remote(own, own, fs.at[phase], fr.at[phase], at.mate)

    def fin_z(phase, buf, values):
        buf[yh, z] = values.astype(jnp.bfloat16)
        for d in (1, 3, 2):
            fin_copy(phase, d, buf).start()

    def fin_y(phase, buf):
        for d in (1, 3, 2):
            line.got(phase, d, buf.at[yh, line.index(d)])
        fin_mate(phase, buf).start()

    def fin_wait(phase, buf):
        dst = buf.at[1 - yh]
        remote(dst, dst, fs.at[phase], fr.at[phase], at.mate).wait_recv()

    def y_total(phase, part, got):
        acc = part[at.yl, pl.ds(pl.multiple_of(32 * yh, 32), 32), :].astype(jnp.float32)
        for d in (1, 3, 2):
            j = ring_y.index(d)
            ring_y.got(phase, d, got.at[j])
            acc += got[j].astype(jnp.float32)
        return acc

    def y_first(phase, d, mine, dst):
        j = ring_y.index(d)
        src = mine.at[lax.rem(j, 2), :, pl.ds(pl.multiple_of(32 * lax.div(j, 2), 32), 32)]
        return ring_y.copy(phase, d, src, dst.at[ring_y.pos])

    def x_second(phase, d, part, dst):
        return ring_x.copy(phase, d, part.at[ring_x.index(d)], dst.at[at.x])

    def turn_to_x(phase, mine, got, part, dst):
        acc = mine[at.yl, :, pl.ds(pl.multiple_of(32 * yh, 32), 32), :].astype(jnp.float32)
        for d in (1, 3, 2):
            j = ring_y.index(d)
            ring_y.got(phase, d, got.at[j])
            acc += got[j].astype(jnp.float32)
        part[...] = acc.astype(jnp.bfloat16)
        for d in (1, 3, 2):
            x_second(phase, d, part, dst).start()

    def x_total(phase, part, got):
        acc = part[at.x].astype(jnp.float32)
        for d in (1, 3, 2):
            j = ring_x.index(d)
            ring_x.got(phase, d, got.at[j])
            acc += got[j].astype(jnp.float32)
        return acc

    weight_grad(act, ghs, md, td)
    core_copy(0, td, rd).start()
    weight_grad(n2, gp, mu, tu)
    core_copy(1, tu, ru).start()
    join_cores(0, md, td, rd)
    to_x(0, md, xd)
    join_cores(1, mu, tu, ru)
    for d in (1, 3, 2):
        y_first(1, d, mu, xu).start()
    grad_normed = line.total(1, ps, pr)
    xhat, scale = norm_parts(after[...])
    vmine[1:2, :] = jnp.sum(grad_normed * xhat, axis=0, keepdims=True)
    vmine[3:4, :] = jnp.sum(grad_normed, axis=0, keepdims=True)
    grad_after = gh[...].astype(jnp.float32) + norm_back(grad_normed, gains[1:2, :], xhat, scale)
    gx[...] = grad_after
    grad_attn = grad_after.astype(jnp.bfloat16)
    for n in range(4):
        gms[:, 256 * n : 256 * n + 256] = nt(grad_attn, tall_tile(wo, n)).astype(jnp.bfloat16)

    def gm_copy(d):
        lanes = pl.ds(pl.multiple_of(256 * line.index(d), 256), 256)
        return line.copy(2, d, gms.at[:, lanes], gm.at[block(z)])

    for d in (1, 3, 2):
        gm_copy(d).start()
    gm[block(z), :] = gms[:, pl.ds(pl.multiple_of(256 * z, 256), 256)]
    gp[block(0), :] = grad_attn
    weight_grad(mixed, gp.at[block(0)], mo, to)
    core_copy(2, to, ro).start()
    for load in loads[10:]:
        load.wait()
    for j in range(4):
        xh[block(j), :] = norm_parts(xa[block(j), :].astype(jnp.float32))[0]
    join_cores(2, mo, to, ro)
    to_x(2, mo, xo)
    for d in (1, 3, 2):
        line.arrived(2, d, gm)
    for d in (1, 3, 2):
        line.give(6, d, ps3, pr3)
    dkv[...] = jnp.zeros_like(dkv)
    dkvo[...] = jnp.zeros_like(dkvo)

    def kv_copy(j):
        return remote(kvs.at[block(j)], kvr.at[block(j)], kvss.at[j], kvsr.at[j], at.mate)

    def attend_back(j):
        wide = slice(0, 128 * (j + 1))
        rows = slice(128 * j, 128 * j + 128)
        for p in range(2):
            lanes = slice(128 * p, 128 * p + 128)
            value_lanes = slice(256 + 128 * p, 384 + 128 * p)
            q, grad = qb[rows, lanes], gm[rows, lanes]
            keys = [kvb[wide, lanes], kvo[wide, lanes]]
            values = [kvb[wide, value_lanes], kvo[wide, value_lanes]]
            outs = []
            for h in range(2):
                q_h, grad_h = only(head_lanes(h), q), only(head_lanes(h), grad)
                probs = [prob[k, 4 * j + 2 * p + h, :, wide].astype(jnp.float32) for k in range(2)]
                back = [nt(grad_h, v) for v in values]
                dot = split_sum(probs[0] * back[0]) + split_sum(probs[1] * back[1])
                slopes = [(share * (b - dot)).astype(jnp.bfloat16) for share, b in zip(probs, back)]
                outs.append(nn(slopes[0], keys[0]) + nn(slopes[1], keys[1]))
                for k, acc in enumerate((dkv, dkvo)):
                    acc[wide, lanes] += tn(slopes[k], q_h) * 0.125
                    acc[wide, value_lanes] += tn(prob[k, 4 * j + 2 * p + h, :, wide], grad_h)
            dp[rows, lanes] = (jnp.where(head_lanes(0), outs[0], outs[1]) * 0.125).astype(jnp.bfloat16)
        kvs[rows, :] = dkvo[rows, :].astype(jnp.bfloat16)
        kv_copy(j).start()

    attend_back(3)
    attend_back(2)
    attend_back(1)
    attend_back(0)
    to_y(0, md, xd, sd, yd)
    weight_grad(n1, dp.at[:, 0:256], mq, tq)
    core_copy(3, tq, rq).start()
    turn_to_x(1, mu, xu, su, yu)
    vmine[0:1, :] = jnp.zeros((1, 1024), jnp.float32)
    vmine[2:3, :] = jnp.zeros((1, 1024), jnp.float32)
    vmine[4:8, :] = jnp.zeros((4, 1024), jnp.float32)
    for j in (3, 2, 1, 0):
        rows = slice(128 * j, 128 * j + 128)
        kv_copy(j).wait_recv()
        dp[rows, 256:768] = (dkv[rows, :] + kvr[rows, :].astype(jnp.float32)).astype(jnp.bfloat16)
    weight_grad(n1, dp.at[:, 256:768], mkv, tkv)
    core_copy(4, tkv, rkv).start()
    fin_z(7, bd, y_total(0, sd, yd))
    to_y(2, mo, xo, so, yo)

    def piece_of(mine):
        def at_piece(q):
            return mine.at[lax.div(q, 8), lax.rem(lax.div(q, 2), 4), pl.ds(pl.multiple_of(32 * lax.rem(q, 2), 32), 32)]

        return at_piece

    def slot_of(got):
        return lambda q: got.at[q]

    def to_plane(phase, mine, got):
        plane.start(phase, piece_of(mine), slot_of(got))
        got[at.m] = mine[at.yl, at.x, pl.ds(pl.multiple_of(32 * yh, 32), 32), :]

    def plane_total(phase, got):
        plane.wait(phase, slot_of(got))
        acc = got[0].astype(jnp.float32)
        for q in range(1, 16):
            acc += got[q].astype(jnp.float32)
        return acc.astype(jnp.bfloat16)

    join_cores(3, mq, tq, rq)
    to_plane(0, mq, rp)
    join_cores(4, mkv, tkv, rkv)
    to_plane(3, mkv, rpkv)

    def last(i, carry):
        d = order(3 - i)
        j = line.index(d)
        values = dp[block(j), :]
        for n in range(4):
            tile = slice(n * 256, (n + 1) * 256)
            ps2[block(j), tile] = nt(values, tall_tile(wq, n)).astype(jnp.bfloat16)

        @pl.when(i < 3)
        def _():
            line.give(3, d, ps2, pr2)

        return carry

    lax.fori_loop(0, 4, last, 0)

    def out_copy(d):
        return line.copy(4, d, outz.at[4 + line.index(d)], outz.at[z])

    fin_z(8, bu, x_total(1, su, yu))
    total_out = y_total(2, so, yo)
    for n in range(4):
        outz[4 + n] = total_out[:, 256 * n : 256 * n + 256].astype(jnp.bfloat16)

    for d in (1, 3, 2):
        out_copy(d).start()
    for j in range(4):
        part = ps2[block(j), :].astype(jnp.float32)
        vmine[0:1, :] += jnp.sum(part * xh[block(j), :], axis=0, keepdims=True)
        vmine[2:3, :] += jnp.sum(part, axis=0, keepdims=True)
    give_core = remote(vmine, vcore, vs.at[0], vr.at[0], at.other)
    give_core.start()
    fin_y(7, bd)

    def tile_of(q):
        return vmine.at[:, pl.ds(pl.multiple_of(128 * lax.div(q, 2), 128), 128)]

    give_core.wait()
    vmine[...] += vcore[...]
    plane.start(1, tile_of, slot_of(vplane))
    vplane[at.m] = vmine[:, pl.ds(pl.multiple_of(128 * col, 128), 128)]
    sendr[...] = pieces_of(mid[...] + gate[:, 0:1] * line.total(6, ps3, pr3))
    plane.start(2, piece(sendr), piece(arrr))
    keep_piece(at, sendr, arrr)
    fin_y(8, bu)
    acc = outz[4 + z].astype(jnp.float32)
    for d in (1, 3, 2):
        line.got(4, d, outz.at[line.index(d)])
        acc += outz[line.index(d)].astype(jnp.float32)
    fin_z(9, bo, acc)
    bq[at.s, :, 0:256] = plane_total(0, rp)
    bq[at.s, :, 256:768] = plane_total(3, rpkv)
    everyone.start(0, bq)
    fin_y(9, bo)
    plane.wait(1, slot_of(vplane))
    vline[z] = jnp.sum(vplane[...], axis=0)

    def vec_copy(d):
        return line.copy(5, d, vline.at[z], vline.at[z])

    for d in (1, 3, 2):
        vec_copy(d).start()
    grad_normed = line.total(3, ps2, pr2)
    scale = norm_parts(xa[block(z), :].astype(jnp.float32))[1]
    gx[...] += norm_back(grad_normed, gains[0:1, :], xh[block(z), :], scale)
    plane.wait(2, piece(arrr))
    left, right = placings(route[0:1, :])
    res[...] = from_pieces(left, right, arrr[...])
    fin_wait(7, bd)
    fin_wait(8, bu)
    for d in (1, 3, 2):
        line.got(5, d, vline.at[line.index(d)])
    gvec[...] = jnp.sum(vline[...], axis=0)
    fin_wait(9, bo)
    everyone.wait(0, bq)
    if_swapped = jnp.logical_not(at.same)
    pl.when(if_swapped)(lambda: give_vec.wait())
    line.sent_all(0, ghs)
    line.sent(1, ps)
    line.sent(3, ps2)
    line.sent(6, ps3)
    for d in (1, 3, 2):
        gm_copy(d).wait_send()
        out_copy(d).wait_send()
        vec_copy(d).wait_send()
        for phase, mine, x_got, part, y_got in ((0, md, xd, sd, yd), (2, mo, xo, so, yo)):
            x_copy(phase, d, mine, x_got).wait_send()
            y_copy(phase, d, part, y_got).wait_send()
        y_first(1, d, mu, xu).wait_send()
        x_second(1, d, su, yu).wait_send()
    for j in range(4):
        kv_copy(j).wait_send()
    plane.sent(0, piece_of(mq), slot_of(rp))
    plane.sent(3, piece_of(mkv), slot_of(rpkv))
    plane.sent(1, tile_of, slot_of(vplane))
    plane.sent(2, piece(sendr), piece(arrr))
    everyone.sent(0, bq)
    for phase, buf in ((7, bd), (8, bu), (9, bo)):
        fin_mate(phase, buf).wait_send()
        for d in (1, 3, 2):
            fin_copy(phase, d, buf).wait_send()

    @pl.when(jnp.logical_not(at.same))
    def _():
        for swap in swaps:
            swap.wait()


def dense_backward_call(gh, after, docs, gains, mixed, route, mid, gate, vec_sum, saved, ps, gin0, gout0):
    bf, f32 = jnp.bfloat16, jnp.float32
    vmem, anywhere = pl.BlockSpec(memory_space=pltpu.VMEM), pl.BlockSpec(memory_space=pl.ANY)
    smem = pl.BlockSpec(memory_space=pltpu.SMEM)
    shape, V, dma = jax.ShapeDtypeStruct, pltpu.VMEM, pltpu.SemaphoreType.DMA
    line, pieces = [V((512, 1024), bf)], [V((256, 512), bf)]
    wide, narrow = [V((2, 4, 64, 1024), bf)], [V((2, 4, 64, 256), bf), V((2, 4, 64, 512), bf)]
    return pl.pallas_call(
        dense_backward_kernel,
        out_shape=[
            shape((128, 1024), f32), shape((2, 4, 32, 1024), bf), shape((2, 4, 32, 1024), bf),
            shape((2, 4, 32, 256), bf), shape((8, 32, 768), bf), shape((8, 128), f32), shape((128, 1024), bf),
            shape((8, 1024), f32), shape((1024, 512), bf),
            shape((512, 1024), bf),
        ],
        in_specs=[vmem, vmem, smem] + [vmem] * 6 + [anywhere] * 15,
        out_specs=[vmem] * 8 + [anywhere] * 2,
        scratch_shapes=[
            *(line * 2), V((512, 1024), f32), *(line * 3), V((512, 1024), f32), *line,
            V((512, 256), bf), V((512, 512), bf), V((512, 512), bf),
            V((2, 4, 2, 2, 32, 768), bf), *([V((2, 4, 2, 2, 32, 1024), bf)] * 3),
            *(line * 6), V((2, 16, 128, 512), bf),
            V((128, 1024), bf), V((512, 256), bf), V((512, 768), bf), V((512, 512), f32), V((512, 512), f32),
            V((512, 512), bf), V((512, 512), bf),
            *(wide * 3), *narrow, *(wide * 3), *narrow, *(wide * 3), *narrow,
            V((4, 2, 64, 1024), bf), V((4, 4, 32, 1024), bf), V((4, 2, 64, 1024), bf),
            V((2, 64, 1024), bf), V((4, 32, 1024), bf), V((2, 64, 1024), bf), *([V((4, 32, 1024), bf)] * 3),
            V((16, 32, 256), bf), V((16, 32, 512), bf), *(pieces * 2),
            V((8, 1024), f32), V((8, 1024), f32), V((16, 8, 128), f32), V((4, 8, 128), f32),
            V((8, 32, 256), bf),
            dma((13,)), dma((10, 6)), dma((10, 6)), dma((3, 3)), dma((3, 3)), dma((3, 3)), dma((3, 3)), dma((4,)),
            dma((4,)), dma((5,)), dma((5,)), dma((4, 15)), dma((4, 15)), dma((1, 7)), dma((1, 7)), dma((3,)),
            dma((3,)), dma((1,)), dma((1,)), dma((10,)), dma((10,)),
        ],
        compiler_params=pltpu.CompilerParams(collective_id=3, has_side_effects=True, vmem_limit_bytes=62 << 20),
        name="dense_backward",
    )(gh, after, docs, gains, mixed, route, mid, gate, vec_sum, *saved, ps, gin0, gout0)


def finish_kernel(
    gvec, vec_sum, vec_swap, res, gx, bd, bu, bo, bq, in0, in1, out0, out1, swapped_in, swapped_out,
    ng, nb, eg, eb, cen, o_res, o_gx, o_gq, o_go, o_gu, o_gd, o_in, o_out,
    b_in, b_out, f_in, f_out, vd, vu, vo, vq, gq, go, gu, gd, vres, vgx, isem, osem,
):
    at = Place()
    swapped = [
        pltpu.make_async_copy(swapped_in, b_in.at[0], isem.at[0]),
        pltpu.make_async_copy(swapped_out, b_out.at[0], isem.at[2]),
    ]
    pairs = [
        (in0, b_in.at[0]), (in1, b_in.at[1]), (out0, b_out.at[0]), (out1, b_out.at[1]), (bd, vd), (bu, vu), (bo, vo),
        (bq, vq), (res, vres), (gx, vgx),
    ]
    loads = [pltpu.make_async_copy(src, dst, isem.at[k]) for k, (src, dst) in enumerate(pairs)]

    @pl.when(at.same)
    def _():
        loads[0].start()
        loads[2].start()

    @pl.when(jnp.logical_not(at.same))
    def _():
        for copy in swapped:
            copy.start()

    for k in (1, 3, 4, 5, 6, 7, 8, 9):
        loads[k].start()
    c = at.c
    mine = jnp.where(c == 0, gvec[0:4, 0:64], gvec[0:4, 64:128])
    ng[...] = mine[0:2]
    nb[...] = mine[2:4]
    vectors = jnp.where(at.same, vec_sum[...], vec_swap[...])
    eg[...] = vectors[0:2]
    eb[...] = vectors[2:4]
    cen[...] = vectors[4:5]
    stores = []

    def store(src, dst):
        stores.append(pltpu.make_async_copy(src, dst, osem.at[len(stores)]))
        stores[-1].start()

    for k in range(4):
        loads[k].wait()
        low, wide, out = ((b_in, f_in, o_in), (b_out, f_out, o_out))[k // 2]
        wide[k % 2] = low[k % 2].astype(jnp.float32)
        store(wide.at[k % 2], out.at[k % 2])
    for k in range(4, 10):
        loads[k].wait()
    store(vres, o_res)
    store(vgx, o_gx)
    lane = lax.broadcasted_iota(jnp.int32, (32, 128), 1) < 64
    for half in range(2):
        rows = slice(32 * half, 32 * half + 32)
        for z in range(4):
            gd[64 * z + 32 * half : 64 * z + 32 * half + 32, :] = vd[half, z].astype(jnp.float32)
            go[rows, 256 * z : 256 * z + 256] = vo[half, z].astype(jnp.float32)
            for part in range(3):
                gq[rows, 1024 * part + 256 * z : 1024 * part + 256 * z + 256] = vq[
                    2 * z + half, :, 256 * part : 256 * part + 256
                ].astype(jnp.float32)
        for n in range(8):
            tile = slice(128 * n, 128 * n + 128)
            quarter = [vu[half, z, :, tile].astype(jnp.float32) for z in range(4)]
            turned = [pltpu.roll(v, 64, 1) for v in quarter]
            first = 512 * n
            gu[rows, first : first + 128] = jnp.where(lane, quarter[0], turned[1])
            gu[rows, first + 128 : first + 256] = jnp.where(lane, quarter[2], turned[3])
            gu[rows, first + 256 : first + 384] = jnp.where(lane, turned[0], quarter[1])
            gu[rows, first + 384 : first + 512] = jnp.where(lane, turned[2], quarter[3])
    for src, dst in ((gq, o_gq), (go, o_go), (gu, o_gu), (gd, o_gd)):
        store(src, dst)
    for copy in stores:
        copy.wait()


def finish_call(gvec, vec_sum, vec_swap, res, gx, bd, bu, bo, bq, in0, in1, out0, out1, swapped_in, swapped_out):
    bf, f32 = jnp.bfloat16, jnp.float32
    vmem, anywhere = pl.BlockSpec(memory_space=pltpu.VMEM), pl.BlockSpec(memory_space=pl.ANY)
    shape, V, dma = jax.ShapeDtypeStruct, pltpu.VMEM, pltpu.SemaphoreType.DMA
    return pl.pallas_call(
        finish_kernel,
        out_shape=[
            shape((2, 64), f32), shape((2, 64), f32), shape((2, 1024), f32), shape((2, 1024), f32),
            shape((1, 1024), f32), shape((128, 1024), bf), shape((128, 1024), f32), shape((64, 3072), f32),
            shape((64, 1024), f32), shape((64, 4096), f32), shape((256, 1024), f32), shape((2, 1024, 512), f32),
            shape((2, 512, 1024), f32),
        ],
        in_specs=[vmem] * 3 + [anywhere] * 12,
        out_specs=[vmem] * 5 + [anywhere] * 8,
        scratch_shapes=[
            V((2, 1024, 512), bf), V((2, 512, 1024), bf), V((2, 1024, 512), f32), V((2, 512, 1024), f32),
            V((2, 4, 32, 1024), bf), V((2, 4, 32, 1024), bf), V((2, 4, 32, 256), bf), V((8, 32, 768), bf),
            V((64, 3072), f32), V((64, 1024), f32), V((64, 4096), f32), V((256, 1024), f32),
            V((128, 1024), bf), V((128, 1024), f32), dma((10,)), dma((10,)),
        ],
        compiler_params=pltpu.CompilerParams(vmem_limit_bytes=62 << 20),
        name="finish",
    )(gvec, vec_sum, vec_swap, res, gx, bd, bu, bo, bq, in0, in1, out0, out1, swapped_in, swapped_out)


def on_device(
    inputs,
    doc_starts,
    route,
    norm_gain,
    norm_bias,
    w_qkv,
    w_out,
    w_up,
    w_down,
    exp_gain,
    exp_bias,
    exp_in,
    exp_out,
    centroid,
    cotangent,
):
    tok_rows, width = 128, 1024
    x = inputs.reshape(tok_rows, width)
    cot = cotangent.reshape(tok_rows, width)
    slots = route.reshape(1, tok_rows)
    hidden, mixed, after, gains, *saved, cz, in0, out0 = dense_forward_call(
        x, norm_gain, norm_bias, doc_starts, slots, cot, w_qkv, w_out, w_up, w_down, exp_in[0], exp_out[0]
    )
    grad_hidden, vec_sum, mid, gate, part, grad_in1, grad_out1, grad_in0, grad_out0 = expert_call(
        hidden, slots, exp_gain[0], exp_bias[0], centroid, cz, exp_in[0], exp_out[0], in0, out0
    )
    grad_x, down, up, out, qkv, norm_grads, result, vec_swap, swapped_in, swapped_out = dense_backward_call(
        grad_hidden, after, doc_starts, gains, mixed, slots, mid, gate, vec_sum, saved, part, grad_in0, grad_out0
    )
    gain, bias, e_gain, e_bias, center, result, grad_x, g_qkv, g_out, g_up, g_down, e_in, e_out = finish_call(
        norm_grads,
        vec_sum,
        vec_swap,
        result,
        grad_x,
        down,
        up,
        out,
        qkv,
        grad_in0,
        grad_in1,
        grad_out0,
        grad_out1,
        swapped_in,
        swapped_out,
    )
    return (
        result[None],
        grad_x[None],
        gain,
        bias,
        g_qkv,
        g_out,
        g_up,
        g_down,
        e_gain[None],
        e_bias[None],
        e_in[None],
        e_out[None],
        center,
    )


def solution(mesh):
    in_specs = (
        P("fsdp", "seq", None),
        P("fsdp", None),
        P("fsdp", "seq", None),
        P(None, "fsdp"),
        P(None, "fsdp"),
        P("fsdp", None),
        P("fsdp", None),
        P("fsdp", None),
        P("fsdp", None),
        P("fsdp", None, None),
        P("fsdp", None, None),
        P("fsdp", None, None, "seq"),
        P("fsdp", None, "seq", None),
        P("fsdp", None),
        P("fsdp", "seq", None),
    )
    out_specs = (
        P("fsdp", "seq", None),
        P("fsdp", "seq", None),
        P(None, "fsdp"),
        P(None, "fsdp"),
        P("fsdp", None),
        P("fsdp", None),
        P("fsdp", None),
        P("fsdp", None),
        P("fsdp", None, None),
        P("fsdp", None, None),
        P("fsdp", None, None, "seq"),
        P("fsdp", None, "seq", None),
        P("fsdp", None),
    )
    return jax.shard_map(
        on_device, mesh=mesh, in_specs=in_specs, out_specs=out_specs, check_vma=False
    )
```

```python
import jax
import jax.numpy as jnp
from jax import lax
from jax.experimental import pallas as pl
from jax.experimental.pallas import tpu as pltpu
from jax.sharding import PartitionSpec as P

MESH = pl.DeviceIdType.MESH
epsilon = 1e-05
masked_score = -1e30


def split_sum(values):
    return jnp.sum(values, axis=-1, keepdims=True)


def norm_parts(values):
    average = split_sum(values) * (1.0 / values.shape[-1])
    centered = values - average
    spread = split_sum(centered * centered) * (1.0 / values.shape[-1])
    scale = lax.rsqrt(spread + epsilon)
    return centered * scale, scale


def norm_back(grad_normed, gain, xhat, scale):
    width = 1.0 / xhat.shape[-1]
    u = grad_normed * gain
    return scale * (u - split_sum(u) * width - xhat * (split_sum(u * xhat) * width))


def gelu_parts(pre):
    inner = 0.7978845608028654
    cubic = 0.044715
    square = pre * pre
    t = jnp.tanh(inner * pre * (1.0 + cubic * square))
    half = 0.5 * (1.0 + t)
    slope = half + 0.5 * pre * (1.0 - t * t) * (inner * (1.0 + 3.0 * cubic * square))
    return pre * half, slope


def nn(a, b):
    return lax.dot_general(a, b, (((1,), (0,)), ((), ())), preferred_element_type=jnp.float32)


def nt(a, b):
    return lax.dot_general(a, b, (((1,), (1,)), ((), ())), preferred_element_type=jnp.float32)


def tn(a, b):
    return lax.dot_general(a, b, (((0,), (0,)), ((), ())), preferred_element_type=jnp.float32)


def remote(src, dst, send, recv, device):
    return pltpu.make_async_remote_copy(
        src_ref=src, dst_ref=dst, send_sem=send, recv_sem=recv, device_id=device, device_id_type=MESH
    )


def greet(bar, device):
    pl.semaphore_signal(bar, inc=1, device_id=device, device_id_type=MESH)


def block(index):
    return pl.ds(pl.multiple_of(index * 128, 128), 128)


def order(i):
    return i + lax.div(i, 2) - 2 * lax.div(i, 3)


class Place:
    def __init__(self):
        self.s, self.f = lax.axis_index("seq"), lax.axis_index("fsdp")
        self.z, self.yh = lax.div(self.s, 2), lax.rem(self.s, 2)
        self.yl, self.col, self.c = lax.div(self.f, 8), lax.div(self.f, 2), lax.rem(self.f, 2)
        self.x = lax.rem(self.col, 4)
        self.m = self.f - self.c + self.yh
        self.other = (self.s, self.f + 1 - 2 * self.c)
        self.mate = (2 * self.z + 1 - self.yh, self.f)
        self.swap_mate = (2 * self.z + 1 - self.yh, self.f + 1 - 2 * self.c)
        self.same = self.c == self.yh


class Ring:
    def __init__(self, at, axis, send, recv):
        self.at, self.axis, self.send, self.recv = at, axis, send, recv
        self.pos = {"z": at.z, "x": at.x, "y": 2 * at.yh + at.yl}[axis]

    def index(self, d):
        return lax.rem(self.pos + d, 4)

    def device(self, j):
        at = self.at
        if self.axis == "z":
            return (2 * j + at.yh, at.f)
        if self.axis == "x":
            return (at.s, at.f - 2 * at.x + 2 * j)
        return (2 * at.z + lax.div(j, 2), 8 * lax.rem(j, 2) + at.f - 8 * at.yl)

    def copy(self, phase, d, src, dst):
        sems = self.send.at[phase, d - 1], self.recv.at[phase, d - 1]
        return remote(src, dst, *sems, self.device(self.index(d)))

    def got(self, phase, d, dst):
        sems = self.send.at[phase, 3 - d], self.recv.at[phase, 3 - d]
        remote(dst, dst, *sems, self.device(self.index(d))).wait_recv()

    def spread(self, phase, buf):
        own = buf.at[block(self.pos)]
        for d in (1, 3, 2):
            self.copy(phase, d, own, own).start()

    def half(self, buf, d, upper):
        return buf.at[pl.ds(pl.multiple_of(128 * self.index(d) + 64 * upper, 64), 64)]

    def moving(self, phase, slot, rows, up):
        to = self.device(self.index(1 if up else 3))
        return remote(rows, rows, self.send.at[phase, slot], self.recv.at[phase, slot], to)

    def parts(self, phase, buf):
        for slot, up, upper in ((2, 0, 0), (0, 1, 1), (3, 0, 1), (1, 1, 0)):
            yield self.moving(phase, slot, self.half(buf, 0, upper), up)

    def onward(self, phase, buf, up):
        return self.moving(phase, 4 + up, self.half(buf, 3 if up else 1, up), up)

    def begin(self, phase, buf):
        for part in self.parts(phase, buf):
            part.start()

    def relay(self, phase, buf):
        for up in (0, 1):
            self.moving(phase, 0 if up else 2, self.half(buf, 3 if up else 1, up), up).wait_recv()
            self.onward(phase, buf, up).start()

    def above(self, phase, buf):
        self.moving(phase, 3, self.half(buf, 1, 1), 0).wait_recv()

    def below(self, phase, buf):
        self.moving(phase, 1, self.half(buf, 3, 0), 1).wait_recv()

    def far(self, phase, buf):
        for up in (0, 1):
            self.moving(phase, 4 + up, self.half(buf, 2, up), up).wait_recv()

    def ready(self, phase, i, buf):
        @pl.when(i == 1)
        def _():
            self.relay(phase, buf)
            self.above(phase, buf)

        pl.when(i == 2)(lambda: self.below(phase, buf))
        pl.when(i == 3)(lambda: self.far(phase, buf))

    def sent_all(self, phase, buf):
        for part in self.parts(phase, buf):
            part.wait_send()
        for up in (0, 1):
            self.onward(phase, buf, up).wait_send()

    def arrived(self, phase, d, buf):
        self.got(phase, d, buf.at[block(self.index(d))])

    def give(self, phase, d, src, dst):
        self.copy(phase, d, src.at[block(self.index(d))], dst.at[block(self.pos)]).start()

    def sent(self, phase, buf):
        own = buf.at[block(self.pos)]
        for d in (1, 3, 2):
            self.copy(phase, d, own, own).wait_send()

    def total(self, phase, own, parts):
        acc = own[block(self.pos), :].astype(jnp.float32)
        for d in (1, 3, 2):
            self.arrived(phase, d, parts)
            acc += parts[block(self.index(d)), :].astype(jnp.float32)
        return acc


class Plane:
    def __init__(self, at, send, recv):
        self.at, self.m = at, at.m
        self.send, self.recv = send, recv

    def device(self, q):
        return (2 * self.at.z + lax.rem(q, 2), q - lax.rem(q, 2) + self.at.c)

    def greet(self, bar):
        def one(i, carry):
            greet(bar, self.device(lax.rem(self.m + i + 1, 16)))
            return carry

        lax.fori_loop(0, 15, one, 0)

    def copy(self, phase, i, src_of, dst_of):
        q = lax.rem(self.m + i + 1, 16)
        return remote(src_of(q), dst_of(self.m), self.send.at[phase, i], self.recv.at[phase, i], self.device(q))

    def start(self, phase, src_of, dst_of):
        def one(i, carry):
            self.copy(phase, i, src_of, dst_of).start()
            return carry

        lax.fori_loop(0, 15, one, 0)

    def wait(self, phase, dst_of):
        def one(i, carry):
            q = lax.rem(self.m + 15 - i, 16)
            dst = dst_of(q)
            remote(dst, dst, self.send.at[phase, i], self.recv.at[phase, i], self.device(q)).wait_recv()
            return carry

        lax.fori_loop(0, 15, one, 0)

    def sent(self, phase, src_of, dst_of):
        def one(i, carry):
            self.copy(phase, i, src_of, dst_of).wait_send()
            return carry

        lax.fori_loop(0, 15, one, 0)


def piece(buf):
    return lambda q: buf.at[pl.ds(pl.multiple_of(q * 16, 16), 16)]


def keep_piece(at, src, dst):
    own = pl.ds(pl.multiple_of(at.m * 16, 16), 16)
    dst[own, :] = src[own, :]


def placings(route):
    row = lax.broadcasted_iota(jnp.int32, (256, 128), 0)
    inner = row & 15
    slot = (row >> 4) * 8 + (inner & 7)
    hit = slot == route
    left = jnp.where(hit & (inner < 8), 1.0, 0.0).astype(jnp.bfloat16)
    right = jnp.where(hit & (inner >= 8), 1.0, 0.0).astype(jnp.bfloat16)
    return left, right


def to_pieces(left, right, rows):
    half = rows.shape[1] // 2
    return (nn(left, rows[:, :half]) + nn(right, rows[:, half:])).astype(jnp.bfloat16)


def from_pieces(left, right, pieces):
    return jnp.concatenate([tn(left, pieces), tn(right, pieces)], axis=1).astype(jnp.bfloat16)


def rows_of(pieces):
    wide = pieces.astype(jnp.float32).reshape(16, 2, 8, 512)
    return jnp.concatenate([wide[:, 0].reshape(128, 512), wide[:, 1].reshape(128, 512)], axis=1)


def pieces_of(rows):
    left = rows[:, :512].reshape(16, 1, 8, 512)
    right = rows[:, 512:].reshape(16, 1, 8, 512)
    return jnp.concatenate([left, right], axis=1).reshape(256, 512).astype(jnp.bfloat16)


class Gather:
    def __init__(self, at, phase, first, src, full, xs, xr, ys, yr, ks, kr):
        self.at, self.phase, self.src, self.full = at, phase, src, full
        self.x_first = first == "x"
        self.rings = [Ring(at, "y", ys, yr), Ring(at, "x", xs, xr)]
        if self.x_first:
            self.rings.reverse()
        self.ks, self.kr = ks, kr

    def pushed(self, d):
        at = self.at
        return self.rings[0].copy(self.phase, d, self.src, self.full.at[at.yl, at.x, at.c, at.yh])

    def passed(self, d):
        at = self.at
        own = self.full.at[at.yl, :, at.c, at.yh] if self.x_first else self.full.at[:, at.x, at.c]
        return self.rings[1].copy(self.phase, d, own, own)

    def core(self, c):
        half = self.full.at[:, :, c]
        return remote(half, half, self.ks.at[self.phase], self.kr.at[self.phase], self.at.other)

    def start(self):
        at = self.at
        for d in (1, 3, 2):
            self.pushed(d).start()
        self.full[at.yl, at.x, at.c, at.yh] = self.src[...]

    def turn(self):
        at, full = self.at, self.full
        for d in (1, 3, 2):
            j = self.rings[0].index(d)
            dst = full.at[at.yl, j, at.c, at.yh] if self.x_first else full.at[lax.rem(j, 2), at.x, at.c, lax.div(j, 2)]
            self.rings[0].got(self.phase, d, dst)
        for d in (1, 3, 2):
            self.passed(d).start()

    def share(self):
        at, full = self.at, self.full
        for d in (1, 3, 2):
            j = self.rings[1].index(d)
            dst = full.at[lax.rem(j, 2), :, at.c, lax.div(j, 2)] if self.x_first else full.at[:, j, at.c]
            self.rings[1].got(self.phase, d, dst)
        self.core(at.c).start()

    def wait(self):
        self.core(1 - self.at.c).wait_recv()

    def sent(self):
        for d in (1, 3, 2):
            self.pushed(d).wait_send()
            self.passed(d).wait_send()
        self.core(self.at.c).wait_send()


def labels(position, first, second):
    return jnp.where(position >= first, 1, 0) + jnp.where(position >= second, 1, 0)


def mask(j, yh, parity, docs):
    first, second = docs[0, 0], docs[0, 1]
    wide = 128 * (j + 1)
    row = lax.broadcasted_iota(jnp.int32, (128, wide), 0) + 128 * (2 * j + yh)
    lane = lax.broadcasted_iota(jnp.int32, (128, wide), 1)
    key = (lane >> 7) * 256 + (lane & 127) + 128 * parity
    return (key <= row) & (labels(key, first, second) == labels(row, first, second))


def masked_scores(q, keys, seen):
    return jnp.where(seen, nt(q, keys) * 0.125, masked_score)


def probabilities(q, keys, seen):
    scores = [masked_scores(q, k, ok) for k, ok in zip(keys, seen)]
    top = jnp.maximum(
        jnp.max(scores[0], axis=-1, keepdims=True), jnp.max(scores[1], axis=-1, keepdims=True)
    )
    weights = [jnp.exp(s - top) for s in scores]
    inverse = 1.0 / (split_sum(weights[0]) + split_sum(weights[1]))
    return [w * inverse for w in weights]


def head_lanes(h):
    lane = lax.broadcasted_iota(jnp.int32, (128, 128), 1)
    return lane < 64 if h == 0 else lane >= 64


def only(keep, values):
    return jnp.where(keep, values.astype(jnp.float32), 0.0).astype(jnp.bfloat16)


def wide_tile(full, tile):
    part = full[:, :, :, :, :, tile]
    return part.reshape(1024, part.shape[-1])


def tall_tile(full, n):
    part = full[n // 2, 2 * (n % 2) : 2 * (n % 2) + 2]
    return part.reshape(256, part.shape[-1])


def dense_forward_kernel(
    x, gain, bias, docs, route, cot, w_qkv, w_out, w_up, w_down, exp_in, exp_out,
    hid, mixed, after, gains,
    o_x, o_n1, o_n2, o_act, o_dg, o_q, o_kv, o_kvo, o_wq, o_wo, o_wu, o_wd, o_cz, o_in0, o_out0,
    sq, su, wq, wo, wu, wd, gtile, gmine, gother,
    xa, n1, n2, cz, qb, kvb, kvo, mixs, act, dg, ps, pr, sendc, arrc, stats, own_sum,
    zs, zr, xs, xr, ys, yr, kvs, kvr, ks, kr, gs, gr, cs, cr, ss, sr, osem,
):
    at = Place()
    z, yh, c, col = at.z, at.yh, at.c, at.col
    line, plane = Ring(at, "z", zs, zr), Plane(at, cs, cr)
    bar = pltpu.get_barrier_semaphore()
    for d in (1, 2, 3):
        greet(bar, line.device(line.index(d)))
    greet(bar, at.other)
    greet(bar, at.swap_mate)
    plane.greet(bar)
    xa[block(z), :] = x[...]
    for part in range(3):
        sq[:, 256 * part : 256 * part + 256] = w_qkv[:, pl.ds(pl.multiple_of(1024 * part + 256 * z, 256), 256)]
    gtile[...] = jnp.zeros_like(gtile)
    for k, ref in enumerate((gain, bias)):
        values = ref[...].astype(jnp.float32)
        none = jnp.zeros_like(values)
        here = jnp.where(c == 0, jnp.concatenate([values, none], 1), jnp.concatenate([none, values], 1))
        gtile[2 * k : 2 * k + 2, :] = here
    half = pl.ds(pl.multiple_of(32 * yh, 32), 32)
    down_rows = w_down.at[pl.ds(pl.multiple_of(64 * z + 32 * yh, 32), 32)]
    sems = (xs, xr, ys, yr, ks, kr)
    left_q, right_q = (wq.at[:, :, :, :, :, 0:384], wq.at[:, :, :, :, :, 384:768])
    qkv_a = Gather(at, 0, "y", sq.at[half, 0:384], left_q, *sems)
    qkv_b = Gather(at, 1, "x", sq.at[half, 384:768], right_q, *sems)
    out = Gather(at, 2, "y", w_out.at[half], wo, *sems)
    up = Gather(at, 3, "y", su.at[half], wu, *sems)
    down = Gather(at, 4, "x", down_rows, wd, *sems)
    low = lax.broadcasted_iota(jnp.int32, (64, 128), 1) < 64
    odd = lax.rem(z, 2) == 1
    for n in range(8):
        first = 512 * n + 128 * lax.div(z, 2)
        a = w_up[:, pl.ds(pl.multiple_of(first, 128), 128)].astype(jnp.float32)
        b = w_up[:, pl.ds(pl.multiple_of(first + 256, 128), 128)].astype(jnp.float32)
        kept = jnp.where(low, a, pltpu.roll(b, 64, 1))
        moved = jnp.where(low, pltpu.roll(a, 64, 1), b)
        su[:, 128 * n : 128 * n + 128] = jnp.where(odd, moved, kept).astype(jnp.bfloat16)
    left, right = placings(route[0:1, :])
    sendc[...] = to_pieces(left, right, cot[...])
    pl.semaphore_wait(bar, 20)
    line.begin(0, xa)
    tile_at = pl.ds(pl.multiple_of(128 * col, 128), 128)

    def gain_copy(i):
        to = (at.s, 2 * lax.rem(col + i + 1, 8) + c)
        return remote(gtile, gmine.at[:, tile_at], gs.at[i], gr.at[i], to)

    def push_gain(i, carry):
        gain_copy(i).start()
        return carry

    lax.fori_loop(0, 7, push_gain, 0)
    gmine[:, tile_at] = gtile[...]
    qkv_a.start()
    qkv_b.start()
    plane.start(0, piece(sendc), piece(arrc))
    keep_piece(at, sendc, arrc)
    qkv_a.turn()
    qkv_b.turn()
    for weight in (out, up, down):
        weight.start()
    line.relay(0, xa)

    def wait_gain(i, carry):
        q = lax.rem(col + 7 - i, 8)
        dst = gmine.at[:, pl.ds(pl.multiple_of(128 * q, 128), 128)]
        remote(dst, dst, gs.at[i], gr.at[i], (at.s, 2 * q + c)).wait_recv()
        return carry

    lax.fori_loop(0, 7, wait_gain, 0)
    gain_core = remote(gmine, gother, gs.at[7], gr.at[7], at.other)
    gain_core.start()
    gain_core.wait_recv()
    gains[...] = gmine[...] + gother[...]
    qkv_a.share()
    qkv_b.share()
    out.turn()
    up.turn()

    def kv_copy(i, j):
        return remote(kvb.at[block(j)], kvo.at[block(j)], kvs.at[i], kvr.at[i], at.mate)

    def project_qkv(i, carry):
        j = line.index(order(i))
        pl.when(i == 1)(lambda: line.above(0, xa))
        pl.when(i == 2)(lambda: line.below(0, xa))
        pl.when(i == 3)(lambda: line.far(0, xa))
        xhat = norm_parts(xa[block(j), :].astype(jnp.float32))[0]
        n1[block(j), :] = (xhat * gains[0:1, :] + gains[2:3, :]).astype(jnp.bfloat16)

        @pl.when(i == 0)
        def _():
            qkv_a.wait()
            qkv_b.wait()

        values = n1[block(j), :]
        kvb[block(j), 0:256] = nn(values, wide_tile(wq, slice(256, 512))).astype(jnp.bfloat16)
        kvb[block(j), 256:512] = nn(values, wide_tile(wq, slice(512, 768))).astype(jnp.bfloat16)
        kv_copy(i, j).start()
        qb[block(j), :] = nn(values, wide_tile(wq, slice(0, 256))).astype(jnp.bfloat16)
        return carry

    lax.fori_loop(0, 4, project_qkv, 0)
    down.turn()
    plane.wait(0, piece(arrc))
    cz[block(z), :] = rows_of(arrc[...]).astype(jnp.bfloat16)
    line.spread(4, cz)

    def heads(j, keys, parity):
        seen = mask(j, yh, parity, docs)
        wide = slice(0, 128 * (j + 1))
        for p in range(2):
            lanes = slice(128 * p, 128 * p + 128)
            q = qb[128 * j : 128 * j + 128, lanes]
            for h in range(2):
                scores = masked_scores(only(head_lanes(h), q), keys[wide, lanes], seen)
                yield 4 * j + 2 * p + h, h, lanes, scores, keys[wide, 256 + 128 * p : 384 + 128 * p]

    first = None
    for j in range(4):
        for k, h, lanes, scores, values in heads(j, kvb, yh):
            top = jnp.max(scores, axis=-1, keepdims=True)
            weights = jnp.exp(scores - top)
            stats[k] = jnp.where(head_lanes(0), top, split_sum(weights))
            summed = nn(weights.astype(jnp.bfloat16), values)
            if h == 0:
                first = summed
            else:
                own_sum[128 * j : 128 * j + 128, lanes] = jnp.where(head_lanes(0), first, summed)
    for i in range(4):
        kv_copy(i, line.index(order(i))).wait_recv()
    swaps = [
        remote(exp_in.at[0], o_in0, ss.at[0], sr.at[0], at.swap_mate),
        remote(exp_out.at[0], o_out0, ss.at[1], sr.at[1], at.swap_mate),
    ]

    @pl.when(c != yh)
    def _():
        swaps[0].start()

    my_lanes = pl.ds(pl.multiple_of(256 * z, 256), 256)

    def mix_copy(d):
        return line.copy(1, d, mixs.at[block(line.index(d))], mixed.at[:, my_lanes])

    for j in range(4):
        rows = slice(128 * j, 128 * j + 128)
        for k, h, lanes, scores, values in heads(j, kvo, 1 - yh):
            top, total = stats[k][:, 0:1], stats[k][:, 64:65]
            new_top = jnp.maximum(top, jnp.max(scores, axis=-1, keepdims=True))
            kept = jnp.exp(top - new_top)
            weights = jnp.exp(scores - new_top)
            inverse = 1.0 / (total * kept + split_sum(weights))
            summed = (own_sum[rows, lanes] * kept + nn(weights.astype(jnp.bfloat16), values)) * inverse
            if h == 0:
                first = summed
            else:
                mixs[rows, lanes] = jnp.where(head_lanes(0), first, summed).astype(jnp.bfloat16)
        pl.when(z != j)(lambda: mix_copy(lax.rem(j + 4 - z, 4)).start())
    mixed[:, my_lanes] = mixs[block(z), :]
    out.share()
    out.wait()
    for d in (1, 3, 2):
        line.got(1, d, mixed.at[:, pl.ds(pl.multiple_of(256 * line.index(d), 256), 256)])
    for n in range(4):
        tile = slice(256 * n, 256 * n + 256)
        after[:, tile] = x[:, tile].astype(jnp.float32) + nn(mixed[...], wide_tile(wo, tile))
    xhat = norm_parts(after[...])[0]
    n2[block(z), :] = (xhat * gains[1:2, :] + gains[3:4, :]).astype(jnp.bfloat16)
    line.begin(2, n2)
    up.share()
    down.share()
    @pl.when(c != yh)
    def _():
        swaps[1].start()

    up.wait()
    down.wait()
    stores = [
        pltpu.make_async_copy(src, dst, osem.at[k])
        for k, (src, dst) in enumerate(
            [(xa, o_x), (n1, o_n1), (qb, o_q), (kvb, o_kv), (kvo, o_kvo), (wq, o_wq), (wo, o_wo), (wu, o_wu), (wd, o_wd)]
        )
    ]
    for store in stores:
        store.start()

    def feed(i, carry):
        d = order(i)
        j = line.index(d)
        line.ready(2, i, n2)
        values = n2[block(j), :]
        for n in range(4):
            tile = slice(n * 256, (n + 1) * 256)
            acted, slope = gelu_parts(nn(values, wide_tile(wu, tile)))
            act[block(j), tile] = acted.astype(jnp.bfloat16)
            dg[block(j), tile] = slope
        values = act[block(j), :]
        for n in range(4):
            tile = slice(n * 256, (n + 1) * 256)
            ps[block(j), tile] = nn(values, wide_tile(wd, tile)).astype(jnp.bfloat16)

        @pl.when(i > 0)
        def _():
            line.give(3, d, ps, pr)

        return carry

    lax.fori_loop(0, 4, feed, 0)
    for d in (1, 3, 2):
        line.arrived(4, d, cz)
    late = [
        pltpu.make_async_copy(src, dst, osem.at[9 + k])
        for k, (src, dst) in enumerate([(n2, o_n2), (act, o_act), (dg, o_dg), (cz, o_cz)])
    ]
    for store in late:
        store.start()
    gain_core.wait_send()

    def sent_gain(i, carry):
        gain_copy(i).wait_send()
        return carry

    lax.fori_loop(0, 7, sent_gain, 0)
    for weight in (qkv_a, qkv_b, out, up, down):
        weight.sent()
    for i in range(4):
        kv_copy(i, line.index(order(i))).wait_send()
    line.sent_all(0, xa)
    for d in (1, 3, 2):
        mix_copy(d).wait_send()
    line.sent_all(2, n2)
    line.sent(4, cz)
    plane.sent(0, piece(sendc), piece(arrc))
    hid[...] = (after[...] + line.total(3, ps, pr)).astype(jnp.bfloat16)
    line.sent(3, ps)

    @pl.when(c != yh)
    def _():
        for swap in swaps:
            swap.wait()

    for store in stores + late:
        store.wait()


def dense_forward_call(x, gain, bias, docs, route, cot, w_qkv, w_out, w_up, w_down, exp_in, exp_out):
    bf, f32 = jnp.bfloat16, jnp.float32
    vmem, anywhere = pl.BlockSpec(memory_space=pltpu.VMEM), pl.BlockSpec(memory_space=pl.ANY)
    smem = pl.BlockSpec(memory_space=pltpu.SMEM)
    shape, V, dma = jax.ShapeDtypeStruct, pltpu.VMEM, pltpu.SemaphoreType.DMA
    line = [V((512, 1024), bf)]
    weight = [(2, 4, 2, 2, 32, 768)] + [(2, 4, 2, 2, 32, 1024)] * 3
    saved = [
        shape((512, 1024), bf), shape((512, 1024), bf), shape((512, 1024), bf), shape((512, 1024), bf),
        shape((512, 1024), f32), shape((512, 256), bf), shape((512, 512), bf), shape((512, 512), bf),
    ] + [shape(w, bf) for w in weight] + [
        shape((512, 1024), bf), shape((1024, 512), bf), shape((512, 1024), bf),
    ]
    return pl.pallas_call(
        dense_forward_kernel,
        out_shape=[shape((128, 1024), bf), shape((128, 1024), bf), shape((128, 1024), f32), shape((8, 1024), f32)]
        + saved,
        in_specs=[vmem] * 3 + [smem] + [vmem] * 6 + [anywhere, anywhere],
        out_specs=[vmem] * 4 + [anywhere] * len(saved),
        scratch_shapes=[
            V((64, 768), bf), V((64, 1024), bf), *[V(w, bf) for w in weight], V((8, 128), f32), V((8, 1024), f32),
            V((8, 1024), f32),
            *(line * 4), V((512, 256), bf), V((512, 512), bf), V((512, 512), bf), V((512, 256), bf),
            *line, V((512, 1024), f32), *(line * 2), V((256, 512), bf), V((256, 512), bf),
            V((16, 128, 128), f32), V((512, 256), f32), dma((5, 6)), dma((5, 6)), dma((5, 3)), dma((5, 3)), dma((5, 3)), dma((5, 3)), dma((4,)), dma((4,)),
            dma((5,)), dma((5,)), dma((8,)), dma((8,)), dma((1, 15)), dma((1, 15)), dma((3,)), dma((3,)), dma((13,)),
        ],
        compiler_params=pltpu.CompilerParams(collective_id=2, has_side_effects=True, vmem_limit_bytes=60 << 20),
        name="dense_forward",
    )(x, gain, bias, docs, route, cot, w_qkv, w_out, w_up, w_down, exp_in, exp_out)


def expert_kernel(
    hid, route, exp_gain, exp_bias, centroid, cz_h, exp_in, exp_out, in0, out0,
    gh, vecg, mid, gate_out, o_ps, gin1, gout1, gin0, gout0,
    w_in, w_out, sendh, sendg, arrh, arrg, cz,
    e0, e1, g0, g1, ps0, ps1, pr0, pb0, pb1,
    act0, act1, dg0, dg1, gp0, gp1,
    arrived, base, xh0, xh1, sc, gates, dots, dots_in,
    ga_in, ga_out, sb_in, sb_out, rb_in, rb_out, vec, vec_own, vec_other, vmine, vcore, vline,
    wsem, zs, zr, cs, cr, ks, kr, osem, bs, br, ss, sr, vs, vr,
):
    at = Place()
    z, yh, c, same = at.z, at.yh, at.c, at.same
    line, plane = Ring(at, "z", zs, zr), Plane(at, cs, cr)
    bar = pltpu.get_barrier_semaphore()
    plane.greet(bar)
    for d in (1, 2, 3):
        greet(bar, line.device(line.index(d)))
    greet(bar, at.other)
    greet(bar, at.swap_mate)
    low, high = slice(0, 512), slice(512, 1024)

    def slot(k, i, half):
        return w_in.at[k, :, half] if i == 0 else w_out.at[k, half, :]

    def load(k, i):
        return pltpu.make_async_copy((exp_in, exp_out)[i].at[k], slot(k, i, low), wsem.at[k, i])

    def swapped(k, i):
        return pltpu.make_async_copy((in0, out0)[i], slot(k, i, low), wsem.at[k, i])

    swap_out = remote(exp_out.at[1], slot(1, 1, low), ss.at[0], sr.at[0], at.swap_mate)
    swap_in = remote(exp_in.at[1], slot(1, 0, low), ss.at[3], sr.at[3], at.swap_mate)

    def share(k, i):
        return remote(slot(k, i, low), slot(k, i, high), bs.at[k, i], br.at[k, i], at.other)

    def on_either(when_same, when_swapped):
        pl.when(same)(when_same)
        pl.when(jnp.logical_not(same))(when_swapped)

    load_c = pltpu.make_async_copy(cz_h, cz, wsem.at[2, 0])

    def begin_same():
        for k, i in ((0, 0), (0, 1), (1, 0), (1, 1)):
            load(k, i).start()

    def begin_swapped():
        for k, i in ((0, 0), (0, 1)):
            swapped(k, i).start()

    on_either(begin_same, begin_swapped)
    load_c.start()
    left, right = placings(route[0:1, :])
    sendh[...] = to_pieces(left, right, hid[...])
    vec_own[0:2, :] = exp_gain[...].astype(jnp.float32)
    vec_own[2:4, :] = exp_bias[...].astype(jnp.float32)
    vec_own[4:5, :] = centroid[...].astype(jnp.float32)
    vec_own[5:8, :] = jnp.zeros((3, 1024), jnp.float32)
    pl.semaphore_wait(bar, 20)
    plane.start(0, piece(sendh), piece(arrh))
    keep_piece(at, sendh, arrh)
    trade = remote(vec_own, vec_other, vs.at[2], vr.at[2], at.other)
    trade.start()

    def wait_loads(k, i):
        on_either(lambda: load(k, i).wait(), lambda: swapped(k, i).wait())
        share(k, i).start()

    wait_loads(0, 0)
    wait_loads(0, 1)
    trade.wait()
    vec[...] = jnp.where(same, vec_own[...], vec_other[...])
    plane.wait(0, piece(arrh))
    gain = [vec[0:1, :], vec[1:2, :]]
    bias = [vec[2:3, :], vec[3:4, :]]
    rows = rows_of(arrh[...])
    arrived[...] = rows
    xhat, scale = norm_parts(rows)
    xh0[...] = xhat
    sc[0] = jnp.broadcast_to(scale, (128, 128))
    e0[block(z), :] = (xhat * gain[0] + bias[0]).astype(jnp.bfloat16)
    line.begin(0, e0)

    @pl.when(jnp.logical_not(same))
    def _():
        swap_in.start()
        swap_out.start()

    gating = jax.nn.sigmoid(split_sum(rows * vec[4:5, :]))
    gates[z] = jnp.broadcast_to(gating, (128, 128))

    def gate_copy(d):
        return line.copy(3, d, gates.at[z], gates.at[z])

    for d in (1, 3, 2):
        gate_copy(d).start()
    share(0, 0).wait_recv()
    share(0, 1).wait_recv()
    load_c.wait()

    def forward(k, j, rows_in, act, dg):
        values = rows_in[block(j), :]
        for n in range(4):
            tile = slice(n * 256, (n + 1) * 256)
            pre = nn(values, w_in[k, :, tile])
            acted, slope = gelu_parts(pre)
            act[block(j), tile] = acted.astype(jnp.bfloat16)
            dg[block(j), tile] = slope

    def project(k, j, act, part):
        values = act[block(j), :]
        for n in range(4):
            tile = slice(n * 256, (n + 1) * 256)
            part[block(j), tile] = nn(values, w_out[k, :, tile]).astype(jnp.bfloat16)

    def backward(k, j, grad, dg, gp, part):
        values = grad[block(j), :]
        for n in range(4):
            tile = slice(n * 256, (n + 1) * 256)
            slope = dg[block(j), tile] * nt(values, w_out[k, tile, :])
            gp[block(j), tile] = slope.astype(jnp.bfloat16)
        pres = gp[block(j), :]
        for n in range(4):
            tile = slice(n * 256, (n + 1) * 256)
            part[block(j), tile] = nt(pres, w_in[k, tile, :]).astype(jnp.bfloat16)

    def sub0(i, carry):
        d = order(i)
        j = line.index(d)

        line.ready(0, i, e0)
        forward(0, j, e0, act0, dg0)
        project(0, j, act0, ps0)

        @pl.when(i > 0)
        def _():
            line.give(1, d, ps0, pr0)

        return carry

    lax.fori_loop(0, 4, sub0, 0)
    on_either(lambda: load(1, 0).wait(), lambda: swap_in.wait())
    share(1, 0).start()
    on_either(lambda: load(1, 1).wait(), lambda: swap_out.wait())
    share(1, 1).start()
    stream = arrived[...] + line.total(1, ps0, pr0)
    base[...] = stream
    xhat, scale = norm_parts(stream)
    xh1[...] = xhat
    sc[1] = jnp.broadcast_to(scale, (128, 128))
    e1[block(z), :] = (xhat * gain[1] + bias[1]).astype(jnp.bfloat16)
    line.begin(2, e1)
    gate = gates[z][:, 0:1]
    mid[...] = arrived[...] + gate * (base[...] - arrived[...])
    gate_out[...] = gates[z]
    line.sent(1, ps0)
    share(1, 0).wait_recv()
    share(1, 1).wait_recv()

    def sub1(i, carry):
        d = order(i)
        j = line.index(d)

        @pl.when(i > 0)
        def _():
            line.got(3, d, gates.at[j])

        g1[block(j), :] = (gates[j][:, 0:1] * cz[block(j), :].astype(jnp.float32)).astype(jnp.bfloat16)

        line.ready(2, i, e1)
        forward(1, j, e1, act1, dg1)
        backward(1, j, g1, dg1, gp1, ps0)

        @pl.when(i > 0)
        def _():
            line.give(4, d, ps0, pb1)

        return carry

    lax.fori_loop(0, 4, sub1, 0)

    def second_part(i, carry):
        d = order(3 - i)
        j = line.index(d)
        project(1, j, act1, ps1)
        products = cz[block(j), :].astype(jnp.float32) * ps1[block(j), :].astype(jnp.float32)
        dots[j] = jnp.broadcast_to(split_sum(products), (128, 128))

        @pl.when(i < 3)
        def _():
            line.copy(5, d, dots.at[j], dots_in.at[z]).start()

        return carry

    lax.fori_loop(0, 4, second_part, 0)
    keep_ps = pltpu.make_async_copy(ps1, o_ps, wsem.at[2, 1])
    keep_ps.start()

    def weight_grads(k, rows_in, gp, act, grad):
        def one(n, carry):
            tile = pl.ds(pl.multiple_of(n * 256, 256), 256)
            tile_b = pl.ds(pl.multiple_of(n * 256 + 512, 256), 256)
            ga_out[k, tile, :] = tn(act[:, tile], grad[...])
            sb_out[k, tile, :] = tn(act[:, tile_b], grad[...]).astype(jnp.bfloat16)
            return carry

        lax.fori_loop(0, 2, one, 0)

        def two(n, carry):
            tile = pl.ds(pl.multiple_of(n * 256, 256), 256)
            ga_in[k, tile, :] = tn(rows_in[:, tile], gp[:, 0:512])
            sb_in[k, tile, :] = tn(rows_in[:, tile], gp[:, 512:1024]).astype(jnp.bfloat16)
            return carry

        lax.fori_loop(0, 4, two, 0)

    def swap(k, i):
        src, dst = ((sb_in, rb_in), (sb_out, rb_out))[i]
        return remote(src.at[k], dst.at[k], ks.at[k, i], kr.at[k, i], at.other)

    def join_cores(k):
        for i in range(2):
            swap(k, i).wait()
        sb_in[k] = (ga_in[k] + rb_in[k].astype(jnp.float32)).astype(jnp.bfloat16)
        sb_out[k] = (ga_out[k] + rb_out[k].astype(jnp.float32)).astype(jnp.bfloat16)

    weight_grads(1, e1, gp1, act1, g1)
    swap(1, 0).start()
    swap(1, 1).start()
    grad_normed = line.total(4, ps0, pb1)
    cot = cz[block(z), :].astype(jnp.float32)
    grad_stream = gates[z][:, 0:1] * cot
    grad_stream += norm_back(grad_normed, gain[1], xh1[...], sc[1][:, 0:1])
    g0[block(z), :] = grad_stream.astype(jnp.bfloat16)
    line.begin(6, g0)
    vmine[1:2, :] = jnp.sum(grad_normed * xh1[...], axis=0, keepdims=True)
    vmine[3:4, :] = jnp.sum(grad_normed, axis=0, keepdims=True)
    line.sent(4, ps0)
    grad_gating = split_sum(cot * (base[...] - arrived[...])) + dots[z][:, 0:1]
    for d in (1, 3, 2):
        line.got(5, d, dots_in.at[line.index(d)])
        grad_gating += dots_in[line.index(d)][:, 0:1]
    gate = gates[z][:, 0:1]
    grad_logit = gate * (1.0 - gate) * grad_gating
    vmine[4:5, :] = jnp.sum(grad_logit * arrived[...], axis=0, keepdims=True)
    base[...] = grad_stream + (1.0 - gate) * cot + grad_logit * vec[4:5, :]
    join_cores(1)
    kept = [
        pltpu.make_async_copy(sb_in.at[1], gin1, osem.at[1, 0]),
        pltpu.make_async_copy(sb_out.at[1], gout1, osem.at[1, 1]),
    ]
    given = [
        remote(sb_in.at[1], gin1, ss.at[1], sr.at[1], at.swap_mate),
        remote(sb_out.at[1], gout1, ss.at[2], sr.at[2], at.swap_mate),
    ]

    def begin(copies):
        for copy in copies:
            copy.start()

    def finish(copies):
        for copy in copies:
            copy.wait()

    on_either(lambda: begin(kept), lambda: begin(given))

    def sub0_back(i, carry):
        d = order(i)
        j = line.index(d)

        line.ready(6, i, g0)
        backward(0, j, g0, dg0, gp0, ps0)

        @pl.when(i > 0)
        def _():
            line.give(7, d, ps0, pb0)

        return carry

    lax.fori_loop(0, 4, sub0_back, 0)
    weight_grads(0, e0, gp0, act0, g0)
    swap(0, 0).start()
    swap(0, 1).start()
    grad_normed = line.total(7, ps0, pb0)
    grad_stream = base[...] + norm_back(grad_normed, gain[0], xh0[...], sc[0][:, 0:1])
    sendg[...] = pieces_of(grad_stream)
    plane.start(1, piece(sendg), piece(arrg))
    keep_piece(at, sendg, arrg)
    vmine[0:1, :] = jnp.sum(grad_normed * xh0[...], axis=0, keepdims=True)
    vmine[2:3, :] = jnp.sum(grad_normed, axis=0, keepdims=True)
    vmine[5:8, :] = jnp.zeros((3, 1024), jnp.float32)
    give_core = remote(vmine, vcore, vs.at[0], vr.at[0], at.other)
    give_core.start()
    give_core.wait_recv()
    vline[z] = vmine[...] + vcore[...]

    def give_line(d):
        return line.copy(8, d, vline.at[z], vline.at[z])

    for d in (1, 3, 2):
        give_line(d).start()
    join_cores(0)
    stores = [
        pltpu.make_async_copy(sb_in.at[0], gin0, osem.at[0, 0]),
        pltpu.make_async_copy(sb_out.at[0], gout0, osem.at[0, 1]),
    ]
    begin(stores)
    plane.wait(1, piece(arrg))
    left, right = placings(route[0:1, :])
    gh[...] = from_pieces(left, right, arrg[...])
    for d in (1, 3, 2):
        line.got(8, d, vline.at[line.index(d)])
    vecg[...] = vline[0] + vline[1] + vline[2] + vline[3]
    give_core.wait_send()
    for d in (1, 3, 2):
        give_line(d).wait_send()
        gate_copy(d).wait_send()
        line.copy(5, d, dots.at[line.index(d)], dots_in.at[z]).wait_send()
    for k in (0, 1):
        for i in range(2):
            share(k, i).wait_send()
    line.sent_all(0, e0)
    line.sent_all(2, e1)
    line.sent_all(6, g0)
    line.sent(7, ps0)
    plane.sent(0, piece(sendh), piece(arrh))
    plane.sent(1, piece(sendg), piece(arrg))
    keep_ps.wait()
    finish(stores)
    on_either(lambda: finish(kept), lambda: finish(given))


def expert_call(hid, route, exp_gain, exp_bias, centroid, cz, exp_in, exp_out, in0, out0):
    bf, f32 = jnp.bfloat16, jnp.float32
    vmem, anywhere = pl.BlockSpec(memory_space=pltpu.VMEM), pl.BlockSpec(memory_space=pl.ANY)
    shape, V, dma = jax.ShapeDtypeStruct, pltpu.VMEM, pltpu.SemaphoreType.DMA
    line, rows, pieces = [V((512, 1024), bf)], [V((128, 1024), f32)], [V((256, 512), bf)]
    wide, small = [V((512, 1024), f32)], [V((4, 128, 128), f32)]
    vectors = [V((8, 1024), f32)]
    return pl.pallas_call(
        expert_kernel,
        out_shape=(
            shape((128, 1024), bf), shape((8, 1024), f32), shape((128, 1024), f32), shape((128, 128), f32),
            shape((512, 1024), bf), shape((1024, 512), bf), shape((512, 1024), bf), shape((1024, 512), bf),
            shape((512, 1024), bf),
        ),
        in_specs=[vmem] * 5 + [anywhere] * 5,
        out_specs=tuple([vmem] * 4 + [anywhere] * 5),
        scratch_shapes=[
            V((2, 1024, 1024), bf), V((2, 1024, 1024), bf), *(pieces * 4), *line,
            *(line * 9), *(line * 2), *(wide * 2), *(line * 2),
            *(rows * 4), *(small * 4),
            V((2, 1024, 512), f32), V((2, 512, 1024), f32),
            V((2, 1024, 512), bf), V((2, 512, 1024), bf), V((2, 1024, 512), bf), V((2, 512, 1024), bf),
            *(vectors * 5), V((4, 8, 1024), f32),
            dma((3, 2)), dma((9, 6)), dma((9, 6)), dma((2, 15)), dma((2, 15)), dma((2, 2)), dma((2, 2)), dma((2, 2)),
            dma((2, 2)), dma((2, 2)), dma((4,)), dma((4,)), dma((3,)), dma((3,)),
        ],
        compiler_params=pltpu.CompilerParams(collective_id=1, has_side_effects=True, vmem_limit_bytes=60 << 20),
        name="experts",
    )(hid, route, exp_gain, exp_bias, centroid, cz, exp_in, exp_out, in0, out0)


class Everyone:
    def __init__(self, at, send, recv):
        self.at, self.send, self.recv = at, send, recv

    def copy(self, phase, i, buf):
        own = buf.at[self.at.s]
        to = (lax.rem(self.at.s + i + 1, 8), self.at.f)
        return remote(own, own, self.send.at[phase, i], self.recv.at[phase, i], to)

    def start(self, phase, buf):
        for i in range(7):
            self.copy(phase, i, buf).start()

    def wait(self, phase, buf):
        for i in range(7):
            q = lax.rem(self.at.s + 7 - i, 8)
            dst = buf.at[q]
            remote(dst, dst, self.send.at[phase, i], self.recv.at[phase, i], (q, self.at.f)).wait_recv()

    def sent(self, phase, buf):
        for i in range(7):
            self.copy(phase, i, buf).wait_send()


def dense_backward_kernel(
    gh, after, docs, gains, mixed, route, mid, gate, vec_sum, x_h, n1_h, n2_h, act_h, dg_h, q_h, kv_h, kvo_h, wq_h, wo_h, wu_h,
    wd_h, ps_h, gin0, gout0,
    gx, bd, bu, bo, bq, gvec, res, vec_swap, fin0, fout0,
    ghs, xa, xh, n1, n2, act, dg, gp, qb, kvb, kvo, wq, wo, wu, wd,
    ps, pr, ps2, pr2, ps3, pr3, prob, gms, gm, dp, dkv, dkvo, kvs, kvr,
    md, mu, mo, mq, mkv, td, tu, to, tq, tkv, rd, ru, ro, rq, rkv, xd, xu, xo, sd, su, so, yd, yu, yo, rp, rpkv, sendr, arrr,
    vmine, vcore, vplane, vline, outz,
    lsem, zs, zr, xs, xr, ys, yr, kvss, kvsr, ks, kr, cs, cr, qs, qr, ss, sr, vs, vr, fs, fr,
):
    at = Place()
    z, yh, c, col = at.z, at.yh, at.c, at.col
    line, ring_x, ring_y = Ring(at, "z", zs, zr), Ring(at, "x", xs, xr), Ring(at, "y", ys, yr)
    plane, everyone = Plane(at, cs, cr), Everyone(at, qs, qr)
    bar = pltpu.get_barrier_semaphore()
    plane.greet(bar)
    for d in (1, 2, 3):
        greet(bar, line.device(line.index(d)))
        greet(bar, (2 * line.index(d) + 1 - yh, at.f))
    greet(bar, at.other)
    greet(bar, at.swap_mate)
    loads = [
        pltpu.make_async_copy(src, dst, lsem.at[k])
        for k, (src, dst) in enumerate(
            [
                (q_h, qb), (kv_h, kvb), (kvo_h, kvo), (wd_h, wd), (dg_h, dg), (wu_h, wu), (act_h, act), (n2_h, n2),
                (wo_h, wo), (ps_h, ps3), (wq_h, wq), (n1_h, n1), (x_h, xa),
            ]
        )
    ]
    for load in loads:
        load.start()
    ghs[block(z), :] = gh[...]
    pl.semaphore_wait(bar, 23)
    line.begin(0, ghs)
    swaps = [
        remote(gin0, fin0, ss.at[0], sr.at[0], at.swap_mate),
        remote(gout0, fout0, ss.at[1], sr.at[1], at.swap_mate),
    ]
    give_vec = remote(vec_sum, vec_swap, ss.at[2], sr.at[2], at.swap_mate)

    @pl.when(jnp.logical_not(at.same))
    def _():
        give_vec.start()
        for swap in swaps:
            swap.start()

    for load in loads[:3]:
        load.wait()
    for j in range(4):
        seen = [mask(j, yh, parity, docs) for parity in (yh, 1 - yh)]
        wide = slice(0, 128 * (j + 1))
        for p in range(2):
            lanes = slice(128 * p, 128 * p + 128)
            keys = [kvb[wide, lanes], kvo[wide, lanes]]
            q = qb[128 * j : 128 * j + 128, lanes]
            for h in range(2):
                found = probabilities(only(head_lanes(h), q), keys, seen)
                for k in range(2):
                    prob[k, 4 * j + 2 * p + h, :, wide] = found[k].astype(jnp.bfloat16)
    for load in loads[3:6]:
        load.wait()

    def feed(i, carry):
        d = order(i)
        j = line.index(d)

        line.ready(0, i, ghs)
        values = ghs[block(j), :]
        for n in range(4):
            tile = slice(n * 256, (n + 1) * 256)
            gp[block(j), tile] = (dg[block(j), tile] * nt(values, tall_tile(wd, n))).astype(jnp.bfloat16)
        pres = gp[block(j), :]
        for n in range(4):
            tile = slice(n * 256, (n + 1) * 256)
            ps[block(j), tile] = nt(pres, tall_tile(wu, n)).astype(jnp.bfloat16)

        @pl.when(i > 0)
        def _():
            line.give(1, d, ps, pr)

        return carry

    lax.fori_loop(0, 4, feed, 0)
    for load in loads[6:10]:
        load.wait()

    def weight_grad(lhs, rhs, mine, theirs):
        def one(n, carry):
            rows = lhs[:, pl.ds(pl.multiple_of(n * 256, 256), 256)]
            grad = tn(rows, rhs[...])
            for half in range(2):
                first = grad[128 * half : 128 * half + 64].astype(jnp.bfloat16)
                second = grad[128 * half + 64 : 128 * half + 128].astype(jnp.bfloat16)
                here = lax.div(n, 2), 2 * lax.rem(n, 2) + half
                mine[here] = jnp.where(c == 0, first, second)
                theirs[here] = jnp.where(c == 0, second, first)
            return carry

        lax.fori_loop(0, 4, one, 0)

    def core_copy(phase, src, dst):
        return remote(src, dst, ks.at[phase], kr.at[phase], at.other)

    def join_cores(phase, mine, theirs, got):
        core_copy(phase, theirs, got).wait()

        def one(n, carry):
            here = lax.div(n, 4), lax.rem(n, 4)
            mine[here] = (mine[here].astype(jnp.float32) + got[here].astype(jnp.float32)).astype(jnp.bfloat16)
            return carry

        lax.fori_loop(0, 8, one, 0)

    def x_copy(phase, d, mine, dst):
        return ring_x.copy(phase, d, mine.at[:, ring_x.index(d)], dst.at[at.x])

    def y_copy(phase, d, part, dst):
        j = ring_y.index(d)
        src = part.at[lax.rem(j, 2), pl.ds(pl.multiple_of(32 * lax.div(j, 2), 32), 32)]
        return ring_y.copy(phase, d, src, dst.at[ring_y.pos])

    def to_x(phase, mine, dst):
        for d in (1, 3, 2):
            x_copy(phase, d, mine, dst).start()

    def to_y(phase, mine, got, part, dst):
        acc = mine[:, at.x].astype(jnp.float32)
        for d in (1, 3, 2):
            j = ring_x.index(d)
            ring_x.got(phase, d, got.at[j])
            acc += got[j].astype(jnp.float32)
        part[...] = acc.astype(jnp.bfloat16)
        for d in (1, 3, 2):
            y_copy(phase, d, part, dst).start()

    def fin_copy(phase, d, buf):
        own = buf.at[yh, z]
        return line.copy(phase, d, own, own)

    def fin_mate(phase, buf):
        own = buf.at[yh]
        return remote(own, own, fs.at[phase], fr.at[phase], at.mate)

    def fin_z(phase, buf, values):
        buf[yh, z] = values.astype(jnp.bfloat16)
        for d in (1, 3, 2):
            fin_copy(phase, d, buf).start()

    def fin_y(phase, buf):
        for d in (1, 3, 2):
            line.got(phase, d, buf.at[yh, line.index(d)])
        fin_mate(phase, buf).start()

    def fin_wait(phase, buf):
        dst = buf.at[1 - yh]
        remote(dst, dst, fs.at[phase], fr.at[phase], at.mate).wait_recv()

    def y_total(phase, part, got):
        acc = part[at.yl, pl.ds(pl.multiple_of(32 * yh, 32), 32), :].astype(jnp.float32)
        for d in (1, 3, 2):
            j = ring_y.index(d)
            ring_y.got(phase, d, got.at[j])
            acc += got[j].astype(jnp.float32)
        return acc

    def y_first(phase, d, mine, dst):
        j = ring_y.index(d)
        src = mine.at[lax.rem(j, 2), :, pl.ds(pl.multiple_of(32 * lax.div(j, 2), 32), 32)]
        return ring_y.copy(phase, d, src, dst.at[ring_y.pos])

    def x_second(phase, d, part, dst):
        return ring_x.copy(phase, d, part.at[ring_x.index(d)], dst.at[at.x])

    def turn_to_x(phase, mine, got, part, dst):
        acc = mine[at.yl, :, pl.ds(pl.multiple_of(32 * yh, 32), 32), :].astype(jnp.float32)
        for d in (1, 3, 2):
            j = ring_y.index(d)
            ring_y.got(phase, d, got.at[j])
            acc += got[j].astype(jnp.float32)
        part[...] = acc.astype(jnp.bfloat16)
        for d in (1, 3, 2):
            x_second(phase, d, part, dst).start()

    def x_total(phase, part, got):
        acc = part[at.x].astype(jnp.float32)
        for d in (1, 3, 2):
            j = ring_x.index(d)
            ring_x.got(phase, d, got.at[j])
            acc += got[j].astype(jnp.float32)
        return acc

    weight_grad(act, ghs, md, td)
    core_copy(0, td, rd).start()
    weight_grad(n2, gp, mu, tu)
    core_copy(1, tu, ru).start()
    join_cores(0, md, td, rd)
    to_x(0, md, xd)
    join_cores(1, mu, tu, ru)
    for d in (1, 3, 2):
        y_first(1, d, mu, xu).start()
    grad_normed = line.total(1, ps, pr)
    xhat, scale = norm_parts(after[...])
    vmine[1:2, :] = jnp.sum(grad_normed * xhat, axis=0, keepdims=True)
    vmine[3:4, :] = jnp.sum(grad_normed, axis=0, keepdims=True)
    grad_after = gh[...].astype(jnp.float32) + norm_back(grad_normed, gains[1:2, :], xhat, scale)
    gx[...] = grad_after
    grad_attn = grad_after.astype(jnp.bfloat16)
    for n in range(4):
        gms[:, 256 * n : 256 * n + 256] = nt(grad_attn, tall_tile(wo, n)).astype(jnp.bfloat16)

    def gm_copy(d):
        lanes = pl.ds(pl.multiple_of(256 * line.index(d), 256), 256)
        return line.copy(2, d, gms.at[:, lanes], gm.at[block(z)])

    for d in (1, 3, 2):
        gm_copy(d).start()
    gm[block(z), :] = gms[:, pl.ds(pl.multiple_of(256 * z, 256), 256)]
    gp[block(0), :] = grad_attn
    weight_grad(mixed, gp.at[block(0)], mo, to)
    core_copy(2, to, ro).start()
    for load in loads[10:]:
        load.wait()
    for j in range(4):
        xh[block(j), :] = norm_parts(xa[block(j), :].astype(jnp.float32))[0]
    join_cores(2, mo, to, ro)
    to_x(2, mo, xo)
    for d in (1, 3, 2):
        line.arrived(2, d, gm)
    for d in (1, 3, 2):
        line.give(6, d, ps3, pr3)
    dkv[...] = jnp.zeros_like(dkv)
    dkvo[...] = jnp.zeros_like(dkvo)

    def kv_copy(j):
        return remote(kvs.at[block(j)], kvr.at[block(j)], kvss.at[j], kvsr.at[j], at.mate)

    def attend_back(j):
        wide = slice(0, 128 * (j + 1))
        rows = slice(128 * j, 128 * j + 128)
        for p in range(2):
            lanes = slice(128 * p, 128 * p + 128)
            value_lanes = slice(256 + 128 * p, 384 + 128 * p)
            q, grad = qb[rows, lanes], gm[rows, lanes]
            keys = [kvb[wide, lanes], kvo[wide, lanes]]
            values = [kvb[wide, value_lanes], kvo[wide, value_lanes]]
            outs = []
            for h in range(2):
                q_h, grad_h = only(head_lanes(h), q), only(head_lanes(h), grad)
                probs = [prob[k, 4 * j + 2 * p + h, :, wide].astype(jnp.float32) for k in range(2)]
                back = [nt(grad_h, v) for v in values]
                dot = split_sum(probs[0] * back[0]) + split_sum(probs[1] * back[1])
                slopes = [(share * (b - dot)).astype(jnp.bfloat16) for share, b in zip(probs, back)]
                outs.append(nn(slopes[0], keys[0]) + nn(slopes[1], keys[1]))
                for k, acc in enumerate((dkv, dkvo)):
                    acc[wide, lanes] += tn(slopes[k], q_h) * 0.125
                    acc[wide, value_lanes] += tn(prob[k, 4 * j + 2 * p + h, :, wide], grad_h)
            dp[rows, lanes] = (jnp.where(head_lanes(0), outs[0], outs[1]) * 0.125).astype(jnp.bfloat16)
        kvs[rows, :] = dkvo[rows, :].astype(jnp.bfloat16)
        kv_copy(j).start()

    attend_back(3)
    attend_back(2)
    attend_back(1)
    attend_back(0)
    to_y(0, md, xd, sd, yd)
    weight_grad(n1, dp.at[:, 0:256], mq, tq)
    core_copy(3, tq, rq).start()
    vmine[0:1, :] = jnp.zeros((1, 1024), jnp.float32)
    vmine[2:3, :] = jnp.zeros((1, 1024), jnp.float32)
    vmine[4:8, :] = jnp.zeros((4, 1024), jnp.float32)
    for j in (3, 2, 1, 0):
        rows = slice(128 * j, 128 * j + 128)
        kv_copy(j).wait_recv()
        dp[rows, 256:768] = (dkv[rows, :] + kvr[rows, :].astype(jnp.float32)).astype(jnp.bfloat16)
    weight_grad(n1, dp.at[:, 256:768], mkv, tkv)
    core_copy(4, tkv, rkv).start()
    turn_to_x(1, mu, xu, su, yu)
    fin_z(7, bd, y_total(0, sd, yd))
    to_y(2, mo, xo, so, yo)

    def piece_of(mine):
        def at_piece(q):
            return mine.at[lax.div(q, 8), lax.rem(lax.div(q, 2), 4), pl.ds(pl.multiple_of(32 * lax.rem(q, 2), 32), 32)]

        return at_piece

    def slot_of(got):
        return lambda q: got.at[q]

    def to_plane(phase, mine, got):
        plane.start(phase, piece_of(mine), slot_of(got))
        got[at.m] = mine[at.yl, at.x, pl.ds(pl.multiple_of(32 * yh, 32), 32), :]

    def plane_total(phase, got):
        plane.wait(phase, slot_of(got))
        acc = got[0].astype(jnp.float32)
        for q in range(1, 16):
            acc += got[q].astype(jnp.float32)
        return acc.astype(jnp.bfloat16)

    join_cores(3, mq, tq, rq)
    to_plane(0, mq, rp)
    join_cores(4, mkv, tkv, rkv)
    to_plane(3, mkv, rpkv)

    def last(i, carry):
        d = order(3 - i)
        j = line.index(d)
        values = dp[block(j), :]
        for n in range(4):
            tile = slice(n * 256, (n + 1) * 256)
            ps2[block(j), tile] = nt(values, tall_tile(wq, n)).astype(jnp.bfloat16)

        @pl.when(i < 3)
        def _():
            line.give(3, d, ps2, pr2)

        return carry

    lax.fori_loop(0, 4, last, 0)

    def out_copy(d):
        return line.copy(4, d, outz.at[4 + line.index(d)], outz.at[z])

    fin_z(8, bu, x_total(1, su, yu))
    total_out = y_total(2, so, yo)
    for n in range(4):
        outz[4 + n] = total_out[:, 256 * n : 256 * n + 256].astype(jnp.bfloat16)

    for d in (1, 3, 2):
        out_copy(d).start()
    for j in range(4):
        part = ps2[block(j), :].astype(jnp.float32)
        vmine[0:1, :] += jnp.sum(part * xh[block(j), :], axis=0, keepdims=True)
        vmine[2:3, :] += jnp.sum(part, axis=0, keepdims=True)
    give_core = remote(vmine, vcore, vs.at[0], vr.at[0], at.other)
    give_core.start()
    fin_y(7, bd)

    def tile_of(q):
        return vmine.at[:, pl.ds(pl.multiple_of(128 * lax.div(q, 2), 128), 128)]

    give_core.wait()
    vmine[...] += vcore[...]
    plane.start(1, tile_of, slot_of(vplane))
    vplane[at.m] = vmine[:, pl.ds(pl.multiple_of(128 * col, 128), 128)]
    sendr[...] = pieces_of(mid[...] + gate[:, 0:1] * line.total(6, ps3, pr3))
    plane.start(2, piece(sendr), piece(arrr))
    keep_piece(at, sendr, arrr)
    fin_y(8, bu)
    acc = outz[4 + z].astype(jnp.float32)
    for d in (1, 3, 2):
        line.got(4, d, outz.at[line.index(d)])
        acc += outz[line.index(d)].astype(jnp.float32)
    fin_z(9, bo, acc)
    bq[at.s, :, 0:256] = plane_total(0, rp)
    bq[at.s, :, 256:768] = plane_total(3, rpkv)
    everyone.start(0, bq)
    fin_y(9, bo)
    plane.wait(1, slot_of(vplane))
    vline[z] = jnp.sum(vplane[...], axis=0)

    def vec_copy(d):
        return line.copy(5, d, vline.at[z], vline.at[z])

    for d in (1, 3, 2):
        vec_copy(d).start()
    grad_normed = line.total(3, ps2, pr2)
    scale = norm_parts(xa[block(z), :].astype(jnp.float32))[1]
    gx[...] += norm_back(grad_normed, gains[0:1, :], xh[block(z), :], scale)
    plane.wait(2, piece(arrr))
    left, right = placings(route[0:1, :])
    res[...] = from_pieces(left, right, arrr[...])
    fin_wait(7, bd)
    fin_wait(8, bu)
    for d in (1, 3, 2):
        line.got(5, d, vline.at[line.index(d)])
    gvec[...] = jnp.sum(vline[...], axis=0)
    fin_wait(9, bo)
    everyone.wait(0, bq)
    if_swapped = jnp.logical_not(at.same)
    pl.when(if_swapped)(lambda: give_vec.wait())
    line.sent_all(0, ghs)
    line.sent(1, ps)
    line.sent(3, ps2)
    line.sent(6, ps3)
    for d in (1, 3, 2):
        gm_copy(d).wait_send()
        out_copy(d).wait_send()
        vec_copy(d).wait_send()
        for phase, mine, x_got, part, y_got in ((0, md, xd, sd, yd), (2, mo, xo, so, yo)):
            x_copy(phase, d, mine, x_got).wait_send()
            y_copy(phase, d, part, y_got).wait_send()
        y_first(1, d, mu, xu).wait_send()
        x_second(1, d, su, yu).wait_send()
    for j in range(4):
        kv_copy(j).wait_send()
    plane.sent(0, piece_of(mq), slot_of(rp))
    plane.sent(3, piece_of(mkv), slot_of(rpkv))
    plane.sent(1, tile_of, slot_of(vplane))
    plane.sent(2, piece(sendr), piece(arrr))
    everyone.sent(0, bq)
    for phase, buf in ((7, bd), (8, bu), (9, bo)):
        fin_mate(phase, buf).wait_send()
        for d in (1, 3, 2):
            fin_copy(phase, d, buf).wait_send()

    @pl.when(jnp.logical_not(at.same))
    def _():
        for swap in swaps:
            swap.wait()


def dense_backward_call(gh, after, docs, gains, mixed, route, mid, gate, vec_sum, saved, ps, gin0, gout0):
    bf, f32 = jnp.bfloat16, jnp.float32
    vmem, anywhere = pl.BlockSpec(memory_space=pltpu.VMEM), pl.BlockSpec(memory_space=pl.ANY)
    smem = pl.BlockSpec(memory_space=pltpu.SMEM)
    shape, V, dma = jax.ShapeDtypeStruct, pltpu.VMEM, pltpu.SemaphoreType.DMA
    line, pieces = [V((512, 1024), bf)], [V((256, 512), bf)]
    wide, narrow = [V((2, 4, 64, 1024), bf)], [V((2, 4, 64, 256), bf), V((2, 4, 64, 512), bf)]
    return pl.pallas_call(
        dense_backward_kernel,
        out_shape=[
            shape((128, 1024), f32), shape((2, 4, 32, 1024), bf), shape((2, 4, 32, 1024), bf),
            shape((2, 4, 32, 256), bf), shape((8, 32, 768), bf), shape((8, 128), f32), shape((128, 1024), bf),
            shape((8, 1024), f32), shape((1024, 512), bf),
            shape((512, 1024), bf),
        ],
        in_specs=[vmem, vmem, smem] + [vmem] * 6 + [anywhere] * 15,
        out_specs=[vmem] * 8 + [anywhere] * 2,
        scratch_shapes=[
            *(line * 2), V((512, 1024), f32), *(line * 3), V((512, 1024), f32), *line,
            V((512, 256), bf), V((512, 512), bf), V((512, 512), bf),
            V((2, 4, 2, 2, 32, 768), bf), *([V((2, 4, 2, 2, 32, 1024), bf)] * 3),
            *(line * 6), V((2, 16, 128, 512), bf),
            V((128, 1024), bf), V((512, 256), bf), V((512, 768), bf), V((512, 512), f32), V((512, 512), f32),
            V((512, 512), bf), V((512, 512), bf),
            *(wide * 3), *narrow, *(wide * 3), *narrow, *(wide * 3), *narrow,
            V((4, 2, 64, 1024), bf), V((4, 4, 32, 1024), bf), V((4, 2, 64, 1024), bf),
            V((2, 64, 1024), bf), V((4, 32, 1024), bf), V((2, 64, 1024), bf), *([V((4, 32, 1024), bf)] * 3),
            V((16, 32, 256), bf), V((16, 32, 512), bf), *(pieces * 2),
            V((8, 1024), f32), V((8, 1024), f32), V((16, 8, 128), f32), V((4, 8, 128), f32),
            V((8, 32, 256), bf),
            dma((13,)), dma((10, 6)), dma((10, 6)), dma((3, 3)), dma((3, 3)), dma((3, 3)), dma((3, 3)), dma((4,)),
            dma((4,)), dma((5,)), dma((5,)), dma((4, 15)), dma((4, 15)), dma((1, 7)), dma((1, 7)), dma((3,)),
            dma((3,)), dma((1,)), dma((1,)), dma((10,)), dma((10,)),
        ],
        compiler_params=pltpu.CompilerParams(collective_id=3, has_side_effects=True, vmem_limit_bytes=62 << 20),
        name="dense_backward",
    )(gh, after, docs, gains, mixed, route, mid, gate, vec_sum, *saved, ps, gin0, gout0)


def finish_kernel(
    gvec, vec_sum, vec_swap, res, gx, bd, bu, bo, bq, in0, in1, out0, out1, swapped_in, swapped_out,
    ng, nb, eg, eb, cen, o_res, o_gx, o_gq, o_go, o_gu, o_gd, o_in, o_out,
    b_in, b_out, f_in, f_out, vd, vu, vo, vq, gq, go, gu, gd, vres, vgx, isem, osem,
):
    at = Place()
    swapped = [
        pltpu.make_async_copy(swapped_in, b_in.at[0], isem.at[0]),
        pltpu.make_async_copy(swapped_out, b_out.at[0], isem.at[2]),
    ]
    pairs = [
        (in0, b_in.at[0]), (in1, b_in.at[1]), (out0, b_out.at[0]), (out1, b_out.at[1]), (bd, vd), (bu, vu), (bo, vo),
        (bq, vq), (res, vres), (gx, vgx),
    ]
    loads = [pltpu.make_async_copy(src, dst, isem.at[k]) for k, (src, dst) in enumerate(pairs)]

    @pl.when(at.same)
    def _():
        loads[0].start()
        loads[2].start()

    @pl.when(jnp.logical_not(at.same))
    def _():
        for copy in swapped:
            copy.start()

    for k in (1, 3, 4, 5, 6, 7, 8, 9):
        loads[k].start()
    c = at.c
    mine = jnp.where(c == 0, gvec[0:4, 0:64], gvec[0:4, 64:128])
    ng[...] = mine[0:2]
    nb[...] = mine[2:4]
    vectors = jnp.where(at.same, vec_sum[...], vec_swap[...])
    eg[...] = vectors[0:2]
    eb[...] = vectors[2:4]
    cen[...] = vectors[4:5]
    stores = []

    def store(src, dst):
        stores.append(pltpu.make_async_copy(src, dst, osem.at[len(stores)]))
        stores[-1].start()

    for k in range(4):
        loads[k].wait()
        low, wide, out = ((b_in, f_in, o_in), (b_out, f_out, o_out))[k // 2]
        wide[k % 2] = low[k % 2].astype(jnp.float32)
        store(wide.at[k % 2], out.at[k % 2])
    for k in range(4, 10):
        loads[k].wait()
    store(vres, o_res)
    store(vgx, o_gx)
    lane = lax.broadcasted_iota(jnp.int32, (32, 128), 1) < 64
    for half in range(2):
        rows = slice(32 * half, 32 * half + 32)
        for z in range(4):
            gd[64 * z + 32 * half : 64 * z + 32 * half + 32, :] = vd[half, z].astype(jnp.float32)
            go[rows, 256 * z : 256 * z + 256] = vo[half, z].astype(jnp.float32)
            for part in range(3):
                gq[rows, 1024 * part + 256 * z : 1024 * part + 256 * z + 256] = vq[
                    2 * z + half, :, 256 * part : 256 * part + 256
                ].astype(jnp.float32)
        for n in range(8):
            tile = slice(128 * n, 128 * n + 128)
            quarter = [vu[half, z, :, tile].astype(jnp.float32) for z in range(4)]
            turned = [pltpu.roll(v, 64, 1) for v in quarter]
            first = 512 * n
            gu[rows, first : first + 128] = jnp.where(lane, quarter[0], turned[1])
            gu[rows, first + 128 : first + 256] = jnp.where(lane, quarter[2], turned[3])
            gu[rows, first + 256 : first + 384] = jnp.where(lane, turned[0], quarter[1])
            gu[rows, first + 384 : first + 512] = jnp.where(lane, turned[2], quarter[3])
    for src, dst in ((gq, o_gq), (go, o_go), (gu, o_gu), (gd, o_gd)):
        store(src, dst)
    for copy in stores:
        copy.wait()


def finish_call(gvec, vec_sum, vec_swap, res, gx, bd, bu, bo, bq, in0, in1, out0, out1, swapped_in, swapped_out):
    bf, f32 = jnp.bfloat16, jnp.float32
    vmem, anywhere = pl.BlockSpec(memory_space=pltpu.VMEM), pl.BlockSpec(memory_space=pl.ANY)
    shape, V, dma = jax.ShapeDtypeStruct, pltpu.VMEM, pltpu.SemaphoreType.DMA
    return pl.pallas_call(
        finish_kernel,
        out_shape=[
            shape((2, 64), f32), shape((2, 64), f32), shape((2, 1024), f32), shape((2, 1024), f32),
            shape((1, 1024), f32), shape((128, 1024), bf), shape((128, 1024), f32), shape((64, 3072), f32),
            shape((64, 1024), f32), shape((64, 4096), f32), shape((256, 1024), f32), shape((2, 1024, 512), f32),
            shape((2, 512, 1024), f32),
        ],
        in_specs=[vmem] * 3 + [anywhere] * 12,
        out_specs=[vmem] * 5 + [anywhere] * 8,
        scratch_shapes=[
            V((2, 1024, 512), bf), V((2, 512, 1024), bf), V((2, 1024, 512), f32), V((2, 512, 1024), f32),
            V((2, 4, 32, 1024), bf), V((2, 4, 32, 1024), bf), V((2, 4, 32, 256), bf), V((8, 32, 768), bf),
            V((64, 3072), f32), V((64, 1024), f32), V((64, 4096), f32), V((256, 1024), f32),
            V((128, 1024), bf), V((128, 1024), f32), dma((10,)), dma((10,)),
        ],
        compiler_params=pltpu.CompilerParams(vmem_limit_bytes=62 << 20),
        name="finish",
    )(gvec, vec_sum, vec_swap, res, gx, bd, bu, bo, bq, in0, in1, out0, out1, swapped_in, swapped_out)


def on_device(
    inputs,
    doc_starts,
    route,
    norm_gain,
    norm_bias,
    w_qkv,
    w_out,
    w_up,
    w_down,
    exp_gain,
    exp_bias,
    exp_in,
    exp_out,
    centroid,
    cotangent,
):
    tok_rows, width = 128, 1024
    x = inputs.reshape(tok_rows, width)
    cot = cotangent.reshape(tok_rows, width)
    slots = route.reshape(1, tok_rows)
    hidden, mixed, after, gains, *saved, cz, in0, out0 = dense_forward_call(
        x, norm_gain, norm_bias, doc_starts, slots, cot, w_qkv, w_out, w_up, w_down, exp_in[0], exp_out[0]
    )
    grad_hidden, vec_sum, mid, gate, part, grad_in1, grad_out1, grad_in0, grad_out0 = expert_call(
        hidden, slots, exp_gain[0], exp_bias[0], centroid, cz, exp_in[0], exp_out[0], in0, out0
    )
    grad_x, down, up, out, qkv, norm_grads, result, vec_swap, swapped_in, swapped_out = dense_backward_call(
        grad_hidden, after, doc_starts, gains, mixed, slots, mid, gate, vec_sum, saved, part, grad_in0, grad_out0
    )
    gain, bias, e_gain, e_bias, center, result, grad_x, g_qkv, g_out, g_up, g_down, e_in, e_out = finish_call(
        norm_grads,
        vec_sum,
        vec_swap,
        result,
        grad_x,
        down,
        up,
        out,
        qkv,
        grad_in0,
        grad_in1,
        grad_out0,
        grad_out1,
        swapped_in,
        swapped_out,
    )
    return (
        result[None],
        grad_x[None],
        gain,
        bias,
        g_qkv,
        g_out,
        g_up,
        g_down,
        e_gain[None],
        e_bias[None],
        e_in[None],
        e_out[None],
        center,
    )


def solution(mesh):
    in_specs = (
        P("fsdp", "seq", None),
        P("fsdp", None),
        P("fsdp", "seq", None),
        P(None, "fsdp"),
        P(None, "fsdp"),
        P("fsdp", None),
        P("fsdp", None),
        P("fsdp", None),
        P("fsdp", None),
        P("fsdp", None, None),
        P("fsdp", None, None),
        P("fsdp", None, None, "seq"),
        P("fsdp", None, "seq", None),
        P("fsdp", None),
        P("fsdp", "seq", None),
    )
    out_specs = (
        P("fsdp", "seq", None),
        P("fsdp", "seq", None),
        P(None, "fsdp"),
        P(None, "fsdp"),
        P("fsdp", None),
        P("fsdp", None),
        P("fsdp", None),
        P("fsdp", None),
        P("fsdp", None, None),
        P("fsdp", None, None),
        P("fsdp", None, None, "seq"),
        P("fsdp", None, "seq", None),
        P("fsdp", None),
    )
    return jax.shard_map(
        on_device, mesh=mesh, in_specs=in_specs, out_specs=out_specs, check_vma=False
    )
```

```python
import jax
import jax.numpy as jnp
from jax import lax
from jax.experimental import pallas as pl
from jax.experimental.pallas import tpu as pltpu
from jax.sharding import PartitionSpec as P

MESH = pl.DeviceIdType.MESH
epsilon = 1e-05
masked_score = -1e30


def split_sum(values):
    return jnp.sum(values, axis=-1, keepdims=True)


def norm_parts(values):
    average = split_sum(values) * (1.0 / values.shape[-1])
    centered = values - average
    spread = split_sum(centered * centered) * (1.0 / values.shape[-1])
    scale = lax.rsqrt(spread + epsilon)
    return centered * scale, scale


def norm_back(grad_normed, gain, xhat, scale):
    width = 1.0 / xhat.shape[-1]
    u = grad_normed * gain
    return scale * (u - split_sum(u) * width - xhat * (split_sum(u * xhat) * width))


def gelu_parts(pre):
    inner = 0.7978845608028654
    cubic = 0.044715
    square = pre * pre
    t = jnp.tanh(inner * pre * (1.0 + cubic * square))
    half = 0.5 * (1.0 + t)
    slope = half + 0.5 * pre * (1.0 - t * t) * (inner * (1.0 + 3.0 * cubic * square))
    return pre * half, slope


def nn(a, b):
    return lax.dot_general(a, b, (((1,), (0,)), ((), ())), preferred_element_type=jnp.float32)


def nt(a, b):
    return lax.dot_general(a, b, (((1,), (1,)), ((), ())), preferred_element_type=jnp.float32)


def tn(a, b):
    return lax.dot_general(a, b, (((0,), (0,)), ((), ())), preferred_element_type=jnp.float32)


def remote(src, dst, send, recv, device):
    return pltpu.make_async_remote_copy(
        src_ref=src, dst_ref=dst, send_sem=send, recv_sem=recv, device_id=device, device_id_type=MESH
    )


def greet(bar, device):
    pl.semaphore_signal(bar, inc=1, device_id=device, device_id_type=MESH)


def block(index):
    return pl.ds(pl.multiple_of(index * 128, 128), 128)


def order(i):
    return i + lax.div(i, 2) - 2 * lax.div(i, 3)


class Place:
    def __init__(self):
        self.s, self.f = lax.axis_index("seq"), lax.axis_index("fsdp")
        self.z, self.yh = lax.div(self.s, 2), lax.rem(self.s, 2)
        self.yl, self.col, self.c = lax.div(self.f, 8), lax.div(self.f, 2), lax.rem(self.f, 2)
        self.x = lax.rem(self.col, 4)
        self.m = self.f - self.c + self.yh
        self.other = (self.s, self.f + 1 - 2 * self.c)
        self.mate = (2 * self.z + 1 - self.yh, self.f)
        self.swap_mate = (2 * self.z + 1 - self.yh, self.f + 1 - 2 * self.c)
        self.same = self.c == self.yh


class Ring:
    def __init__(self, at, axis, send, recv):
        self.at, self.axis, self.send, self.recv = at, axis, send, recv
        self.pos = {"z": at.z, "x": at.x, "y": 2 * at.yh + at.yl}[axis]

    def index(self, d):
        return lax.rem(self.pos + d, 4)

    def device(self, j):
        at = self.at
        if self.axis == "z":
            return (2 * j + at.yh, at.f)
        if self.axis == "x":
            return (at.s, at.f - 2 * at.x + 2 * j)
        return (2 * at.z + lax.div(j, 2), 8 * lax.rem(j, 2) + at.f - 8 * at.yl)

    def copy(self, phase, d, src, dst):
        sems = self.send.at[phase, d - 1], self.recv.at[phase, d - 1]
        return remote(src, dst, *sems, self.device(self.index(d)))

    def got(self, phase, d, dst):
        sems = self.send.at[phase, 3 - d], self.recv.at[phase, 3 - d]
        remote(dst, dst, *sems, self.device(self.index(d))).wait_recv()

    def spread(self, phase, buf):
        own = buf.at[block(self.pos)]
        for d in (1, 3, 2):
            self.copy(phase, d, own, own).start()

    def half(self, buf, d, upper):
        return buf.at[pl.ds(pl.multiple_of(128 * self.index(d) + 64 * upper, 64), 64)]

    def moving(self, phase, slot, rows, up):
        to = self.device(self.index(1 if up else 3))
        return remote(rows, rows, self.send.at[phase, slot], self.recv.at[phase, slot], to)

    def parts(self, phase, buf):
        for slot, up, upper in ((2, 0, 0), (0, 1, 1), (3, 0, 1), (1, 1, 0)):
            yield self.moving(phase, slot, self.half(buf, 0, upper), up)

    def onward(self, phase, buf, up):
        return self.moving(phase, 4 + up, self.half(buf, 3 if up else 1, up), up)

    def begin(self, phase, buf):
        for part in self.parts(phase, buf):
            part.start()

    def relay(self, phase, buf):
        for up in (0, 1):
            self.moving(phase, 0 if up else 2, self.half(buf, 3 if up else 1, up), up).wait_recv()
            self.onward(phase, buf, up).start()

    def above(self, phase, buf):
        self.moving(phase, 3, self.half(buf, 1, 1), 0).wait_recv()

    def below(self, phase, buf):
        self.moving(phase, 1, self.half(buf, 3, 0), 1).wait_recv()

    def far(self, phase, buf):
        for up in (0, 1):
            self.moving(phase, 4 + up, self.half(buf, 2, up), up).wait_recv()

    def ready(self, phase, i, buf):
        @pl.when(i == 1)
        def _():
            self.relay(phase, buf)
            self.above(phase, buf)

        pl.when(i == 2)(lambda: self.below(phase, buf))
        pl.when(i == 3)(lambda: self.far(phase, buf))

    def sent_all(self, phase, buf):
        for part in self.parts(phase, buf):
            part.wait_send()
        for up in (0, 1):
            self.onward(phase, buf, up).wait_send()

    def arrived(self, phase, d, buf):
        self.got(phase, d, buf.at[block(self.index(d))])

    def give(self, phase, d, src, dst):
        self.copy(phase, d, src.at[block(self.index(d))], dst.at[block(self.pos)]).start()

    def sent(self, phase, buf):
        own = buf.at[block(self.pos)]
        for d in (1, 3, 2):
            self.copy(phase, d, own, own).wait_send()

    def total(self, phase, own, parts):
        acc = own[block(self.pos), :].astype(jnp.float32)
        for d in (1, 3, 2):
            self.arrived(phase, d, parts)
            acc += parts[block(self.index(d)), :].astype(jnp.float32)
        return acc


class Plane:
    def __init__(self, at, send, recv):
        self.at, self.m = at, at.m
        self.send, self.recv = send, recv

    def device(self, q):
        return (2 * self.at.z + lax.rem(q, 2), q - lax.rem(q, 2) + self.at.c)

    def greet(self, bar):
        def one(i, carry):
            greet(bar, self.device(lax.rem(self.m + i + 1, 16)))
            return carry

        lax.fori_loop(0, 15, one, 0)

    def copy(self, phase, i, src_of, dst_of):
        q = lax.rem(self.m + i + 1, 16)
        return remote(src_of(q), dst_of(self.m), self.send.at[phase, i], self.recv.at[phase, i], self.device(q))

    def start(self, phase, src_of, dst_of):
        def one(i, carry):
            self.copy(phase, i, src_of, dst_of).start()
            return carry

        lax.fori_loop(0, 15, one, 0)

    def wait(self, phase, dst_of):
        def one(i, carry):
            q = lax.rem(self.m + 15 - i, 16)
            dst = dst_of(q)
            remote(dst, dst, self.send.at[phase, i], self.recv.at[phase, i], self.device(q)).wait_recv()
            return carry

        lax.fori_loop(0, 15, one, 0)

    def sent(self, phase, src_of, dst_of):
        def one(i, carry):
            self.copy(phase, i, src_of, dst_of).wait_send()
            return carry

        lax.fori_loop(0, 15, one, 0)


def piece(buf):
    return lambda q: buf.at[pl.ds(pl.multiple_of(q * 16, 16), 16)]


def keep_piece(at, src, dst):
    own = pl.ds(pl.multiple_of(at.m * 16, 16), 16)
    dst[own, :] = src[own, :]


def placings(route):
    row = lax.broadcasted_iota(jnp.int32, (256, 128), 0)
    inner = row & 15
    slot = (row >> 4) * 8 + (inner & 7)
    hit = slot == route
    left = jnp.where(hit & (inner < 8), 1.0, 0.0).astype(jnp.bfloat16)
    right = jnp.where(hit & (inner >= 8), 1.0, 0.0).astype(jnp.bfloat16)
    return left, right


def to_pieces(left, right, rows):
    half = rows.shape[1] // 2
    return (nn(left, rows[:, :half]) + nn(right, rows[:, half:])).astype(jnp.bfloat16)


def from_pieces(left, right, pieces):
    return jnp.concatenate([tn(left, pieces), tn(right, pieces)], axis=1).astype(jnp.bfloat16)


def rows_of(pieces):
    wide = pieces.astype(jnp.float32).reshape(16, 2, 8, 512)
    return jnp.concatenate([wide[:, 0].reshape(128, 512), wide[:, 1].reshape(128, 512)], axis=1)


def pieces_of(rows):
    left = rows[:, :512].reshape(16, 1, 8, 512)
    right = rows[:, 512:].reshape(16, 1, 8, 512)
    return jnp.concatenate([left, right], axis=1).reshape(256, 512).astype(jnp.bfloat16)


class Gather:
    def __init__(self, at, phase, first, src, full, xs, xr, ys, yr, ks, kr):
        self.at, self.phase, self.src, self.full = at, phase, src, full
        self.x_first = first == "x"
        self.rings = [Ring(at, "y", ys, yr), Ring(at, "x", xs, xr)]
        if self.x_first:
            self.rings.reverse()
        self.ks, self.kr = ks, kr

    def pushed(self, d):
        at = self.at
        return self.rings[0].copy(self.phase, d, self.src, self.full.at[at.yl, at.x, at.c, at.yh])

    def passed(self, d):
        at = self.at
        own = self.full.at[at.yl, :, at.c, at.yh] if self.x_first else self.full.at[:, at.x, at.c]
        return self.rings[1].copy(self.phase, d, own, own)

    def core(self, c):
        half = self.full.at[:, :, c]
        return remote(half, half, self.ks.at[self.phase], self.kr.at[self.phase], self.at.other)

    def start(self):
        at = self.at
        for d in (1, 3, 2):
            self.pushed(d).start()
        self.full[at.yl, at.x, at.c, at.yh] = self.src[...]

    def turn(self):
        at, full = self.at, self.full
        for d in (1, 3, 2):
            j = self.rings[0].index(d)
            dst = full.at[at.yl, j, at.c, at.yh] if self.x_first else full.at[lax.rem(j, 2), at.x, at.c, lax.div(j, 2)]
            self.rings[0].got(self.phase, d, dst)
        for d in (1, 3, 2):
            self.passed(d).start()

    def share(self):
        at, full = self.at, self.full
        for d in (1, 3, 2):
            j = self.rings[1].index(d)
            dst = full.at[lax.rem(j, 2), :, at.c, lax.div(j, 2)] if self.x_first else full.at[:, j, at.c]
            self.rings[1].got(self.phase, d, dst)
        self.core(at.c).start()

    def wait(self):
        self.core(1 - self.at.c).wait_recv()

    def sent(self):
        for d in (1, 3, 2):
            self.pushed(d).wait_send()
            self.passed(d).wait_send()
        self.core(self.at.c).wait_send()


def labels(position, first, second):
    return jnp.where(position >= first, 1, 0) + jnp.where(position >= second, 1, 0)


def mask(j, yh, parity, docs):
    first, second = docs[0, 0], docs[0, 1]
    wide = 128 * (j + 1)
    row = lax.broadcasted_iota(jnp.int32, (128, wide), 0) + 128 * (2 * j + yh)
    lane = lax.broadcasted_iota(jnp.int32, (128, wide), 1)
    key = (lane >> 7) * 256 + (lane & 127) + 128 * parity
    return (key <= row) & (labels(key, first, second) == labels(row, first, second))


def masked_scores(q, keys, seen):
    return jnp.where(seen, nt(q, keys) * 0.125, masked_score)


def probabilities(q, keys, seen):
    scores = [masked_scores(q, k, ok) for k, ok in zip(keys, seen)]
    top = jnp.maximum(
        jnp.max(scores[0], axis=-1, keepdims=True), jnp.max(scores[1], axis=-1, keepdims=True)
    )
    weights = [jnp.exp(s - top) for s in scores]
    inverse = 1.0 / (split_sum(weights[0]) + split_sum(weights[1]))
    return [w * inverse for w in weights]


def head_lanes(h):
    lane = lax.broadcasted_iota(jnp.int32, (128, 128), 1)
    return lane < 64 if h == 0 else lane >= 64


def only(keep, values):
    return jnp.where(keep, values.astype(jnp.float32), 0.0).astype(jnp.bfloat16)


def wide_tile(full, tile):
    part = full[:, :, :, :, :, tile]
    return part.reshape(1024, part.shape[-1])


def tall_tile(full, n):
    part = full[n // 2, 2 * (n % 2) : 2 * (n % 2) + 2]
    return part.reshape(256, part.shape[-1])


def dense_forward_kernel(
    x, gain, bias, docs, route, cot, w_qkv, w_out, w_up, w_down, exp_in, exp_out,
    hid, mixed, after, gains,
    o_x, o_n1, o_n2, o_act, o_dg, o_q, o_kv, o_kvo, o_wq, o_wo, o_wu, o_wd, o_cz, o_in0, o_out0,
    sq, su, wq, wo, wu, wd, gtile, gmine, gother,
    xa, n1, n2, cz, qb, kvb, kvo, mixs, act, dg, ps, pr, sendc, arrc, stats, own_sum,
    zs, zr, xs, xr, ys, yr, kvs, kvr, ks, kr, gs, gr, cs, cr, ss, sr, osem,
):
    at = Place()
    z, yh, c, col = at.z, at.yh, at.c, at.col
    line, plane = Ring(at, "z", zs, zr), Plane(at, cs, cr)
    bar = pltpu.get_barrier_semaphore()
    for d in (1, 2, 3):
        greet(bar, line.device(line.index(d)))
    greet(bar, at.other)
    greet(bar, at.swap_mate)
    plane.greet(bar)
    xa[block(z), :] = x[...]
    for part in range(3):
        sq[:, 256 * part : 256 * part + 256] = w_qkv[:, pl.ds(pl.multiple_of(1024 * part + 256 * z, 256), 256)]
    gtile[...] = jnp.zeros_like(gtile)
    for k, ref in enumerate((gain, bias)):
        values = ref[...].astype(jnp.float32)
        none = jnp.zeros_like(values)
        here = jnp.where(c == 0, jnp.concatenate([values, none], 1), jnp.concatenate([none, values], 1))
        gtile[2 * k : 2 * k + 2, :] = here
    half = pl.ds(pl.multiple_of(32 * yh, 32), 32)
    down_rows = w_down.at[pl.ds(pl.multiple_of(64 * z + 32 * yh, 32), 32)]
    sems = (xs, xr, ys, yr, ks, kr)
    left_q, right_q = (wq.at[:, :, :, :, :, 0:384], wq.at[:, :, :, :, :, 384:768])
    qkv_a = Gather(at, 0, "y", sq.at[half, 0:384], left_q, *sems)
    qkv_b = Gather(at, 1, "x", sq.at[half, 384:768], right_q, *sems)
    out = Gather(at, 2, "y", w_out.at[half], wo, *sems)
    up = Gather(at, 3, "y", su.at[half], wu, *sems)
    down = Gather(at, 4, "x", down_rows, wd, *sems)
    low = lax.broadcasted_iota(jnp.int32, (64, 128), 1) < 64
    odd = lax.rem(z, 2) == 1
    for n in range(8):
        first = 512 * n + 128 * lax.div(z, 2)
        a = w_up[:, pl.ds(pl.multiple_of(first, 128), 128)].astype(jnp.float32)
        b = w_up[:, pl.ds(pl.multiple_of(first + 256, 128), 128)].astype(jnp.float32)
        kept = jnp.where(low, a, pltpu.roll(b, 64, 1))
        moved = jnp.where(low, pltpu.roll(a, 64, 1), b)
        su[:, 128 * n : 128 * n + 128] = jnp.where(odd, moved, kept).astype(jnp.bfloat16)
    left, right = placings(route[0:1, :])
    sendc[...] = to_pieces(left, right, cot[...])
    pl.semaphore_wait(bar, 20)
    line.begin(0, xa)
    tile_at = pl.ds(pl.multiple_of(128 * col, 128), 128)

    def gain_copy(i):
        to = (at.s, 2 * lax.rem(col + i + 1, 8) + c)
        return remote(gtile, gmine.at[:, tile_at], gs.at[i], gr.at[i], to)

    def push_gain(i, carry):
        gain_copy(i).start()
        return carry

    lax.fori_loop(0, 7, push_gain, 0)
    gmine[:, tile_at] = gtile[...]
    qkv_a.start()
    qkv_b.start()
    plane.start(0, piece(sendc), piece(arrc))
    keep_piece(at, sendc, arrc)
    qkv_a.turn()
    qkv_b.turn()
    for weight in (out, up, down):
        weight.start()
    line.relay(0, xa)

    def wait_gain(i, carry):
        q = lax.rem(col + 7 - i, 8)
        dst = gmine.at[:, pl.ds(pl.multiple_of(128 * q, 128), 128)]
        remote(dst, dst, gs.at[i], gr.at[i], (at.s, 2 * q + c)).wait_recv()
        return carry

    lax.fori_loop(0, 7, wait_gain, 0)
    gain_core = remote(gmine, gother, gs.at[7], gr.at[7], at.other)
    gain_core.start()
    gain_core.wait_recv()
    gains[...] = gmine[...] + gother[...]
    qkv_a.share()
    qkv_b.share()
    out.turn()
    up.turn()

    def kv_copy(i, j):
        return remote(kvb.at[block(j)], kvo.at[block(j)], kvs.at[i], kvr.at[i], at.mate)

    def project_qkv(i, carry):
        j = line.index(order(i))
        pl.when(i == 1)(lambda: line.above(0, xa))
        pl.when(i == 2)(lambda: line.below(0, xa))
        pl.when(i == 3)(lambda: line.far(0, xa))
        xhat = norm_parts(xa[block(j), :].astype(jnp.float32))[0]
        n1[block(j), :] = (xhat * gains[0:1, :] + gains[2:3, :]).astype(jnp.bfloat16)

        @pl.when(i == 0)
        def _():
            qkv_a.wait()
            qkv_b.wait()

        values = n1[block(j), :]
        kvb[block(j), 0:256] = nn(values, wide_tile(wq, slice(256, 512))).astype(jnp.bfloat16)
        kvb[block(j), 256:512] = nn(values, wide_tile(wq, slice(512, 768))).astype(jnp.bfloat16)
        kv_copy(i, j).start()
        qb[block(j), :] = nn(values, wide_tile(wq, slice(0, 256))).astype(jnp.bfloat16)
        return carry

    lax.fori_loop(0, 4, project_qkv, 0)
    down.turn()
    plane.wait(0, piece(arrc))
    cz[block(z), :] = rows_of(arrc[...]).astype(jnp.bfloat16)
    line.spread(4, cz)

    def heads(j, keys, parity):
        seen = mask(j, yh, parity, docs)
        wide = slice(0, 128 * (j + 1))
        for p in range(2):
            lanes = slice(128 * p, 128 * p + 128)
            q = qb[128 * j : 128 * j + 128, lanes]
            for h in range(2):
                scores = masked_scores(only(head_lanes(h), q), keys[wide, lanes], seen)
                yield 4 * j + 2 * p + h, h, lanes, scores, keys[wide, 256 + 128 * p : 384 + 128 * p]

    first = None
    for j in range(4):
        for k, h, lanes, scores, values in heads(j, kvb, yh):
            top = jnp.max(scores, axis=-1, keepdims=True)
            weights = jnp.exp(scores - top)
            stats[k] = jnp.where(head_lanes(0), top, split_sum(weights))
            summed = nn(weights.astype(jnp.bfloat16), values)
            if h == 0:
                first = summed
            else:
                own_sum[128 * j : 128 * j + 128, lanes] = jnp.where(head_lanes(0), first, summed)
    for i in range(4):
        kv_copy(i, line.index(order(i))).wait_recv()
    swaps = [
        remote(exp_in.at[0], o_in0, ss.at[0], sr.at[0], at.swap_mate),
        remote(exp_out.at[0], o_out0, ss.at[1], sr.at[1], at.swap_mate),
    ]

    @pl.when(c != yh)
    def _():
        swaps[0].start()

    my_lanes = pl.ds(pl.multiple_of(256 * z, 256), 256)

    def mix_copy(d):
        return line.copy(1, d, mixs.at[block(line.index(d))], mixed.at[:, my_lanes])

    for j in range(4):
        rows = slice(128 * j, 128 * j + 128)
        for k, h, lanes, scores, values in heads(j, kvo, 1 - yh):
            top, total = stats[k][:, 0:1], stats[k][:, 64:65]
            new_top = jnp.maximum(top, jnp.max(scores, axis=-1, keepdims=True))
            kept = jnp.exp(top - new_top)
            weights = jnp.exp(scores - new_top)
            inverse = 1.0 / (total * kept + split_sum(weights))
            summed = (own_sum[rows, lanes] * kept + nn(weights.astype(jnp.bfloat16), values)) * inverse
            if h == 0:
                first = summed
            else:
                mixs[rows, lanes] = jnp.where(head_lanes(0), first, summed).astype(jnp.bfloat16)
        pl.when(z != j)(lambda: mix_copy(lax.rem(j + 4 - z, 4)).start())
    mixed[:, my_lanes] = mixs[block(z), :]
    out.share()
    out.wait()
    for d in (1, 3, 2):
        line.got(1, d, mixed.at[:, pl.ds(pl.multiple_of(256 * line.index(d), 256), 256)])
    for n in range(4):
        tile = slice(256 * n, 256 * n + 256)
        after[:, tile] = x[:, tile].astype(jnp.float32) + nn(mixed[...], wide_tile(wo, tile))
    xhat = norm_parts(after[...])[0]
    n2[block(z), :] = (xhat * gains[1:2, :] + gains[3:4, :]).astype(jnp.bfloat16)
    line.begin(2, n2)
    up.share()
    down.share()
    @pl.when(c != yh)
    def _():
        swaps[1].start()

    up.wait()
    down.wait()
    stores = [
        pltpu.make_async_copy(src, dst, osem.at[k])
        for k, (src, dst) in enumerate(
            [(xa, o_x), (n1, o_n1), (qb, o_q), (kvb, o_kv), (kvo, o_kvo), (wq, o_wq), (wo, o_wo), (wu, o_wu), (wd, o_wd)]
        )
    ]
    for store in stores:
        store.start()

    def feed(i, carry):
        d = order(i)
        j = line.index(d)
        line.ready(2, i, n2)
        values = n2[block(j), :]
        for n in range(4):
            tile = slice(n * 256, (n + 1) * 256)
            acted, slope = gelu_parts(nn(values, wide_tile(wu, tile)))
            act[block(j), tile] = acted.astype(jnp.bfloat16)
            dg[block(j), tile] = slope
        values = act[block(j), :]
        for n in range(4):
            tile = slice(n * 256, (n + 1) * 256)
            ps[block(j), tile] = nn(values, wide_tile(wd, tile)).astype(jnp.bfloat16)

        @pl.when(i > 0)
        def _():
            line.give(3, d, ps, pr)

        return carry

    lax.fori_loop(0, 4, feed, 0)
    for d in (1, 3, 2):
        line.arrived(4, d, cz)
    late = [
        pltpu.make_async_copy(src, dst, osem.at[9 + k])
        for k, (src, dst) in enumerate([(n2, o_n2), (act, o_act), (dg, o_dg), (cz, o_cz)])
    ]
    for store in late:
        store.start()
    gain_core.wait_send()

    def sent_gain(i, carry):
        gain_copy(i).wait_send()
        return carry

    lax.fori_loop(0, 7, sent_gain, 0)
    for weight in (qkv_a, qkv_b, out, up, down):
        weight.sent()
    for i in range(4):
        kv_copy(i, line.index(order(i))).wait_send()
    line.sent_all(0, xa)
    for d in (1, 3, 2):
        mix_copy(d).wait_send()
    line.sent_all(2, n2)
    line.sent(4, cz)
    plane.sent(0, piece(sendc), piece(arrc))
    hid[...] = (after[...] + line.total(3, ps, pr)).astype(jnp.bfloat16)
    line.sent(3, ps)

    @pl.when(c != yh)
    def _():
        for swap in swaps:
            swap.wait()

    for store in stores + late:
        store.wait()


def dense_forward_call(x, gain, bias, docs, route, cot, w_qkv, w_out, w_up, w_down, exp_in, exp_out):
    bf, f32 = jnp.bfloat16, jnp.float32
    vmem, anywhere = pl.BlockSpec(memory_space=pltpu.VMEM), pl.BlockSpec(memory_space=pl.ANY)
    smem = pl.BlockSpec(memory_space=pltpu.SMEM)
    shape, V, dma = jax.ShapeDtypeStruct, pltpu.VMEM, pltpu.SemaphoreType.DMA
    line = [V((512, 1024), bf)]
    weight = [(2, 4, 2, 2, 32, 768)] + [(2, 4, 2, 2, 32, 1024)] * 3
    saved = [
        shape((512, 1024), bf), shape((512, 1024), bf), shape((512, 1024), bf), shape((512, 1024), bf),
        shape((512, 1024), f32), shape((512, 256), bf), shape((512, 512), bf), shape((512, 512), bf),
    ] + [shape(w, bf) for w in weight] + [
        shape((512, 1024), bf), shape((1024, 512), bf), shape((512, 1024), bf),
    ]
    return pl.pallas_call(
        dense_forward_kernel,
        out_shape=[shape((128, 1024), bf), shape((128, 1024), bf), shape((128, 1024), f32), shape((8, 1024), f32)]
        + saved,
        in_specs=[vmem] * 3 + [smem] + [vmem] * 6 + [anywhere, anywhere],
        out_specs=[vmem] * 4 + [anywhere] * len(saved),
        scratch_shapes=[
            V((64, 768), bf), V((64, 1024), bf), *[V(w, bf) for w in weight], V((8, 128), f32), V((8, 1024), f32),
            V((8, 1024), f32),
            *(line * 4), V((512, 256), bf), V((512, 512), bf), V((512, 512), bf), V((512, 256), bf),
            *line, V((512, 1024), f32), *(line * 2), V((256, 512), bf), V((256, 512), bf),
            V((16, 128, 128), f32), V((512, 256), f32), dma((5, 6)), dma((5, 6)), dma((5, 3)), dma((5, 3)), dma((5, 3)), dma((5, 3)), dma((4,)), dma((4,)),
            dma((5,)), dma((5,)), dma((8,)), dma((8,)), dma((1, 15)), dma((1, 15)), dma((3,)), dma((3,)), dma((13,)),
        ],
        compiler_params=pltpu.CompilerParams(collective_id=2, has_side_effects=True, vmem_limit_bytes=60 << 20),
        name="dense_forward",
    )(x, gain, bias, docs, route, cot, w_qkv, w_out, w_up, w_down, exp_in, exp_out)


def expert_kernel(
    hid, route, exp_gain, exp_bias, centroid, cz_h, exp_in, exp_out, in0, out0,
    gh, vecg, mid, gate_out, o_ps, gin1, gout1, gin0, gout0,
    w_in, w_out, sendh, sendg, arrh, arrg, cz,
    e0, e1, g0, g1, ps0, ps1, pr0, pb0, pb1,
    act0, act1, dg0, dg1, gp0, gp1,
    arrived, base, xh0, xh1, sc, gates, dots, dots_in,
    ga_in, ga_out, sb_in, sb_out, rb_in, rb_out, vec, vec_own, vec_other, vmine, vcore, vline,
    wsem, zs, zr, cs, cr, ks, kr, osem, bs, br, ss, sr, vs, vr,
):
    at = Place()
    z, yh, c, same = at.z, at.yh, at.c, at.same
    line, plane = Ring(at, "z", zs, zr), Plane(at, cs, cr)
    bar = pltpu.get_barrier_semaphore()
    plane.greet(bar)
    for d in (1, 2, 3):
        greet(bar, line.device(line.index(d)))
    greet(bar, at.other)
    greet(bar, at.swap_mate)
    low, high = slice(0, 512), slice(512, 1024)

    def slot(k, i, half):
        return w_in.at[k, :, half] if i == 0 else w_out.at[k, half, :]

    def load(k, i):
        return pltpu.make_async_copy((exp_in, exp_out)[i].at[k], slot(k, i, low), wsem.at[k, i])

    def swapped(k, i):
        return pltpu.make_async_copy((in0, out0)[i], slot(k, i, low), wsem.at[k, i])

    swap_out = remote(exp_out.at[1], slot(1, 1, low), ss.at[0], sr.at[0], at.swap_mate)
    swap_in = remote(exp_in.at[1], slot(1, 0, low), ss.at[3], sr.at[3], at.swap_mate)

    def share(k, i):
        return remote(slot(k, i, low), slot(k, i, high), bs.at[k, i], br.at[k, i], at.other)

    def on_either(when_same, when_swapped):
        pl.when(same)(when_same)
        pl.when(jnp.logical_not(same))(when_swapped)

    load_c = pltpu.make_async_copy(cz_h, cz, wsem.at[2, 0])

    def begin_same():
        for k, i in ((0, 0), (0, 1), (1, 0), (1, 1)):
            load(k, i).start()

    def begin_swapped():
        for k, i in ((0, 0), (0, 1)):
            swapped(k, i).start()

    on_either(begin_same, begin_swapped)
    load_c.start()
    left, right = placings(route[0:1, :])
    sendh[...] = to_pieces(left, right, hid[...])
    vec_own[0:2, :] = exp_gain[...].astype(jnp.float32)
    vec_own[2:4, :] = exp_bias[...].astype(jnp.float32)
    vec_own[4:5, :] = centroid[...].astype(jnp.float32)
    vec_own[5:8, :] = jnp.zeros((3, 1024), jnp.float32)
    pl.semaphore_wait(bar, 20)
    plane.start(0, piece(sendh), piece(arrh))
    keep_piece(at, sendh, arrh)
    trade = remote(vec_own, vec_other, vs.at[2], vr.at[2], at.other)
    trade.start()

    def wait_loads(k, i):
        on_either(lambda: load(k, i).wait(), lambda: swapped(k, i).wait())
        share(k, i).start()

    wait_loads(0, 0)
    wait_loads(0, 1)
    trade.wait()
    vec[...] = jnp.where(same, vec_own[...], vec_other[...])
    plane.wait(0, piece(arrh))
    gain = [vec[0:1, :], vec[1:2, :]]
    bias = [vec[2:3, :], vec[3:4, :]]
    rows = rows_of(arrh[...])
    arrived[...] = rows
    xhat, scale = norm_parts(rows)
    xh0[...] = xhat
    sc[0] = jnp.broadcast_to(scale, (128, 128))
    e0[block(z), :] = (xhat * gain[0] + bias[0]).astype(jnp.bfloat16)
    line.begin(0, e0)

    @pl.when(jnp.logical_not(same))
    def _():
        swap_in.start()
        swap_out.start()

    gating = jax.nn.sigmoid(split_sum(rows * vec[4:5, :]))
    gates[z] = jnp.broadcast_to(gating, (128, 128))

    def gate_copy(d):
        return line.copy(3, d, gates.at[z], gates.at[z])

    for d in (1, 3, 2):
        gate_copy(d).start()
    share(0, 0).wait_recv()
    share(0, 1).wait_recv()
    load_c.wait()

    def forward(k, j, rows_in, act, dg):
        values = rows_in[block(j), :]
        for n in range(4):
            tile = slice(n * 256, (n + 1) * 256)
            pre = nn(values, w_in[k, :, tile])
            acted, slope = gelu_parts(pre)
            act[block(j), tile] = acted.astype(jnp.bfloat16)
            dg[block(j), tile] = slope

    def project(k, j, act, part):
        values = act[block(j), :]
        for n in range(4):
            tile = slice(n * 256, (n + 1) * 256)
            part[block(j), tile] = nn(values, w_out[k, :, tile]).astype(jnp.bfloat16)

    def backward(k, j, grad, dg, gp, part):
        values = grad[block(j), :]
        for n in range(4):
            tile = slice(n * 256, (n + 1) * 256)
            slope = dg[block(j), tile] * nt(values, w_out[k, tile, :])
            gp[block(j), tile] = slope.astype(jnp.bfloat16)
        pres = gp[block(j), :]
        for n in range(4):
            tile = slice(n * 256, (n + 1) * 256)
            part[block(j), tile] = nt(pres, w_in[k, tile, :]).astype(jnp.bfloat16)

    def sub0(i, carry):
        d = order(i)
        j = line.index(d)

        line.ready(0, i, e0)
        forward(0, j, e0, act0, dg0)
        project(0, j, act0, ps0)

        @pl.when(i > 0)
        def _():
            line.give(1, d, ps0, pr0)

        return carry

    lax.fori_loop(0, 4, sub0, 0)
    on_either(lambda: load(1, 0).wait(), lambda: swap_in.wait())
    share(1, 0).start()
    on_either(lambda: load(1, 1).wait(), lambda: swap_out.wait())
    share(1, 1).start()
    stream = arrived[...] + line.total(1, ps0, pr0)
    base[...] = stream
    xhat, scale = norm_parts(stream)
    xh1[...] = xhat
    sc[1] = jnp.broadcast_to(scale, (128, 128))
    e1[block(z), :] = (xhat * gain[1] + bias[1]).astype(jnp.bfloat16)
    line.begin(2, e1)
    gate = gates[z][:, 0:1]
    mid[...] = arrived[...] + gate * (base[...] - arrived[...])
    gate_out[...] = gates[z]
    line.sent(1, ps0)
    share(1, 0).wait_recv()
    share(1, 1).wait_recv()

    def sub1(i, carry):
        d = order(i)
        j = line.index(d)

        @pl.when(i > 0)
        def _():
            line.got(3, d, gates.at[j])

        g1[block(j), :] = (gates[j][:, 0:1] * cz[block(j), :].astype(jnp.float32)).astype(jnp.bfloat16)

        line.ready(2, i, e1)
        forward(1, j, e1, act1, dg1)
        backward(1, j, g1, dg1, gp1, ps0)

        @pl.when(i > 0)
        def _():
            line.give(4, d, ps0, pb1)

        return carry

    lax.fori_loop(0, 4, sub1, 0)

    def second_part(i, carry):
        d = order(3 - i)
        j = line.index(d)
        project(1, j, act1, ps1)
        products = cz[block(j), :].astype(jnp.float32) * ps1[block(j), :].astype(jnp.float32)
        dots[j] = jnp.broadcast_to(split_sum(products), (128, 128))

        @pl.when(i < 3)
        def _():
            line.copy(5, d, dots.at[j], dots_in.at[z]).start()

        return carry

    lax.fori_loop(0, 4, second_part, 0)
    keep_ps = pltpu.make_async_copy(ps1, o_ps, wsem.at[2, 1])
    keep_ps.start()

    def weight_grads(k, rows_in, gp, act, grad):
        def one(n, carry):
            tile = pl.ds(pl.multiple_of(n * 256, 256), 256)
            tile_b = pl.ds(pl.multiple_of(n * 256 + 512, 256), 256)
            ga_out[k, tile, :] = tn(act[:, tile], grad[...])
            sb_out[k, tile, :] = tn(act[:, tile_b], grad[...]).astype(jnp.bfloat16)
            return carry

        lax.fori_loop(0, 2, one, 0)

        def two(n, carry):
            tile = pl.ds(pl.multiple_of(n * 256, 256), 256)
            ga_in[k, tile, :] = tn(rows_in[:, tile], gp[:, 0:512])
            sb_in[k, tile, :] = tn(rows_in[:, tile], gp[:, 512:1024]).astype(jnp.bfloat16)
            return carry

        lax.fori_loop(0, 4, two, 0)

    def swap(k, i):
        src, dst = ((sb_in, rb_in), (sb_out, rb_out))[i]
        return remote(src.at[k], dst.at[k], ks.at[k, i], kr.at[k, i], at.other)

    def join_cores(k):
        for i in range(2):
            swap(k, i).wait()
        sb_in[k] = (ga_in[k] + rb_in[k].astype(jnp.float32)).astype(jnp.bfloat16)
        sb_out[k] = (ga_out[k] + rb_out[k].astype(jnp.float32)).astype(jnp.bfloat16)

    weight_grads(1, e1, gp1, act1, g1)
    swap(1, 0).start()
    swap(1, 1).start()
    grad_normed = line.total(4, ps0, pb1)
    cot = cz[block(z), :].astype(jnp.float32)
    grad_stream = gates[z][:, 0:1] * cot
    grad_stream += norm_back(grad_normed, gain[1], xh1[...], sc[1][:, 0:1])
    g0[block(z), :] = grad_stream.astype(jnp.bfloat16)
    line.begin(6, g0)
    vmine[1:2, :] = jnp.sum(grad_normed * xh1[...], axis=0, keepdims=True)
    vmine[3:4, :] = jnp.sum(grad_normed, axis=0, keepdims=True)
    line.sent(4, ps0)
    grad_gating = split_sum(cot * (base[...] - arrived[...])) + dots[z][:, 0:1]
    for d in (1, 3, 2):
        line.got(5, d, dots_in.at[line.index(d)])
        grad_gating += dots_in[line.index(d)][:, 0:1]
    gate = gates[z][:, 0:1]
    grad_logit = gate * (1.0 - gate) * grad_gating
    vmine[4:5, :] = jnp.sum(grad_logit * arrived[...], axis=0, keepdims=True)
    base[...] = grad_stream + (1.0 - gate) * cot + grad_logit * vec[4:5, :]
    join_cores(1)
    kept = [
        pltpu.make_async_copy(sb_in.at[1], gin1, osem.at[1, 0]),
        pltpu.make_async_copy(sb_out.at[1], gout1, osem.at[1, 1]),
    ]
    given = [
        remote(sb_in.at[1], gin1, ss.at[1], sr.at[1], at.swap_mate),
        remote(sb_out.at[1], gout1, ss.at[2], sr.at[2], at.swap_mate),
    ]

    def begin(copies):
        for copy in copies:
            copy.start()

    def finish(copies):
        for copy in copies:
            copy.wait()

    on_either(lambda: begin(kept), lambda: begin(given))

    def sub0_back(i, carry):
        d = order(i)
        j = line.index(d)

        line.ready(6, i, g0)
        backward(0, j, g0, dg0, gp0, ps0)

        @pl.when(i > 0)
        def _():
            line.give(7, d, ps0, pb0)

        return carry

    lax.fori_loop(0, 4, sub0_back, 0)
    weight_grads(0, e0, gp0, act0, g0)
    swap(0, 0).start()
    swap(0, 1).start()
    grad_normed = line.total(7, ps0, pb0)
    grad_stream = base[...] + norm_back(grad_normed, gain[0], xh0[...], sc[0][:, 0:1])
    sendg[...] = pieces_of(grad_stream)
    plane.start(1, piece(sendg), piece(arrg))
    keep_piece(at, sendg, arrg)
    vmine[0:1, :] = jnp.sum(grad_normed * xh0[...], axis=0, keepdims=True)
    vmine[2:3, :] = jnp.sum(grad_normed, axis=0, keepdims=True)
    vmine[5:8, :] = jnp.zeros((3, 1024), jnp.float32)
    give_core = remote(vmine, vcore, vs.at[0], vr.at[0], at.other)
    give_core.start()
    give_core.wait_recv()
    vline[z] = vmine[...] + vcore[...]

    def give_line(d):
        return line.copy(8, d, vline.at[z], vline.at[z])

    for d in (1, 3, 2):
        give_line(d).start()
    join_cores(0)
    stores = [
        pltpu.make_async_copy(sb_in.at[0], gin0, osem.at[0, 0]),
        pltpu.make_async_copy(sb_out.at[0], gout0, osem.at[0, 1]),
    ]
    begin(stores)
    plane.wait(1, piece(arrg))
    left, right = placings(route[0:1, :])
    gh[...] = from_pieces(left, right, arrg[...])
    for d in (1, 3, 2):
        line.got(8, d, vline.at[line.index(d)])
    vecg[...] = vline[0] + vline[1] + vline[2] + vline[3]
    give_core.wait_send()
    for d in (1, 3, 2):
        give_line(d).wait_send()
        gate_copy(d).wait_send()
        line.copy(5, d, dots.at[line.index(d)], dots_in.at[z]).wait_send()
    for k in (0, 1):
        for i in range(2):
            share(k, i).wait_send()
    line.sent_all(0, e0)
    line.sent_all(2, e1)
    line.sent_all(6, g0)
    line.sent(7, ps0)
    plane.sent(0, piece(sendh), piece(arrh))
    plane.sent(1, piece(sendg), piece(arrg))
    keep_ps.wait()
    finish(stores)
    on_either(lambda: finish(kept), lambda: finish(given))


def expert_call(hid, route, exp_gain, exp_bias, centroid, cz, exp_in, exp_out, in0, out0):
    bf, f32 = jnp.bfloat16, jnp.float32
    vmem, anywhere = pl.BlockSpec(memory_space=pltpu.VMEM), pl.BlockSpec(memory_space=pl.ANY)
    shape, V, dma = jax.ShapeDtypeStruct, pltpu.VMEM, pltpu.SemaphoreType.DMA
    line, rows, pieces = [V((512, 1024), bf)], [V((128, 1024), f32)], [V((256, 512), bf)]
    wide, small = [V((512, 1024), f32)], [V((4, 128, 128), f32)]
    vectors = [V((8, 1024), f32)]
    return pl.pallas_call(
        expert_kernel,
        out_shape=(
            shape((128, 1024), bf), shape((8, 1024), f32), shape((128, 1024), f32), shape((128, 128), f32),
            shape((512, 1024), bf), shape((1024, 512), bf), shape((512, 1024), bf), shape((1024, 512), bf),
            shape((512, 1024), bf),
        ),
        in_specs=[vmem] * 5 + [anywhere] * 5,
        out_specs=tuple([vmem] * 4 + [anywhere] * 5),
        scratch_shapes=[
            V((2, 1024, 1024), bf), V((2, 1024, 1024), bf), *(pieces * 4), *line,
            *(line * 9), *(line * 2), *(wide * 2), *(line * 2),
            *(rows * 4), *(small * 4),
            V((2, 1024, 512), f32), V((2, 512, 1024), f32),
            V((2, 1024, 512), bf), V((2, 512, 1024), bf), V((2, 1024, 512), bf), V((2, 512, 1024), bf),
            *(vectors * 5), V((4, 8, 1024), f32),
            dma((3, 2)), dma((9, 6)), dma((9, 6)), dma((2, 15)), dma((2, 15)), dma((2, 2)), dma((2, 2)), dma((2, 2)),
            dma((2, 2)), dma((2, 2)), dma((4,)), dma((4,)), dma((3,)), dma((3,)),
        ],
        compiler_params=pltpu.CompilerParams(collective_id=1, has_side_effects=True, vmem_limit_bytes=60 << 20),
        name="experts",
    )(hid, route, exp_gain, exp_bias, centroid, cz, exp_in, exp_out, in0, out0)


class Everyone:
    def __init__(self, at, send, recv):
        self.at, self.send, self.recv = at, send, recv

    def copy(self, phase, i, buf):
        own = buf.at[self.at.s]
        to = (lax.rem(self.at.s + i + 1, 8), self.at.f)
        return remote(own, own, self.send.at[phase, i], self.recv.at[phase, i], to)

    def start(self, phase, buf):
        for i in range(7):
            self.copy(phase, i, buf).start()

    def wait(self, phase, buf):
        for i in range(7):
            q = lax.rem(self.at.s + 7 - i, 8)
            dst = buf.at[q]
            remote(dst, dst, self.send.at[phase, i], self.recv.at[phase, i], (q, self.at.f)).wait_recv()

    def sent(self, phase, buf):
        for i in range(7):
            self.copy(phase, i, buf).wait_send()


def dense_backward_kernel(
    gh, after, docs, gains, mixed, route, mid, gate, vec_sum, x_h, n1_h, n2_h, act_h, dg_h, q_h, kv_h, kvo_h, wq_h, wo_h, wu_h,
    wd_h, ps_h, gin0, gout0,
    gx, bd, bu, bo, bq, gvec, res, vec_swap, fin0, fout0,
    ghs, xa, xh, n1, n2, act, dg, gp, qb, kvb, kvo, wq, wo, wu, wd,
    ps, pr, ps2, pr2, ps3, pr3, prob, gms, gm, dp, dkv, dkvo, kvs, kvr,
    md, mu, mo, mq, mkv, td, tu, to, tq, tkv, rd, ru, ro, rq, rkv, xd, xu, xo, sd, su, so, yd, yu, yo, rp, rpkv, sendr, arrr,
    vmine, vcore, vplane, vline, outz,
    lsem, zs, zr, xs, xr, ys, yr, kvss, kvsr, ks, kr, cs, cr, qs, qr, ss, sr, vs, vr, fs, fr,
):
    at = Place()
    z, yh, c, col = at.z, at.yh, at.c, at.col
    line, ring_x, ring_y = Ring(at, "z", zs, zr), Ring(at, "x", xs, xr), Ring(at, "y", ys, yr)
    plane, everyone = Plane(at, cs, cr), Everyone(at, qs, qr)
    bar = pltpu.get_barrier_semaphore()
    plane.greet(bar)
    for d in (1, 2, 3):
        greet(bar, line.device(line.index(d)))
        greet(bar, (2 * line.index(d) + 1 - yh, at.f))
    greet(bar, at.other)
    greet(bar, at.swap_mate)
    loads = [
        pltpu.make_async_copy(src, dst, lsem.at[k])
        for k, (src, dst) in enumerate(
            [
                (q_h, qb), (kv_h, kvb), (kvo_h, kvo), (wd_h, wd), (dg_h, dg), (wu_h, wu), (act_h, act), (n2_h, n2),
                (wo_h, wo), (ps_h, ps3), (wq_h, wq), (n1_h, n1), (x_h, xa),
            ]
        )
    ]
    for load in loads:
        load.start()
    ghs[block(z), :] = gh[...]
    pl.semaphore_wait(bar, 23)
    line.begin(0, ghs)
    swaps = [
        remote(gin0, fin0, ss.at[0], sr.at[0], at.swap_mate),
        remote(gout0, fout0, ss.at[1], sr.at[1], at.swap_mate),
    ]
    give_vec = remote(vec_sum, vec_swap, ss.at[2], sr.at[2], at.swap_mate)

    @pl.when(jnp.logical_not(at.same))
    def _():
        give_vec.start()
        for swap in swaps:
            swap.start()

    for load in loads[:3]:
        load.wait()
    for j in range(4):
        seen = [mask(j, yh, parity, docs) for parity in (yh, 1 - yh)]
        wide = slice(0, 128 * (j + 1))
        for p in range(2):
            lanes = slice(128 * p, 128 * p + 128)
            keys = [kvb[wide, lanes], kvo[wide, lanes]]
            q = qb[128 * j : 128 * j + 128, lanes]
            for h in range(2):
                found = probabilities(only(head_lanes(h), q), keys, seen)
                for k in range(2):
                    prob[k, 4 * j + 2 * p + h, :, wide] = found[k].astype(jnp.bfloat16)
    for load in loads[3:6]:
        load.wait()

    def feed(i, carry):
        d = order(i)
        j = line.index(d)

        line.ready(0, i, ghs)
        values = ghs[block(j), :]
        for n in range(4):
            tile = slice(n * 256, (n + 1) * 256)
            gp[block(j), tile] = (dg[block(j), tile] * nt(values, tall_tile(wd, n))).astype(jnp.bfloat16)
        pres = gp[block(j), :]
        for n in range(4):
            tile = slice(n * 256, (n + 1) * 256)
            ps[block(j), tile] = nt(pres, tall_tile(wu, n)).astype(jnp.bfloat16)

        @pl.when(i > 0)
        def _():
            line.give(1, d, ps, pr)

        return carry

    lax.fori_loop(0, 4, feed, 0)
    for load in loads[6:10]:
        load.wait()

    def weight_grad(lhs, rhs, mine, theirs):
        def one(n, carry):
            rows = lhs[:, pl.ds(pl.multiple_of(n * 256, 256), 256)]
            grad = tn(rows, rhs[...])
            for half in range(2):
                first = grad[128 * half : 128 * half + 64].astype(jnp.bfloat16)
                second = grad[128 * half + 64 : 128 * half + 128].astype(jnp.bfloat16)
                here = lax.div(n, 2), 2 * lax.rem(n, 2) + half
                mine[here] = jnp.where(c == 0, first, second)
                theirs[here] = jnp.where(c == 0, second, first)
            return carry

        lax.fori_loop(0, 4, one, 0)

    def core_copy(phase, src, dst):
        return remote(src, dst, ks.at[phase], kr.at[phase], at.other)

    def join_cores(phase, mine, theirs, got):
        core_copy(phase, theirs, got).wait()

        def one(n, carry):
            here = lax.div(n, 4), lax.rem(n, 4)
            mine[here] = (mine[here].astype(jnp.float32) + got[here].astype(jnp.float32)).astype(jnp.bfloat16)
            return carry

        lax.fori_loop(0, 8, one, 0)

    def x_copy(phase, d, mine, dst):
        return ring_x.copy(phase, d, mine.at[:, ring_x.index(d)], dst.at[at.x])

    def y_copy(phase, d, part, dst):
        j = ring_y.index(d)
        src = part.at[lax.rem(j, 2), pl.ds(pl.multiple_of(32 * lax.div(j, 2), 32), 32)]
        return ring_y.copy(phase, d, src, dst.at[ring_y.pos])

    def to_x(phase, mine, dst):
        for d in (1, 3, 2):
            x_copy(phase, d, mine, dst).start()

    def to_y(phase, mine, got, part, dst):
        acc = mine[:, at.x].astype(jnp.float32)
        for d in (1, 3, 2):
            j = ring_x.index(d)
            ring_x.got(phase, d, got.at[j])
            acc += got[j].astype(jnp.float32)
        part[...] = acc.astype(jnp.bfloat16)
        for d in (1, 3, 2):
            y_copy(phase, d, part, dst).start()

    def fin_copy(phase, d, buf):
        own = buf.at[yh, z]
        return line.copy(phase, d, own, own)

    def fin_mate(phase, buf):
        own = buf.at[yh]
        return remote(own, own, fs.at[phase], fr.at[phase], at.mate)

    def fin_z(phase, buf, values):
        buf[yh, z] = values.astype(jnp.bfloat16)
        for d in (1, 3, 2):
            fin_copy(phase, d, buf).start()

    def fin_y(phase, buf):
        for d in (1, 3, 2):
            line.got(phase, d, buf.at[yh, line.index(d)])
        fin_mate(phase, buf).start()

    def fin_wait(phase, buf):
        dst = buf.at[1 - yh]
        remote(dst, dst, fs.at[phase], fr.at[phase], at.mate).wait_recv()

    def y_total(phase, part, got):
        acc = part[at.yl, pl.ds(pl.multiple_of(32 * yh, 32), 32), :].astype(jnp.float32)
        for d in (1, 3, 2):
            j = ring_y.index(d)
            ring_y.got(phase, d, got.at[j])
            acc += got[j].astype(jnp.float32)
        return acc

    def y_first(phase, d, mine, dst):
        j = ring_y.index(d)
        src = mine.at[lax.rem(j, 2), :, pl.ds(pl.multiple_of(32 * lax.div(j, 2), 32), 32)]
        return ring_y.copy(phase, d, src, dst.at[ring_y.pos])

    def x_second(phase, d, part, dst):
        return ring_x.copy(phase, d, part.at[ring_x.index(d)], dst.at[at.x])

    def turn_to_x(phase, mine, got, part, dst):
        acc = mine[at.yl, :, pl.ds(pl.multiple_of(32 * yh, 32), 32), :].astype(jnp.float32)
        for d in (1, 3, 2):
            j = ring_y.index(d)
            ring_y.got(phase, d, got.at[j])
            acc += got[j].astype(jnp.float32)
        part[...] = acc.astype(jnp.bfloat16)
        for d in (1, 3, 2):
            x_second(phase, d, part, dst).start()

    def x_total(phase, part, got):
        acc = part[at.x].astype(jnp.float32)
        for d in (1, 3, 2):
            j = ring_x.index(d)
            ring_x.got(phase, d, got.at[j])
            acc += got[j].astype(jnp.float32)
        return acc

    weight_grad(act, ghs, md, td)
    core_copy(0, td, rd).start()
    weight_grad(n2, gp, mu, tu)
    core_copy(1, tu, ru).start()
    join_cores(0, md, td, rd)
    to_x(0, md, xd)
    join_cores(1, mu, tu, ru)
    for d in (1, 3, 2):
        y_first(1, d, mu, xu).start()
    grad_normed = line.total(1, ps, pr)
    xhat, scale = norm_parts(after[...])
    vmine[1:2, :] = jnp.sum(grad_normed * xhat, axis=0, keepdims=True)
    vmine[3:4, :] = jnp.sum(grad_normed, axis=0, keepdims=True)
    grad_after = gh[...].astype(jnp.float32) + norm_back(grad_normed, gains[1:2, :], xhat, scale)
    gx[...] = grad_after
    grad_attn = grad_after.astype(jnp.bfloat16)
    for n in range(4):
        gms[:, 256 * n : 256 * n + 256] = nt(grad_attn, tall_tile(wo, n)).astype(jnp.bfloat16)

    def gm_copy(d):
        lanes = pl.ds(pl.multiple_of(256 * line.index(d), 256), 256)
        return line.copy(2, d, gms.at[:, lanes], gm.at[block(z)])

    for d in (1, 3, 2):
        gm_copy(d).start()
    gm[block(z), :] = gms[:, pl.ds(pl.multiple_of(256 * z, 256), 256)]
    gp[block(0), :] = grad_attn
    weight_grad(mixed, gp.at[block(0)], mo, to)
    core_copy(2, to, ro).start()
    for load in loads[10:]:
        load.wait()

    def normalise(j, carry):
        xh[block(j), :] = norm_parts(xa[block(j), :].astype(jnp.float32))[0]
        return carry

    lax.fori_loop(0, 4, normalise, 0)
    join_cores(2, mo, to, ro)
    to_x(2, mo, xo)
    for d in (1, 3, 2):
        line.arrived(2, d, gm)
    for d in (1, 3, 2):
        line.give(6, d, ps3, pr3)
    dkv[...] = jnp.zeros_like(dkv)
    dkvo[...] = jnp.zeros_like(dkvo)

    def kv_copy(j):
        return remote(kvs.at[block(j)], kvr.at[block(j)], kvss.at[j], kvsr.at[j], at.mate)

    def attend_back(j):
        wide = slice(0, 128 * (j + 1))
        rows = slice(128 * j, 128 * j + 128)
        for p in range(2):
            lanes = slice(128 * p, 128 * p + 128)
            value_lanes = slice(256 + 128 * p, 384 + 128 * p)
            q, grad = qb[rows, lanes], gm[rows, lanes]
            keys = [kvb[wide, lanes], kvo[wide, lanes]]
            values = [kvb[wide, value_lanes], kvo[wide, value_lanes]]
            outs = []
            for h in range(2):
                q_h, grad_h = only(head_lanes(h), q), only(head_lanes(h), grad)
                probs = [prob[k, 4 * j + 2 * p + h, :, wide].astype(jnp.float32) for k in range(2)]
                back = [nt(grad_h, v) for v in values]
                dot = split_sum(probs[0] * back[0]) + split_sum(probs[1] * back[1])
                slopes = [(share * (b - dot)).astype(jnp.bfloat16) for share, b in zip(probs, back)]
                outs.append(nn(slopes[0], keys[0]) + nn(slopes[1], keys[1]))
                for k, acc in enumerate((dkv, dkvo)):
                    acc[wide, lanes] += tn(slopes[k], q_h) * 0.125
                    acc[wide, value_lanes] += tn(prob[k, 4 * j + 2 * p + h, :, wide], grad_h)
            dp[rows, lanes] = (jnp.where(head_lanes(0), outs[0], outs[1]) * 0.125).astype(jnp.bfloat16)
        kvs[rows, :] = dkvo[rows, :].astype(jnp.bfloat16)
        kv_copy(j).start()

    attend_back(3)
    attend_back(2)
    attend_back(1)
    attend_back(0)
    to_y(0, md, xd, sd, yd)
    weight_grad(n1, dp.at[:, 0:256], mq, tq)
    core_copy(3, tq, rq).start()
    turn_to_x(1, mu, xu, su, yu)
    vmine[0:1, :] = jnp.zeros((1, 1024), jnp.float32)
    vmine[2:3, :] = jnp.zeros((1, 1024), jnp.float32)
    vmine[4:8, :] = jnp.zeros((4, 1024), jnp.float32)
    for j in (3, 2, 1, 0):
        rows = slice(128 * j, 128 * j + 128)
        kv_copy(j).wait_recv()
        dp[rows, 256:768] = (dkv[rows, :] + kvr[rows, :].astype(jnp.float32)).astype(jnp.bfloat16)
    weight_grad(n1, dp.at[:, 256:768], mkv, tkv)
    core_copy(4, tkv, rkv).start()
    fin_z(7, bd, y_total(0, sd, yd))
    to_y(2, mo, xo, so, yo)

    def piece_of(mine):
        def at_piece(q):
            return mine.at[lax.div(q, 8), lax.rem(lax.div(q, 2), 4), pl.ds(pl.multiple_of(32 * lax.rem(q, 2), 32), 32)]

        return at_piece

    def slot_of(got):
        return lambda q: got.at[q]

    def to_plane(phase, mine, got):
        plane.start(phase, piece_of(mine), slot_of(got))
        got[at.m] = mine[at.yl, at.x, pl.ds(pl.multiple_of(32 * yh, 32), 32), :]

    def plane_total(phase, got):
        plane.wait(phase, slot_of(got))
        acc = jnp.zeros(got.shape[1:], jnp.float32)
        acc = lax.fori_loop(0, 16, lambda q, total: total + got[q].astype(jnp.float32), acc)
        return acc.astype(jnp.bfloat16)

    join_cores(3, mq, tq, rq)
    to_plane(0, mq, rp)
    join_cores(4, mkv, tkv, rkv)
    to_plane(3, mkv, rpkv)

    def last(i, carry):
        d = order(3 - i)
        j = line.index(d)
        values = dp[block(j), :]
        for n in range(4):
            tile = slice(n * 256, (n + 1) * 256)
            ps2[block(j), tile] = nt(values, tall_tile(wq, n)).astype(jnp.bfloat16)

        @pl.when(i < 3)
        def _():
            line.give(3, d, ps2, pr2)

        return carry

    lax.fori_loop(0, 4, last, 0)

    def out_copy(d):
        return line.copy(4, d, outz.at[4 + line.index(d)], outz.at[z])

    fin_z(8, bu, x_total(1, su, yu))
    total_out = y_total(2, so, yo)
    for n in range(4):
        outz[4 + n] = total_out[:, 256 * n : 256 * n + 256].astype(jnp.bfloat16)

    for d in (1, 3, 2):
        out_copy(d).start()

    def sum_rows(j, carry):
        part = ps2[block(j), :].astype(jnp.float32)
        vmine[0:1, :] += jnp.sum(part * xh[block(j), :], axis=0, keepdims=True)
        vmine[2:3, :] += jnp.sum(part, axis=0, keepdims=True)
        return carry

    lax.fori_loop(0, 4, sum_rows, 0)
    give_core = remote(vmine, vcore, vs.at[0], vr.at[0], at.other)
    give_core.start()
    fin_y(7, bd)

    def tile_of(q):
        return vmine.at[:, pl.ds(pl.multiple_of(128 * lax.div(q, 2), 128), 128)]

    give_core.wait()
    vmine[...] += vcore[...]
    plane.start(1, tile_of, slot_of(vplane))
    vplane[at.m] = vmine[:, pl.ds(pl.multiple_of(128 * col, 128), 128)]
    sendr[...] = pieces_of(mid[...] + gate[:, 0:1] * line.total(6, ps3, pr3))
    plane.start(2, piece(sendr), piece(arrr))
    keep_piece(at, sendr, arrr)
    fin_y(8, bu)
    acc = outz[4 + z].astype(jnp.float32)
    for d in (1, 3, 2):
        line.got(4, d, outz.at[line.index(d)])
        acc += outz[line.index(d)].astype(jnp.float32)
    fin_z(9, bo, acc)
    bq[at.s, :, 0:256] = plane_total(0, rp)
    bq[at.s, :, 256:768] = plane_total(3, rpkv)
    everyone.start(0, bq)
    fin_y(9, bo)
    plane.wait(1, slot_of(vplane))
    vline[z] = jnp.sum(vplane[...], axis=0)

    def vec_copy(d):
        return line.copy(5, d, vline.at[z], vline.at[z])

    for d in (1, 3, 2):
        vec_copy(d).start()
    grad_normed = line.total(3, ps2, pr2)
    scale = norm_parts(xa[block(z), :].astype(jnp.float32))[1]
    gx[...] += norm_back(grad_normed, gains[0:1, :], xh[block(z), :], scale)
    plane.wait(2, piece(arrr))
    left, right = placings(route[0:1, :])
    res[...] = from_pieces(left, right, arrr[...])
    fin_wait(7, bd)
    fin_wait(8, bu)
    for d in (1, 3, 2):
        line.got(5, d, vline.at[line.index(d)])
    gvec[...] = jnp.sum(vline[...], axis=0)
    fin_wait(9, bo)
    everyone.wait(0, bq)
    if_swapped = jnp.logical_not(at.same)
    pl.when(if_swapped)(lambda: give_vec.wait())
    line.sent_all(0, ghs)
    line.sent(1, ps)
    line.sent(3, ps2)
    line.sent(6, ps3)
    for d in (1, 3, 2):
        gm_copy(d).wait_send()
        out_copy(d).wait_send()
        vec_copy(d).wait_send()
        for phase, mine, x_got, part, y_got in ((0, md, xd, sd, yd), (2, mo, xo, so, yo)):
            x_copy(phase, d, mine, x_got).wait_send()
            y_copy(phase, d, part, y_got).wait_send()
        y_first(1, d, mu, xu).wait_send()
        x_second(1, d, su, yu).wait_send()
    for j in range(4):
        kv_copy(j).wait_send()
    plane.sent(0, piece_of(mq), slot_of(rp))
    plane.sent(3, piece_of(mkv), slot_of(rpkv))
    plane.sent(1, tile_of, slot_of(vplane))
    plane.sent(2, piece(sendr), piece(arrr))
    everyone.sent(0, bq)
    for phase, buf in ((7, bd), (8, bu), (9, bo)):
        fin_mate(phase, buf).wait_send()
        for d in (1, 3, 2):
            fin_copy(phase, d, buf).wait_send()

    @pl.when(jnp.logical_not(at.same))
    def _():
        for swap in swaps:
            swap.wait()


def dense_backward_call(gh, after, docs, gains, mixed, route, mid, gate, vec_sum, saved, ps, gin0, gout0):
    bf, f32 = jnp.bfloat16, jnp.float32
    vmem, anywhere = pl.BlockSpec(memory_space=pltpu.VMEM), pl.BlockSpec(memory_space=pl.ANY)
    smem = pl.BlockSpec(memory_space=pltpu.SMEM)
    shape, V, dma = jax.ShapeDtypeStruct, pltpu.VMEM, pltpu.SemaphoreType.DMA
    line, pieces = [V((512, 1024), bf)], [V((256, 512), bf)]
    wide, narrow = [V((2, 4, 64, 1024), bf)], [V((2, 4, 64, 256), bf), V((2, 4, 64, 512), bf)]
    return pl.pallas_call(
        dense_backward_kernel,
        out_shape=[
            shape((128, 1024), f32), shape((2, 4, 32, 1024), bf), shape((2, 4, 32, 1024), bf),
            shape((2, 4, 32, 256), bf), shape((8, 32, 768), bf), shape((8, 128), f32), shape((128, 1024), bf),
            shape((8, 1024), f32), shape((1024, 512), bf),
            shape((512, 1024), bf),
        ],
        in_specs=[vmem, vmem, smem] + [vmem] * 6 + [anywhere] * 15,
        out_specs=[vmem] * 8 + [anywhere] * 2,
        scratch_shapes=[
            *(line * 2), V((512, 1024), f32), *(line * 3), V((512, 1024), f32), *line,
            V((512, 256), bf), V((512, 512), bf), V((512, 512), bf),
            V((2, 4, 2, 2, 32, 768), bf), *([V((2, 4, 2, 2, 32, 1024), bf)] * 3),
            *(line * 6), V((2, 16, 128, 512), bf),
            V((128, 1024), bf), V((512, 256), bf), V((512, 768), bf), V((512, 512), f32), V((512, 512), f32),
            V((512, 512), bf), V((512, 512), bf),
            *(wide * 3), *narrow, *(wide * 3), *narrow, *(wide * 3), *narrow,
            V((4, 2, 64, 1024), bf), V((4, 4, 32, 1024), bf), V((4, 2, 64, 1024), bf),
            V((2, 64, 1024), bf), V((4, 32, 1024), bf), V((2, 64, 1024), bf), *([V((4, 32, 1024), bf)] * 3),
            V((16, 32, 256), bf), V((16, 32, 512), bf), *(pieces * 2),
            V((8, 1024), f32), V((8, 1024), f32), V((16, 8, 128), f32), V((4, 8, 128), f32),
            V((8, 32, 256), bf),
            dma((13,)), dma((10, 6)), dma((10, 6)), dma((3, 3)), dma((3, 3)), dma((3, 3)), dma((3, 3)), dma((4,)),
            dma((4,)), dma((5,)), dma((5,)), dma((4, 15)), dma((4, 15)), dma((1, 7)), dma((1, 7)), dma((3,)),
            dma((3,)), dma((1,)), dma((1,)), dma((10,)), dma((10,)),
        ],
        compiler_params=pltpu.CompilerParams(collective_id=3, has_side_effects=True, vmem_limit_bytes=62 << 20),
        name="dense_backward",
    )(gh, after, docs, gains, mixed, route, mid, gate, vec_sum, *saved, ps, gin0, gout0)


def finish_kernel(
    gvec, vec_sum, vec_swap, res, gx, bd, bu, bo, bq, in0, in1, out0, out1, swapped_in, swapped_out,
    ng, nb, eg, eb, cen, o_res, o_gx, o_gq, o_go, o_gu, o_gd, o_in, o_out,
    b_in, b_out, f_in, f_out, vd, vu, vo, vq, gq, go, gu, gd, vres, vgx, isem, osem,
):
    at = Place()
    swapped = [
        pltpu.make_async_copy(swapped_in, b_in.at[0], isem.at[0]),
        pltpu.make_async_copy(swapped_out, b_out.at[0], isem.at[2]),
    ]
    pairs = [
        (in0, b_in.at[0]), (in1, b_in.at[1]), (out0, b_out.at[0]), (out1, b_out.at[1]), (bd, vd), (bu, vu), (bo, vo),
        (bq, vq), (res, vres), (gx, vgx),
    ]
    loads = [pltpu.make_async_copy(src, dst, isem.at[k]) for k, (src, dst) in enumerate(pairs)]

    @pl.when(at.same)
    def _():
        loads[0].start()
        loads[2].start()

    @pl.when(jnp.logical_not(at.same))
    def _():
        for copy in swapped:
            copy.start()

    for k in (1, 3, 4, 5, 6, 7, 8, 9):
        loads[k].start()
    c = at.c
    mine = jnp.where(c == 0, gvec[0:4, 0:64], gvec[0:4, 64:128])
    ng[...] = mine[0:2]
    nb[...] = mine[2:4]
    vectors = jnp.where(at.same, vec_sum[...], vec_swap[...])
    eg[...] = vectors[0:2]
    eb[...] = vectors[2:4]
    cen[...] = vectors[4:5]
    stores = []

    def store(src, dst):
        stores.append(pltpu.make_async_copy(src, dst, osem.at[len(stores)]))
        stores[-1].start()

    for k in range(4):
        loads[k].wait()
        low, wide, out = ((b_in, f_in, o_in), (b_out, f_out, o_out))[k // 2]
        wide[k % 2] = low[k % 2].astype(jnp.float32)
        store(wide.at[k % 2], out.at[k % 2])
    for k in range(4, 10):
        loads[k].wait()
    store(vres, o_res)
    store(vgx, o_gx)
    lane = lax.broadcasted_iota(jnp.int32, (32, 128), 1) < 64
    for half in range(2):
        rows = slice(32 * half, 32 * half + 32)
        for z in range(4):
            gd[64 * z + 32 * half : 64 * z + 32 * half + 32, :] = vd[half, z].astype(jnp.float32)
            go[rows, 256 * z : 256 * z + 256] = vo[half, z].astype(jnp.float32)
            for part in range(3):
                gq[rows, 1024 * part + 256 * z : 1024 * part + 256 * z + 256] = vq[
                    2 * z + half, :, 256 * part : 256 * part + 256
                ].astype(jnp.float32)
        for n in range(8):
            tile = slice(128 * n, 128 * n + 128)
            quarter = [vu[half, z, :, tile].astype(jnp.float32) for z in range(4)]
            turned = [pltpu.roll(v, 64, 1) for v in quarter]
            first = 512 * n
            gu[rows, first : first + 128] = jnp.where(lane, quarter[0], turned[1])
            gu[rows, first + 128 : first + 256] = jnp.where(lane, quarter[2], turned[3])
            gu[rows, first + 256 : first + 384] = jnp.where(lane, turned[0], quarter[1])
            gu[rows, first + 384 : first + 512] = jnp.where(lane, turned[2], quarter[3])
    for src, dst in ((gq, o_gq), (go, o_go), (gu, o_gu), (gd, o_gd)):
        store(src, dst)
    for copy in stores:
        copy.wait()


def finish_call(gvec, vec_sum, vec_swap, res, gx, bd, bu, bo, bq, in0, in1, out0, out1, swapped_in, swapped_out):
    bf, f32 = jnp.bfloat16, jnp.float32
    vmem, anywhere = pl.BlockSpec(memory_space=pltpu.VMEM), pl.BlockSpec(memory_space=pl.ANY)
    shape, V, dma = jax.ShapeDtypeStruct, pltpu.VMEM, pltpu.SemaphoreType.DMA
    return pl.pallas_call(
        finish_kernel,
        out_shape=[
            shape((2, 64), f32), shape((2, 64), f32), shape((2, 1024), f32), shape((2, 1024), f32),
            shape((1, 1024), f32), shape((128, 1024), bf), shape((128, 1024), f32), shape((64, 3072), f32),
            shape((64, 1024), f32), shape((64, 4096), f32), shape((256, 1024), f32), shape((2, 1024, 512), f32),
            shape((2, 512, 1024), f32),
        ],
        in_specs=[vmem] * 3 + [anywhere] * 12,
        out_specs=[vmem] * 5 + [anywhere] * 8,
        scratch_shapes=[
            V((2, 1024, 512), bf), V((2, 512, 1024), bf), V((2, 1024, 512), f32), V((2, 512, 1024), f32),
            V((2, 4, 32, 1024), bf), V((2, 4, 32, 1024), bf), V((2, 4, 32, 256), bf), V((8, 32, 768), bf),
            V((64, 3072), f32), V((64, 1024), f32), V((64, 4096), f32), V((256, 1024), f32),
            V((128, 1024), bf), V((128, 1024), f32), dma((10,)), dma((10,)),
        ],
        compiler_params=pltpu.CompilerParams(vmem_limit_bytes=62 << 20),
        name="finish",
    )(gvec, vec_sum, vec_swap, res, gx, bd, bu, bo, bq, in0, in1, out0, out1, swapped_in, swapped_out)


def on_device(
    inputs,
    doc_starts,
    route,
    norm_gain,
    norm_bias,
    w_qkv,
    w_out,
    w_up,
    w_down,
    exp_gain,
    exp_bias,
    exp_in,
    exp_out,
    centroid,
    cotangent,
):
    tok_rows, width = 128, 1024
    x = inputs.reshape(tok_rows, width)
    cot = cotangent.reshape(tok_rows, width)
    slots = route.reshape(1, tok_rows)
    hidden, mixed, after, gains, *saved, cz, in0, out0 = dense_forward_call(
        x, norm_gain, norm_bias, doc_starts, slots, cot, w_qkv, w_out, w_up, w_down, exp_in[0], exp_out[0]
    )
    grad_hidden, vec_sum, mid, gate, part, grad_in1, grad_out1, grad_in0, grad_out0 = expert_call(
        hidden, slots, exp_gain[0], exp_bias[0], centroid, cz, exp_in[0], exp_out[0], in0, out0
    )
    grad_x, down, up, out, qkv, norm_grads, result, vec_swap, swapped_in, swapped_out = dense_backward_call(
        grad_hidden, after, doc_starts, gains, mixed, slots, mid, gate, vec_sum, saved, part, grad_in0, grad_out0
    )
    gain, bias, e_gain, e_bias, center, result, grad_x, g_qkv, g_out, g_up, g_down, e_in, e_out = finish_call(
        norm_grads,
        vec_sum,
        vec_swap,
        result,
        grad_x,
        down,
        up,
        out,
        qkv,
        grad_in0,
        grad_in1,
        grad_out0,
        grad_out1,
        swapped_in,
        swapped_out,
    )
    return (
        result[None],
        grad_x[None],
        gain,
        bias,
        g_qkv,
        g_out,
        g_up,
        g_down,
        e_gain[None],
        e_bias[None],
        e_in[None],
        e_out[None],
        center,
    )


def solution(mesh):
    in_specs = (
        P("fsdp", "seq", None),
        P("fsdp", None),
        P("fsdp", "seq", None),
        P(None, "fsdp"),
        P(None, "fsdp"),
        P("fsdp", None),
        P("fsdp", None),
        P("fsdp", None),
        P("fsdp", None),
        P("fsdp", None, None),
        P("fsdp", None, None),
        P("fsdp", None, None, "seq"),
        P("fsdp", None, "seq", None),
        P("fsdp", None),
        P("fsdp", "seq", None),
    )
    out_specs = (
        P("fsdp", "seq", None),
        P("fsdp", "seq", None),
        P(None, "fsdp"),
        P(None, "fsdp"),
        P("fsdp", None),
        P("fsdp", None),
        P("fsdp", None),
        P("fsdp", None),
        P("fsdp", None, None),
        P("fsdp", None, None),
        P("fsdp", None, None, "seq"),
        P("fsdp", None, "seq", None),
        P("fsdp", None),
    )
    return jax.shard_map(
        on_device, mesh=mesh, in_specs=in_specs, out_specs=out_specs, check_vma=False
    )
```
